32 devices in a mesh: dp: 2 (over x), expert: 16 (over z, y, core).
Axes of the slice: x: 2, y: 2, z: 4, core: 2. Of those that a mesh axis runs over, the one named last changes fastest.
Arguments:
- grad_out: bfloat16 [4096, 2048], P(('dp', 'expert')), may hold values from -6 to 6
- gates: bfloat16 [4096, 6], P(('dp', 'expert')), may hold values from 0.049804688 to 0.59765625
- routes: int32 [4096, 6], P(('dp', 'expert')), may hold values from 0 to 15, all different within a row; in each aligned block of 128 rows (0 to 127, 128 to 255, ...) at most 64 rows name the same one
- hidden: bfloat16 [2, 16, 1024, 704], P('dp', 'expert'), may hold values from -0.23925781 to 0.23925781
- down_weight: bfloat16 [16, 704, 2048], P('expert', 'dp'), may hold values from -0.125 to 0.125
Outputs:
- grad_weight: bfloat16 [16, 704, 2048], P('expert', 'dp')
- grad_hidden: bfloat16 [2, 16, 1024, 704], P('dp', 'expert')
- grad_gates: float32 [4096, 6], P(('dp', 'expert'))
The draws below stay inside these ranges and needn't reach their ends.
Inputs may be any that keep to these rules, and one draw needn't show every extreme that they name: `routes`: each row names 6 different experts; within the rows of one device no expert is named more than 64 times, a bound that some block reaches.
All inputs are finite; a program needn't handle non-finite values.
Results may differ from the reference program's by a relative error of at most 0.017.
Values may be sent and summed in bfloat16 or wider, within the bound.
No kernel may reach another device: no remote copies, remote signals or barrier semaphores. Data moves between devices by JAX's collectives and lax.ppermute only.
A program may use at most 64 MiB of HBM per device.

```python
import math
from functools import partial
import jax
import jax.numpy as jnp
import numpy as np
from jax import lax

D = 2048
TOP = 6
HID = 704
TOK_DEV = 128
EXPERTS = 16
CAP = 64
TOKENS = 4096
N_DP = 2
N_EXPERT = 16


def block_levels(rng, dims, cuts, low, top_value):
    def one(dim, parts):
        draws = jax.random.uniform(jax.random.fold_in(jax.random.fold_in(rng, 6), dim), (parts,), jnp.float32, low / len(cuts), top_value / len(cuts))
        return jnp.repeat(jnp.exp(draws), dims[dim] // parts).reshape((-1,) + (1,) * (len(dims) - dim - 1))

    gain = one(*cuts[0])
    for cut in cuts[1:]:
        gain = gain * one(*cut)
    return gain


def routed_block(rng, own, number, rows, count, top, most, lean):
    sequence = jax.random.permutation(rng, count)
    heavy_load, ordinary = portions_of(count, rows * top, most, lean, True), portions_of(count, rows * top, most, lean, False)
    places = jnp.arange(count)

    def named(tallies, rotation):
        used = int((tallies > 0).sum())
        fixed = max(1, used // 4)
        shifted = fixed + (places - fixed + rotation * (used - fixed)) % max(1, count - fixed)
        return jnp.zeros((count,), jnp.int32).at[sequence[jnp.where(places < fixed, places, shifted)]].set(jnp.asarray(tallies, jnp.int32))

    tallies = jnp.where(number % 4 == 0, named(heavy_load, number // 4), named(ordinary, number - number // 4 - 1))
    mixed = jax.random.permutation(jax.random.fold_in(own, 3), count)
    donor, taker = mixed[0:count // 2 * 2:2], mixed[1:count // 2 * 2:2]
    room = jnp.minimum(tallies[donor] - 1, most - tallies[taker]) // 2
    room = jnp.where((donor == sequence[0]) | (taker == sequence[0]) | (tallies[taker] == 0), 0, jnp.maximum(room, 0))
    shifted = jax.random.randint(jax.random.fold_in(own, 4), (count // 2,), 0, 1 << 20) % (room + 1)
    tallies = tallies.at[donor].add(-shifted).at[taker].add(shifted)
    items = jnp.searchsorted(jnp.cumsum(tallies), jnp.arange(rows * top), side="right").astype(jnp.int32)
    table = items.reshape(top, rows).T
    table = table[jax.random.permutation(jax.random.fold_in(own, 1), rows)]
    rotation = jax.random.randint(jax.random.fold_in(own, 2), (rows, 1), 0, top)
    return jnp.take_along_axis(table, (jnp.arange(top)[None, :] + rotation) % top, axis=1)


def portions_of(count, total, reach, lean, full):
    loads = [(1 << 20) // math.isqrt(standing ** lean) + 1 for standing in range(1, count + 1)]
    largest = reach if full else min(reach, max(-(-total // count), total * loads[0] // sum(loads)))
    least = 1 if total - largest >= count - 1 else 0
    given, rest = [largest] + [least] * (count - 1), total - largest - least * (count - 1)
    while rest > 0:
        free = [i for i in range(1, count) if given[i] < largest] or [i for i in range(1, count) if given[i] < reach]
        pool, budget = sum([loads[i] for i in free]), rest
        for i in free:
            extra = min(reach - given[i], max(1, budget * loads[i] // pool), rest)
            given[i] = given[i] + extra
            rest = rest - extra
    return np.array(given)


def normal_values(rng, extent, scale, reach, pieces=(), kind=jnp.bfloat16):
    values = jax.random.normal(rng, extent, jnp.float32) * scale
    if len(pieces) > 0:
        values = block_levels(rng, extent, pieces, -0.22, 0.18) * values
    return jnp.clip(values, min=-reach, max=reach).astype(kind)


def setup_inputs(seed: int = 0) -> dict:
    splits = jax.random.split(jax.random.key(seed), 6)
    grad_out = normal_values(splits[0], (TOKENS, D), 1.0, 6.0, ((0, 32),))
    gates = jnp.clip(0.049804688 + 0.54785156 * jax.random.uniform(splits[1], (TOKENS, TOP), jnp.float32) ** block_levels(splits[1], (TOKENS, TOP), ((0, 32),), -0.2, 0.2), 0.049804688, 0.59765625).astype(jnp.bfloat16)
    routes_keys = jax.random.split(jax.random.fold_in(splits[2], 1), TOKENS // TOK_DEV)
    routes_turns = jax.random.permutation(jax.random.fold_in(splits[2], 3), TOKENS // TOK_DEV)
    routes = jax.vmap(lambda own, number: routed_block(jax.random.fold_in(splits[2], 2), own, number, TOK_DEV, EXPERTS, TOP, CAP, 2))(routes_keys, routes_turns).reshape((TOKENS, TOP))
    hidden = normal_values(splits[3], (N_DP, EXPERTS, N_EXPERT * CAP, HID), 0.04, 0.23925781, ((0, 2), (1, 16)))
    down_weight = normal_values(splits[4], (EXPERTS, HID, D), D ** -0.5, 0.125, ((0, 16), (1, 2)))
    return {"grad_out": grad_out, "gates": gates, "routes": routes, "hidden": hidden, "down_weight": down_weight}


def group_pass(down_weight, accum, inputs):
    grad_rows, gate_rows, route_rows, saved = inputs
    owners = N_EXPERT
    flat = route_rows.reshape(owners, TOK_DEV * TOP)
    onehot = (flat[:, :, None] == jnp.arange(EXPERTS, dtype=jnp.int32)[None, None, :]).astype(jnp.int32)
    before = jnp.cumsum(onehot, axis=1) - onehot
    slot = jnp.sum(before * onehot, axis=2)
    source = jnp.arange(owners, dtype=jnp.int32)[:, None]
    target = (flat * (owners * CAP) + source * CAP + slot).reshape(-1).astype(jnp.int32)
    repeated = jnp.repeat(grad_rows, TOP, axis=0)
    rows = jnp.zeros((EXPERTS * owners * CAP, D), grad_rows.dtype).at[target].set(repeated)
    rows = rows.reshape(EXPERTS, owners * CAP, D)
    gate_slots = jnp.zeros((EXPERTS * owners * CAP,), gate_rows.dtype).at[target].set(gate_rows.reshape(-1))
    gate_slots = gate_slots.reshape(EXPERTS, owners * CAP)

    def per_expert(items):
        rows_one, gate_one, saved_one, weight_one = items
        raw = jnp.dot(rows_one, weight_one.T, preferred_element_type=jnp.float32)
        factor = gate_one.astype(jnp.float32)[:, None]
        grad_hid = (factor * raw).astype(jnp.bfloat16)
        slot_grads = jnp.sum(raw * saved_one.astype(jnp.float32), axis=1)
        scaled = (factor * rows_one.astype(jnp.float32)).astype(jnp.bfloat16)
        part_grad = jnp.dot(saved_one.T, scaled, preferred_element_type=jnp.float32).astype(jnp.bfloat16)
        return grad_hid, slot_grads, part_grad

    grad_hid, slot_grads, part_grad = lax.map(per_expert, (rows, gate_slots, saved, down_weight))
    grad_gate = slot_grads.reshape(-1)[target].reshape(owners * TOK_DEV, TOP)
    return accum + part_grad.astype(jnp.float32), (grad_hid, grad_gate)


def reference(grad_out, gates, routes, hidden, down_weight):
    group_rows = N_EXPERT * TOK_DEV
    inputs = (grad_out.reshape(N_DP, group_rows, D), gates.reshape(N_DP, group_rows, TOP),
              routes.reshape(N_DP, group_rows, TOP), hidden)
    start = jnp.zeros((EXPERTS, HID, D), jnp.float32)
    accum, outputs = lax.scan(partial(group_pass, down_weight), start, inputs)
    grad_hidden, grad_gates = outputs
    return accum.astype(jnp.bfloat16), grad_hidden, grad_gates.reshape(TOKENS, TOP)
```

```python
import functools

import jax
import jax.numpy as jnp
from jax import lax
from jax.experimental import pallas as pl
from jax.experimental.pallas import tpu as pltpu
from jax.sharding import PartitionSpec as P

NZ, NY, NC = 4, 2, 2
CHUNKS = 2
LANES = 128
NT = (((1,), (1,)), ((), ()))
VMEM = pl.BlockSpec(memory_space=pltpu.VMEM)


def params(mib):
    return pltpu.CompilerParams(vmem_limit_bytes=mib * 2**20)


def ring(z):
    return z ^ (z >> 1)


def ring_pairs():
    size = NY * NC
    return [
        (ring(p) * size + rest, ring((p + 1) % NZ) * size + rest)
        for p in range(NZ)
        for rest in range(size)
    ]


def swap_pairs(bit):
    return [(i, i ^ bit) for i in range(NZ * NY * NC)]


def pack_kernel(experts, width, routes_ref, gates_ref, grad_ref, *outs):
    chosen, tokens = routes_ref.shape
    routes = routes_ref[...]
    gates = gates_ref[...].astype(jnp.float32)
    expert = lax.broadcasted_iota(jnp.int32, (experts, tokens), 0)
    dense = jnp.zeros((experts, tokens), jnp.float32)
    named = jnp.zeros((experts, tokens), jnp.float32)
    for k in range(chosen):
        hit = routes[k : k + 1, :] == expert
        dense = jnp.where(hit, gates[k : k + 1, :], dense)
        named = jnp.where(hit, 1.0, named)
    earlier = (
        lax.broadcasted_iota(jnp.int32, (tokens, tokens), 0)
        < lax.broadcasted_iota(jnp.int32, (tokens, tokens), 1)
    )
    slots = jnp.dot(
        named.astype(jnp.bfloat16),
        jnp.where(earlier, 1.0, 0.0).astype(jnp.bfloat16),
        preferred_element_type=jnp.float32,
    )
    slots = jnp.where(named > 0, slots, -1.0)
    outs[0][:, :width] = grad_ref[:, :width]
    outs[0][:, width:] = jnp.zeros((tokens, tokens), jnp.bfloat16)
    outs[0][:experts, width:] = dense.astype(jnp.bfloat16)
    outs[0][experts : 2 * experts, width:] = slots.astype(jnp.bfloat16)
    for c in range(1, len(outs)):
        outs[c][...] = grad_ref[:, c * width : (c + 1) * width]


def pair_place(arrival):
    index = lax.axis_index("expert")
    z, y = index >> 2, (index >> 1) & 1
    z = ring((ring(z) - arrival // NY) & (NZ - 1))
    return z * NY + (y ^ (arrival % NY))


def products(half, width, hs_ref, rows_ref, send_ref, own_ref, n):
    mine = lax.axis_index("dp")
    cols = pl.ds(pl.multiple_of(n * 256, 256), 256)
    block = rows_ref[:, cols]
    other = hs_ref[pl.ds(pl.multiple_of((1 - mine) * half, 16), half), :]
    send_ref[:, cols] = jnp.dot(other, block, preferred_element_type=jnp.float32).astype(
        jnp.bfloat16
    )
    own = hs_ref[pl.ds(pl.multiple_of(mine * half, 16), half), :]
    own_ref[:, cols] = jnp.dot(own, block, preferred_element_type=jnp.float32)


def dispatch(xs, pmat_ref, rows_ref, n):
    cols = pl.ds(pl.multiple_of(n * 256, 256), 256)
    for a in range(len(xs) // 2):
        where = pl.ds(pl.multiple_of(pair_place(a) * LANES, LANES), LANES)
        both = jnp.concatenate([xs[2 * a][:, cols], xs[2 * a + 1][:, cols]], axis=0)
        rows_ref[where, cols] = jnp.dot(
            pmat_ref[where, :], both, preferred_element_type=jnp.float32
        ).astype(jnp.bfloat16)


def first_kernel(experts, capacity, half, width, *refs):
    n_blocks = experts
    xs = refs[:n_blocks]
    hidden_ref = refs[n_blocks]
    rows_ref, send_ref, own_ref, pmat_ref, gslot_ref, hs_ref = refs[n_blocks + 1 :]
    me = lax.axis_index("expert")
    core = me & 1
    tokens = xs[0].shape[0]
    expert = lax.broadcasted_iota(jnp.int32, (experts, tokens), 0) == me
    slot = lax.broadcasted_iota(jnp.int32, (LANES, tokens), 0).astype(jnp.float32)
    for a in range(n_blocks // 2):
        place = pair_place(a)
        where = pl.ds(pl.multiple_of(place * LANES, LANES), LANES)
        halves, gates = [], []
        for b, x_ref in enumerate((xs[2 * a], xs[2 * a + 1])):
            ext = x_ref[: 2 * experts, width:].astype(jnp.float32)
            gate = jnp.sum(jnp.where(expert, ext[:experts], 0.0), axis=0, keepdims=True)
            number = jnp.sum(jnp.where(expert, ext[experts:], 0.0), axis=0, keepdims=True)
            offset = ((core ^ b) * capacity).astype(jnp.float32)
            number = jnp.where(number >= 0, number + offset, -1.0)
            halves.append(jnp.where(slot == number, 1.0, 0.0).astype(jnp.bfloat16))
            gates.append(gate)
        one_hot = jnp.concatenate(halves, axis=1)
        pmat_ref[where, :] = one_hot
        gate_pair = jnp.concatenate(gates, axis=1).astype(jnp.bfloat16)
        gslot = lax.dot_general(
            jnp.broadcast_to(gate_pair, (16, 2 * tokens)),
            one_hot,
            NT,
            preferred_element_type=jnp.float32,
        )
        gslot_ref[:, where] = gslot[:1]
    hs_ref[...] = (hidden_ref[...].astype(jnp.float32) * gslot_ref[...]).astype(jnp.bfloat16)

    @pl.loop(0, width // 256)
    def _(n):
        dispatch(xs, pmat_ref, rows_ref, n)
        products(half, width, hs_ref, rows_ref, send_ref, own_ref, n)


def later_kernel(experts, half, width, *refs):
    xs = refs[:experts]
    pmat_ref, hs_ref, rows_ref, send_ref, own_ref = refs[experts:]

    @pl.loop(0, width // 256)
    def _(n):
        dispatch(xs, pmat_ref, rows_ref, n)
        products(half, width, hs_ref, rows_ref, send_ref, own_ref, n)


def raw_kernel(half, chunks, *refs):
    rows = refs[:chunks]
    own_ref, got_ref, hidden_ref, gslot_ref, pmat_ref, grad_ref, back_ref = refs[chunks:]
    mine = lax.axis_index("dp")
    core = lax.axis_index("expert") & 1
    step = pl.program_id(0)
    width = rows[0].shape[1]
    gates = gslot_ref[...]
    total = jnp.zeros(gates.shape, jnp.float32)
    for w_ref, d in ((own_ref, mine), (got_ref, 1 - mine)):
        units = pl.ds(pl.multiple_of(d * half, 16), half)
        raw = sum(
            lax.dot_general(
                w_ref[:, c * width : (c + 1) * width],
                rows[c][...],
                NT,
                preferred_element_type=jnp.float32,
            )
            for c in range(chunks)
        )
        grad_ref[units, :] = (raw * gates).astype(jnp.bfloat16)
        total += jnp.sum(
            raw * hidden_ref[units, :].astype(jnp.float32), axis=0, keepdims=True
        )
    for i in range(gates.shape[1] // LANES):
        part = jnp.broadcast_to(total[:, i * LANES : (i + 1) * LANES], (8, LANES))
        one_hot = pmat_ref[i * LANES : (i + 1) * LANES, :].astype(jnp.float32)
        back = jnp.dot(
            part, one_hot, preferred_element_type=jnp.float32, precision=lax.Precision.HIGHEST
        )
        pair = (step * (gates.shape[1] // LANES) + i) * 2
        back_ref[pl.ds(pair + core, 1), :] = back[:1, :LANES]
        back_ref[pl.ds(pair + 1 - core, 1), :] = back[:1, LANES:]


def gates_kernel(routes_ref, back_ref, out_ref):
    back = back_ref[...]
    routes = routes_ref[...]
    expert = lax.broadcasted_iota(jnp.int32, back.shape, 0)
    for k in range(out_ref.shape[0]):
        hit = expert == routes[k : k + 1, :]
        out_ref[k : k + 1, :] = jnp.sum(jnp.where(hit, back, 0.0), axis=0, keepdims=True)


def ring_shards(grad_out, gates, routes, hidden, down_weight):
    experts = lax.axis_size("expert")
    tokens, chosen = routes.shape
    model = grad_out.shape[1]
    slots, units = hidden.shape[2:]
    half = down_weight.shape[1]
    capacity = slots // experts
    width = model // CHUNKS
    bf16, f32 = jnp.bfloat16, jnp.float32
    hidden_t = hidden[0, 0].T
    routes_t, gates_t = routes.T, gates.T
    weight = down_weight[0]
    swap_dp = [(0, 1), (1, 0)]

    chunks = pl.pallas_call(
        functools.partial(pack_kernel, experts, width),
        out_shape=[
            jax.ShapeDtypeStruct((tokens, width + (tokens if c == 0 else 0)), bf16)
            for c in range(CHUNKS)
        ],
        in_specs=[VMEM] * 3,
        out_specs=[VMEM] * CHUNKS,
        compiler_params=params(16),
        name="pack",
    )(routes_t, gates_t, grad_out)

    got_weight = lax.ppermute(weight, "dp", swap_dp)

    blocks = []
    for x in chunks:
        along_z = [x]
        for _ in range(NZ - 1):
            along_z.append(lax.ppermute(along_z[-1], "expert", ring_pairs()))
        arrived = []
        for block in along_z:
            for one in (block, lax.ppermute(block, "expert", swap_pairs(2))):
                arrived += [one, lax.ppermute(one, "expert", swap_pairs(1))]
        blocks.append(arrived)

    flops = 2 * slots * width * (units + 2 * tokens)
    rows, send, own = [], [], []
    shapes = [
        jax.ShapeDtypeStruct((slots, width), bf16),
        jax.ShapeDtypeStruct((half, width), bf16),
        jax.ShapeDtypeStruct((half, width), f32),
    ]
    for c in range(CHUNKS):
        cost = pl.CostEstimate(flops=flops, bytes_accessed=12 * 2**20, transcendentals=0)
        if c == 0:
            row, out, keep, pmat, gslot, hs = pl.pallas_call(
                functools.partial(first_kernel, experts, capacity, half, width),
                out_shape=shapes
                + [
                    jax.ShapeDtypeStruct((slots, 2 * tokens), bf16),
                    jax.ShapeDtypeStruct((1, slots), f32),
                    jax.ShapeDtypeStruct((units, slots), bf16),
                ],
                in_specs=[VMEM] * (experts + 1),
                out_specs=[VMEM] * 6,
                compiler_params=params(40),
                cost_estimate=cost,
                name="first_chunk",
            )(*blocks[0], hidden_t)
        else:
            row, out, keep = pl.pallas_call(
                functools.partial(later_kernel, experts, half, width),
                out_shape=shapes,
                in_specs=[VMEM] * (experts + 2),
                out_specs=[VMEM] * 3,
                compiler_params=params(40),
                cost_estimate=cost,
                name="later_chunk",
            )(*blocks[c], pmat, hs)
        rows.append(row)
        send.append(lax.ppermute(out, "dp", swap_dp))
        own.append(keep)

    tile = 256
    grad_hidden, back = pl.pallas_call(
        functools.partial(raw_kernel, half, CHUNKS),
        grid=(slots // tile,),
        out_shape=[
            jax.ShapeDtypeStruct((units, slots), bf16),
            jax.ShapeDtypeStruct((experts, tokens), f32),
        ],
        in_specs=[pl.BlockSpec((tile, width), lambda i: (i, 0))] * CHUNKS
        + [pl.BlockSpec((half, model), lambda i: (0, 0))] * 2
        + [
            pl.BlockSpec((units, tile), lambda i: (0, i)),
            pl.BlockSpec((1, tile), lambda i: (0, i)),
            pl.BlockSpec((tile, 2 * tokens), lambda i: (i, 0)),
        ],
        out_specs=[
            pl.BlockSpec((units, tile), lambda i: (0, i)),
            pl.BlockSpec((experts, tokens), lambda i: (0, 0)),
        ],
        compiler_params=params(40),
        cost_estimate=pl.CostEstimate(
            flops=2 * slots * model * units, bytes_accessed=12 * 2**20, transcendentals=0
        ),
        name="raw",
    )(*rows, weight, got_weight, hidden_t, gslot, pmat)

    returned = lax.all_to_all(back, "expert", split_axis=0, concat_axis=0, tiled=True)
    grad_gates = pl.pallas_call(
        gates_kernel,
        out_shape=jax.ShapeDtypeStruct((chosen, tokens), f32),
        in_specs=[VMEM] * 2,
        out_specs=VMEM,
        name="grad_gates",
    )(routes_t, returned)

    grad_weight = jnp.concatenate(
        [(mine + theirs.astype(f32)).astype(bf16) for mine, theirs in zip(own, send)], axis=1
    )
    return grad_weight[None], grad_hidden.T[None, None], grad_gates.T


def shards(grad_out, gates, routes, hidden, down_weight):
    owners = lax.axis_size("expert")
    token_count, chosen = routes.shape
    width = grad_out.shape[1]
    slots = hidden.shape[2]
    capacity = slots // owners
    flat = routes.reshape(-1)
    onehot = (flat[:, None] == jnp.arange(owners, dtype=jnp.int32)[None, :]).astype(jnp.int32)
    before = jnp.cumsum(onehot, axis=0) - onehot
    slot = jnp.sum(before * onehot, axis=1)
    target = flat * capacity + slot
    send_rows = (
        jnp.zeros((owners * capacity, width), grad_out.dtype)
        .at[target]
        .set(jnp.repeat(grad_out, chosen, axis=0))
    )
    send_gate = jnp.zeros((owners * capacity,), gates.dtype).at[target].set(gates.reshape(-1))
    send_rows = send_rows.reshape(owners, capacity, width)
    send_gate = send_gate.reshape(owners, capacity)
    saved = hidden[0, 0]
    local_weight = down_weight[0]
    contract = (((1,), (1,)), ((), ()))
    rows, gate_slots = (
        lax.all_to_all(send_rows, "expert", split_axis=0, concat_axis=0, tiled=True),
        lax.all_to_all(send_gate, "expert", split_axis=0, concat_axis=0, tiled=True),
    )
    rows = rows.reshape(slots, width)
    whole_weight = lax.all_gather(local_weight, "dp", axis=0, tiled=True)
    raw = lax.dot_general(rows, whole_weight, contract, preferred_element_type=jnp.float32)
    factor = gate_slots.reshape(slots, 1).astype(jnp.float32)
    grad_hidden = (factor * raw).astype(jnp.bfloat16)
    slot_grads = jnp.sum(raw * saved.astype(jnp.float32), axis=1)
    returned = lax.all_to_all(
        slot_grads.reshape(owners, capacity), "expert", split_axis=0, concat_axis=0, tiled=True
    )
    grad_gates = returned.reshape(-1)[target].reshape(token_count, chosen)
    scaled = (factor * rows.astype(jnp.float32)).astype(jnp.bfloat16)
    summed = lax.psum_scatter(
        lax.dot_general(
            saved, scaled, (((0,), (0,)), ((), ())), preferred_element_type=jnp.float32
        ).astype(jnp.bfloat16),
        "dp",
        scatter_dimension=0,
        tiled=True,
    )
    return (summed[None], grad_hidden[None, None], grad_gates)


def solution(mesh):
    small = mesh.shape["dp"] == 2 and mesh.shape["expert"] == NZ * NY * NC
    return jax.shard_map(
        ring_shards if small else shards,
        mesh=mesh,
        in_specs=(
            P(("dp", "expert"), None),
            P(("dp", "expert"), None),
            P(("dp", "expert"), None),
            P("dp", "expert", None, None),
            P("expert", "dp", None),
        ),
        out_specs=(
            P("expert", "dp", None),
            P("dp", "expert", None, None),
            P(("dp", "expert"), None),
        ),
        check_vma=False,
    )
```

```python
import functools

import jax
import jax.numpy as jnp
from jax import lax
from jax.experimental import pallas as pl
from jax.experimental.pallas import tpu as pltpu
from jax.sharding import PartitionSpec as P

NZ, NY, NC = 4, 2, 2
CHUNKS = 2
LANES = 128
NT = (((1,), (1,)), ((), ()))
VMEM = pl.BlockSpec(memory_space=pltpu.VMEM)


def params(mib):
    return pltpu.CompilerParams(vmem_limit_bytes=mib * 2**20)


def ring(z):
    return z ^ (z >> 1)


def ring_pairs():
    size = NY * NC
    return [
        (ring(p) * size + rest, ring((p + 1) % NZ) * size + rest)
        for p in range(NZ)
        for rest in range(size)
    ]


def swap_pairs(bit):
    return [(i, i ^ bit) for i in range(NZ * NY * NC)]


def pack_kernel(experts, width, routes_ref, gates_ref, grad_ref, *outs):
    chosen, tokens = routes_ref.shape
    routes = routes_ref[...]
    gates = gates_ref[...].astype(jnp.float32)
    expert = lax.broadcasted_iota(jnp.int32, (experts, tokens), 0)
    dense = jnp.zeros((experts, tokens), jnp.float32)
    named = jnp.zeros((experts, tokens), jnp.float32)
    for k in range(chosen):
        hit = routes[k : k + 1, :] == expert
        dense = jnp.where(hit, gates[k : k + 1, :], dense)
        named = jnp.where(hit, 1.0, named)
    earlier = (
        lax.broadcasted_iota(jnp.int32, (tokens, tokens), 0)
        < lax.broadcasted_iota(jnp.int32, (tokens, tokens), 1)
    )
    slots = jnp.dot(
        named.astype(jnp.bfloat16),
        jnp.where(earlier, 1.0, 0.0).astype(jnp.bfloat16),
        preferred_element_type=jnp.float32,
    )
    slots = jnp.where(named > 0, slots, -1.0)
    outs[0][:, :width] = grad_ref[:, :width]
    outs[0][:, width:] = jnp.zeros((tokens, tokens), jnp.bfloat16)
    outs[0][:experts, width:] = dense.astype(jnp.bfloat16)
    outs[0][experts : 2 * experts, width:] = slots.astype(jnp.bfloat16)
    for c in range(1, len(outs)):
        outs[c][...] = grad_ref[:, c * width : (c + 1) * width]


def pair_place(arrival):
    return arrival


def products(half, width, hs_ref, rows_ref, send_ref, own_ref, n):
    mine = lax.axis_index("dp")
    cols = pl.ds(pl.multiple_of(n * 256, 256), 256)
    block = rows_ref[:, cols]
    other = hs_ref[pl.ds(pl.multiple_of((1 - mine) * half, 16), half), :]
    send_ref[:, cols] = jnp.dot(other, block, preferred_element_type=jnp.float32).astype(
        jnp.bfloat16
    )
    own = hs_ref[pl.ds(pl.multiple_of(mine * half, 16), half), :]
    own_ref[:, cols] = jnp.dot(own, block, preferred_element_type=jnp.float32)


def dispatch(xs, pmat_ref, rows_ref, n):
    cols = pl.ds(pl.multiple_of(n * 256, 256), 256)
    for a in range(len(xs) // 2):
        where = pl.ds(pair_place(a) * LANES, LANES)
        both = jnp.concatenate([xs[2 * a][:, cols], xs[2 * a + 1][:, cols]], axis=0)
        rows_ref[where, cols] = jnp.dot(
            pmat_ref[where, :], both, preferred_element_type=jnp.float32
        ).astype(jnp.bfloat16)


def first_kernel(experts, capacity, half, width, *refs):
    n_blocks = experts
    xs = [refs[0].at[j] for j in range(n_blocks)]
    hidden_ref = refs[1]
    rows_ref, send_ref, own_ref, pmat_ref, gslot_ref, hs_ref = refs[2:]
    me = lax.axis_index("expert")
    core = 0
    tokens = xs[0].shape[0]
    expert = lax.broadcasted_iota(jnp.int32, (experts, tokens), 0) == me
    slot = lax.broadcasted_iota(jnp.int32, (LANES, tokens), 0).astype(jnp.float32)
    for a in range(n_blocks // 2):
        place = pair_place(a)
        where = pl.ds(place * LANES, LANES)
        halves, gates = [], []
        for b, x_ref in enumerate((xs[2 * a], xs[2 * a + 1])):
            ext = x_ref[: 2 * experts, width:].astype(jnp.float32)
            gate = jnp.sum(jnp.where(expert, ext[:experts], 0.0), axis=0, keepdims=True)
            number = jnp.sum(jnp.where(expert, ext[experts:], 0.0), axis=0, keepdims=True)
            offset = float(b * capacity)
            number = jnp.where(number >= 0, number + offset, -1.0)
            halves.append(jnp.where(slot == number, 1.0, 0.0).astype(jnp.bfloat16))
            gates.append(gate)
        one_hot = jnp.concatenate(halves, axis=1)
        pmat_ref[where, :] = one_hot
        gate_pair = jnp.concatenate(gates, axis=1).astype(jnp.bfloat16)
        gslot = lax.dot_general(
            jnp.broadcast_to(gate_pair, (16, 2 * tokens)),
            one_hot,
            NT,
            preferred_element_type=jnp.float32,
        )
        gslot_ref[:, where] = gslot[:1]
    hs_ref[...] = (hidden_ref[...].astype(jnp.float32) * gslot_ref[...]).astype(jnp.bfloat16)

    @pl.loop(0, width // 256)
    def _(n):
        dispatch(xs, pmat_ref, rows_ref, n)
        products(half, width, hs_ref, rows_ref, send_ref, own_ref, n)


def later_kernel(experts, half, width, *refs):
    xs = [refs[0].at[j] for j in range(experts)]
    pmat_ref, hs_ref, rows_ref, send_ref, own_ref = refs[1:]

    @pl.loop(0, width // 256)
    def _(n):
        dispatch(xs, pmat_ref, rows_ref, n)
        products(half, width, hs_ref, rows_ref, send_ref, own_ref, n)


def raw_kernel(half, chunks, *refs):
    rows = refs[:chunks]
    own_ref, got_ref, hidden_ref, gslot_ref, pmat_ref, grad_ref, back_ref = refs[chunks:]
    mine = lax.axis_index("dp")
    core = 0
    step = pl.program_id(0)
    width = rows[0].shape[1]
    gates = gslot_ref[...]
    total = jnp.zeros(gates.shape, jnp.float32)
    for w_ref, d in ((own_ref, mine), (got_ref, 1 - mine)):
        units = pl.ds(pl.multiple_of(d * half, 16), half)
        raw = sum(
            lax.dot_general(
                w_ref[:, c * width : (c + 1) * width],
                rows[c][...],
                NT,
                preferred_element_type=jnp.float32,
            )
            for c in range(chunks)
        )
        grad_ref[units, :] = (raw * gates).astype(jnp.bfloat16)
        total += jnp.sum(
            raw * hidden_ref[units, :].astype(jnp.float32), axis=0, keepdims=True
        )
    for i in range(gates.shape[1] // LANES):
        part = jnp.broadcast_to(total[:, i * LANES : (i + 1) * LANES], (8, LANES))
        one_hot = pmat_ref[i * LANES : (i + 1) * LANES, :].astype(jnp.float32)
        back = jnp.dot(
            part, one_hot, preferred_element_type=jnp.float32, precision=lax.Precision.HIGHEST
        )
        pair = (step * (gates.shape[1] // LANES) + i) * 2
        back_ref[pl.ds(pair + core, 1), :] = back[:1, :LANES]
        back_ref[pl.ds(pair + 1 - core, 1), :] = back[:1, LANES:]


def gates_kernel(routes_ref, back_ref, out_ref):
    back = back_ref[...]
    routes = routes_ref[...]
    expert = lax.broadcasted_iota(jnp.int32, back.shape, 0)
    for k in range(out_ref.shape[0]):
        hit = expert == routes[k : k + 1, :]
        out_ref[k : k + 1, :] = jnp.sum(jnp.where(hit, back, 0.0), axis=0, keepdims=True)


def ring_shards(grad_out, gates, routes, hidden, down_weight):
    experts = lax.axis_size("expert")
    tokens, chosen = routes.shape
    model = grad_out.shape[1]
    slots, units = hidden.shape[2:]
    half = down_weight.shape[1]
    capacity = slots // experts
    width = model // CHUNKS
    bf16, f32 = jnp.bfloat16, jnp.float32
    hidden_t = hidden[0, 0].T
    routes_t, gates_t = routes.T, gates.T
    weight = down_weight[0]
    swap_dp = [(0, 1), (1, 0)]

    chunks = pl.pallas_call(
        functools.partial(pack_kernel, experts, width),
        out_shape=[
            jax.ShapeDtypeStruct((tokens, width + (tokens if c == 0 else 0)), bf16)
            for c in range(CHUNKS)
        ],
        in_specs=[VMEM] * 3,
        out_specs=[VMEM] * CHUNKS,
        compiler_params=params(16),
        name="pack",
    )(routes_t, gates_t, grad_out)

    got_weight = lax.ppermute(weight, "dp", swap_dp)

    blocks = []
    for x in chunks:
        arrived = [lax.all_gather(x, "expert")]
        blocks.append(arrived)

    flops = 2 * slots * width * (units + 2 * tokens)
    rows, send, own = [], [], []
    shapes = [
        jax.ShapeDtypeStruct((slots, width), bf16),
        jax.ShapeDtypeStruct((half, width), bf16),
        jax.ShapeDtypeStruct((half, width), f32),
    ]
    for c in range(CHUNKS):
        cost = pl.CostEstimate(flops=flops, bytes_accessed=12 * 2**20, transcendentals=0)
        if c == 0:
            row, out, keep, pmat, gslot, hs = pl.pallas_call(
                functools.partial(first_kernel, experts, capacity, half, width),
                out_shape=shapes
                + [
                    jax.ShapeDtypeStruct((slots, 2 * tokens), bf16),
                    jax.ShapeDtypeStruct((1, slots), f32),
                    jax.ShapeDtypeStruct((units, slots), bf16),
                ],
                in_specs=[VMEM] * 2,
                out_specs=[VMEM] * 6,
                compiler_params=params(40),
                cost_estimate=cost,
                name="first_chunk",
            )(*blocks[0], hidden_t)
        else:
            row, out, keep = pl.pallas_call(
                functools.partial(later_kernel, experts, half, width),
                out_shape=shapes,
                in_specs=[VMEM] * 3,
                out_specs=[VMEM] * 3,
                compiler_params=params(40),
                cost_estimate=cost,
                name="later_chunk",
            )(*blocks[c], pmat, hs)
        rows.append(row)
        send.append(lax.ppermute(out, "dp", swap_dp))
        own.append(keep)

    tile = 256
    grad_hidden, back = pl.pallas_call(
        functools.partial(raw_kernel, half, CHUNKS),
        grid=(slots // tile,),
        out_shape=[
            jax.ShapeDtypeStruct((units, slots), bf16),
            jax.ShapeDtypeStruct((experts, tokens), f32),
        ],
        in_specs=[pl.BlockSpec((tile, width), lambda i: (i, 0))] * CHUNKS
        + [pl.BlockSpec((half, model), lambda i: (0, 0))] * 2
        + [
            pl.BlockSpec((units, tile), lambda i: (0, i)),
            pl.BlockSpec((1, tile), lambda i: (0, i)),
            pl.BlockSpec((tile, 2 * tokens), lambda i: (i, 0)),
        ],
        out_specs=[
            pl.BlockSpec((units, tile), lambda i: (0, i)),
            pl.BlockSpec((experts, tokens), lambda i: (0, 0)),
        ],
        compiler_params=params(40),
        cost_estimate=pl.CostEstimate(
            flops=2 * slots * model * units, bytes_accessed=12 * 2**20, transcendentals=0
        ),
        name="raw",
    )(*rows, weight, got_weight, hidden_t, gslot, pmat)

    returned = lax.all_to_all(back, "expert", split_axis=0, concat_axis=0, tiled=True)
    grad_gates = pl.pallas_call(
        gates_kernel,
        out_shape=jax.ShapeDtypeStruct((chosen, tokens), f32),
        in_specs=[VMEM] * 2,
        out_specs=VMEM,
        name="grad_gates",
    )(routes_t, returned)

    grad_weight = jnp.concatenate(
        [(mine + theirs.astype(f32)).astype(bf16) for mine, theirs in zip(own, send)], axis=1
    )
    return grad_weight[None], grad_hidden.T[None, None], grad_gates.T


def shards(grad_out, gates, routes, hidden, down_weight):
    owners = lax.axis_size("expert")
    token_count, chosen = routes.shape
    width = grad_out.shape[1]
    slots = hidden.shape[2]
    capacity = slots // owners
    flat = routes.reshape(-1)
    onehot = (flat[:, None] == jnp.arange(owners, dtype=jnp.int32)[None, :]).astype(jnp.int32)
    before = jnp.cumsum(onehot, axis=0) - onehot
    slot = jnp.sum(before * onehot, axis=1)
    target = flat * capacity + slot
    send_rows = (
        jnp.zeros((owners * capacity, width), grad_out.dtype)
        .at[target]
        .set(jnp.repeat(grad_out, chosen, axis=0))
    )
    send_gate = jnp.zeros((owners * capacity,), gates.dtype).at[target].set(gates.reshape(-1))
    send_rows = send_rows.reshape(owners, capacity, width)
    send_gate = send_gate.reshape(owners, capacity)
    saved = hidden[0, 0]
    local_weight = down_weight[0]
    contract = (((1,), (1,)), ((), ()))
    rows, gate_slots = (
        lax.all_to_all(send_rows, "expert", split_axis=0, concat_axis=0, tiled=True),
        lax.all_to_all(send_gate, "expert", split_axis=0, concat_axis=0, tiled=True),
    )
    rows = rows.reshape(slots, width)
    whole_weight = lax.all_gather(local_weight, "dp", axis=0, tiled=True)
    raw = lax.dot_general(rows, whole_weight, contract, preferred_element_type=jnp.float32)
    factor = gate_slots.reshape(slots, 1).astype(jnp.float32)
    grad_hidden = (factor * raw).astype(jnp.bfloat16)
    slot_grads = jnp.sum(raw * saved.astype(jnp.float32), axis=1)
    returned = lax.all_to_all(
        slot_grads.reshape(owners, capacity), "expert", split_axis=0, concat_axis=0, tiled=True
    )
    grad_gates = returned.reshape(-1)[target].reshape(token_count, chosen)
    scaled = (factor * rows.astype(jnp.float32)).astype(jnp.bfloat16)
    summed = lax.psum_scatter(
        lax.dot_general(
            saved, scaled, (((0,), (0,)), ((), ())), preferred_element_type=jnp.float32
        ).astype(jnp.bfloat16),
        "dp",
        scatter_dimension=0,
        tiled=True,
    )
    return (summed[None], grad_hidden[None, None], grad_gates)


def solution(mesh):
    small = mesh.shape["dp"] == 2 and mesh.shape["expert"] == NZ * NY * NC
    return jax.shard_map(
        ring_shards if small else shards,
        mesh=mesh,
        in_specs=(
            P(("dp", "expert"), None),
            P(("dp", "expert"), None),
            P(("dp", "expert"), None),
            P("dp", "expert", None, None),
            P("expert", "dp", None),
        ),
        out_specs=(
            P("expert", "dp", None),
            P("dp", "expert", None, None),
            P(("dp", "expert"), None),
        ),
        check_vma=False,
    )
```

```python
import functools

import jax
import jax.numpy as jnp
from jax import lax
from jax.experimental import pallas as pl
from jax.experimental.pallas import tpu as pltpu
from jax.sharding import PartitionSpec as P

NZ, NY, NC = 4, 2, 2
CHUNKS = 2
LANES = 128
NT = (((1,), (1,)), ((), ()))
VMEM = pl.BlockSpec(memory_space=pltpu.VMEM)


def params(mib):
    return pltpu.CompilerParams(vmem_limit_bytes=mib * 2**20)


def ring(z):
    return z ^ (z >> 1)


def ring_pairs(step):
    size = NY * NC
    return [
        (ring(p) * size + rest, ring((p + step) % NZ) * size + rest)
        for p in range(NZ)
        for rest in range(size)
    ]


def swap_pairs(bit):
    return [(i, i ^ bit) for i in range(NZ * NY * NC)]


def pack_kernel(experts, routes_ref, gates_ref, grad_ref, out_ref):
    chosen, tokens = routes_ref.shape
    width = grad_ref.shape[1]
    routes = routes_ref[...]
    gates = gates_ref[...].astype(jnp.float32)
    expert = lax.broadcasted_iota(jnp.int32, (experts, tokens), 0)
    dense = jnp.zeros((experts, tokens), jnp.float32)
    named = jnp.zeros((experts, tokens), jnp.float32)
    for k in range(chosen):
        hit = routes[k : k + 1, :] == expert
        dense = jnp.where(hit, gates[k : k + 1, :], dense)
        named = jnp.where(hit, 1.0, named)
    earlier = (
        lax.broadcasted_iota(jnp.int32, (tokens, tokens), 0)
        < lax.broadcasted_iota(jnp.int32, (tokens, tokens), 1)
    )
    slots = jnp.dot(
        named.astype(jnp.bfloat16),
        jnp.where(earlier, 1.0, 0.0).astype(jnp.bfloat16),
        preferred_element_type=jnp.float32,
    )
    slots = jnp.where(named > 0, slots, -1.0)
    out_ref[:, :width] = grad_ref[...]
    out_ref[:, width:] = jnp.zeros((tokens, tokens), jnp.bfloat16)
    out_ref[:experts, width:] = dense.astype(jnp.bfloat16)
    out_ref[experts : 2 * experts, width:] = slots.astype(jnp.bfloat16)


def later_pack_kernel(grad_ref, after_ref, out_ref):
    del after_ref
    out_ref[...] = grad_ref[...]


def pair_place(arrival):
    index = lax.axis_index("expert")
    z, y = index >> 2, (index >> 1) & 1
    z = ring((ring(z) - arrival // NY) & (NZ - 1))
    return z * NY + (y ^ (arrival % NY))


def products(half, width, hs_ref, rows_ref, send_ref, own_ref, n):
    mine = lax.axis_index("dp")
    cols = pl.ds(pl.multiple_of(n * 256, 256), 256)
    block = rows_ref[:, cols]
    other = hs_ref[pl.ds(pl.multiple_of((1 - mine) * half, 16), half), :]
    send_ref[:, cols] = jnp.dot(other, block, preferred_element_type=jnp.float32).astype(
        jnp.bfloat16
    )
    own = hs_ref[pl.ds(pl.multiple_of(mine * half, 16), half), :]
    own_ref[:, cols] = jnp.dot(own, block, preferred_element_type=jnp.float32)


def dispatch(xs, pmat_ref, rows_ref, n):
    cols = pl.ds(pl.multiple_of(n * 256, 256), 256)
    for a in range(len(xs) // 2):
        where = pl.ds(pl.multiple_of(pair_place(a) * LANES, LANES), LANES)
        both = jnp.concatenate([xs[2 * a][:, cols], xs[2 * a + 1][:, cols]], axis=0)
        rows_ref[where, cols] = jnp.dot(
            pmat_ref[where, :], both, preferred_element_type=jnp.float32
        ).astype(jnp.bfloat16)


def first_kernel(experts, capacity, half, width, *refs):
    n_blocks = experts
    xs = refs[:n_blocks]
    hidden_ref = refs[n_blocks]
    rows_ref, send_ref, own_ref, pmat_ref, gslot_ref, hs_ref = refs[n_blocks + 1 :]
    me = lax.axis_index("expert")
    core = me & 1
    tokens = xs[0].shape[0]
    expert = lax.broadcasted_iota(jnp.int32, (experts, tokens), 0) == me
    slot = lax.broadcasted_iota(jnp.int32, (LANES, tokens), 0).astype(jnp.float32)
    for a in range(n_blocks // 2):
        place = pair_place(a)
        where = pl.ds(pl.multiple_of(place * LANES, LANES), LANES)
        halves, gates = [], []
        for b, x_ref in enumerate((xs[2 * a], xs[2 * a + 1])):
            ext = x_ref[: 2 * experts, width:].astype(jnp.float32)
            gate = jnp.sum(jnp.where(expert, ext[:experts], 0.0), axis=0, keepdims=True)
            number = jnp.sum(jnp.where(expert, ext[experts:], 0.0), axis=0, keepdims=True)
            offset = ((core ^ b) * capacity).astype(jnp.float32)
            number = jnp.where(number >= 0, number + offset, -1.0)
            halves.append(jnp.where(slot == number, 1.0, 0.0).astype(jnp.bfloat16))
            gates.append(gate)
        one_hot = jnp.concatenate(halves, axis=1)
        pmat_ref[where, :] = one_hot
        gate_pair = jnp.concatenate(gates, axis=1).astype(jnp.bfloat16)
        gslot = lax.dot_general(
            jnp.broadcast_to(gate_pair, (16, 2 * tokens)),
            one_hot,
            NT,
            preferred_element_type=jnp.float32,
        )
        gslot_ref[:, where] = gslot[:1]
    hs_ref[...] = (hidden_ref[...].astype(jnp.float32) * gslot_ref[...]).astype(jnp.bfloat16)

    @pl.loop(0, width // 256)
    def _(n):
        dispatch(xs, pmat_ref, rows_ref, n)
        products(half, width, hs_ref, rows_ref, send_ref, own_ref, n)


def later_kernel(experts, half, width, *refs):
    xs = refs[:experts]
    pmat_ref, hs_ref, rows_ref, send_ref, own_ref = refs[experts:]

    @pl.loop(0, width // 256)
    def _(n):
        dispatch(xs, pmat_ref, rows_ref, n)
        products(half, width, hs_ref, rows_ref, send_ref, own_ref, n)


def raw_part_kernel(half, rows_ref, own_ref, got_ref, raw_ref):
    mine = lax.axis_index("dp")
    for w_ref, d in ((own_ref, mine), (got_ref, 1 - mine)):
        units = pl.ds(pl.multiple_of(d * half, 16), half)
        raw_ref[units, :] = lax.dot_general(
            w_ref[...], rows_ref[...], NT, preferred_element_type=jnp.float32
        )


def raw_kernel(half, *refs):
    rows_ref, own_ref, got_ref, sum_ref, hidden_ref, gslot_ref, pmat_ref, grad_ref, back_ref = refs
    mine = lax.axis_index("dp")
    core = lax.axis_index("expert") & 1
    step = pl.program_id(0)
    gates = gslot_ref[...]
    total = jnp.zeros(gates.shape, jnp.float32)
    for w_ref, d in ((own_ref, mine), (got_ref, 1 - mine)):
        units = pl.ds(pl.multiple_of(d * half, 16), half)
        raw = sum_ref[units, :] + lax.dot_general(
            w_ref[...], rows_ref[...], NT, preferred_element_type=jnp.float32
        )
        grad_ref[units, :] = (raw * gates).astype(jnp.bfloat16)
        total += jnp.sum(
            raw * hidden_ref[units, :].astype(jnp.float32), axis=0, keepdims=True
        )
    for i in range(gates.shape[1] // LANES):
        part = jnp.broadcast_to(total[:, i * LANES : (i + 1) * LANES], (8, LANES))
        one_hot = pmat_ref[i * LANES : (i + 1) * LANES, :].astype(jnp.float32)
        back = jnp.dot(
            part, one_hot, preferred_element_type=jnp.float32, precision=lax.Precision.HIGHEST
        )
        pair = (step * (gates.shape[1] // LANES) + i) * 2
        back_ref[pl.ds(pair + core, 1), :] = back[:1, :LANES]
        back_ref[pl.ds(pair + 1 - core, 1), :] = back[:1, LANES:]


def finish_kernel(own_ref, got_ref, *refs):
    refs[-1][...] = (own_ref[...] + got_ref[...].astype(jnp.float32)).astype(jnp.bfloat16)


def gates_kernel(routes_ref, back_ref, out_ref):
    back = back_ref[...]
    routes = routes_ref[...]
    expert = lax.broadcasted_iota(jnp.int32, back.shape, 0)
    for k in range(out_ref.shape[0]):
        hit = expert == routes[k : k + 1, :]
        out_ref[k : k + 1, :] = jnp.sum(jnp.where(hit, back, 0.0), axis=0, keepdims=True)


def ring_shards(grad_out, gates, routes, hidden, down_weight):
    experts = lax.axis_size("expert")
    tokens, chosen = routes.shape
    model = grad_out.shape[1]
    slots, units = hidden.shape[2:]
    half = down_weight.shape[1]
    capacity = slots // experts
    width = model // CHUNKS
    tile = 256
    bf16, f32 = jnp.bfloat16, jnp.float32
    shape = jax.ShapeDtypeStruct
    hidden_t = hidden[0, 0].T
    routes_t, gates_t = routes.T, gates.T
    weight = down_weight[0]
    columns = [pl.BlockSpec((half, width), lambda i, c=c: (0, c)) for c in range(CHUNKS)]

    def forward(x):
        return lax.ppermute(x, "expert", ring_pairs(1))

    def backward(x):
        return lax.ppermute(x, "expert", ring_pairs(-1))

    def across(x):
        return lax.ppermute(x, "expert", swap_pairs(2))

    def sibling(x):
        return lax.ppermute(x, "expert", swap_pairs(1))

    def swap(x):
        return lax.ppermute(x, "dp", [(0, 1), (1, 0)])

    def behind(x, *others):
        return lax.optimization_barrier((x, *others))[0]

    def with_siblings(column, facing):
        return [z for pair in zip(column, facing) for b in pair for z in (b, sibling(b))]

    def pack():
        return pl.pallas_call(
            functools.partial(pack_kernel, experts),
            out_shape=shape((tokens, width + tokens), bf16),
            grid=(1,),
            in_specs=[pl.BlockSpec((chosen, tokens), lambda i: (0, 0))] * 2
            + [pl.BlockSpec((tokens, width), lambda i: (0, 0))],
            out_specs=pl.BlockSpec((tokens, width + tokens), lambda i: (0, 0)),
            compiler_params=params(8),
            name="pack",
        )(routes_t, gates_t, grad_out)

    def later_pack(c, after):
        return pl.pallas_call(
            later_pack_kernel,
            out_shape=shape((tokens, width), bf16),
            grid=(1,),
            in_specs=[
                pl.BlockSpec((tokens, width), lambda i: (0, c)),
                pl.BlockSpec(memory_space=pl.ANY),
            ],
            out_specs=pl.BlockSpec((tokens, width), lambda i: (0, 0)),
            compiler_params=params(8),
            name="later_pack",
        )(grad_out, after)

    chunk_shapes = [
        shape((slots, width), bf16),
        shape((half, width), bf16),
        shape((half, width), f32),
    ]

    def first_chunk(blocks):
        return pl.pallas_call(
            functools.partial(first_kernel, experts, capacity, half, width),
            out_shape=chunk_shapes
            + [
                shape((slots, 2 * tokens), bf16),
                shape((1, slots), f32),
                shape((units, slots), bf16),
            ],
            in_specs=[VMEM] * (experts + 1),
            out_specs=[VMEM] * 6,
            compiler_params=params(40),
            name="first_chunk",
        )(*blocks, hidden_t)

    def later_chunk(blocks, pmat, hs):
        return pl.pallas_call(
            functools.partial(later_kernel, experts, half, width),
            out_shape=chunk_shapes,
            in_specs=[VMEM] * (experts + 2),
            out_specs=[VMEM] * 3,
            compiler_params=params(40),
            name="later_chunk",
        )(*blocks, pmat, hs)

    def raw_part(rows, got_weight):
        return pl.pallas_call(
            functools.partial(raw_part_kernel, half),
            grid=(slots // tile,),
            out_shape=shape((units, slots), f32),
            in_specs=[pl.BlockSpec((tile, width), lambda i: (i, 0)), columns[0], columns[0]],
            out_specs=pl.BlockSpec((units, tile), lambda i: (0, i)),
            compiler_params=params(24),
            name="raw_part",
        )(rows, weight, got_weight)

    def raw_rest(rows, got_weight, raw, gslot, pmat):
        by_slot = pl.BlockSpec((units, tile), lambda i: (0, i))
        return pl.pallas_call(
            functools.partial(raw_kernel, half),
            grid=(slots // tile,),
            out_shape=[shape((units, slots), bf16), shape((experts, tokens), f32)],
            in_specs=[
                pl.BlockSpec((tile, width), lambda i: (i, 0)),
                columns[1],
                columns[1],
                by_slot,
                by_slot,
                pl.BlockSpec((1, tile), lambda i: (0, i)),
                pl.BlockSpec((tile, 2 * tokens), lambda i: (i, 0)),
            ],
            out_specs=[by_slot, pl.BlockSpec((experts, tokens), lambda i: (0, 0))],
            compiler_params=params(24),
            name="raw",
        )(rows, weight, got_weight, raw, hidden_t, gslot, pmat)

    def finish(c, own, got, *before):
        part = 256
        spec = pl.BlockSpec((half, part), lambda i: (0, i))
        return pl.pallas_call(
            finish_kernel,
            grid=(width // part,),
            out_shape=shape((half, model), bf16),
            in_specs=[spec, spec] + [pl.BlockSpec(memory_space=pl.ANY)] * len(before),
            out_specs=pl.BlockSpec((half, part), lambda i: (0, c * (width // part) + i)),
            input_output_aliases={2: 0} if before else {},
            compiler_params=params(8),
            name="finish",
        )(own, got, *before)

    got_weight = swap(weight)

    x = pack()
    pred, succ, facing = forward(x), backward(x), across(x)
    far = forward(pred)
    blocks = with_siblings(
        [behind(x, succ), pred, far, succ], [facing, across(pred), across(far), across(succ)]
    )
    rows0, send0, own0, pmat, gslot, hs = first_chunk(blocks)
    got0 = swap(send0)
    raw = raw_part(rows0, got_weight)

    x = later_pack(1, far)
    pred, succ, facing = forward(x), backward(x), across(x)
    pred, facing = behind(pred, rows0), behind(facing, rows0)
    far = forward(pred)
    across_far = behind(across(far), raw, got0)
    blocks = with_siblings(
        [x, pred, far, succ], [facing, across(pred), across_far, backward(facing)]
    )
    rows1, send1, own1 = later_chunk(blocks, pmat, hs)
    got1 = swap(send1)

    grad_hidden, back = raw_rest(rows1, got_weight, raw, gslot, pmat)
    returned = lax.all_to_all(back, "expert", split_axis=0, concat_axis=0, tiled=True)
    grad_gates = pl.pallas_call(
        gates_kernel,
        out_shape=shape((chosen, tokens), f32),
        in_specs=[VMEM] * 2,
        out_specs=VMEM,
        name="grad_gates",
    )(routes_t, returned)

    grad_weight = finish(1, own1, got1, finish(0, own0, got0))
    return grad_weight[None], grad_hidden.T[None, None], grad_gates.T


def shards(grad_out, gates, routes, hidden, down_weight):
    owners = lax.axis_size("expert")
    token_count, chosen = routes.shape
    width = grad_out.shape[1]
    slots = hidden.shape[2]
    capacity = slots // owners
    flat = routes.reshape(-1)
    onehot = (flat[:, None] == jnp.arange(owners, dtype=jnp.int32)[None, :]).astype(jnp.int32)
    before = jnp.cumsum(onehot, axis=0) - onehot
    slot = jnp.sum(before * onehot, axis=1)
    target = flat * capacity + slot
    send_rows = (
        jnp.zeros((owners * capacity, width), grad_out.dtype)
        .at[target]
        .set(jnp.repeat(grad_out, chosen, axis=0))
    )
    send_gate = jnp.zeros((owners * capacity,), gates.dtype).at[target].set(gates.reshape(-1))
    send_rows = send_rows.reshape(owners, capacity, width)
    send_gate = send_gate.reshape(owners, capacity)
    saved = hidden[0, 0]
    local_weight = down_weight[0]
    contract = (((1,), (1,)), ((), ()))
    rows, gate_slots = (
        lax.all_to_all(send_rows, "expert", split_axis=0, concat_axis=0, tiled=True),
        lax.all_to_all(send_gate, "expert", split_axis=0, concat_axis=0, tiled=True),
    )
    rows = rows.reshape(slots, width)
    whole_weight = lax.all_gather(local_weight, "dp", axis=0, tiled=True)
    raw = lax.dot_general(rows, whole_weight, contract, preferred_element_type=jnp.float32)
    factor = gate_slots.reshape(slots, 1).astype(jnp.float32)
    grad_hidden = (factor * raw).astype(jnp.bfloat16)
    slot_grads = jnp.sum(raw * saved.astype(jnp.float32), axis=1)
    returned = lax.all_to_all(
        slot_grads.reshape(owners, capacity), "expert", split_axis=0, concat_axis=0, tiled=True
    )
    grad_gates = returned.reshape(-1)[target].reshape(token_count, chosen)
    scaled = (factor * rows.astype(jnp.float32)).astype(jnp.bfloat16)
    summed = lax.psum_scatter(
        lax.dot_general(
            saved, scaled, (((0,), (0,)), ((), ())), preferred_element_type=jnp.float32
        ).astype(jnp.bfloat16),
        "dp",
        scatter_dimension=0,
        tiled=True,
    )
    return (summed[None], grad_hidden[None, None], grad_gates)


def solution(mesh):
    small = mesh.shape["dp"] == 2 and mesh.shape["expert"] == NZ * NY * NC
    return jax.shard_map(
        ring_shards if small else shards,
        mesh=mesh,
        in_specs=(
            P(("dp", "expert"), None),
            P(("dp", "expert"), None),
            P(("dp", "expert"), None),
            P("dp", "expert", None, None),
            P("expert", "dp", None),
        ),
        out_specs=(
            P("expert", "dp", None),
            P("dp", "expert", None, None),
            P(("dp", "expert"), None),
        ),
        check_vma=False,
    )
```

```python
import functools

import jax
import jax.numpy as jnp
from jax import lax
from jax.experimental import pallas as pl
from jax.experimental.pallas import tpu as pltpu
from jax.sharding import PartitionSpec as P

NZ, NY, NC = 4, 2, 2
CHUNKS = 2
PIECES = 2
PART = 256
LANES = 128
NT = (((1,), (1,)), ((), ()))
VMEM = pl.BlockSpec(memory_space=pltpu.VMEM)
ANY = pl.BlockSpec(memory_space=pl.ANY)


def params(mib):
    return pltpu.CompilerParams(vmem_limit_bytes=mib * 2**20)


def cost(micros):
    return pl.CostEstimate(
        flops=micros * 10**9, bytes_accessed=micros * 3 * 2**20, transcendentals=0
    )


def ring(z):
    return z ^ (z >> 1)


def ring_pairs(step):
    size = NY * NC
    return [
        (ring(p) * size + rest, ring((p + step) % NZ) * size + rest)
        for p in range(NZ)
        for rest in range(size)
    ]


def swap_pairs(bit):
    return [(i, i ^ bit) for i in range(NZ * NY * NC)]


def pack_kernel(experts, width, routes_hbm, gates_hbm, grad_hbm, out_ref, routes_ref, gates_ref, sems):
    copies = [
        pltpu.make_async_copy(src, dst, sems.at[i])
        for i, (src, dst) in enumerate(
            (
                (routes_hbm, routes_ref),
                (gates_hbm, gates_ref),
                (grad_hbm.at[:, :width], out_ref.at[:, :width]),
            )
        )
    ]
    for copy in copies:
        copy.start()
    copies[0].wait()
    copies[1].wait()
    chosen, tokens = routes_ref.shape
    routes = routes_ref[...]
    gates = gates_ref[...].astype(jnp.float32)
    expert = lax.broadcasted_iota(jnp.int32, (experts, tokens), 0)
    dense = jnp.zeros((experts, tokens), jnp.float32)
    named = jnp.zeros((experts, tokens), jnp.float32)
    for k in range(chosen):
        hit = routes[k : k + 1, :] == expert
        dense = jnp.where(hit, gates[k : k + 1, :], dense)
        named = jnp.where(hit, 1.0, named)
    earlier = (
        lax.broadcasted_iota(jnp.int32, (tokens, tokens), 0)
        < lax.broadcasted_iota(jnp.int32, (tokens, tokens), 1)
    )
    slots = jnp.dot(
        named.astype(jnp.bfloat16),
        jnp.where(earlier, 1.0, 0.0).astype(jnp.bfloat16),
        preferred_element_type=jnp.float32,
    )
    slots = jnp.where(named > 0, slots, -1.0)
    out_ref[:, width:] = jnp.zeros((tokens, tokens), jnp.bfloat16)
    out_ref[:experts, width:] = dense.astype(jnp.bfloat16)
    out_ref[experts : 2 * experts, width:] = slots.astype(jnp.bfloat16)
    copies[2].wait()


def later_pack_kernel(low, grad_hbm, after_ref, out_ref, sem):
    del after_ref
    copy = pltpu.make_async_copy(grad_hbm.at[:, pl.ds(low, out_ref.shape[1])], out_ref, sem)
    copy.start()
    copy.wait()


def pair_place(arrival):
    index = lax.axis_index("expert")
    z, y = index >> 2, (index >> 1) & 1
    z = ring((ring(z) - arrival // NY) & (NZ - 1))
    return z * NY + (y ^ (arrival % NY))


def pick(xs, pmat_ref, mine_ref, theirs_ref):
    capacity = mine_ref.shape[0] // len(xs)

    @pl.loop(0, mine_ref.shape[1] // 256)
    def _(n):
        cols = pl.ds(pl.multiple_of(n * 256, 256), 256)
        for a, x_ref in enumerate(xs):
            rows = jnp.dot(
                pmat_ref[a * 2 * capacity : (a + 1) * 2 * capacity, :],
                x_ref[:, cols],
                preferred_element_type=jnp.float32,
            ).astype(jnp.bfloat16)
            where = pl.ds(pl.multiple_of(pair_place(a) * capacity, capacity), capacity)
            mine_ref[where, cols] = rows[:capacity]
            theirs_ref[where, cols] = rows[capacity:]


def first_pick_kernel(experts, capacity, *refs):
    pairs = experts // 2
    xs = refs[:pairs]
    mine_ref, theirs_ref, pmat_ref, gslot_ref, other_ref = refs[pairs:]
    width = mine_ref.shape[1]
    me = lax.axis_index("expert")
    core = me & 1
    tokens = xs[0].shape[0]
    expert = lax.broadcasted_iota(jnp.int32, (experts, tokens), 0)
    slot = lax.broadcasted_iota(jnp.int32, (2 * capacity, tokens), 0).astype(jnp.float32)
    offset = (core * capacity).astype(jnp.float32)
    other_ref[...] = jnp.zeros(other_ref.shape, jnp.float32)
    for a, x_ref in enumerate(xs):
        place = pl.ds(pair_place(a), 1)
        ext = x_ref[: 2 * experts, width:].astype(jnp.float32)
        one_hot = jnp.zeros(slot.shape, jnp.float32)
        for s, (who, to_ref) in enumerate(((me, gslot_ref), (me ^ 1, other_ref))):
            gate = jnp.sum(jnp.where(expert == who, ext[:experts], 0.0), axis=0, keepdims=True)
            number = jnp.sum(jnp.where(expert == who, ext[experts:], 0.0), axis=0, keepdims=True)
            routed = number >= 0
            spot = jnp.where(routed, number + s * capacity, -1.0)
            one_hot = jnp.where(slot == spot, 1.0, one_hot)
            spot = jnp.where(routed, number + offset, -1.0)
            by_slot = lax.dot_general(
                jnp.broadcast_to(gate.astype(jnp.bfloat16), (16, tokens)),
                jnp.where(slot == spot, 1.0, 0.0).astype(jnp.bfloat16),
                NT,
                preferred_element_type=jnp.float32,
            )
            to_ref[place, :] = by_slot[:1]
        pmat_ref[a * 2 * capacity : (a + 1) * 2 * capacity, :] = one_hot.astype(jnp.bfloat16)
    theirs_ref[pairs * capacity :, :] = jnp.zeros((16, width), jnp.bfloat16)
    theirs_ref[pairs * capacity :, : 2 * capacity] = other_ref[...].astype(jnp.bfloat16)
    pick(xs, pmat_ref, mine_ref, theirs_ref)


def pick_kernel(*refs):
    pick(refs[:-3], *refs[-3:])


def products(half, capacity, mine_ref, got_ref, hs_ref, rows_ref, *outs):
    mine = lax.axis_index("dp")
    core = lax.axis_index("expert") & 1
    pairs = mine_ref.shape[0] // capacity
    pieces = len(outs) // 2
    piece = mine_ref.shape[1] // pieces
    for q in range(pieces):

        @pl.loop(0, piece // 256)
        def _(n, q=q):
            cols = pl.ds(pl.multiple_of(q * piece + n * 256, 256), 256)
            out = pl.ds(pl.multiple_of(n * 256, 256), 256)
            for p in range(pairs):
                for c, ref in ((core, mine_ref), (1 - core, got_ref)):
                    to = pl.ds(pl.multiple_of((2 * p + c) * capacity, capacity), capacity)
                    rows_ref[to, cols] = ref[p * capacity : (p + 1) * capacity, cols]
            block = rows_ref[:, cols]
            for d, ref in ((1 - mine, outs[q]), (mine, outs[pieces + q])):
                units = pl.ds(pl.multiple_of(d * half, 16), half)
                ref[:, out] = jnp.dot(
                    hs_ref[units, :], block, preferred_element_type=jnp.float32
                ).astype(jnp.bfloat16)


def first_products_kernel(half, capacity, mine_ref, got_ref, gslot_ref, hidden_ref, *outs):
    gates_ref, hs_ref = outs[:2]
    pairs = mine_ref.shape[0] // capacity
    got = got_ref[pairs * capacity :, : 2 * capacity].astype(jnp.float32)
    by_pair = gslot_ref[...] + got[:pairs]
    for p in range(pairs):
        gates_ref[:, p * 2 * capacity : (p + 1) * 2 * capacity] = by_pair[p : p + 1, :]
    hs_ref[...] = (hidden_ref[...].astype(jnp.float32) * gates_ref[...]).astype(jnp.bfloat16)
    products(half, capacity, mine_ref, got_ref, hs_ref, *outs[2:])


def raw_halves(half, rows_ref, own_ref, got_refs):
    mine = lax.axis_index("dp")

    def times(w_ref, rows):
        return lax.dot_general(w_ref[...], rows, NT, preferred_element_type=jnp.float32)

    yield pl.ds(pl.multiple_of(mine * half, 16), half), times(own_ref, rows_ref[...])
    part = got_refs[0].shape[1]
    yield (
        pl.ds(pl.multiple_of((1 - mine) * half, 16), half),
        sum(times(ref, rows_ref[:, q * part : (q + 1) * part]) for q, ref in enumerate(got_refs)),
    )


def raw_part_kernel(half, rows_ref, own_ref, *refs):
    for units, raw in raw_halves(half, rows_ref, own_ref, refs[:-1]):
        refs[-1][units, :] = raw


def raw_kernel(half, capacity, rows_ref, own_ref, *refs):
    sum_ref, hidden_ref, gates_ref, grad_ref, back_ref = refs[-5:]
    step = pl.program_id(0)
    gates = gates_ref[...]
    total = jnp.zeros(gates.shape, jnp.float32)
    for units, raw in raw_halves(half, rows_ref, own_ref, refs[:-5]):
        raw += sum_ref[units, :]
        grad_ref[units, :] = (raw * gates).astype(jnp.bfloat16)
        total += jnp.sum(
            raw * hidden_ref[units, :].astype(jnp.float32), axis=0, keepdims=True
        )
    blocks = gates.shape[1] // capacity
    for i in range(blocks):
        back_ref[pl.ds(step * blocks + i, 1), :] = total[:, i * capacity : (i + 1) * capacity]


def gates_kernel(routes_ref, slots_ref, back_ref, out_ref):
    back = back_ref[...]
    routes = routes_ref[...]
    experts, capacity = back.shape
    tokens = routes.shape[1]
    slots = slots_ref[experts : 2 * experts, :].astype(jnp.float32)
    expert = lax.broadcasted_iota(jnp.int32, (experts, tokens), 0)
    slot = lax.broadcasted_iota(jnp.int32, (capacity, tokens), 0).astype(jnp.float32)
    for k in range(out_ref.shape[0]):
        hit = expert == routes[k : k + 1, :]
        number = jnp.sum(jnp.where(hit, slots, 0.0), axis=0, keepdims=True)
        by_expert = jnp.dot(
            back,
            jnp.where(slot == number, 1.0, 0.0),
            preferred_element_type=jnp.float32,
            precision=lax.Precision.HIGHEST,
        )
        out_ref[k : k + 1, :] = jnp.sum(jnp.where(hit, by_expert, 0.0), axis=0, keepdims=True)


def finish_kernel(own_ref, got_ref, *refs):
    refs[-1][...] = (
        own_ref[...].astype(jnp.float32) + got_ref[...].astype(jnp.float32)
    ).astype(jnp.bfloat16)


def ring_shards(grad_out, gates, routes, hidden, down_weight):
    experts = lax.axis_size("expert")
    tokens, chosen = routes.shape
    model = grad_out.shape[1]
    slots, units = hidden.shape[2:]
    half = down_weight.shape[1]
    capacity = slots // experts
    width = model // CHUNKS
    tile = 256
    bf16, f32 = jnp.bfloat16, jnp.float32
    shape = jax.ShapeDtypeStruct
    hidden_t = hidden[0, 0].T
    routes_t, gates_t = routes.T, gates.T
    weight = down_weight[0]
    columns = [pl.BlockSpec((half, width), lambda i, c=c: (0, c)) for c in range(CHUNKS)]
    parts = [pl.BlockSpec((half, PART), lambda i: (0, 0))] * (width // PART)
    dma = pltpu.SemaphoreType.DMA

    def forward(x):
        return lax.ppermute(x, "expert", ring_pairs(1))

    def backward(x):
        return lax.ppermute(x, "expert", ring_pairs(-1))

    def across(x):
        return lax.ppermute(x, "expert", swap_pairs(2))

    def sibling(x):
        return lax.ppermute(x, "expert", swap_pairs(1))

    def swap(x):
        return lax.ppermute(x, "dp", [(0, 1), (1, 0)])

    def behind(x, *others):
        return lax.optimization_barrier((x, *others))[0]

    def pack():
        return pl.pallas_call(
            functools.partial(pack_kernel, experts, width),
            out_shape=shape((tokens, width + tokens), bf16),
            in_specs=[ANY] * 3,
            out_specs=VMEM,
            scratch_shapes=[
                pltpu.VMEM(routes_t.shape, routes_t.dtype),
                pltpu.VMEM(gates_t.shape, gates_t.dtype),
                dma((3,)),
            ],
            compiler_params=params(48),
            name="pack",
        )(routes_t, gates_t, grad_out)

    def later_pack(c, after):
        return pl.pallas_call(
            functools.partial(later_pack_kernel, c * width),
            out_shape=shape((tokens, width), bf16),
            in_specs=[ANY] * 2,
            out_specs=VMEM,
            scratch_shapes=[dma],
            compiler_params=params(48),
            name="later_pack",
        )(grad_out, after)

    mine_shape = shape((slots // 2, width), bf16)

    def first_pick(blocks):
        return pl.pallas_call(
            functools.partial(first_pick_kernel, experts, capacity),
            out_shape=[
                mine_shape,
                shape((slots // 2 + 16, width), bf16),
                shape((slots, tokens), bf16),
                shape((experts // 2, 2 * capacity), f32),
            ],
            in_specs=[VMEM] * len(blocks),
            out_specs=[VMEM] * 4,
            scratch_shapes=[pltpu.VMEM((16, 2 * capacity), f32)],
            compiler_params=params(24),
            cost_estimate=cost(3),
            name="first_pick",
        )(*blocks)

    def later_pick(blocks, pmat):
        return pl.pallas_call(
            pick_kernel,
            out_shape=[mine_shape] * 2,
            in_specs=[VMEM] * (len(blocks) + 1),
            out_specs=[VMEM] * 2,
            compiler_params=params(24),
            name="pick",
        )(*blocks, pmat)

    piece = width // PIECES
    product_shapes = [shape((slots, width), bf16)] + [shape((half, piece), bf16)] * 2 * PIECES

    def first_products(mine, got, gslot):
        slot_gates, hs, rows, *halves = pl.pallas_call(
            functools.partial(first_products_kernel, half, capacity),
            out_shape=[shape((1, slots), f32), shape((units, slots), bf16)] + product_shapes,
            in_specs=[VMEM] * 4,
            out_specs=[VMEM] * (3 + 2 * PIECES),
            compiler_params=params(24),
            cost_estimate=cost(3),
            name="first_products",
        )(mine, got, gslot, hidden_t)
        return rows, halves[:PIECES], halves[PIECES:], slot_gates, hs

    def later_products(mine, got, hs):
        rows, *halves = pl.pallas_call(
            functools.partial(products, half, capacity),
            out_shape=product_shapes,
            in_specs=[VMEM] * 3,
            out_specs=[VMEM] * (1 + 2 * PIECES),
            compiler_params=params(24),
            name="products",
        )(mine, got, hs)
        return rows, halves[:PIECES], halves[PIECES:]

    def raw_part(rows, got_weight):
        return pl.pallas_call(
            functools.partial(raw_part_kernel, half),
            grid=(slots // tile,),
            out_shape=shape((units, slots), f32),
            in_specs=[pl.BlockSpec((tile, width), lambda i: (i, 0)), columns[0]] + parts,
            out_specs=pl.BlockSpec((units, tile), lambda i: (0, i)),
            compiler_params=params(24),
            cost_estimate=cost(3),
            name="raw_part",
        )(rows, weight, *got_weight)

    def raw_rest(rows, got_weight, raw, slot_gates):
        by_slot = pl.BlockSpec((units, tile), lambda i: (0, i))
        return pl.pallas_call(
            functools.partial(raw_kernel, half, capacity),
            grid=(slots // tile,),
            out_shape=[shape((units, slots), bf16), shape((experts, capacity), f32)],
            in_specs=[
                pl.BlockSpec((tile, width), lambda i: (i, 0)),
                columns[1],
                *parts,
                by_slot,
                by_slot,
                pl.BlockSpec((1, tile), lambda i: (0, i)),
            ],
            out_specs=[by_slot, pl.BlockSpec((experts, capacity), lambda i: (0, 0))],
            compiler_params=params(24),
            name="raw",
        )(rows, weight, *got_weight, raw, hidden_t, slot_gates)

    def finish(place, own, got, *before):
        spec = pl.BlockSpec((half // 2, piece), lambda i: (i, 0))
        return pl.pallas_call(
            finish_kernel,
            grid=(2,),
            out_shape=shape((half, model), bf16),
            in_specs=[spec, spec] + [ANY] * len(before),
            out_specs=pl.BlockSpec((half // 2, piece), lambda i: (i, place)),
            input_output_aliases={2: 0} if before else {},
            compiler_params=params(8),
            name="finish",
        )(own, got, *before)

    got_weight = [swap(weight[:, k : k + PART]) for k in range(0, model, PART)]
    x0 = pack()
    pred0, facing0 = forward(x0), across(x0)
    done = (facing0, got_weight[0])
    far0, pred_across0 = forward(behind(pred0, *done)), across(behind(pred0, *done))
    done = (far0, pred_across0, got_weight[1])
    succ0, far_across0 = backward(behind(x0, *done)), across(behind(far0, *done))
    done = (succ0, far_across0, got_weight[2], got_weight[3])
    x1 = later_pack(1, far_across0)
    pred1, succ_across0 = forward(behind(x1, *done)), across(behind(succ0, *done))
    done = (pred1, succ_across0)
    far1, facing1 = forward(behind(pred1, *done)), across(behind(x1, *done))
    mine0, theirs0, pmat, gslot = first_pick(
        [x0, facing0, pred0, pred_across0, far0, far_across0, succ0, behind(succ_across0, pred1)]
    )
    done = (far1, facing1, mine0, got_weight[4])
    succ1, pred_across1 = backward(behind(x1, *done)), across(behind(pred1, *done))
    got = sibling(behind(theirs0, facing1))
    done = (succ1, pred_across1, got, *got_weight[5:7])
    facing_back1, far_across1 = backward(behind(facing1, *done)), across(behind(far1, *done))
    rows0, send0, own0, slot_gates, hs = first_products(mine0, got, gslot)
    got0 = [swap(part) for part in send0]
    raw = raw_part(rows0, got_weight[: len(parts)])
    mine1, theirs1 = later_pick(
        [x1, facing1, pred1, pred_across1, far1, far_across1, succ1, facing_back1],
        behind(pmat, raw, got_weight[7]),
    )
    rows1, send1, own1 = later_products(mine1, sibling(theirs1), behind(hs, got0[0]))
    got1 = [swap(part) for part in send1]

    grad_hidden, back = raw_rest(rows1, got_weight[len(parts) :], raw, slot_gates)
    returned = lax.all_to_all(back, "expert", split_axis=0, concat_axis=0, tiled=True)
    grad_gates = pl.pallas_call(
        gates_kernel,
        grid=(1,),
        out_shape=shape((chosen, tokens), f32),
        in_specs=[
            pl.BlockSpec((chosen, tokens), lambda i: (0, 0)),
            pl.BlockSpec((2 * experts, tokens), lambda i: (0, width // tokens)),
            pl.BlockSpec((experts, capacity), lambda i: (0, 0)),
        ],
        out_specs=pl.BlockSpec((chosen, tokens), lambda i: (0, 0)),
        name="grad_gates",
    )(routes_t, x0, returned)

    grad_weight = ()
    for i, (own, got) in enumerate(zip((*own0, *own1), (*got0, *got1))):
        if i == 0:
            own = behind(own, back)
        grad_weight = (finish(i, own, got, *grad_weight),)
    grad_weight = grad_weight[0]
    return grad_weight[None], grad_hidden.T[None, None], grad_gates.T


def shards(grad_out, gates, routes, hidden, down_weight):
    owners = lax.axis_size("expert")
    token_count, chosen = routes.shape
    width = grad_out.shape[1]
    slots = hidden.shape[2]
    capacity = slots // owners
    flat = routes.reshape(-1)
    onehot = (flat[:, None] == jnp.arange(owners, dtype=jnp.int32)[None, :]).astype(jnp.int32)
    before = jnp.cumsum(onehot, axis=0) - onehot
    slot = jnp.sum(before * onehot, axis=1)
    target = flat * capacity + slot
    send_rows = (
        jnp.zeros((owners * capacity, width), grad_out.dtype)
        .at[target]
        .set(jnp.repeat(grad_out, chosen, axis=0))
    )
    send_gate = jnp.zeros((owners * capacity,), gates.dtype).at[target].set(gates.reshape(-1))
    send_rows = send_rows.reshape(owners, capacity, width)
    send_gate = send_gate.reshape(owners, capacity)
    saved = hidden[0, 0]
    local_weight = down_weight[0]
    contract = (((1,), (1,)), ((), ()))
    rows, gate_slots = (
        lax.all_to_all(send_rows, "expert", split_axis=0, concat_axis=0, tiled=True),
        lax.all_to_all(send_gate, "expert", split_axis=0, concat_axis=0, tiled=True),
    )
    rows = rows.reshape(slots, width)
    whole_weight = lax.all_gather(local_weight, "dp", axis=0, tiled=True)
    raw = lax.dot_general(rows, whole_weight, contract, preferred_element_type=jnp.float32)
    factor = gate_slots.reshape(slots, 1).astype(jnp.float32)
    grad_hidden = (factor * raw).astype(jnp.bfloat16)
    slot_grads = jnp.sum(raw * saved.astype(jnp.float32), axis=1)
    returned = lax.all_to_all(
        slot_grads.reshape(owners, capacity), "expert", split_axis=0, concat_axis=0, tiled=True
    )
    grad_gates = returned.reshape(-1)[target].reshape(token_count, chosen)
    scaled = (factor * rows.astype(jnp.float32)).astype(jnp.bfloat16)
    summed = lax.psum_scatter(
        lax.dot_general(
            saved, scaled, (((0,), (0,)), ((), ())), preferred_element_type=jnp.float32
        ).astype(jnp.bfloat16),
        "dp",
        scatter_dimension=0,
        tiled=True,
    )
    return (summed[None], grad_hidden[None, None], grad_gates)


def solution(mesh):
    small = mesh.shape["dp"] == 2 and mesh.shape["expert"] == NZ * NY * NC
    return jax.shard_map(
        ring_shards if small else shards,
        mesh=mesh,
        in_specs=(
            P(("dp", "expert"), None),
            P(("dp", "expert"), None),
            P(("dp", "expert"), None),
            P("dp", "expert", None, None),
            P("expert", "dp", None),
        ),
        out_specs=(
            P("expert", "dp", None),
            P("dp", "expert", None, None),
            P(("dp", "expert"), None),
        ),
        check_vma=False,
    )
```

```python
import functools

import jax
import jax.numpy as jnp
from jax import lax
from jax.experimental import pallas as pl
from jax.experimental.pallas import tpu as pltpu
from jax.sharding import PartitionSpec as P

NZ, NY, NC = 4, 2, 2
CHUNKS = 2
PIECES = 2
PART = 512
LANES = 128
NT = (((1,), (1,)), ((), ()))
VMEM = pl.BlockSpec(memory_space=pltpu.VMEM)
ANY = pl.BlockSpec(memory_space=pl.ANY)


def params(mib):
    return pltpu.CompilerParams(vmem_limit_bytes=mib * 2**20)


def cost(micros):
    return pl.CostEstimate(
        flops=micros * 10**9, bytes_accessed=micros * 3 * 2**20, transcendentals=0
    )


def ring(z):
    return z ^ (z >> 1)


def ring_pairs(step):
    size = NY * NC
    return [
        (ring(p) * size + rest, ring((p + step) % NZ) * size + rest)
        for p in range(NZ)
        for rest in range(size)
    ]


def swap_pairs(bit):
    return [(i, i ^ bit) for i in range(NZ * NY * NC)]


def pack_kernel(experts, width, routes_hbm, gates_hbm, grad_hbm, out_ref, routes_ref, gates_ref, sems):
    copies = [
        pltpu.make_async_copy(src, dst, sems.at[i])
        for i, (src, dst) in enumerate(
            (
                (routes_hbm, routes_ref),
                (gates_hbm, gates_ref),
                (grad_hbm.at[:, :width], out_ref.at[:, :width]),
            )
        )
    ]
    for copy in copies:
        copy.start()
    copies[0].wait()
    copies[1].wait()
    chosen, tokens = routes_ref.shape
    routes = routes_ref[...]
    gates = gates_ref[...].astype(jnp.float32)
    expert = lax.broadcasted_iota(jnp.int32, (experts, tokens), 0)
    dense = jnp.zeros((experts, tokens), jnp.float32)
    named = jnp.zeros((experts, tokens), jnp.float32)
    for k in range(chosen):
        hit = routes[k : k + 1, :] == expert
        dense = jnp.where(hit, gates[k : k + 1, :], dense)
        named = jnp.where(hit, 1.0, named)
    earlier = (
        lax.broadcasted_iota(jnp.int32, (tokens, tokens), 0)
        < lax.broadcasted_iota(jnp.int32, (tokens, tokens), 1)
    )
    slots = jnp.dot(
        named.astype(jnp.bfloat16),
        jnp.where(earlier, 1.0, 0.0).astype(jnp.bfloat16),
        preferred_element_type=jnp.float32,
    )
    slots = jnp.where(named > 0, slots, -1.0)
    out_ref[:, width:] = jnp.zeros((tokens, tokens), jnp.bfloat16)
    out_ref[:experts, width:] = dense.astype(jnp.bfloat16)
    out_ref[experts : 2 * experts, width:] = slots.astype(jnp.bfloat16)
    copies[2].wait()


def later_pack_kernel(low, grad_hbm, after_ref, out_ref, sem):
    del after_ref
    copy = pltpu.make_async_copy(grad_hbm.at[:, pl.ds(low, out_ref.shape[1])], out_ref, sem)
    copy.start()
    copy.wait()


def pair_place(arrival):
    index = lax.axis_index("expert")
    z, y = index >> 2, (index >> 1) & 1
    z = ring((ring(z) - arrival // NY) & (NZ - 1))
    return z * NY + (y ^ (arrival % NY))


def pick(xs, pmat_ref, mine_ref, theirs_ref):
    capacity = mine_ref.shape[0] // len(xs)

    @pl.loop(0, mine_ref.shape[1] // 256)
    def _(n):
        cols = pl.ds(pl.multiple_of(n * 256, 256), 256)
        for a, x_ref in enumerate(xs):
            rows = jnp.dot(
                pmat_ref[a * 2 * capacity : (a + 1) * 2 * capacity, :],
                x_ref[:, cols],
                preferred_element_type=jnp.float32,
            ).astype(jnp.bfloat16)
            where = pl.ds(pl.multiple_of(pair_place(a) * capacity, capacity), capacity)
            mine_ref[where, cols] = rows[:capacity]
            theirs_ref[where, cols] = rows[capacity:]


def first_pick_kernel(experts, capacity, *refs):
    pairs = experts // 2
    xs = refs[:pairs]
    mine_ref, theirs_ref, pmat_ref, gslot_ref, other_ref = refs[pairs:]
    width = mine_ref.shape[1]
    me = lax.axis_index("expert")
    core = me & 1
    tokens = xs[0].shape[0]
    expert = lax.broadcasted_iota(jnp.int32, (experts, tokens), 0)
    slot = lax.broadcasted_iota(jnp.int32, (2 * capacity, tokens), 0).astype(jnp.float32)
    offset = (core * capacity).astype(jnp.float32)
    other_ref[...] = jnp.zeros(other_ref.shape, jnp.float32)
    for a, x_ref in enumerate(xs):
        place = pl.ds(pair_place(a), 1)
        ext = x_ref[: 2 * experts, width:].astype(jnp.float32)
        one_hot = jnp.zeros(slot.shape, jnp.float32)
        for s, (who, to_ref) in enumerate(((me, gslot_ref), (me ^ 1, other_ref))):
            gate = jnp.sum(jnp.where(expert == who, ext[:experts], 0.0), axis=0, keepdims=True)
            number = jnp.sum(jnp.where(expert == who, ext[experts:], 0.0), axis=0, keepdims=True)
            routed = number >= 0
            spot = jnp.where(routed, number + s * capacity, -1.0)
            one_hot = jnp.where(slot == spot, 1.0, one_hot)
            spot = jnp.where(routed, number + offset, -1.0)
            by_slot = lax.dot_general(
                jnp.broadcast_to(gate.astype(jnp.bfloat16), (16, tokens)),
                jnp.where(slot == spot, 1.0, 0.0).astype(jnp.bfloat16),
                NT,
                preferred_element_type=jnp.float32,
            )
            to_ref[place, :] = by_slot[:1]
        pmat_ref[a * 2 * capacity : (a + 1) * 2 * capacity, :] = one_hot.astype(jnp.bfloat16)
    theirs_ref[pairs * capacity :, :] = jnp.zeros((16, width), jnp.bfloat16)
    theirs_ref[pairs * capacity :, : 2 * capacity] = other_ref[...].astype(jnp.bfloat16)
    pick(xs, pmat_ref, mine_ref, theirs_ref)


def pick_kernel(*refs):
    pick(refs[:-3], *refs[-3:])


def products(half, capacity, mine_ref, got_ref, hs_ref, rows_ref, *outs):
    mine = lax.axis_index("dp")
    core = lax.axis_index("expert") & 1
    pairs = mine_ref.shape[0] // capacity
    pieces = len(outs) // 2
    piece = mine_ref.shape[1] // pieces
    for q in range(pieces):

        @pl.loop(0, piece // 256)
        def _(n, q=q):
            cols = pl.ds(pl.multiple_of(q * piece + n * 256, 256), 256)
            out = pl.ds(pl.multiple_of(n * 256, 256), 256)
            for p in range(pairs):
                for c, ref in ((core, mine_ref), (1 - core, got_ref)):
                    to = pl.ds(pl.multiple_of((2 * p + c) * capacity, capacity), capacity)
                    rows_ref[to, cols] = ref[p * capacity : (p + 1) * capacity, cols]
            block = rows_ref[:, cols]
            for d, ref in ((1 - mine, outs[q]), (mine, outs[pieces + q])):
                units = pl.ds(pl.multiple_of(d * half, 16), half)
                ref[:, out] = jnp.dot(
                    hs_ref[units, :], block, preferred_element_type=jnp.float32
                ).astype(jnp.bfloat16)


def first_products_kernel(half, capacity, mine_ref, got_ref, gslot_ref, hidden_ref, *outs):
    gates_ref, hs_ref = outs[:2]
    pairs = mine_ref.shape[0] // capacity
    got = got_ref[pairs * capacity :, : 2 * capacity].astype(jnp.float32)
    by_pair = gslot_ref[...] + got[:pairs]
    for p in range(pairs):
        gates_ref[:, p * 2 * capacity : (p + 1) * 2 * capacity] = by_pair[p : p + 1, :]
    hs_ref[...] = (hidden_ref[...].astype(jnp.float32) * gates_ref[...]).astype(jnp.bfloat16)
    products(half, capacity, mine_ref, got_ref, hs_ref, *outs[2:])


def raw_halves(half, rows_ref, own_ref, got_refs):
    mine = lax.axis_index("dp")

    def times(w_ref, rows):
        return lax.dot_general(w_ref[...], rows, NT, preferred_element_type=jnp.float32)

    yield pl.ds(pl.multiple_of(mine * half, 16), half), times(own_ref, rows_ref[...])
    part = got_refs[0].shape[1]
    yield (
        pl.ds(pl.multiple_of((1 - mine) * half, 16), half),
        sum(times(ref, rows_ref[:, q * part : (q + 1) * part]) for q, ref in enumerate(got_refs)),
    )


def raw_part_kernel(half, rows_ref, own_ref, *refs):
    for units, raw in raw_halves(half, rows_ref, own_ref, refs[:-1]):
        refs[-1][units, :] = raw


def raw_kernel(half, capacity, rows_ref, own_ref, *refs):
    sum_ref, hidden_ref, gates_ref, grad_ref, back_ref = refs[-5:]
    step = pl.program_id(0)
    gates = gates_ref[...]
    total = jnp.zeros(gates.shape, jnp.float32)
    for units, raw in raw_halves(half, rows_ref, own_ref, refs[:-5]):
        raw += sum_ref[units, :]
        grad_ref[units, :] = (raw * gates).astype(jnp.bfloat16)
        total += jnp.sum(
            raw * hidden_ref[units, :].astype(jnp.float32), axis=0, keepdims=True
        )
    blocks = gates.shape[1] // capacity
    for i in range(blocks):
        back_ref[pl.ds(step * blocks + i, 1), :] = total[:, i * capacity : (i + 1) * capacity]


def gates_kernel(routes_ref, slots_ref, back_ref, out_ref):
    back = back_ref[...]
    routes = routes_ref[...]
    experts, capacity = back.shape
    tokens = routes.shape[1]
    slots = slots_ref[experts : 2 * experts, :].astype(jnp.float32)
    expert = lax.broadcasted_iota(jnp.int32, (experts, tokens), 0)
    slot = lax.broadcasted_iota(jnp.int32, (capacity, tokens), 0).astype(jnp.float32)
    for k in range(out_ref.shape[0]):
        hit = expert == routes[k : k + 1, :]
        number = jnp.sum(jnp.where(hit, slots, 0.0), axis=0, keepdims=True)
        by_expert = jnp.dot(
            back,
            jnp.where(slot == number, 1.0, 0.0),
            preferred_element_type=jnp.float32,
            precision=lax.Precision.HIGHEST,
        )
        out_ref[k : k + 1, :] = jnp.sum(jnp.where(hit, by_expert, 0.0), axis=0, keepdims=True)


def finish_kernel(own_ref, got_ref, *refs):
    refs[-1][...] = (
        own_ref[...].astype(jnp.float32) + got_ref[...].astype(jnp.float32)
    ).astype(jnp.bfloat16)


def ring_shards(grad_out, gates, routes, hidden, down_weight):
    experts = lax.axis_size("expert")
    tokens, chosen = routes.shape
    model = grad_out.shape[1]
    slots, units = hidden.shape[2:]
    half = down_weight.shape[1]
    capacity = slots // experts
    width = model // CHUNKS
    tile = 256
    bf16, f32 = jnp.bfloat16, jnp.float32
    shape = jax.ShapeDtypeStruct
    hidden_t = hidden[0, 0].T
    routes_t, gates_t = routes.T, gates.T
    weight = down_weight[0]
    columns = [pl.BlockSpec((half, width), lambda i, c=c: (0, c)) for c in range(CHUNKS)]
    parts = [pl.BlockSpec((half, PART), lambda i: (0, 0))] * (width // PART)
    dma = pltpu.SemaphoreType.DMA

    def forward(x):
        return lax.ppermute(x, "expert", ring_pairs(1))

    def backward(x):
        return lax.ppermute(x, "expert", ring_pairs(-1))

    def across(x):
        return lax.ppermute(x, "expert", swap_pairs(2))

    def sibling(x):
        return lax.ppermute(x, "expert", swap_pairs(1))

    def swap(x):
        return lax.ppermute(x, "dp", [(0, 1), (1, 0)])

    def behind(x, *others):
        return lax.optimization_barrier((x, *others))[0]

    def pack():
        return pl.pallas_call(
            functools.partial(pack_kernel, experts, width),
            out_shape=shape((tokens, width + tokens), bf16),
            in_specs=[ANY] * 3,
            out_specs=VMEM,
            scratch_shapes=[
                pltpu.VMEM(routes_t.shape, routes_t.dtype),
                pltpu.VMEM(gates_t.shape, gates_t.dtype),
                dma((3,)),
            ],
            compiler_params=params(48),
            name="pack",
        )(routes_t, gates_t, grad_out)

    def later_pack(c, after):
        return pl.pallas_call(
            functools.partial(later_pack_kernel, c * width),
            out_shape=shape((tokens, width), bf16),
            in_specs=[ANY] * 2,
            out_specs=VMEM,
            scratch_shapes=[dma],
            compiler_params=params(48),
            name="later_pack",
        )(grad_out, after)

    mine_shape = shape((slots // 2, width), bf16)

    def first_pick(blocks):
        return pl.pallas_call(
            functools.partial(first_pick_kernel, experts, capacity),
            out_shape=[
                mine_shape,
                shape((slots // 2 + 16, width), bf16),
                shape((slots, tokens), bf16),
                shape((experts // 2, 2 * capacity), f32),
            ],
            in_specs=[VMEM] * len(blocks),
            out_specs=[VMEM] * 4,
            scratch_shapes=[pltpu.VMEM((16, 2 * capacity), f32)],
            compiler_params=params(24),
            cost_estimate=cost(3),
            name="first_pick",
        )(*blocks)

    def later_pick(blocks, pmat):
        return pl.pallas_call(
            pick_kernel,
            out_shape=[mine_shape] * 2,
            in_specs=[VMEM] * (len(blocks) + 1),
            out_specs=[VMEM] * 2,
            compiler_params=params(24),
            name="pick",
        )(*blocks, pmat)

    piece = width // PIECES
    product_shapes = [shape((slots, width), bf16)] + [shape((half, piece), bf16)] * 2 * PIECES

    def first_products(mine, got, gslot):
        slot_gates, hs, rows, *halves = pl.pallas_call(
            functools.partial(first_products_kernel, half, capacity),
            out_shape=[shape((1, slots), f32), shape((units, slots), bf16)] + product_shapes,
            in_specs=[VMEM] * 4,
            out_specs=[VMEM] * (3 + 2 * PIECES),
            compiler_params=params(24),
            cost_estimate=cost(3),
            name="first_products",
        )(mine, got, gslot, hidden_t)
        return rows, halves[:PIECES], halves[PIECES:], slot_gates, hs

    def later_products(mine, got, hs):
        rows, *halves = pl.pallas_call(
            functools.partial(products, half, capacity),
            out_shape=product_shapes,
            in_specs=[VMEM] * 3,
            out_specs=[VMEM] * (1 + 2 * PIECES),
            compiler_params=params(24),
            name="products",
        )(mine, got, hs)
        return rows, halves[:PIECES], halves[PIECES:]

    def raw_part(rows, got_weight):
        return pl.pallas_call(
            functools.partial(raw_part_kernel, half),
            grid=(slots // tile,),
            out_shape=shape((units, slots), f32),
            in_specs=[pl.BlockSpec((tile, width), lambda i: (i, 0)), columns[0]] + parts,
            out_specs=pl.BlockSpec((units, tile), lambda i: (0, i)),
            compiler_params=params(24),
            cost_estimate=cost(3),
            name="raw_part",
        )(rows, weight, *got_weight)

    def raw_rest(rows, got_weight, raw, slot_gates):
        by_slot = pl.BlockSpec((units, tile), lambda i: (0, i))
        return pl.pallas_call(
            functools.partial(raw_kernel, half, capacity),
            grid=(slots // tile,),
            out_shape=[shape((units, slots), bf16), shape((experts, capacity), f32)],
            in_specs=[
                pl.BlockSpec((tile, width), lambda i: (i, 0)),
                columns[1],
                *parts,
                by_slot,
                by_slot,
                pl.BlockSpec((1, tile), lambda i: (0, i)),
            ],
            out_specs=[by_slot, pl.BlockSpec((experts, capacity), lambda i: (0, 0))],
            compiler_params=params(24),
            name="raw",
        )(rows, weight, *got_weight, raw, hidden_t, slot_gates)

    def finish(place, own, got, *before):
        spec = pl.BlockSpec((half // 2, piece), lambda i: (i, 0))
        return pl.pallas_call(
            finish_kernel,
            grid=(2,),
            out_shape=shape((half, model), bf16),
            in_specs=[spec, spec] + [ANY] * len(before),
            out_specs=pl.BlockSpec((half // 2, piece), lambda i: (i, place)),
            input_output_aliases={2: 0} if before else {},
            compiler_params=params(8),
            name="finish",
        )(own, got, *before)

    w = [swap(weight[:, k : k + PART]) for k in range(0, model, PART)]
    x0 = pack()
    f0, r0, y0 = forward(x0), backward(x0), across(x0)
    ff0, yf0 = forward(behind(f0, w[0])), across(behind(f0, w[0]))
    x1 = later_pack(1, r0)
    f1, yr0 = forward(x1), across(behind(r0, y0))
    r1, yff0 = backward(behind(x1, ff0)), across(behind(ff0, yf0, w[1]))
    mine0, theirs0, pmat, gslot = first_pick(
        [x0, y0, f0, yf0, ff0, yff0, r0, behind(yr0, f1, w[2])]
    )
    ff1, y1 = forward(f1), across(behind(x1, yr0))
    yf1 = across(behind(f1, yff0, w[3]))
    ry1 = backward(behind(y1, r1, mine0, w[3]))
    got = sibling(theirs0)
    rows0, send0, own0, slot_gates, hs = first_products(mine0, got, gslot)
    got0 = [swap(part) for part in send0]
    yff1 = across(behind(ff1, y1))
    raw = raw_part(rows0, w[: len(parts)])
    mine1, theirs1 = later_pick(
        [x1, y1, f1, yf1, ff1, yff1, r1, ry1], behind(pmat, raw, got0[0])
    )
    rows1, send1, own1 = later_products(mine1, sibling(theirs1), hs)
    got1 = [swap(part) for part in send1]

    grad_hidden, back = raw_rest(rows1, w[len(parts) :], raw, slot_gates)
    returned = lax.all_to_all(back, "expert", split_axis=0, concat_axis=0, tiled=True)
    grad_gates = pl.pallas_call(
        gates_kernel,
        grid=(1,),
        out_shape=shape((chosen, tokens), f32),
        in_specs=[
            pl.BlockSpec((chosen, tokens), lambda i: (0, 0)),
            pl.BlockSpec((2 * experts, tokens), lambda i: (0, width // tokens)),
            pl.BlockSpec((experts, capacity), lambda i: (0, 0)),
        ],
        out_specs=pl.BlockSpec((chosen, tokens), lambda i: (0, 0)),
        name="grad_gates",
    )(routes_t, x0, returned)

    grad_weight = ()
    for i, (own, got) in enumerate(zip((*own0, *own1), (*got0, *got1))):
        if i == 0:
            own = behind(own, back)
        grad_weight = (finish(i, own, got, *grad_weight),)
    grad_weight = grad_weight[0]
    return grad_weight[None], grad_hidden.T[None, None], grad_gates.T


def shards(grad_out, gates, routes, hidden, down_weight):
    owners = lax.axis_size("expert")
    token_count, chosen = routes.shape
    width = grad_out.shape[1]
    slots = hidden.shape[2]
    capacity = slots // owners
    flat = routes.reshape(-1)
    onehot = (flat[:, None] == jnp.arange(owners, dtype=jnp.int32)[None, :]).astype(jnp.int32)
    before = jnp.cumsum(onehot, axis=0) - onehot
    slot = jnp.sum(before * onehot, axis=1)
    target = flat * capacity + slot
    send_rows = (
        jnp.zeros((owners * capacity, width), grad_out.dtype)
        .at[target]
        .set(jnp.repeat(grad_out, chosen, axis=0))
    )
    send_gate = jnp.zeros((owners * capacity,), gates.dtype).at[target].set(gates.reshape(-1))
    send_rows = send_rows.reshape(owners, capacity, width)
    send_gate = send_gate.reshape(owners, capacity)
    saved = hidden[0, 0]
    local_weight = down_weight[0]
    contract = (((1,), (1,)), ((), ()))
    rows, gate_slots = (
        lax.all_to_all(send_rows, "expert", split_axis=0, concat_axis=0, tiled=True),
        lax.all_to_all(send_gate, "expert", split_axis=0, concat_axis=0, tiled=True),
    )
    rows = rows.reshape(slots, width)
    whole_weight = lax.all_gather(local_weight, "dp", axis=0, tiled=True)
    raw = lax.dot_general(rows, whole_weight, contract, preferred_element_type=jnp.float32)
    factor = gate_slots.reshape(slots, 1).astype(jnp.float32)
    grad_hidden = (factor * raw).astype(jnp.bfloat16)
    slot_grads = jnp.sum(raw * saved.astype(jnp.float32), axis=1)
    returned = lax.all_to_all(
        slot_grads.reshape(owners, capacity), "expert", split_axis=0, concat_axis=0, tiled=True
    )
    grad_gates = returned.reshape(-1)[target].reshape(token_count, chosen)
    scaled = (factor * rows.astype(jnp.float32)).astype(jnp.bfloat16)
    summed = lax.psum_scatter(
        lax.dot_general(
            saved, scaled, (((0,), (0,)), ((), ())), preferred_element_type=jnp.float32
        ).astype(jnp.bfloat16),
        "dp",
        scatter_dimension=0,
        tiled=True,
    )
    return (summed[None], grad_hidden[None, None], grad_gates)


def solution(mesh):
    small = mesh.shape["dp"] == 2 and mesh.shape["expert"] == NZ * NY * NC
    return jax.shard_map(
        ring_shards if small else shards,
        mesh=mesh,
        in_specs=(
            P(("dp", "expert"), None),
            P(("dp", "expert"), None),
            P(("dp", "expert"), None),
            P("dp", "expert", None, None),
            P("expert", "dp", None),
        ),
        out_specs=(
            P("expert", "dp", None),
            P("dp", "expert", None, None),
            P(("dp", "expert"), None),
        ),
        check_vma=False,
    )
```

```python
import functools

import jax
import jax.numpy as jnp
from jax import lax
from jax.experimental import pallas as pl
from jax.experimental.pallas import tpu as pltpu
from jax.sharding import PartitionSpec as P

NZ, NY, NC = 4, 2, 2
CHUNKS = 2
PIECES = 2
LANES = 128
NT = (((1,), (1,)), ((), ()))
VMEM = pl.BlockSpec(memory_space=pltpu.VMEM)
ANY = pl.BlockSpec(memory_space=pl.ANY)


def params(mib):
    return pltpu.CompilerParams(vmem_limit_bytes=mib * 2**20)


def cost(micros):
    return pl.CostEstimate(
        flops=micros * 10**9, bytes_accessed=micros * 3 * 2**20, transcendentals=0
    )


def ring(z):
    return z ^ (z >> 1)


def ring_pairs(step):
    size = NY * NC
    return [
        (ring(p) * size + rest, ring((p + step) % NZ) * size + rest)
        for p in range(NZ)
        for rest in range(size)
    ]


def swap_pairs(bit):
    return [(i, i ^ bit) for i in range(NZ * NY * NC)]


def pack_kernel(experts, width, routes_hbm, gates_hbm, grad_hbm, out_ref, routes_ref, gates_ref, sems):
    copies = [
        pltpu.make_async_copy(src, dst, sems.at[i])
        for i, (src, dst) in enumerate(
            (
                (routes_hbm, routes_ref),
                (gates_hbm, gates_ref),
                (grad_hbm.at[:, :width], out_ref.at[:, :width]),
            )
        )
    ]
    for copy in copies:
        copy.start()
    copies[0].wait()
    copies[1].wait()
    chosen, tokens = routes_ref.shape
    routes = routes_ref[...]
    gates = gates_ref[...].astype(jnp.float32)
    expert = lax.broadcasted_iota(jnp.int32, (experts, tokens), 0)
    dense = jnp.zeros((experts, tokens), jnp.float32)
    named = jnp.zeros((experts, tokens), jnp.float32)
    for k in range(chosen):
        hit = routes[k : k + 1, :] == expert
        dense = jnp.where(hit, gates[k : k + 1, :], dense)
        named = jnp.where(hit, 1.0, named)
    earlier = (
        lax.broadcasted_iota(jnp.int32, (tokens, tokens), 0)
        < lax.broadcasted_iota(jnp.int32, (tokens, tokens), 1)
    )
    slots = jnp.dot(
        named.astype(jnp.bfloat16),
        jnp.where(earlier, 1.0, 0.0).astype(jnp.bfloat16),
        preferred_element_type=jnp.float32,
    )
    slots = jnp.where(named > 0, slots, -1.0)
    out_ref[:, width:] = jnp.zeros((tokens, tokens), jnp.bfloat16)
    out_ref[:experts, width:] = dense.astype(jnp.bfloat16)
    out_ref[experts : 2 * experts, width:] = slots.astype(jnp.bfloat16)
    copies[2].wait()


def later_pack_kernel(low, grad_hbm, after_ref, out_ref, sem):
    del after_ref
    copy = pltpu.make_async_copy(grad_hbm.at[:, pl.ds(low, out_ref.shape[1])], out_ref, sem)
    copy.start()
    copy.wait()


def pair_place(arrival):
    index = lax.axis_index("expert")
    z, y = index >> 2, (index >> 1) & 1
    z = ring((ring(z) - arrival // NY) & (NZ - 1))
    return z * NY + (y ^ (arrival % NY))


def pick(xs, pmat_ref, mine_ref, theirs_ref):
    capacity = mine_ref.shape[0] // len(xs)

    @pl.loop(0, mine_ref.shape[1] // 256)
    def _(n):
        cols = pl.ds(pl.multiple_of(n * 256, 256), 256)
        for a, x_ref in enumerate(xs):
            rows = jnp.dot(
                pmat_ref[a * 2 * capacity : (a + 1) * 2 * capacity, :],
                x_ref[:, cols],
                preferred_element_type=jnp.float32,
            ).astype(jnp.bfloat16)
            where = pl.ds(pl.multiple_of(pair_place(a) * capacity, capacity), capacity)
            mine_ref[where, cols] = rows[:capacity]
            theirs_ref[where, cols] = rows[capacity:]


def first_pick_kernel(experts, capacity, *refs):
    pairs = experts // 2
    xs = refs[:pairs]
    mine_ref, theirs_ref, pmat_ref, gslot_ref, other_ref = refs[pairs:]
    width = mine_ref.shape[1]
    me = lax.axis_index("expert")
    core = me & 1
    tokens = xs[0].shape[0]
    expert = lax.broadcasted_iota(jnp.int32, (experts, tokens), 0)
    slot = lax.broadcasted_iota(jnp.int32, (2 * capacity, tokens), 0).astype(jnp.float32)
    offset = (core * capacity).astype(jnp.float32)
    other_ref[...] = jnp.zeros(other_ref.shape, jnp.float32)
    for a, x_ref in enumerate(xs):
        place = pl.ds(pair_place(a), 1)
        ext = x_ref[: 2 * experts, width:].astype(jnp.float32)
        one_hot = jnp.zeros(slot.shape, jnp.float32)
        for s, (who, to_ref) in enumerate(((me, gslot_ref), (me ^ 1, other_ref))):
            gate = jnp.sum(jnp.where(expert == who, ext[:experts], 0.0), axis=0, keepdims=True)
            number = jnp.sum(jnp.where(expert == who, ext[experts:], 0.0), axis=0, keepdims=True)
            routed = number >= 0
            spot = jnp.where(routed, number + s * capacity, -1.0)
            one_hot = jnp.where(slot == spot, 1.0, one_hot)
            spot = jnp.where(routed, number + offset, -1.0)
            by_slot = lax.dot_general(
                jnp.broadcast_to(gate.astype(jnp.bfloat16), (16, tokens)),
                jnp.where(slot == spot, 1.0, 0.0).astype(jnp.bfloat16),
                NT,
                preferred_element_type=jnp.float32,
            )
            to_ref[place, :] = by_slot[:1]
        pmat_ref[a * 2 * capacity : (a + 1) * 2 * capacity, :] = one_hot.astype(jnp.bfloat16)
    theirs_ref[pairs * capacity :, :] = jnp.zeros((16, width), jnp.bfloat16)
    theirs_ref[pairs * capacity :, : 2 * capacity] = other_ref[...].astype(jnp.bfloat16)
    pick(xs, pmat_ref, mine_ref, theirs_ref)


def pick_kernel(*refs):
    pick(refs[:-3], *refs[-3:])


def products(half, capacity, mine_ref, got_ref, hs_ref, rows_ref, *outs):
    mine = lax.axis_index("dp")
    core = lax.axis_index("expert") & 1
    pairs = mine_ref.shape[0] // capacity
    pieces = len(outs) // 2
    piece = mine_ref.shape[1] // pieces
    for q in range(pieces):

        @pl.loop(0, piece // 256)
        def _(n, q=q):
            cols = pl.ds(pl.multiple_of(q * piece + n * 256, 256), 256)
            out = pl.ds(pl.multiple_of(n * 256, 256), 256)
            for p in range(pairs):
                for c, ref in ((core, mine_ref), (1 - core, got_ref)):
                    to = pl.ds(pl.multiple_of((2 * p + c) * capacity, capacity), capacity)
                    rows_ref[to, cols] = ref[p * capacity : (p + 1) * capacity, cols]
            block = rows_ref[:, cols]
            for d, ref in ((1 - mine, outs[q]), (mine, outs[pieces + q])):
                units = pl.ds(pl.multiple_of(d * half, 16), half)
                ref[:, out] = jnp.dot(
                    hs_ref[units, :], block, preferred_element_type=jnp.float32
                ).astype(jnp.bfloat16)


def first_products_kernel(half, capacity, mine_ref, got_ref, gslot_ref, hidden_ref, *outs):
    gates_ref, hs_ref = outs[:2]
    pairs = mine_ref.shape[0] // capacity
    got = got_ref[pairs * capacity :, : 2 * capacity].astype(jnp.float32)
    by_pair = gslot_ref[...] + got[:pairs]
    for p in range(pairs):
        gates_ref[:, p * 2 * capacity : (p + 1) * 2 * capacity] = by_pair[p : p + 1, :]
    hs_ref[...] = (hidden_ref[...].astype(jnp.float32) * gates_ref[...]).astype(jnp.bfloat16)
    products(half, capacity, mine_ref, got_ref, hs_ref, *outs[2:])


def raw_parts(half, rows_ref, own_ref, got_refs):
    mine = lax.axis_index("dp")
    at = mine * half
    for w_ref in (own_ref, *got_refs):
        units = pl.ds(pl.multiple_of(at, 16), w_ref.shape[0])
        yield units, lax.dot_general(
            w_ref[...], rows_ref[...], NT, preferred_element_type=jnp.float32
        )
        at = at + w_ref.shape[0] if w_ref is not own_ref else (1 - mine) * half


def raw_part_kernel(half, rows_ref, own_ref, *refs):
    for units, raw in raw_parts(half, rows_ref, own_ref, refs[:-1]):
        refs[-1][units, :] = raw


def raw_kernel(half, capacity, rows_ref, own_ref, *refs):
    sum_ref, hidden_ref, gates_ref, grad_ref, back_ref = refs[-5:]
    step = pl.program_id(0)
    gates = gates_ref[...]
    total = jnp.zeros(gates.shape, jnp.float32)
    for units, raw in raw_parts(half, rows_ref, own_ref, refs[:-5]):
        raw += sum_ref[units, :]
        grad_ref[units, :] = (raw * gates).astype(jnp.bfloat16)
        total += jnp.sum(
            raw * hidden_ref[units, :].astype(jnp.float32), axis=0, keepdims=True
        )
    blocks = gates.shape[1] // capacity
    for i in range(blocks):
        back_ref[pl.ds(step * blocks + i, 1), :] = total[:, i * capacity : (i + 1) * capacity]


def gates_kernel(routes_ref, slots_ref, back_ref, out_ref):
    back = back_ref[...]
    routes = routes_ref[...]
    experts, capacity = back.shape
    tokens = routes.shape[1]
    slots = slots_ref[experts : 2 * experts, :].astype(jnp.float32)
    expert = lax.broadcasted_iota(jnp.int32, (experts, tokens), 0)
    slot = lax.broadcasted_iota(jnp.int32, (capacity, tokens), 0).astype(jnp.float32)
    for k in range(out_ref.shape[0]):
        hit = expert == routes[k : k + 1, :]
        number = jnp.sum(jnp.where(hit, slots, 0.0), axis=0, keepdims=True)
        by_expert = jnp.dot(
            back,
            jnp.where(slot == number, 1.0, 0.0),
            preferred_element_type=jnp.float32,
            precision=lax.Precision.HIGHEST,
        )
        out_ref[k : k + 1, :] = jnp.sum(jnp.where(hit, by_expert, 0.0), axis=0, keepdims=True)


def finish_kernel(own_ref, got_ref, *refs):
    refs[-1][...] = (
        own_ref[...].astype(jnp.float32) + got_ref[...].astype(jnp.float32)
    ).astype(jnp.bfloat16)


def ring_shards(grad_out, gates, routes, hidden, down_weight):
    experts = lax.axis_size("expert")
    tokens, chosen = routes.shape
    model = grad_out.shape[1]
    slots, units = hidden.shape[2:]
    half = down_weight.shape[1]
    capacity = slots // experts
    width = model // CHUNKS
    tile = 256
    bf16, f32 = jnp.bfloat16, jnp.float32
    shape = jax.ShapeDtypeStruct
    hidden_t = hidden[0, 0].T
    routes_t, gates_t = routes.T, gates.T
    weight = down_weight[0]
    columns = [pl.BlockSpec((half, width), lambda i, c=c: (0, c)) for c in range(CHUNKS)]
    split = half * 6 // 11 // 32 * 32
    parts = [
        [pl.BlockSpec((n, width), lambda i, c=c: (0, c)) for n in (split, half - split)]
        for c in range(CHUNKS)
    ]
    dma = pltpu.SemaphoreType.DMA

    def forward(x):
        return lax.ppermute(x, "expert", ring_pairs(1))

    def backward(x):
        return lax.ppermute(x, "expert", ring_pairs(-1))

    def across(x):
        return lax.ppermute(x, "expert", swap_pairs(2))

    def sibling(x):
        return lax.ppermute(x, "expert", swap_pairs(1))

    def swap(x):
        return lax.ppermute(x, "dp", [(0, 1), (1, 0)])

    def behind(x, *others):
        return lax.optimization_barrier((x, *others))[0]

    def pack():
        return pl.pallas_call(
            functools.partial(pack_kernel, experts, width),
            out_shape=shape((tokens, width + tokens), bf16),
            in_specs=[ANY] * 3,
            out_specs=VMEM,
            scratch_shapes=[
                pltpu.VMEM(routes_t.shape, routes_t.dtype),
                pltpu.VMEM(gates_t.shape, gates_t.dtype),
                dma((3,)),
            ],
            compiler_params=params(48),
            name="pack",
        )(routes_t, gates_t, grad_out)

    def later_pack(c, after):
        return pl.pallas_call(
            functools.partial(later_pack_kernel, c * width),
            out_shape=shape((tokens, width), bf16),
            in_specs=[ANY] * 2,
            out_specs=VMEM,
            scratch_shapes=[dma],
            compiler_params=params(48),
            name="later_pack",
        )(grad_out, after)

    mine_shape = shape((slots // 2, width), bf16)

    def first_pick(blocks):
        return pl.pallas_call(
            functools.partial(first_pick_kernel, experts, capacity),
            out_shape=[
                mine_shape,
                shape((slots // 2 + 16, width), bf16),
                shape((slots, tokens), bf16),
                shape((experts // 2, 2 * capacity), f32),
            ],
            in_specs=[VMEM] * len(blocks),
            out_specs=[VMEM] * 4,
            scratch_shapes=[pltpu.VMEM((16, 2 * capacity), f32)],
            compiler_params=params(24),
            cost_estimate=cost(3),
            name="first_pick",
        )(*blocks)

    def later_pick(blocks, pmat):
        return pl.pallas_call(
            pick_kernel,
            out_shape=[mine_shape] * 2,
            in_specs=[VMEM] * (len(blocks) + 1),
            out_specs=[VMEM] * 2,
            compiler_params=params(24),
            name="pick",
        )(*blocks, pmat)

    piece = width // PIECES
    product_shapes = [shape((slots, width), bf16)] + [shape((half, piece), bf16)] * 2 * PIECES

    def first_products(mine, got, gslot):
        slot_gates, hs, rows, *halves = pl.pallas_call(
            functools.partial(first_products_kernel, half, capacity),
            out_shape=[shape((1, slots), f32), shape((units, slots), bf16)] + product_shapes,
            in_specs=[VMEM] * 4,
            out_specs=[VMEM] * (3 + 2 * PIECES),
            compiler_params=params(24),
            cost_estimate=cost(3),
            name="first_products",
        )(mine, got, gslot, hidden_t)
        return rows, halves[:PIECES], halves[PIECES:], slot_gates, hs

    def later_products(mine, got, hs):
        rows, *halves = pl.pallas_call(
            functools.partial(products, half, capacity),
            out_shape=product_shapes,
            in_specs=[VMEM] * 3,
            out_specs=[VMEM] * (1 + 2 * PIECES),
            compiler_params=params(24),
            name="products",
        )(mine, got, hs)
        return rows, halves[:PIECES], halves[PIECES:]

    def raw_part(rows, got_weight):
        return pl.pallas_call(
            functools.partial(raw_part_kernel, half),
            grid=(slots // tile,),
            out_shape=shape((units, slots), f32),
            in_specs=[pl.BlockSpec((tile, width), lambda i: (i, 0)), columns[0]] + parts[0],
            out_specs=pl.BlockSpec((units, tile), lambda i: (0, i)),
            compiler_params=params(24),
            cost_estimate=cost(3),
            name="raw_part",
        )(rows, weight, *got_weight)

    def raw_rest(rows, got_weight, raw, slot_gates):
        by_slot = pl.BlockSpec((units, tile), lambda i: (0, i))
        return pl.pallas_call(
            functools.partial(raw_kernel, half, capacity),
            grid=(slots // tile,),
            out_shape=[shape((units, slots), bf16), shape((experts, capacity), f32)],
            in_specs=[
                pl.BlockSpec((tile, width), lambda i: (i, 0)),
                columns[1],
                *parts[1],
                by_slot,
                by_slot,
                pl.BlockSpec((1, tile), lambda i: (0, i)),
            ],
            out_specs=[by_slot, pl.BlockSpec((experts, capacity), lambda i: (0, 0))],
            compiler_params=params(24),
            name="raw",
        )(rows, weight, *got_weight, raw, hidden_t, slot_gates)

    def finish(place, own, got, *before):
        spec = pl.BlockSpec((half // 2, piece), lambda i: (i, 0))
        return pl.pallas_call(
            finish_kernel,
            grid=(2,),
            out_shape=shape((half, model), bf16),
            in_specs=[spec, spec] + [ANY] * len(before),
            out_specs=pl.BlockSpec((half // 2, piece), lambda i: (i, place)),
            input_output_aliases={2: 0} if before else {},
            compiler_params=params(8),
            name="finish",
        )(own, got, *before)

    x0 = pack()
    w = [swap(weight[:split]), swap(weight[split:])]
    x1 = later_pack(1, x0)
    f0, r0, y0 = forward(x0), backward(x0), across(x0)
    ff0, yf0 = forward(f0), across(f0)
    y1 = across(behind(x1, y0))
    f1, yr0 = forward(behind(x1, r0)), across(behind(r0, y1))
    yff0 = across(behind(ff0, yf0, w[0]))
    ry1 = backward(behind(y1, ff0))
    mine0, theirs0, pmat, gslot = first_pick([x0, y0, f0, yf0, ff0, yff0, r0, behind(yr0, w[1])])
    got = sibling(behind(theirs0, f1))
    ff1, yf1 = forward(f1), across(behind(f1, yff0))
    r1 = backward(behind(x1, ry1))
    rows0, send0, own0, slot_gates, hs = first_products(mine0, got, gslot)
    got0 = [swap(part) for part in send0]
    yff1 = across(behind(ff1, yf1))
    raw = raw_part(rows0, w)
    mine1, theirs1 = later_pick(
        [x1, y1, f1, yf1, ff1, yff1, r1, ry1], behind(pmat, raw, got0[0])
    )
    rows1, send1, own1 = later_products(mine1, sibling(theirs1), hs)
    got1 = [swap(part) for part in send1]

    grad_hidden, back = raw_rest(rows1, w, raw, slot_gates)
    returned = lax.all_to_all(back, "expert", split_axis=0, concat_axis=0, tiled=True)
    grad_gates = pl.pallas_call(
        gates_kernel,
        grid=(1,),
        out_shape=shape((chosen, tokens), f32),
        in_specs=[
            pl.BlockSpec((chosen, tokens), lambda i: (0, 0)),
            pl.BlockSpec((2 * experts, tokens), lambda i: (0, width // tokens)),
            pl.BlockSpec((experts, capacity), lambda i: (0, 0)),
        ],
        out_specs=pl.BlockSpec((chosen, tokens), lambda i: (0, 0)),
        name="grad_gates",
    )(routes_t, x0, returned)

    grad_weight = ()
    for i, (own, got) in enumerate(zip((*own0, *own1), (*got0, *got1))):
        if i == 0:
            own = behind(own, back)
        grad_weight = (finish(i, own, got, *grad_weight),)
    grad_weight = grad_weight[0]
    return grad_weight[None], grad_hidden.T[None, None], grad_gates.T


def shards(grad_out, gates, routes, hidden, down_weight):
    owners = lax.axis_size("expert")
    token_count, chosen = routes.shape
    width = grad_out.shape[1]
    slots = hidden.shape[2]
    capacity = slots // owners
    flat = routes.reshape(-1)
    onehot = (flat[:, None] == jnp.arange(owners, dtype=jnp.int32)[None, :]).astype(jnp.int32)
    before = jnp.cumsum(onehot, axis=0) - onehot
    slot = jnp.sum(before * onehot, axis=1)
    target = flat * capacity + slot
    send_rows = (
        jnp.zeros((owners * capacity, width), grad_out.dtype)
        .at[target]
        .set(jnp.repeat(grad_out, chosen, axis=0))
    )
    send_gate = jnp.zeros((owners * capacity,), gates.dtype).at[target].set(gates.reshape(-1))
    send_rows = send_rows.reshape(owners, capacity, width)
    send_gate = send_gate.reshape(owners, capacity)
    saved = hidden[0, 0]
    local_weight = down_weight[0]
    contract = (((1,), (1,)), ((), ()))
    rows, gate_slots = (
        lax.all_to_all(send_rows, "expert", split_axis=0, concat_axis=0, tiled=True),
        lax.all_to_all(send_gate, "expert", split_axis=0, concat_axis=0, tiled=True),
    )
    rows = rows.reshape(slots, width)
    whole_weight = lax.all_gather(local_weight, "dp", axis=0, tiled=True)
    raw = lax.dot_general(rows, whole_weight, contract, preferred_element_type=jnp.float32)
    factor = gate_slots.reshape(slots, 1).astype(jnp.float32)
    grad_hidden = (factor * raw).astype(jnp.bfloat16)
    slot_grads = jnp.sum(raw * saved.astype(jnp.float32), axis=1)
    returned = lax.all_to_all(
        slot_grads.reshape(owners, capacity), "expert", split_axis=0, concat_axis=0, tiled=True
    )
    grad_gates = returned.reshape(-1)[target].reshape(token_count, chosen)
    scaled = (factor * rows.astype(jnp.float32)).astype(jnp.bfloat16)
    summed = lax.psum_scatter(
        lax.dot_general(
            saved, scaled, (((0,), (0,)), ((), ())), preferred_element_type=jnp.float32
        ).astype(jnp.bfloat16),
        "dp",
        scatter_dimension=0,
        tiled=True,
    )
    return (summed[None], grad_hidden[None, None], grad_gates)


def solution(mesh):
    small = mesh.shape["dp"] == 2 and mesh.shape["expert"] == NZ * NY * NC
    return jax.shard_map(
        ring_shards if small else shards,
        mesh=mesh,
        in_specs=(
            P(("dp", "expert"), None),
            P(("dp", "expert"), None),
            P(("dp", "expert"), None),
            P("dp", "expert", None, None),
            P("expert", "dp", None),
        ),
        out_specs=(
            P("expert", "dp", None),
            P("dp", "expert", None, None),
            P(("dp", "expert"), None),
        ),
        check_vma=False,
    )
```

```python
import functools

import jax
import jax.numpy as jnp
from jax import lax
from jax.experimental import pallas as pl
from jax.experimental.pallas import tpu as pltpu
from jax.sharding import PartitionSpec as P

NZ, NY, NC = 4, 2, 2
CHUNKS = 2
PIECES = (2, 2)
PART = 512
LANES = 128
NT = (((1,), (1,)), ((), ()))
VMEM = pl.BlockSpec(memory_space=pltpu.VMEM)
ANY = pl.BlockSpec(memory_space=pl.ANY)


def params(mib):
    return pltpu.CompilerParams(vmem_limit_bytes=mib * 2**20)


def cost(micros):
    return pl.CostEstimate(
        flops=micros * 10**9, bytes_accessed=micros * 3 * 2**20, transcendentals=0
    )


def ring(z):
    return z ^ (z >> 1)


def ring_pairs(step):
    size = NY * NC
    return [
        (ring(p) * size + rest, ring((p + step) % NZ) * size + rest)
        for p in range(NZ)
        for rest in range(size)
    ]


def swap_pairs(bit):
    return [(i, i ^ bit) for i in range(NZ * NY * NC)]


def pack_kernel(experts, width, routes_hbm, gates_hbm, grad_hbm, out_ref, routes_ref, gates_ref, sems):
    copies = [
        pltpu.make_async_copy(src, dst, sems.at[i])
        for i, (src, dst) in enumerate(
            (
                (routes_hbm, routes_ref),
                (gates_hbm, gates_ref),
                (grad_hbm.at[:, :width], out_ref.at[:, :width]),
            )
        )
    ]
    for copy in copies:
        copy.start()
    copies[0].wait()
    copies[1].wait()
    chosen, tokens = routes_ref.shape
    routes = routes_ref[...]
    gates = gates_ref[...].astype(jnp.float32)
    expert = lax.broadcasted_iota(jnp.int32, (experts, tokens), 0)
    dense = jnp.zeros((experts, tokens), jnp.float32)
    named = jnp.zeros((experts, tokens), jnp.float32)
    for k in range(chosen):
        hit = routes[k : k + 1, :] == expert
        dense = jnp.where(hit, gates[k : k + 1, :], dense)
        named = jnp.where(hit, 1.0, named)
    earlier = (
        lax.broadcasted_iota(jnp.int32, (tokens, tokens), 0)
        < lax.broadcasted_iota(jnp.int32, (tokens, tokens), 1)
    )
    slots = jnp.dot(
        named.astype(jnp.bfloat16),
        jnp.where(earlier, 1.0, 0.0).astype(jnp.bfloat16),
        preferred_element_type=jnp.float32,
    )
    slots = jnp.where(named > 0, slots, -1.0)
    out_ref[:, width:] = jnp.zeros((tokens, tokens), jnp.bfloat16)
    out_ref[:experts, width:] = dense.astype(jnp.bfloat16)
    out_ref[experts : 2 * experts, width:] = slots.astype(jnp.bfloat16)
    copies[2].wait()


def later_pack_kernel(low, grad_hbm, after_ref, out_ref, sem):
    del after_ref
    copy = pltpu.make_async_copy(grad_hbm.at[:, pl.ds(low, out_ref.shape[1])], out_ref, sem)
    copy.start()
    copy.wait()


def pair_place(arrival):
    index = lax.axis_index("expert")
    z, y = index >> 2, (index >> 1) & 1
    z = ring((ring(z) - arrival // NY) & (NZ - 1))
    return z * NY + (y ^ (arrival % NY))


def pick(xs, pmat_ref, mine_ref, theirs_ref):
    capacity = mine_ref.shape[0] // len(xs)

    @pl.loop(0, mine_ref.shape[1] // 256)
    def _(n):
        cols = pl.ds(pl.multiple_of(n * 256, 256), 256)
        for a, x_ref in enumerate(xs):
            rows = jnp.dot(
                pmat_ref[a * 2 * capacity : (a + 1) * 2 * capacity, :],
                x_ref[:, cols],
                preferred_element_type=jnp.float32,
            ).astype(jnp.bfloat16)
            where = pl.ds(pl.multiple_of(pair_place(a) * capacity, capacity), capacity)
            mine_ref[where, cols] = rows[:capacity]
            theirs_ref[where, cols] = rows[capacity:]


def first_pick_kernel(experts, capacity, *refs):
    pairs = experts // 2
    xs = refs[:pairs]
    mine_ref, theirs_ref, pmat_ref, gslot_ref, other_ref = refs[pairs:]
    width = mine_ref.shape[1]
    me = lax.axis_index("expert")
    core = me & 1
    tokens = xs[0].shape[0]
    expert = lax.broadcasted_iota(jnp.int32, (experts, tokens), 0)
    slot = lax.broadcasted_iota(jnp.int32, (2 * capacity, tokens), 0).astype(jnp.float32)
    offset = (core * capacity).astype(jnp.float32)
    other_ref[...] = jnp.zeros(other_ref.shape, jnp.float32)
    for a, x_ref in enumerate(xs):
        place = pl.ds(pair_place(a), 1)
        ext = x_ref[: 2 * experts, width:].astype(jnp.float32)
        one_hot = jnp.zeros(slot.shape, jnp.float32)
        for s, (who, to_ref) in enumerate(((me, gslot_ref), (me ^ 1, other_ref))):
            gate = jnp.sum(jnp.where(expert == who, ext[:experts], 0.0), axis=0, keepdims=True)
            number = jnp.sum(jnp.where(expert == who, ext[experts:], 0.0), axis=0, keepdims=True)
            routed = number >= 0
            spot = jnp.where(routed, number + s * capacity, -1.0)
            one_hot = jnp.where(slot == spot, 1.0, one_hot)
            spot = jnp.where(routed, number + offset, -1.0)
            by_slot = lax.dot_general(
                jnp.broadcast_to(gate.astype(jnp.bfloat16), (16, tokens)),
                jnp.where(slot == spot, 1.0, 0.0).astype(jnp.bfloat16),
                NT,
                preferred_element_type=jnp.float32,
            )
            to_ref[place, :] = by_slot[:1]
        pmat_ref[a * 2 * capacity : (a + 1) * 2 * capacity, :] = one_hot.astype(jnp.bfloat16)
    theirs_ref[pairs * capacity :, :] = jnp.zeros((16, width), jnp.bfloat16)
    theirs_ref[pairs * capacity :, : 2 * capacity] = other_ref[...].astype(jnp.bfloat16)
    pick(xs, pmat_ref, mine_ref, theirs_ref)


def pick_kernel(*refs):
    pick(refs[:-3], *refs[-3:])


def products(half, capacity, mine_ref, got_ref, hs_ref, rows_ref, *outs):
    mine = lax.axis_index("dp")
    core = lax.axis_index("expert") & 1
    pairs = mine_ref.shape[0] // capacity
    pieces = len(outs) // 2
    piece = mine_ref.shape[1] // pieces
    for q in range(pieces):

        @pl.loop(0, piece // 256)
        def _(n, q=q):
            cols = pl.ds(pl.multiple_of(q * piece + n * 256, 256), 256)
            out = pl.ds(pl.multiple_of(n * 256, 256), 256)
            for p in range(pairs):
                for c, ref in ((core, mine_ref), (1 - core, got_ref)):
                    to = pl.ds(pl.multiple_of((2 * p + c) * capacity, capacity), capacity)
                    rows_ref[to, cols] = ref[p * capacity : (p + 1) * capacity, cols]
            block = rows_ref[:, cols]
            for d, ref in ((1 - mine, outs[q]), (mine, outs[pieces + q])):
                units = pl.ds(pl.multiple_of(d * half, 16), half)
                ref[:, out] = jnp.dot(
                    hs_ref[units, :], block, preferred_element_type=jnp.float32
                ).astype(jnp.bfloat16)


def first_products_kernel(half, capacity, mine_ref, got_ref, gslot_ref, hidden_ref, *outs):
    gates_ref, hs_ref = outs[:2]
    pairs = mine_ref.shape[0] // capacity
    got = got_ref[pairs * capacity :, : 2 * capacity].astype(jnp.float32)
    by_pair = gslot_ref[...] + got[:pairs]
    for p in range(pairs):
        gates_ref[:, p * 2 * capacity : (p + 1) * 2 * capacity] = by_pair[p : p + 1, :]
    hs_ref[...] = (hidden_ref[...].astype(jnp.float32) * gates_ref[...]).astype(jnp.bfloat16)
    products(half, capacity, mine_ref, got_ref, hs_ref, *outs[2:])


def weight_parts(half, own_ref, got_refs):
    mine = lax.axis_index("dp")
    yield pl.ds(pl.multiple_of(mine * half, 16), half), 0, own_ref
    part = got_refs[0].shape[1]
    for q, ref in enumerate(got_refs):
        yield pl.ds(pl.multiple_of((1 - mine) * half, 16), half), q * part, ref


def raw_halves(half, rows_ref, own_ref, got_refs):
    raws = {}
    for units, low, w_ref in weight_parts(half, own_ref, got_refs):
        term = lax.dot_general(
            w_ref[...],
            rows_ref[:, low : low + w_ref.shape[1]],
            NT,
            preferred_element_type=jnp.float32,
        )
        key = w_ref is own_ref
        raws[key] = (units, raws[key][1] + term if key in raws else term)
    return raws.values()


def raw_part_kernel(half, capacity, rows_ref, own_ref, *refs):
    *got_refs, hidden_ref, raw_ref, back_ref = refs
    total = jnp.zeros((1, rows_ref.shape[0]), jnp.float32)
    for units, raw in raw_halves(half, rows_ref, own_ref, got_refs):
        raw_ref[units, :] = raw
        total += jnp.sum(
            raw * hidden_ref[units, :].astype(jnp.float32), axis=0, keepdims=True
        )
    blocks = total.shape[1] // capacity
    for i in range(blocks):
        to = pl.ds(pl.program_id(0) * blocks + i, 1)
        back_ref[to, :] = total[:, i * capacity : (i + 1) * capacity]


def raw_kernel(half, rows_ref, own_ref, *refs):
    *got_refs, sum_ref, gates_ref, grad_ref = refs
    for units, raw in raw_halves(half, rows_ref, own_ref, got_refs):
        grad_ref[units, :] = ((raw + sum_ref[units, :]) * gates_ref[...]).astype(jnp.bfloat16)


def forward_kernel(half, own_ref, *refs):
    *got_refs, hidden_ref, out_ref = refs
    mine = lax.axis_index("dp")
    own_units = pl.ds(pl.multiple_of(mine * half, 16), half)
    got_units = pl.ds(pl.multiple_of((1 - mine) * half, 16), half)
    part = got_refs[0].shape[1]
    turned = (((0,), (0,)), ((), ()))
    for q, ref in enumerate(got_refs):
        cols = slice(q * part, (q + 1) * part)
        out_ref[:, cols] = lax.dot_general(
            hidden_ref[own_units, :], own_ref[:, cols], turned, preferred_element_type=jnp.float32
        ) + lax.dot_general(
            hidden_ref[got_units, :], ref[...], turned, preferred_element_type=jnp.float32
        )


def slot_grads_kernel(rows_ref, forward_ref, part_ref, back_ref):
    capacity = back_ref.shape[1]
    pair = 2 * capacity
    for p in range(rows_ref.shape[0] // pair):
        at = slice(p * pair, (p + 1) * pair)
        some = jnp.zeros((pair, LANES), jnp.float32)
        for n in range(0, rows_ref.shape[1], LANES):
            cols = slice(n, n + LANES)
            some += rows_ref[at, cols].astype(jnp.float32) * forward_ref[at, cols]
        total = jnp.sum(some.T, axis=0, keepdims=True)
        for i in range(2):
            to = slice(2 * p + i, 2 * p + i + 1)
            back_ref[to, :] = part_ref[to, :] + total[:, i * capacity : (i + 1) * capacity]


def gates_kernel(routes_ref, slots_ref, back_ref, out_ref):
    back = back_ref[...]
    routes = routes_ref[...]
    experts, capacity = back.shape
    tokens = routes.shape[1]
    slots = slots_ref[experts : 2 * experts, :].astype(jnp.float32)
    expert = lax.broadcasted_iota(jnp.int32, (experts, tokens), 0)
    slot = lax.broadcasted_iota(jnp.int32, (capacity, tokens), 0).astype(jnp.float32)
    for k in range(out_ref.shape[0]):
        hit = expert == routes[k : k + 1, :]
        number = jnp.sum(jnp.where(hit, slots, 0.0), axis=0, keepdims=True)
        by_expert = jnp.dot(
            back,
            jnp.where(slot == number, 1.0, 0.0),
            preferred_element_type=jnp.float32,
            precision=lax.Precision.HIGHEST,
        )
        out_ref[k : k + 1, :] = jnp.sum(jnp.where(hit, by_expert, 0.0), axis=0, keepdims=True)


def finish_kernel(own_ref, got_ref, *refs):
    refs[-1][...] = (
        own_ref[...].astype(jnp.float32) + got_ref[...].astype(jnp.float32)
    ).astype(jnp.bfloat16)


def ring_shards(grad_out, gates, routes, hidden, down_weight):
    experts = lax.axis_size("expert")
    tokens, chosen = routes.shape
    model = grad_out.shape[1]
    slots, units = hidden.shape[2:]
    half = down_weight.shape[1]
    capacity = slots // experts
    width = model // CHUNKS
    tile = 256
    bf16, f32 = jnp.bfloat16, jnp.float32
    shape = jax.ShapeDtypeStruct
    hidden_t = hidden[0, 0].T
    routes_t, gates_t = routes.T, gates.T
    weight = down_weight[0]
    columns = [pl.BlockSpec((half, width), lambda i, c=c: (0, c)) for c in range(CHUNKS)]
    parts = [pl.BlockSpec((half, PART), lambda i: (0, 0))] * (width // PART)
    dma = pltpu.SemaphoreType.DMA

    def forward(x):
        return lax.ppermute(x, "expert", ring_pairs(1))

    def backward(x):
        return lax.ppermute(x, "expert", ring_pairs(-1))

    def across(x):
        return lax.ppermute(x, "expert", swap_pairs(2))

    def sibling(x):
        return lax.ppermute(x, "expert", swap_pairs(1))

    def swap(x):
        return lax.ppermute(x, "dp", [(0, 1), (1, 0)])

    def behind(x, *others):
        return lax.optimization_barrier((x, *others))[0]

    def pack():
        return pl.pallas_call(
            functools.partial(pack_kernel, experts, width),
            out_shape=shape((tokens, width + tokens), bf16),
            in_specs=[ANY] * 3,
            out_specs=VMEM,
            scratch_shapes=[
                pltpu.VMEM(routes_t.shape, routes_t.dtype),
                pltpu.VMEM(gates_t.shape, gates_t.dtype),
                dma((3,)),
            ],
            compiler_params=params(48),
            name="pack",
        )(routes_t, gates_t, grad_out)

    def later_pack(c, after):
        return pl.pallas_call(
            functools.partial(later_pack_kernel, c * width),
            out_shape=shape((tokens, width), bf16),
            in_specs=[ANY] * 2,
            out_specs=VMEM,
            scratch_shapes=[dma],
            compiler_params=params(48),
            name="later_pack",
        )(grad_out, after)

    mine_shape = shape((slots // 2, width), bf16)

    def first_pick(blocks):
        return pl.pallas_call(
            functools.partial(first_pick_kernel, experts, capacity),
            out_shape=[
                mine_shape,
                shape((slots // 2 + 16, width), bf16),
                shape((slots, tokens), bf16),
                shape((experts // 2, 2 * capacity), f32),
            ],
            in_specs=[VMEM] * len(blocks),
            out_specs=[VMEM] * 4,
            scratch_shapes=[pltpu.VMEM((16, 2 * capacity), f32)],
            compiler_params=params(24),
            cost_estimate=cost(3),
            name="first_pick",
        )(*blocks)

    def later_pick(blocks, pmat):
        return pl.pallas_call(
            pick_kernel,
            out_shape=[mine_shape] * 2,
            in_specs=[VMEM] * (len(blocks) + 1),
            out_specs=[VMEM] * 2,
            compiler_params=params(24),
            name="pick",
        )(*blocks, pmat)

    def product_shapes(c):
        piece = shape((half, width // PIECES[c]), bf16)
        return [shape((slots, width), bf16)] + [piece] * (2 * PIECES[c])

    def first_products(mine, got, gslot):
        slot_gates, hs, rows, *halves = pl.pallas_call(
            functools.partial(first_products_kernel, half, capacity),
            out_shape=[shape((1, slots), f32), shape((units, slots), bf16)] + product_shapes(0),
            in_specs=[VMEM] * 4,
            out_specs=[VMEM] * (3 + 2 * PIECES[0]),
            compiler_params=params(24),
            cost_estimate=cost(3),
            name="first_products",
        )(mine, got, gslot, hidden_t)
        return rows, halves[: PIECES[0]], halves[PIECES[0] :], slot_gates, hs

    def later_products(mine, got, hs):
        rows, *halves = pl.pallas_call(
            functools.partial(products, half, capacity),
            out_shape=product_shapes(1),
            in_specs=[VMEM] * 3,
            out_specs=[VMEM] * (1 + 2 * PIECES[1]),
            compiler_params=params(24),
            name="products",
        )(mine, got, hs)
        return rows, halves[: PIECES[1]], halves[PIECES[1] :]

    by_slot = pl.BlockSpec((units, tile), lambda i: (0, i))
    some_rows = pl.BlockSpec((tile, width), lambda i: (i, 0))
    back_shape = shape((experts, capacity), f32)

    def raw_part(rows, got_weight):
        return pl.pallas_call(
            functools.partial(raw_part_kernel, half, capacity),
            grid=(slots // tile,),
            out_shape=[shape((units, slots), f32), back_shape],
            in_specs=[some_rows, columns[0], *parts, by_slot],
            out_specs=[by_slot, pl.BlockSpec((experts, capacity), lambda i: (0, 0))],
            compiler_params=params(24),
            cost_estimate=cost(3),
            name="raw_part",
        )(rows, weight, *got_weight, hidden_t)

    def raw_rest(rows, got_weight, raw, slot_gates):
        return pl.pallas_call(
            functools.partial(raw_kernel, half),
            grid=(slots // tile,),
            out_shape=shape((units, slots), bf16),
            in_specs=[
                some_rows,
                columns[1],
                *parts,
                by_slot,
                pl.BlockSpec((1, tile), lambda i: (0, i)),
            ],
            out_specs=by_slot,
            compiler_params=params(24),
            name="raw",
        )(rows, weight, *got_weight, raw, slot_gates)

    def forward_columns(got_weight):
        return pl.pallas_call(
            functools.partial(forward_kernel, half),
            grid=(slots // tile,),
            out_shape=shape((slots, width), f32),
            in_specs=[columns[1], *parts, by_slot],
            out_specs=some_rows,
            compiler_params=params(24),
            cost_estimate=cost(4),
            name="hidden_weight",
        )(weight, *got_weight, hidden_t)

    def slot_grads(rows, forwarded, part):
        return pl.pallas_call(
            slot_grads_kernel,
            out_shape=back_shape,
            in_specs=[VMEM] * 3,
            out_specs=VMEM,
            compiler_params=params(24),
            name="slot_grads",
        )(rows, forwarded, part)

    def finish(low, own, got, *before):
        piece = own.shape[1]
        spec = pl.BlockSpec((half // 2, piece), lambda i: (i, 0))
        return pl.pallas_call(
            finish_kernel,
            grid=(2,),
            out_shape=shape((half, model), bf16),
            in_specs=[spec, spec] + [ANY] * len(before),
            out_specs=pl.BlockSpec((half // 2, piece), lambda i: (i, low // piece)),
            input_output_aliases={2: 0} if before else {},
            compiler_params=params(8),
            name="finish",
        )(own, got, *before)

    w = [swap(weight[:, k : k + PART]) for k in range(0, model, PART)]
    x0 = pack()
    f0, r0, y0 = forward(x0), backward(x0), across(x0)
    ff0, yf0 = forward(behind(f0, w[0])), across(behind(f0, w[0]))
    x1 = later_pack(1, r0)
    f1, yr0 = forward(x1), across(behind(r0, y0))
    yff0 = across(behind(ff0, yf0, w[1]))
    mine0, theirs0, pmat, gslot = first_pick(
        [x0, y0, f0, yf0, ff0, yff0, r0, behind(yr0, f1, w[2])]
    )
    ff1, yf1 = forward(f1), across(behind(f1, yr0))
    r1, y1 = backward(behind(x1, ff0)), across(behind(x1, yff0))
    got = sibling(theirs0)
    rows0, send0, own0, slot_gates, hs = first_products(mine0, got, gslot)
    got0 = [swap(part) for part in send0]
    done = (ff1, yf1, r1, y1)
    yff1, ry1 = across(behind(ff1, *done)), backward(behind(y1, *done))
    raw, part = raw_part(rows0, w[: len(parts)])
    forwarded = forward_columns(w[len(parts) :])
    mine1, theirs1 = later_pick(
        [x1, y1, f1, yf1, ff1, yff1, r1, ry1], behind(pmat, raw, forwarded)
    )
    rows1, send1, own1 = later_products(mine1, sibling(behind(theirs1, *got0)), hs)
    got1 = [swap(half) for half in send1]

    back = slot_grads(rows1, forwarded, part)
    returned = lax.all_to_all(back, "expert", split_axis=0, concat_axis=0, tiled=True)
    grad_gates = pl.pallas_call(
        gates_kernel,
        grid=(1,),
        out_shape=shape((chosen, tokens), f32),
        in_specs=[
            pl.BlockSpec((chosen, tokens), lambda i: (0, 0)),
            pl.BlockSpec((2 * experts, tokens), lambda i: (0, width // tokens)),
            pl.BlockSpec((experts, capacity), lambda i: (0, 0)),
        ],
        out_specs=pl.BlockSpec((chosen, tokens), lambda i: (0, 0)),
        name="grad_gates",
    )(routes_t, x0, returned)

    grad_hidden = raw_rest(rows1, w[len(parts) :], raw, slot_gates)
    grad_weight, low = (), 0
    for own, got in zip((*own0, *own1), (*got0, *got1)):
        if low == 0:
            own = behind(own, back)
        grad_weight = (finish(low, own, got, *grad_weight),)
        low += own.shape[1]
    grad_weight = grad_weight[0]
    return grad_weight[None], grad_hidden.T[None, None], grad_gates.T


def shards(grad_out, gates, routes, hidden, down_weight):
    owners = lax.axis_size("expert")
    token_count, chosen = routes.shape
    width = grad_out.shape[1]
    slots = hidden.shape[2]
    capacity = slots // owners
    flat = routes.reshape(-1)
    onehot = (flat[:, None] == jnp.arange(owners, dtype=jnp.int32)[None, :]).astype(jnp.int32)
    before = jnp.cumsum(onehot, axis=0) - onehot
    slot = jnp.sum(before * onehot, axis=1)
    target = flat * capacity + slot
    send_rows = (
        jnp.zeros((owners * capacity, width), grad_out.dtype)
        .at[target]
        .set(jnp.repeat(grad_out, chosen, axis=0))
    )
    send_gate = jnp.zeros((owners * capacity,), gates.dtype).at[target].set(gates.reshape(-1))
    send_rows = send_rows.reshape(owners, capacity, width)
    send_gate = send_gate.reshape(owners, capacity)
    saved = hidden[0, 0]
    local_weight = down_weight[0]
    contract = (((1,), (1,)), ((), ()))
    rows, gate_slots = (
        lax.all_to_all(send_rows, "expert", split_axis=0, concat_axis=0, tiled=True),
        lax.all_to_all(send_gate, "expert", split_axis=0, concat_axis=0, tiled=True),
    )
    rows = rows.reshape(slots, width)
    whole_weight = lax.all_gather(local_weight, "dp", axis=0, tiled=True)
    raw = lax.dot_general(rows, whole_weight, contract, preferred_element_type=jnp.float32)
    factor = gate_slots.reshape(slots, 1).astype(jnp.float32)
    grad_hidden = (factor * raw).astype(jnp.bfloat16)
    slot_grads = jnp.sum(raw * saved.astype(jnp.float32), axis=1)
    returned = lax.all_to_all(
        slot_grads.reshape(owners, capacity), "expert", split_axis=0, concat_axis=0, tiled=True
    )
    grad_gates = returned.reshape(-1)[target].reshape(token_count, chosen)
    scaled = (factor * rows.astype(jnp.float32)).astype(jnp.bfloat16)
    summed = lax.psum_scatter(
        lax.dot_general(
            saved, scaled, (((0,), (0,)), ((), ())), preferred_element_type=jnp.float32
        ).astype(jnp.bfloat16),
        "dp",
        scatter_dimension=0,
        tiled=True,
    )
    return (summed[None], grad_hidden[None, None], grad_gates)


def solution(mesh):
    small = mesh.shape["dp"] == 2 and mesh.shape["expert"] == NZ * NY * NC
    return jax.shard_map(
        ring_shards if small else shards,
        mesh=mesh,
        in_specs=(
            P(("dp", "expert"), None),
            P(("dp", "expert"), None),
            P(("dp", "expert"), None),
            P("dp", "expert", None, None),
            P("expert", "dp", None),
        ),
        out_specs=(
            P("expert", "dp", None),
            P("dp", "expert", None, None),
            P(("dp", "expert"), None),
        ),
        check_vma=False,
    )
```

```python
import functools

import jax
import jax.numpy as jnp
from jax import lax
from jax.experimental import pallas as pl
from jax.experimental.pallas import tpu as pltpu
from jax.sharding import PartitionSpec as P

NZ, NY, NC = 4, 2, 2
CHUNKS = 2
PIECES = (2, 2)
LANES = 128
NT = (((1,), (1,)), ((), ()))
VMEM = pl.BlockSpec(memory_space=pltpu.VMEM)
ANY = pl.BlockSpec(memory_space=pl.ANY)


def params(mib):
    return pltpu.CompilerParams(vmem_limit_bytes=mib * 2**20)


def cost(micros):
    return pl.CostEstimate(
        flops=micros * 10**9, bytes_accessed=micros * 3 * 2**20, transcendentals=0
    )


def ring(z):
    return z ^ (z >> 1)


def ring_pairs(step):
    size = NY * NC
    return [
        (ring(p) * size + rest, ring((p + step) % NZ) * size + rest)
        for p in range(NZ)
        for rest in range(size)
    ]


def swap_pairs(bit):
    return [(i, i ^ bit) for i in range(NZ * NY * NC)]


def pack_kernel(experts, width, routes_hbm, gates_hbm, grad_hbm, out_ref, routes_ref, gates_ref, sems):
    copies = [
        pltpu.make_async_copy(src, dst, sems.at[i])
        for i, (src, dst) in enumerate(
            (
                (routes_hbm, routes_ref),
                (gates_hbm, gates_ref),
                (grad_hbm.at[:, :width], out_ref.at[:, :width]),
            )
        )
    ]
    for copy in copies:
        copy.start()
    copies[0].wait()
    copies[1].wait()
    chosen, tokens = routes_ref.shape
    routes = routes_ref[...]
    gates = gates_ref[...].astype(jnp.float32)
    expert = lax.broadcasted_iota(jnp.int32, (experts, tokens), 0)
    dense = jnp.zeros((experts, tokens), jnp.float32)
    named = jnp.zeros((experts, tokens), jnp.float32)
    for k in range(chosen):
        hit = routes[k : k + 1, :] == expert
        dense = jnp.where(hit, gates[k : k + 1, :], dense)
        named = jnp.where(hit, 1.0, named)
    earlier = (
        lax.broadcasted_iota(jnp.int32, (tokens, tokens), 0)
        < lax.broadcasted_iota(jnp.int32, (tokens, tokens), 1)
    )
    slots = jnp.dot(
        named.astype(jnp.bfloat16),
        jnp.where(earlier, 1.0, 0.0).astype(jnp.bfloat16),
        preferred_element_type=jnp.float32,
    )
    slots = jnp.where(named > 0, slots, -1.0)
    out_ref[:, width:] = jnp.zeros((tokens, tokens), jnp.bfloat16)
    out_ref[:experts, width:] = dense.astype(jnp.bfloat16)
    out_ref[experts : 2 * experts, width:] = slots.astype(jnp.bfloat16)
    copies[2].wait()


def later_pack_kernel(low, grad_hbm, after_ref, out_ref, sem):
    del after_ref
    copy = pltpu.make_async_copy(grad_hbm.at[:, pl.ds(low, out_ref.shape[1])], out_ref, sem)
    copy.start()
    copy.wait()


def pair_place(arrival):
    index = lax.axis_index("expert")
    z, y = index >> 2, (index >> 1) & 1
    z = ring((ring(z) - arrival // NY) & (NZ - 1))
    return z * NY + (y ^ (arrival % NY))


def pick(xs, pmat_ref, mine_ref, theirs_ref):
    capacity = mine_ref.shape[0] // len(xs)

    @pl.loop(0, mine_ref.shape[1] // 256)
    def _(n):
        cols = pl.ds(pl.multiple_of(n * 256, 256), 256)
        for a, x_ref in enumerate(xs):
            rows = jnp.dot(
                pmat_ref[a * 2 * capacity : (a + 1) * 2 * capacity, :],
                x_ref[:, cols],
                preferred_element_type=jnp.float32,
            ).astype(jnp.bfloat16)
            where = pl.ds(pl.multiple_of(pair_place(a) * capacity, capacity), capacity)
            mine_ref[where, cols] = rows[:capacity]
            theirs_ref[where, cols] = rows[capacity:]


def first_pick_kernel(experts, capacity, *refs):
    pairs = experts // 2
    xs = refs[:pairs]
    mine_ref, theirs_ref, pmat_ref, gslot_ref, other_ref = refs[pairs:]
    width = mine_ref.shape[1]
    me = lax.axis_index("expert")
    core = me & 1
    tokens = xs[0].shape[0]
    expert = lax.broadcasted_iota(jnp.int32, (experts, tokens), 0)
    slot = lax.broadcasted_iota(jnp.int32, (2 * capacity, tokens), 0).astype(jnp.float32)
    offset = (core * capacity).astype(jnp.float32)
    other_ref[...] = jnp.zeros(other_ref.shape, jnp.float32)
    for a, x_ref in enumerate(xs):
        place = pl.ds(pair_place(a), 1)
        ext = x_ref[: 2 * experts, width:].astype(jnp.float32)
        one_hot = jnp.zeros(slot.shape, jnp.float32)
        for s, (who, to_ref) in enumerate(((me, gslot_ref), (me ^ 1, other_ref))):
            gate = jnp.sum(jnp.where(expert == who, ext[:experts], 0.0), axis=0, keepdims=True)
            number = jnp.sum(jnp.where(expert == who, ext[experts:], 0.0), axis=0, keepdims=True)
            routed = number >= 0
            spot = jnp.where(routed, number + s * capacity, -1.0)
            one_hot = jnp.where(slot == spot, 1.0, one_hot)
            spot = jnp.where(routed, number + offset, -1.0)
            by_slot = lax.dot_general(
                jnp.broadcast_to(gate.astype(jnp.bfloat16), (16, tokens)),
                jnp.where(slot == spot, 1.0, 0.0).astype(jnp.bfloat16),
                NT,
                preferred_element_type=jnp.float32,
            )
            to_ref[place, :] = by_slot[:1]
        pmat_ref[a * 2 * capacity : (a + 1) * 2 * capacity, :] = one_hot.astype(jnp.bfloat16)
    theirs_ref[pairs * capacity :, :] = jnp.zeros((16, width), jnp.bfloat16)
    theirs_ref[pairs * capacity :, : 2 * capacity] = other_ref[...].astype(jnp.bfloat16)
    pick(xs, pmat_ref, mine_ref, theirs_ref)


def pick_kernel(*refs):
    pick(refs[:-3], *refs[-3:])


def products(half, capacity, mine_ref, got_ref, hs_ref, rows_ref, *outs):
    mine = lax.axis_index("dp")
    core = lax.axis_index("expert") & 1
    pairs = mine_ref.shape[0] // capacity
    pieces = len(outs) // 2
    piece = mine_ref.shape[1] // pieces
    for q in range(pieces):

        @pl.loop(0, piece // 256)
        def _(n, q=q):
            cols = pl.ds(pl.multiple_of(q * piece + n * 256, 256), 256)
            out = pl.ds(pl.multiple_of(n * 256, 256), 256)
            for p in range(pairs):
                for c, ref in ((core, mine_ref), (1 - core, got_ref)):
                    to = pl.ds(pl.multiple_of((2 * p + c) * capacity, capacity), capacity)
                    rows_ref[to, cols] = ref[p * capacity : (p + 1) * capacity, cols]
            block = rows_ref[:, cols]
            for d, ref in ((1 - mine, outs[q]), (mine, outs[pieces + q])):
                units = pl.ds(pl.multiple_of(d * half, 16), half)
                ref[:, out] = jnp.dot(
                    hs_ref[units, :], block, preferred_element_type=jnp.float32
                ).astype(jnp.bfloat16)


def first_products_kernel(half, capacity, mine_ref, got_ref, gslot_ref, hidden_ref, *outs):
    gates_ref, hs_ref = outs[:2]
    pairs = mine_ref.shape[0] // capacity
    got = got_ref[pairs * capacity :, : 2 * capacity].astype(jnp.float32)
    by_pair = gslot_ref[...] + got[:pairs]
    for p in range(pairs):
        gates_ref[:, p * 2 * capacity : (p + 1) * 2 * capacity] = by_pair[p : p + 1, :]
    hs_ref[...] = (hidden_ref[...].astype(jnp.float32) * gates_ref[...]).astype(jnp.bfloat16)
    products(half, capacity, mine_ref, got_ref, hs_ref, *outs[2:])


def weight_parts(half, own_ref, got_refs):
    mine = lax.axis_index("dp")
    yield pl.ds(pl.multiple_of(mine * half, 16), half), own_ref
    low = (1 - mine) * half
    for ref in got_refs:
        yield pl.ds(pl.multiple_of(low, 16), ref.shape[0]), ref
        low = low + ref.shape[0]


def raw_parts(half, rows_ref, own_ref, got_refs):
    for units, w_ref in weight_parts(half, own_ref, got_refs):
        yield units, lax.dot_general(
            w_ref[...], rows_ref[...], NT, preferred_element_type=jnp.float32
        )


def raw_part_kernel(half, capacity, rows_ref, own_ref, *refs):
    *got_refs, hidden_ref, raw_ref, back_ref = refs
    total = jnp.zeros((1, rows_ref.shape[0]), jnp.float32)
    for units, raw in raw_parts(half, rows_ref, own_ref, got_refs):
        raw_ref[units, :] = raw
        total += jnp.sum(
            raw * hidden_ref[units, :].astype(jnp.float32), axis=0, keepdims=True
        )
    blocks = total.shape[1] // capacity
    for i in range(blocks):
        to = pl.ds(pl.program_id(0) * blocks + i, 1)
        back_ref[to, :] = total[:, i * capacity : (i + 1) * capacity]


def raw_kernel(half, rows_ref, own_ref, *refs):
    *got_refs, sum_ref, gates_ref, grad_ref = refs
    for units, raw in raw_parts(half, rows_ref, own_ref, got_refs):
        grad_ref[units, :] = ((raw + sum_ref[units, :]) * gates_ref[...]).astype(jnp.bfloat16)


def forward_kernel(half, own_ref, *refs):
    *got_refs, hidden_ref, out_ref = refs
    out_ref[...] = sum(
        lax.dot_general(
            hidden_ref[units, :],
            w_ref[...],
            (((0,), (0,)), ((), ())),
            preferred_element_type=jnp.float32,
        )
        for units, w_ref in weight_parts(half, own_ref, got_refs)
    ).astype(out_ref.dtype)


def slot_grads_kernel(rows_ref, forward_ref, part_ref, back_ref):
    capacity = back_ref.shape[1]
    pair = 2 * capacity
    for p in range(rows_ref.shape[0] // pair):
        at = slice(p * pair, (p + 1) * pair)
        some = jnp.zeros((pair, LANES), jnp.float32)
        for n in range(0, rows_ref.shape[1], LANES):
            cols = slice(n, n + LANES)
            some += rows_ref[at, cols].astype(jnp.float32) * forward_ref[at, cols].astype(
                jnp.float32
            )
        total = jnp.sum(some.T, axis=0, keepdims=True)
        for i in range(2):
            to = slice(2 * p + i, 2 * p + i + 1)
            back_ref[to, :] = part_ref[to, :] + total[:, i * capacity : (i + 1) * capacity]


def gates_kernel(routes_ref, slots_ref, back_ref, out_ref):
    back = back_ref[...]
    routes = routes_ref[...]
    experts, capacity = back.shape
    tokens = routes.shape[1]
    slots = slots_ref[experts : 2 * experts, :].astype(jnp.float32)
    expert = lax.broadcasted_iota(jnp.int32, (experts, tokens), 0)
    slot = lax.broadcasted_iota(jnp.int32, (capacity, tokens), 0).astype(jnp.float32)
    for k in range(out_ref.shape[0]):
        hit = expert == routes[k : k + 1, :]
        number = jnp.sum(jnp.where(hit, slots, 0.0), axis=0, keepdims=True)
        by_expert = jnp.dot(
            back,
            jnp.where(slot == number, 1.0, 0.0),
            preferred_element_type=jnp.float32,
            precision=lax.Precision.HIGHEST,
        )
        out_ref[k : k + 1, :] = jnp.sum(jnp.where(hit, by_expert, 0.0), axis=0, keepdims=True)


def finish_kernel(own_ref, got_ref, *refs):
    refs[-1][...] = (
        own_ref[...].astype(jnp.float32) + got_ref[...].astype(jnp.float32)
    ).astype(jnp.bfloat16)


def ring_shards(grad_out, gates, routes, hidden, down_weight):
    experts = lax.axis_size("expert")
    tokens, chosen = routes.shape
    model = grad_out.shape[1]
    slots, units = hidden.shape[2:]
    half = down_weight.shape[1]
    capacity = slots // experts
    width = model // CHUNKS
    tile = 256
    bf16, f32 = jnp.bfloat16, jnp.float32
    shape = jax.ShapeDtypeStruct
    hidden_t = hidden[0, 0].T
    routes_t, gates_t = routes.T, gates.T
    weight = down_weight[0]
    columns = [pl.BlockSpec((half, width), lambda i, c=c: (0, c)) for c in range(CHUNKS)]
    split = half // 32 * 16
    parts = [
        [pl.BlockSpec((n, width), lambda i, c=c: (0, c)) for n in (split, half - split)]
        for c in range(CHUNKS)
    ]
    dma = pltpu.SemaphoreType.DMA

    def forward(x):
        return lax.ppermute(x, "expert", ring_pairs(1))

    def backward(x):
        return lax.ppermute(x, "expert", ring_pairs(-1))

    def across(x):
        return lax.ppermute(x, "expert", swap_pairs(2))

    def sibling(x):
        return lax.ppermute(x, "expert", swap_pairs(1))

    def swap(x):
        return lax.ppermute(x, "dp", [(0, 1), (1, 0)])

    def behind(x, *others):
        return lax.optimization_barrier((x, *others))[0]

    def pack():
        return pl.pallas_call(
            functools.partial(pack_kernel, experts, width),
            out_shape=shape((tokens, width + tokens), bf16),
            in_specs=[ANY] * 3,
            out_specs=VMEM,
            scratch_shapes=[
                pltpu.VMEM(routes_t.shape, routes_t.dtype),
                pltpu.VMEM(gates_t.shape, gates_t.dtype),
                dma((3,)),
            ],
            compiler_params=params(48),
            name="pack",
        )(routes_t, gates_t, grad_out)

    def later_pack(c, after):
        return pl.pallas_call(
            functools.partial(later_pack_kernel, c * width),
            out_shape=shape((tokens, width), bf16),
            in_specs=[ANY] * 2,
            out_specs=VMEM,
            scratch_shapes=[dma],
            compiler_params=params(48),
            name="later_pack",
        )(grad_out, after)

    mine_shape = shape((slots // 2, width), bf16)

    def first_pick(blocks):
        return pl.pallas_call(
            functools.partial(first_pick_kernel, experts, capacity),
            out_shape=[
                mine_shape,
                shape((slots // 2 + 16, width), bf16),
                shape((slots, tokens), bf16),
                shape((experts // 2, 2 * capacity), f32),
            ],
            in_specs=[VMEM] * len(blocks),
            out_specs=[VMEM] * 4,
            scratch_shapes=[pltpu.VMEM((16, 2 * capacity), f32)],
            compiler_params=params(24),
            cost_estimate=cost(3),
            name="first_pick",
        )(*blocks)

    def later_pick(blocks, pmat):
        return pl.pallas_call(
            pick_kernel,
            out_shape=[mine_shape] * 2,
            in_specs=[VMEM] * (len(blocks) + 1),
            out_specs=[VMEM] * 2,
            compiler_params=params(24),
            name="pick",
        )(*blocks, pmat)

    def product_shapes(c):
        piece = shape((half, width // PIECES[c]), bf16)
        return [shape((slots, width), bf16)] + [piece] * (2 * PIECES[c])

    def first_products(mine, got, gslot):
        slot_gates, hs, rows, *halves = pl.pallas_call(
            functools.partial(first_products_kernel, half, capacity),
            out_shape=[shape((1, slots), f32), shape((units, slots), bf16)] + product_shapes(0),
            in_specs=[VMEM] * 4,
            out_specs=[VMEM] * (3 + 2 * PIECES[0]),
            compiler_params=params(24),
            cost_estimate=cost(3),
            name="first_products",
        )(mine, got, gslot, hidden_t)
        return rows, halves[: PIECES[0]], halves[PIECES[0] :], slot_gates, hs

    def later_products(mine, got, hs):
        rows, *halves = pl.pallas_call(
            functools.partial(products, half, capacity),
            out_shape=product_shapes(1),
            in_specs=[VMEM] * 3,
            out_specs=[VMEM] * (1 + 2 * PIECES[1]),
            compiler_params=params(24),
            name="products",
        )(mine, got, hs)
        return rows, halves[: PIECES[1]], halves[PIECES[1] :]

    by_slot = pl.BlockSpec((units, tile), lambda i: (0, i))
    some_rows = pl.BlockSpec((tile, width), lambda i: (i, 0))
    back_shape = shape((experts, capacity), f32)

    def raw_part(rows, got_weight):
        return pl.pallas_call(
            functools.partial(raw_part_kernel, half, capacity),
            grid=(slots // tile,),
            out_shape=[shape((units, slots), f32), back_shape],
            in_specs=[some_rows, columns[0], *parts[0], by_slot],
            out_specs=[by_slot, pl.BlockSpec((experts, capacity), lambda i: (0, 0))],
            compiler_params=params(24),
            cost_estimate=cost(3),
            name="raw_part",
        )(rows, weight, *got_weight, hidden_t)

    def raw_rest(rows, got_weight, raw, slot_gates):
        return pl.pallas_call(
            functools.partial(raw_kernel, half),
            grid=(slots // tile,),
            out_shape=shape((units, slots), bf16),
            in_specs=[
                some_rows,
                columns[1],
                *parts[1],
                by_slot,
                pl.BlockSpec((1, tile), lambda i: (0, i)),
            ],
            out_specs=by_slot,
            compiler_params=params(24),
            name="raw",
        )(rows, weight, *got_weight, raw, slot_gates)

    def forward_columns(got_weight):
        return pl.pallas_call(
            functools.partial(forward_kernel, half),
            grid=(slots // tile,),
            out_shape=shape((slots, width), bf16),
            in_specs=[columns[1], *parts[1], by_slot],
            out_specs=some_rows,
            compiler_params=params(24),
            cost_estimate=cost(4),
            name="hidden_weight",
        )(weight, *got_weight, hidden_t)

    def slot_grads(rows, forwarded, part):
        return pl.pallas_call(
            slot_grads_kernel,
            out_shape=back_shape,
            in_specs=[VMEM] * 3,
            out_specs=VMEM,
            compiler_params=params(24),
            name="slot_grads",
        )(rows, forwarded, part)

    def finish(low, own, got, *before):
        piece = own.shape[1]
        spec = pl.BlockSpec((half // 2, piece), lambda i: (i, 0))
        return pl.pallas_call(
            finish_kernel,
            grid=(2,),
            out_shape=shape((half, model), bf16),
            in_specs=[spec, spec] + [ANY] * len(before),
            out_specs=pl.BlockSpec((half // 2, piece), lambda i: (i, low // piece)),
            input_output_aliases={2: 0} if before else {},
            compiler_params=params(8),
            name="finish",
        )(own, got, *before)

    x0 = pack()
    w = [swap(weight[:split]), swap(weight[split:])]
    f0, y0 = forward(x0), across(x0)
    done = (f0, y0)
    ff0, yf0 = forward(behind(f0, *done)), across(behind(f0, *done))
    done = (ff0, yf0)
    r0, yff0 = backward(behind(x0, *done)), across(behind(ff0, *done))
    x1 = later_pack(1, ff0)
    done = (r0, yff0, w[0])
    f1, yr0 = forward(behind(x1, *done)), across(behind(r0, *done))
    done = (f1, yr0)
    ff1, y1 = forward(behind(f1, *done)), across(behind(x1, *done))
    mine0, theirs0, pmat, gslot = first_pick([x0, y0, f0, yf0, ff0, yff0, r0, behind(yr0, f1, w[1])])
    got = sibling(theirs0)
    done = (ff1, y1, mine0)
    r1, yf1 = backward(behind(x1, *done)), across(behind(f1, *done))
    rows0, send0, own0, slot_gates, hs = first_products(mine0, got, gslot)
    got0 = [swap(part) for part in send0]
    done = (r1, yf1, rows0)
    ry1, yff1 = backward(behind(y1, *done)), across(behind(ff1, *done))
    raw, part = raw_part(rows0, w)
    forwarded = forward_columns(w)
    mine1, theirs1 = later_pick(
        [x1, y1, f1, yf1, ff1, yff1, r1, ry1], behind(pmat, raw, forwarded)
    )
    rows1, send1, own1 = later_products(mine1, sibling(behind(theirs1, *got0)), hs)
    got1 = [swap(half) for half in send1]

    back = slot_grads(rows1, forwarded, part)
    returned = lax.all_to_all(back, "expert", split_axis=0, concat_axis=0, tiled=True)
    grad_gates = pl.pallas_call(
        gates_kernel,
        grid=(1,),
        out_shape=shape((chosen, tokens), f32),
        in_specs=[
            pl.BlockSpec((chosen, tokens), lambda i: (0, 0)),
            pl.BlockSpec((2 * experts, tokens), lambda i: (0, width // tokens)),
            pl.BlockSpec((experts, capacity), lambda i: (0, 0)),
        ],
        out_specs=pl.BlockSpec((chosen, tokens), lambda i: (0, 0)),
        name="grad_gates",
    )(routes_t, x0, returned)

    grad_hidden = raw_rest(rows1, w, raw, slot_gates)
    grad_weight, low = (), 0
    for own, got in zip((*own0, *own1), (*got0, *got1)):
        if low == 0:
            own = behind(own, back)
        grad_weight = (finish(low, own, got, *grad_weight),)
        low += own.shape[1]
    grad_weight = grad_weight[0]
    return grad_weight[None], grad_hidden.T[None, None], grad_gates.T


def shards(grad_out, gates, routes, hidden, down_weight):
    owners = lax.axis_size("expert")
    token_count, chosen = routes.shape
    width = grad_out.shape[1]
    slots = hidden.shape[2]
    capacity = slots // owners
    flat = routes.reshape(-1)
    onehot = (flat[:, None] == jnp.arange(owners, dtype=jnp.int32)[None, :]).astype(jnp.int32)
    before = jnp.cumsum(onehot, axis=0) - onehot
    slot = jnp.sum(before * onehot, axis=1)
    target = flat * capacity + slot
    send_rows = (
        jnp.zeros((owners * capacity, width), grad_out.dtype)
        .at[target]
        .set(jnp.repeat(grad_out, chosen, axis=0))
    )
    send_gate = jnp.zeros((owners * capacity,), gates.dtype).at[target].set(gates.reshape(-1))
    send_rows = send_rows.reshape(owners, capacity, width)
    send_gate = send_gate.reshape(owners, capacity)
    saved = hidden[0, 0]
    local_weight = down_weight[0]
    contract = (((1,), (1,)), ((), ()))
    rows, gate_slots = (
        lax.all_to_all(send_rows, "expert", split_axis=0, concat_axis=0, tiled=True),
        lax.all_to_all(send_gate, "expert", split_axis=0, concat_axis=0, tiled=True),
    )
    rows = rows.reshape(slots, width)
    whole_weight = lax.all_gather(local_weight, "dp", axis=0, tiled=True)
    raw = lax.dot_general(rows, whole_weight, contract, preferred_element_type=jnp.float32)
    factor = gate_slots.reshape(slots, 1).astype(jnp.float32)
    grad_hidden = (factor * raw).astype(jnp.bfloat16)
    slot_grads = jnp.sum(raw * saved.astype(jnp.float32), axis=1)
    returned = lax.all_to_all(
        slot_grads.reshape(owners, capacity), "expert", split_axis=0, concat_axis=0, tiled=True
    )
    grad_gates = returned.reshape(-1)[target].reshape(token_count, chosen)
    scaled = (factor * rows.astype(jnp.float32)).astype(jnp.bfloat16)
    summed = lax.psum_scatter(
        lax.dot_general(
            saved, scaled, (((0,), (0,)), ((), ())), preferred_element_type=jnp.float32
        ).astype(jnp.bfloat16),
        "dp",
        scatter_dimension=0,
        tiled=True,
    )
    return (summed[None], grad_hidden[None, None], grad_gates)


def solution(mesh):
    small = mesh.shape["dp"] == 2 and mesh.shape["expert"] == NZ * NY * NC
    return jax.shard_map(
        ring_shards if small else shards,
        mesh=mesh,
        in_specs=(
            P(("dp", "expert"), None),
            P(("dp", "expert"), None),
            P(("dp", "expert"), None),
            P("dp", "expert", None, None),
            P("expert", "dp", None),
        ),
        out_specs=(
            P("expert", "dp", None),
            P("dp", "expert", None, None),
            P(("dp", "expert"), None),
        ),
        check_vma=False,
    )
```

```python
import functools

import jax
import jax.numpy as jnp
from jax import lax
from jax.experimental import pallas as pl
from jax.experimental.pallas import tpu as pltpu
from jax.sharding import PartitionSpec as P

NZ, NY, NC = 4, 2, 2
CHUNKS = (4, 4)
PIECES = (2, 2)
LANES = 128
NT = (((1,), (1,)), ((), ()))
VMEM = pl.BlockSpec(memory_space=pltpu.VMEM)
ANY = pl.BlockSpec(memory_space=pl.ANY)


def params(mib):
    return pltpu.CompilerParams(vmem_limit_bytes=mib * 2**20)


def cost(micros):
    return pl.CostEstimate(
        flops=micros * 10**9, bytes_accessed=micros * 3 * 2**20, transcendentals=0
    )


def ring(z):
    return z ^ (z >> 1)


def ring_pairs(step):
    size = NY * NC
    return [
        (ring(p) * size + rest, ring((p + step) % NZ) * size + rest)
        for p in range(NZ)
        for rest in range(size)
    ]


def swap_pairs(bit):
    return [(i, i ^ bit) for i in range(NZ * NY * NC)]


def pack_kernel(experts, width, routes_hbm, gates_hbm, grad_hbm, out_ref, routes_ref, gates_ref, sems):
    copies = [
        pltpu.make_async_copy(src, dst, sems.at[i])
        for i, (src, dst) in enumerate(
            (
                (routes_hbm, routes_ref),
                (gates_hbm, gates_ref),
                (grad_hbm.at[:, :width], out_ref.at[:, :width]),
            )
        )
    ]
    for copy in copies:
        copy.start()
    copies[0].wait()
    copies[1].wait()
    chosen, tokens = routes_ref.shape
    routes = routes_ref[...]
    gates = gates_ref[...].astype(jnp.float32)
    expert = lax.broadcasted_iota(jnp.int32, (experts, tokens), 0)
    dense = jnp.zeros((experts, tokens), jnp.float32)
    named = jnp.zeros((experts, tokens), jnp.float32)
    for k in range(chosen):
        hit = routes[k : k + 1, :] == expert
        dense = jnp.where(hit, gates[k : k + 1, :], dense)
        named = jnp.where(hit, 1.0, named)
    earlier = (
        lax.broadcasted_iota(jnp.int32, (tokens, tokens), 0)
        < lax.broadcasted_iota(jnp.int32, (tokens, tokens), 1)
    )
    slots = jnp.dot(
        named.astype(jnp.bfloat16),
        jnp.where(earlier, 1.0, 0.0).astype(jnp.bfloat16),
        preferred_element_type=jnp.float32,
    )
    slots = jnp.where(named > 0, slots, -1.0)
    out_ref[:, width:] = jnp.zeros((tokens, tokens), jnp.bfloat16)
    out_ref[:experts, width:] = dense.astype(jnp.bfloat16)
    out_ref[experts : 2 * experts, width:] = slots.astype(jnp.bfloat16)
    copies[2].wait()


def later_pack_kernel(low, grad_hbm, after_ref, out_ref, sem):
    del after_ref
    copy = pltpu.make_async_copy(grad_hbm.at[:, pl.ds(low, out_ref.shape[1])], out_ref, sem)
    copy.start()
    copy.wait()


def pair_place(arrival):
    index = lax.axis_index("expert")
    z, y = index >> 2, (index >> 1) & 1
    z = ring((ring(z) - arrival // NY) & (NZ - 1))
    return z * NY + (y ^ (arrival % NY))


def pick(xs, pmat_ref, mine_ref, theirs_ref):
    capacity = mine_ref.shape[0] // len(xs)

    @pl.loop(0, mine_ref.shape[1] // 256)
    def _(n):
        cols = pl.ds(pl.multiple_of(n * 256, 256), 256)
        for a, x_ref in enumerate(xs):
            rows = jnp.dot(
                pmat_ref[a * 2 * capacity : (a + 1) * 2 * capacity, :],
                x_ref[:, cols],
                preferred_element_type=jnp.float32,
            ).astype(jnp.bfloat16)
            where = pl.ds(pl.multiple_of(pair_place(a) * capacity, capacity), capacity)
            mine_ref[where, cols] = rows[:capacity]
            theirs_ref[where, cols] = rows[capacity:]


def first_pick_kernel(experts, capacity, *refs):
    pairs = experts // 2
    xs = refs[:pairs]
    mine_ref, theirs_ref, pmat_ref, gslot_ref, other_ref = refs[pairs:]
    width = mine_ref.shape[1]
    me = lax.axis_index("expert")
    core = me & 1
    tokens = xs[0].shape[0]
    expert = lax.broadcasted_iota(jnp.int32, (experts, tokens), 0)
    slot = lax.broadcasted_iota(jnp.int32, (2 * capacity, tokens), 0).astype(jnp.float32)
    offset = (core * capacity).astype(jnp.float32)
    other_ref[...] = jnp.zeros(other_ref.shape, jnp.float32)
    for a, x_ref in enumerate(xs):
        place = pl.ds(pair_place(a), 1)
        ext = x_ref[: 2 * experts, width:].astype(jnp.float32)
        one_hot = jnp.zeros(slot.shape, jnp.float32)
        for s, (who, to_ref) in enumerate(((me, gslot_ref), (me ^ 1, other_ref))):
            gate = jnp.sum(jnp.where(expert == who, ext[:experts], 0.0), axis=0, keepdims=True)
            number = jnp.sum(jnp.where(expert == who, ext[experts:], 0.0), axis=0, keepdims=True)
            routed = number >= 0
            spot = jnp.where(routed, number + s * capacity, -1.0)
            one_hot = jnp.where(slot == spot, 1.0, one_hot)
            spot = jnp.where(routed, number + offset, -1.0)
            by_slot = lax.dot_general(
                jnp.broadcast_to(gate.astype(jnp.bfloat16), (16, tokens)),
                jnp.where(slot == spot, 1.0, 0.0).astype(jnp.bfloat16),
                NT,
                preferred_element_type=jnp.float32,
            )
            to_ref[place, :] = by_slot[:1]
        pmat_ref[a * 2 * capacity : (a + 1) * 2 * capacity, :] = one_hot.astype(jnp.bfloat16)
    theirs_ref[pairs * capacity :, :] = jnp.zeros((16, width), jnp.bfloat16)
    theirs_ref[pairs * capacity :, : 2 * capacity] = other_ref[...].astype(jnp.bfloat16)
    pick(xs, pmat_ref, mine_ref, theirs_ref)


def pick_kernel(*refs):
    pick(refs[:-3], *refs[-3:])


def products(half, capacity, mine_ref, got_ref, hs_ref, rows_ref, *outs):
    mine = lax.axis_index("dp")
    core = lax.axis_index("expert") & 1
    pairs = mine_ref.shape[0] // capacity
    pieces = len(outs) // 2
    piece = mine_ref.shape[1] // pieces
    for q in range(pieces):

        @pl.loop(0, piece // 256)
        def _(n, q=q):
            cols = pl.ds(pl.multiple_of(q * piece + n * 256, 256), 256)
            out = pl.ds(pl.multiple_of(n * 256, 256), 256)
            for p in range(pairs):
                for c, ref in ((core, mine_ref), (1 - core, got_ref)):
                    to = pl.ds(pl.multiple_of((2 * p + c) * capacity, capacity), capacity)
                    rows_ref[to, cols] = ref[p * capacity : (p + 1) * capacity, cols]
            block = rows_ref[:, cols]
            for d, ref in ((1 - mine, outs[q]), (mine, outs[pieces + q])):
                units = pl.ds(pl.multiple_of(d * half, 16), half)
                ref[:, out] = jnp.dot(
                    hs_ref[units, :], block, preferred_element_type=jnp.float32
                ).astype(jnp.bfloat16)


def first_products_kernel(half, capacity, mine_ref, got_ref, gslot_ref, hidden_ref, *outs):
    gates_ref, hs_ref = outs[:2]
    pairs = mine_ref.shape[0] // capacity
    got = got_ref[pairs * capacity :, : 2 * capacity].astype(jnp.float32)
    by_pair = gslot_ref[...] + got[:pairs]
    for p in range(pairs):
        gates_ref[:, p * 2 * capacity : (p + 1) * 2 * capacity] = by_pair[p : p + 1, :]
    hs_ref[...] = (hidden_ref[...].astype(jnp.float32) * gates_ref[...]).astype(jnp.bfloat16)
    products(half, capacity, mine_ref, got_ref, hs_ref, *outs[2:])


def weight_parts(half, own_ref, got_refs):
    mine = lax.axis_index("dp")
    yield pl.ds(pl.multiple_of(mine * half, 16), half), own_ref
    low = (1 - mine) * half
    for ref in got_refs:
        yield pl.ds(pl.multiple_of(low, 16), ref.shape[0]), ref
        low = low + ref.shape[0]


def raw_parts(half, cols, rows_ref, own_ref, got_refs):
    for units, w_ref in weight_parts(half, own_ref, got_refs):
        yield units, lax.dot_general(
            w_ref[:, cols], rows_ref[...], NT, preferred_element_type=jnp.float32
        )


def raw_part_kernel(half, capacity, cols, rows_ref, own_ref, *refs):
    *got_refs, hidden_ref, raw_ref, back_ref = refs
    total = jnp.zeros((1, rows_ref.shape[0]), jnp.float32)
    for units, raw in raw_parts(half, cols, rows_ref, own_ref, got_refs):
        raw_ref[units, :] = raw
        total += jnp.sum(
            raw * hidden_ref[units, :].astype(jnp.float32), axis=0, keepdims=True
        )
    blocks = total.shape[1] // capacity
    for i in range(blocks):
        to = pl.ds(pl.program_id(0) * blocks + i, 1)
        back_ref[to, :] = total[:, i * capacity : (i + 1) * capacity]


def raw_kernel(half, cols, rows_ref, own_ref, *refs):
    *got_refs, sum_ref, gates_ref, grad_ref = refs
    for units, raw in raw_parts(half, cols, rows_ref, own_ref, got_refs):
        grad_ref[units, :] = ((raw + sum_ref[units, :]) * gates_ref[...]).astype(jnp.bfloat16)


def forward_kernel(half, cols, own_ref, *refs):
    *got_refs, hidden_ref, out_ref = refs
    out_ref[...] = sum(
        lax.dot_general(
            hidden_ref[units, :],
            w_ref[:, cols],
            (((0,), (0,)), ((), ())),
            preferred_element_type=jnp.float32,
        )
        for units, w_ref in weight_parts(half, own_ref, got_refs)
    ).astype(out_ref.dtype)


def slot_grads_kernel(rows_ref, forward_ref, part_ref, back_ref):
    capacity = back_ref.shape[1]
    pair = 2 * capacity
    for p in range(rows_ref.shape[0] // pair):
        at = slice(p * pair, (p + 1) * pair)
        some = jnp.zeros((pair, LANES), jnp.float32)
        for n in range(0, rows_ref.shape[1], LANES):
            cols = slice(n, n + LANES)
            some += rows_ref[at, cols].astype(jnp.float32) * forward_ref[at, cols].astype(
                jnp.float32
            )
        total = jnp.sum(some.T, axis=0, keepdims=True)
        for i in range(2):
            to = slice(2 * p + i, 2 * p + i + 1)
            back_ref[to, :] = part_ref[to, :] + total[:, i * capacity : (i + 1) * capacity]


def gates_kernel(routes_ref, slots_ref, back_ref, out_ref):
    back = back_ref[...]
    routes = routes_ref[...]
    experts, capacity = back.shape
    tokens = routes.shape[1]
    slots = slots_ref[experts : 2 * experts, :].astype(jnp.float32)
    expert = lax.broadcasted_iota(jnp.int32, (experts, tokens), 0)
    slot = lax.broadcasted_iota(jnp.int32, (capacity, tokens), 0).astype(jnp.float32)
    for k in range(out_ref.shape[0]):
        hit = expert == routes[k : k + 1, :]
        number = jnp.sum(jnp.where(hit, slots, 0.0), axis=0, keepdims=True)
        by_expert = jnp.dot(
            back,
            jnp.where(slot == number, 1.0, 0.0),
            preferred_element_type=jnp.float32,
            precision=lax.Precision.HIGHEST,
        )
        out_ref[k : k + 1, :] = jnp.sum(jnp.where(hit, by_expert, 0.0), axis=0, keepdims=True)


def finish_kernel(low, own_ref, got_ref, *refs):
    out_hbm, sum_ref, sem = refs[-3:]
    sum_ref[...] = (
        own_ref[...].astype(jnp.float32) + got_ref[...].astype(jnp.float32)
    ).astype(jnp.bfloat16)
    copy = pltpu.make_async_copy(sum_ref, out_hbm.at[:, pl.ds(low, sum_ref.shape[1])], sem)
    copy.start()
    copy.wait()


def ring_shards(grad_out, gates, routes, hidden, down_weight):
    experts = lax.axis_size("expert")
    tokens, chosen = routes.shape
    model = grad_out.shape[1]
    slots, units = hidden.shape[2:]
    half = down_weight.shape[1]
    capacity = slots // experts
    widths = [model // 8 * n for n in CHUNKS]
    columns = [slice(0, widths[0]), slice(widths[0], model)]
    tile = 256
    bf16, f32 = jnp.bfloat16, jnp.float32
    shape = jax.ShapeDtypeStruct
    hidden_t = hidden[0, 0].T
    routes_t, gates_t = routes.T, gates.T
    weight = down_weight[0]
    split = half // 32 * 16
    weight_specs = [
        pl.BlockSpec((n, model), lambda i: (0, 0)) for n in (half, split, half - split)
    ]
    dma = pltpu.SemaphoreType.DMA

    def forward(x):
        return lax.ppermute(x, "expert", ring_pairs(1))

    def backward(x):
        return lax.ppermute(x, "expert", ring_pairs(-1))

    def across(x):
        return lax.ppermute(x, "expert", swap_pairs(2))

    def sibling(x):
        return lax.ppermute(x, "expert", swap_pairs(1))

    def swap(x):
        return lax.ppermute(x, "dp", [(0, 1), (1, 0)])

    def behind(x, *others):
        return lax.optimization_barrier((x, *others))[0]

    def pack():
        return pl.pallas_call(
            functools.partial(pack_kernel, experts, widths[0]),
            out_shape=shape((tokens, widths[0] + tokens), bf16),
            in_specs=[ANY] * 3,
            out_specs=VMEM,
            scratch_shapes=[
                pltpu.VMEM(routes_t.shape, routes_t.dtype),
                pltpu.VMEM(gates_t.shape, gates_t.dtype),
                dma((3,)),
            ],
            compiler_params=params(48),
            name="pack",
        )(routes_t, gates_t, grad_out)

    def later_pack(after):
        return pl.pallas_call(
            functools.partial(later_pack_kernel, widths[0]),
            out_shape=shape((tokens, widths[1]), bf16),
            in_specs=[ANY] * 2,
            out_specs=VMEM,
            scratch_shapes=[dma],
            compiler_params=params(48),
            name="later_pack",
        )(grad_out, after)

    def first_pick(blocks):
        return pl.pallas_call(
            functools.partial(first_pick_kernel, experts, capacity),
            out_shape=[
                shape((slots // 2, widths[0]), bf16),
                shape((slots // 2 + 16, widths[0]), bf16),
                shape((slots, tokens), bf16),
                shape((experts // 2, 2 * capacity), f32),
            ],
            in_specs=[VMEM] * len(blocks),
            out_specs=[VMEM] * 4,
            scratch_shapes=[pltpu.VMEM((16, 2 * capacity), f32)],
            compiler_params=params(24),
            cost_estimate=cost(3),
            name="first_pick",
        )(*blocks)

    def later_pick(blocks, pmat):
        return pl.pallas_call(
            pick_kernel,
            out_shape=[shape((slots // 2, widths[1]), bf16)] * 2,
            in_specs=[VMEM] * (len(blocks) + 1),
            out_specs=[VMEM] * 2,
            compiler_params=params(24),
            name="pick",
        )(*blocks, pmat)

    def product_shapes(c):
        piece = shape((half, widths[c] // PIECES[c]), bf16)
        return [shape((slots, widths[c]), bf16)] + [piece] * (2 * PIECES[c])

    def first_products(mine, got, gslot):
        slot_gates, hs, rows, *halves = pl.pallas_call(
            functools.partial(first_products_kernel, half, capacity),
            out_shape=[shape((1, slots), f32), shape((units, slots), bf16)] + product_shapes(0),
            in_specs=[VMEM] * 4,
            out_specs=[VMEM] * (3 + 2 * PIECES[0]),
            compiler_params=params(24),
            cost_estimate=cost(3),
            name="first_products",
        )(mine, got, gslot, hidden_t)
        return rows, halves[: PIECES[0]], halves[PIECES[0] :], slot_gates, hs

    def later_products(mine, got, hs):
        rows, *halves = pl.pallas_call(
            functools.partial(products, half, capacity),
            out_shape=product_shapes(1),
            in_specs=[VMEM] * 3,
            out_specs=[VMEM] * (1 + 2 * PIECES[1]),
            compiler_params=params(24),
            name="products",
        )(mine, got, hs)
        return rows, halves[: PIECES[1]], halves[PIECES[1] :]

    by_slot = pl.BlockSpec((units, tile), lambda i: (0, i))
    by_row = [pl.BlockSpec((tile, n), lambda i: (i, 0)) for n in widths]
    back_shape = shape((experts, capacity), f32)

    def raw_part(rows, got_weight):
        return pl.pallas_call(
            functools.partial(raw_part_kernel, half, capacity, columns[0]),
            grid=(slots // tile,),
            out_shape=[shape((units, slots), f32), back_shape],
            in_specs=[by_row[0], *weight_specs, by_slot],
            out_specs=[by_slot, pl.BlockSpec((experts, capacity), lambda i: (0, 0))],
            compiler_params=params(24),
            cost_estimate=cost(3),
            name="raw_part",
        )(rows, weight, *got_weight, hidden_t)

    def raw_rest(rows, got_weight, raw, slot_gates):
        return pl.pallas_call(
            functools.partial(raw_kernel, half, columns[1]),
            grid=(slots // tile,),
            out_shape=shape((units, slots), bf16),
            in_specs=[
                by_row[1],
                *weight_specs,
                by_slot,
                pl.BlockSpec((1, tile), lambda i: (0, i)),
            ],
            out_specs=by_slot,
            compiler_params=params(48),
            name="raw",
        )(rows, weight, *got_weight, raw, slot_gates)

    def forward_columns(got_weight):
        return pl.pallas_call(
            functools.partial(forward_kernel, half, columns[1]),
            grid=(slots // tile,),
            out_shape=shape((slots, widths[1]), bf16),
            in_specs=[*weight_specs, by_slot],
            out_specs=by_row[1],
            compiler_params=params(24),
            cost_estimate=cost(3),
            name="hidden_weight",
        )(weight, *got_weight, hidden_t)

    def slot_grads(rows, forwarded, part):
        return pl.pallas_call(
            slot_grads_kernel,
            out_shape=back_shape,
            in_specs=[VMEM] * 3,
            out_specs=VMEM,
            compiler_params=params(24),
            name="slot_grads",
        )(rows, forwarded, part)

    def finish(low, own, got, *before):
        return pl.pallas_call(
            functools.partial(finish_kernel, low),
            out_shape=shape((half, model), bf16),
            in_specs=[VMEM] * 2 + [ANY] * len(before),
            out_specs=ANY,
            scratch_shapes=[pltpu.VMEM(own.shape, bf16), dma],
            input_output_aliases={2: 0} if before else {},
            compiler_params=params(8),
            name="finish",
        )(own, got, *before)

    x0 = pack()
    later = behind(weight, x0)
    w = [swap(later[:split]), swap(later[split:])]
    f0, r0, y0 = forward(x0), backward(x0), across(x0)
    ff0, yf0 = forward(f0), across(f0)
    x1 = later_pack(r0)
    f1, yr0 = forward(x1), across(behind(r0, y0))
    yff0 = across(behind(ff0, yf0, w[0]))
    mine0, theirs0, pmat, gslot = first_pick(
        [x0, y0, f0, yf0, ff0, yff0, r0, behind(yr0, f1, w[1])]
    )
    ff1, y1 = forward(f1), across(behind(x1, yr0))
    r1, yf1 = backward(behind(x1, ff0)), across(behind(f1, yr0))
    got = sibling(theirs0)
    rows0, send0, own0, slot_gates, hs = first_products(mine0, got, gslot)
    got0 = [swap(part) for part in send0]
    yff1, ry1 = across(behind(ff1, y1, yf1, r1)), backward(behind(y1, yf1, r1))
    raw, part = raw_part(rows0, w)
    forwarded = forward_columns(w)
    mine1, theirs1 = later_pick(
        [x1, y1, f1, yf1, ff1, yff1, r1, ry1], behind(pmat, raw, forwarded)
    )
    grad_weight = finish(0, own0[0], got0[0])
    grad_weight = finish(widths[0] // 2, own0[1], got0[1], grad_weight)
    got = sibling(behind(theirs1, *got0))
    rows1, send1, own1 = later_products(mine1, got, behind(hs, grad_weight))
    got1 = [swap(part) for part in send1]

    back = slot_grads(rows1, forwarded, part)
    returned = lax.all_to_all(back, "expert", split_axis=0, concat_axis=0, tiled=True)
    grad_gates = pl.pallas_call(
        gates_kernel,
        grid=(1,),
        out_shape=shape((chosen, tokens), f32),
        in_specs=[
            pl.BlockSpec((chosen, tokens), lambda i: (0, 0)),
            pl.BlockSpec((2 * experts, tokens), lambda i: (0, widths[0] // tokens)),
            pl.BlockSpec((experts, capacity), lambda i: (0, 0)),
        ],
        out_specs=pl.BlockSpec((chosen, tokens), lambda i: (0, 0)),
        name="grad_gates",
    )(routes_t, x0, returned)

    grad_hidden = raw_rest(rows1, w, raw, slot_gates)
    grad_weight = finish(widths[0], own1[0], got1[0], grad_weight)
    grad_weight = finish(widths[0] + widths[1] // 2, own1[1], got1[1], grad_weight)
    return grad_weight[None], grad_hidden.T[None, None], grad_gates.T


def shards(grad_out, gates, routes, hidden, down_weight):
    owners = lax.axis_size("expert")
    token_count, chosen = routes.shape
    width = grad_out.shape[1]
    slots = hidden.shape[2]
    capacity = slots // owners
    flat = routes.reshape(-1)
    onehot = (flat[:, None] == jnp.arange(owners, dtype=jnp.int32)[None, :]).astype(jnp.int32)
    before = jnp.cumsum(onehot, axis=0) - onehot
    slot = jnp.sum(before * onehot, axis=1)
    target = flat * capacity + slot
    send_rows = (
        jnp.zeros((owners * capacity, width), grad_out.dtype)
        .at[target]
        .set(jnp.repeat(grad_out, chosen, axis=0))
    )
    send_gate = jnp.zeros((owners * capacity,), gates.dtype).at[target].set(gates.reshape(-1))
    send_rows = send_rows.reshape(owners, capacity, width)
    send_gate = send_gate.reshape(owners, capacity)
    saved = hidden[0, 0]
    local_weight = down_weight[0]
    contract = (((1,), (1,)), ((), ()))
    rows, gate_slots = (
        lax.all_to_all(send_rows, "expert", split_axis=0, concat_axis=0, tiled=True),
        lax.all_to_all(send_gate, "expert", split_axis=0, concat_axis=0, tiled=True),
    )
    rows = rows.reshape(slots, width)
    whole_weight = lax.all_gather(local_weight, "dp", axis=0, tiled=True)
    raw = lax.dot_general(rows, whole_weight, contract, preferred_element_type=jnp.float32)
    factor = gate_slots.reshape(slots, 1).astype(jnp.float32)
    grad_hidden = (factor * raw).astype(jnp.bfloat16)
    slot_grads = jnp.sum(raw * saved.astype(jnp.float32), axis=1)
    returned = lax.all_to_all(
        slot_grads.reshape(owners, capacity), "expert", split_axis=0, concat_axis=0, tiled=True
    )
    grad_gates = returned.reshape(-1)[target].reshape(token_count, chosen)
    scaled = (factor * rows.astype(jnp.float32)).astype(jnp.bfloat16)
    summed = lax.psum_scatter(
        lax.dot_general(
            saved, scaled, (((0,), (0,)), ((), ())), preferred_element_type=jnp.float32
        ).astype(jnp.bfloat16),
        "dp",
        scatter_dimension=0,
        tiled=True,
    )
    return (summed[None], grad_hidden[None, None], grad_gates)


def solution(mesh):
    small = mesh.shape["dp"] == 2 and mesh.shape["expert"] == NZ * NY * NC
    return jax.shard_map(
        ring_shards if small else shards,
        mesh=mesh,
        in_specs=(
            P(("dp", "expert"), None),
            P(("dp", "expert"), None),
            P(("dp", "expert"), None),
            P("dp", "expert", None, None),
            P("expert", "dp", None),
        ),
        out_specs=(
            P("expert", "dp", None),
            P("dp", "expert", None, None),
            P(("dp", "expert"), None),
        ),
        check_vma=False,
    )
```

```python
import functools

import jax
import jax.numpy as jnp
from jax import lax
from jax.experimental import pallas as pl
from jax.experimental.pallas import tpu as pltpu
from jax.sharding import PartitionSpec as P

NZ, NY, NC = 4, 2, 2
CHUNKS = (4, 4)
PIECES = (2, 2)
LANES = 128
NT = (((1,), (1,)), ((), ()))
VMEM = pl.BlockSpec(memory_space=pltpu.VMEM)
ANY = pl.BlockSpec(memory_space=pl.ANY)


def params(mib):
    return pltpu.CompilerParams(vmem_limit_bytes=mib * 2**20)


def cost(micros):
    return pl.CostEstimate(
        flops=micros * 10**9, bytes_accessed=micros * 3 * 2**20, transcendentals=0
    )


def ring(z):
    return z ^ (z >> 1)


def ring_pairs(step):
    size = NY * NC
    return [
        (ring(p) * size + rest, ring((p + step) % NZ) * size + rest)
        for p in range(NZ)
        for rest in range(size)
    ]


def swap_pairs(bit):
    return [(i, i ^ bit) for i in range(NZ * NY * NC)]


def pack_kernel(experts, width, *refs):
    routes_hbm, gates_hbm, grad_hbm, weight_hbm, out_ref, low_ref, high_ref, *scratch = refs
    routes_ref, gates_ref, sems = scratch
    low = low_ref.shape[0]
    copies = [
        pltpu.make_async_copy(src, dst, sems.at[i])
        for i, (src, dst) in enumerate(
            (
                (routes_hbm, routes_ref),
                (gates_hbm, gates_ref),
                (grad_hbm.at[:, :width], out_ref.at[:, :width]),
                (weight_hbm.at[:low], low_ref),
                (weight_hbm.at[low:], high_ref),
            )
        )
    ]
    for copy in copies:
        copy.start()
    copies[0].wait()
    copies[1].wait()
    chosen, tokens = routes_ref.shape
    routes = routes_ref[...]
    gates = gates_ref[...].astype(jnp.float32)
    expert = lax.broadcasted_iota(jnp.int32, (experts, tokens), 0)
    dense = jnp.zeros((experts, tokens), jnp.float32)
    named = jnp.zeros((experts, tokens), jnp.float32)
    for k in range(chosen):
        hit = routes[k : k + 1, :] == expert
        dense = jnp.where(hit, gates[k : k + 1, :], dense)
        named = jnp.where(hit, 1.0, named)
    earlier = (
        lax.broadcasted_iota(jnp.int32, (tokens, tokens), 0)
        < lax.broadcasted_iota(jnp.int32, (tokens, tokens), 1)
    )
    slots = jnp.dot(
        named.astype(jnp.bfloat16),
        jnp.where(earlier, 1.0, 0.0).astype(jnp.bfloat16),
        preferred_element_type=jnp.float32,
    )
    slots = jnp.where(named > 0, slots, -1.0)
    out_ref[:, width:] = jnp.zeros((tokens, tokens), jnp.bfloat16)
    out_ref[:experts, width:] = dense.astype(jnp.bfloat16)
    out_ref[experts : 2 * experts, width:] = slots.astype(jnp.bfloat16)
    for copy in copies[2:]:
        copy.wait()


def later_pack_kernel(low, grad_hbm, after_ref, out_ref, sem):
    del after_ref
    copy = pltpu.make_async_copy(grad_hbm.at[:, pl.ds(low, out_ref.shape[1])], out_ref, sem)
    copy.start()
    copy.wait()


def pair_place(arrival):
    index = lax.axis_index("expert")
    z, y = index >> 2, (index >> 1) & 1
    z = ring((ring(z) - arrival // NY) & (NZ - 1))
    return z * NY + (y ^ (arrival % NY))


def pick(xs, pmat_ref, mine_ref, theirs_ref):
    capacity = mine_ref.shape[0] // len(xs)

    @pl.loop(0, mine_ref.shape[1] // 256)
    def _(n):
        cols = pl.ds(pl.multiple_of(n * 256, 256), 256)
        for a, x_ref in enumerate(xs):
            rows = jnp.dot(
                pmat_ref[a * 2 * capacity : (a + 1) * 2 * capacity, :],
                x_ref[:, cols],
                preferred_element_type=jnp.float32,
            ).astype(jnp.bfloat16)
            where = pl.ds(pl.multiple_of(pair_place(a) * capacity, capacity), capacity)
            mine_ref[where, cols] = rows[:capacity]
            theirs_ref[where, cols] = rows[capacity:]


def first_pick_kernel(experts, capacity, *refs):
    pairs = experts // 2
    xs = refs[:pairs]
    mine_ref, theirs_ref, pmat_ref, gslot_ref, other_ref = refs[pairs:]
    width = mine_ref.shape[1]
    me = lax.axis_index("expert")
    core = me & 1
    tokens = xs[0].shape[0]
    expert = lax.broadcasted_iota(jnp.int32, (experts, tokens), 0)
    slot = lax.broadcasted_iota(jnp.int32, (2 * capacity, tokens), 0).astype(jnp.float32)
    offset = (core * capacity).astype(jnp.float32)
    other_ref[...] = jnp.zeros(other_ref.shape, jnp.float32)
    for a, x_ref in enumerate(xs):
        place = pl.ds(pair_place(a), 1)
        ext = x_ref[: 2 * experts, width:].astype(jnp.float32)
        one_hot = jnp.zeros(slot.shape, jnp.float32)
        for s, (who, to_ref) in enumerate(((me, gslot_ref), (me ^ 1, other_ref))):
            gate = jnp.sum(jnp.where(expert == who, ext[:experts], 0.0), axis=0, keepdims=True)
            number = jnp.sum(jnp.where(expert == who, ext[experts:], 0.0), axis=0, keepdims=True)
            routed = number >= 0
            spot = jnp.where(routed, number + s * capacity, -1.0)
            one_hot = jnp.where(slot == spot, 1.0, one_hot)
            spot = jnp.where(routed, number + offset, -1.0)
            by_slot = lax.dot_general(
                jnp.broadcast_to(gate.astype(jnp.bfloat16), (16, tokens)),
                jnp.where(slot == spot, 1.0, 0.0).astype(jnp.bfloat16),
                NT,
                preferred_element_type=jnp.float32,
            )
            to_ref[place, :] = by_slot[:1]
        pmat_ref[a * 2 * capacity : (a + 1) * 2 * capacity, :] = one_hot.astype(jnp.bfloat16)
    theirs_ref[pairs * capacity :, :] = jnp.zeros((16, width), jnp.bfloat16)
    theirs_ref[pairs * capacity :, : 2 * capacity] = other_ref[...].astype(jnp.bfloat16)
    pick(xs, pmat_ref, mine_ref, theirs_ref)


def pick_kernel(*refs):
    pick(refs[:-3], *refs[-3:])


def products(half, capacity, mine_ref, got_ref, hs_ref, rows_ref, *outs):
    mine = lax.axis_index("dp")
    core = lax.axis_index("expert") & 1
    pairs = mine_ref.shape[0] // capacity
    pieces = len(outs) // 2
    piece = mine_ref.shape[1] // pieces
    for q in range(pieces):

        @pl.loop(0, piece // 256)
        def _(n, q=q):
            cols = pl.ds(pl.multiple_of(q * piece + n * 256, 256), 256)
            out = pl.ds(pl.multiple_of(n * 256, 256), 256)
            for p in range(pairs):
                for c, ref in ((core, mine_ref), (1 - core, got_ref)):
                    to = pl.ds(pl.multiple_of((2 * p + c) * capacity, capacity), capacity)
                    rows_ref[to, cols] = ref[p * capacity : (p + 1) * capacity, cols]
            block = rows_ref[:, cols]
            for d, ref in ((1 - mine, outs[q]), (mine, outs[pieces + q])):
                units = pl.ds(pl.multiple_of(d * half, 16), half)
                ref[:, out] = jnp.dot(
                    hs_ref[units, :], block, preferred_element_type=jnp.float32
                ).astype(jnp.bfloat16)


def first_products_kernel(half, capacity, mine_ref, got_ref, gslot_ref, hidden_ref, *outs):
    gates_ref, hs_ref = outs[:2]
    pairs = mine_ref.shape[0] // capacity
    got = got_ref[pairs * capacity :, : 2 * capacity].astype(jnp.float32)
    by_pair = gslot_ref[...] + got[:pairs]
    for p in range(pairs):
        gates_ref[:, p * 2 * capacity : (p + 1) * 2 * capacity] = by_pair[p : p + 1, :]
    hs_ref[...] = (hidden_ref[...].astype(jnp.float32) * gates_ref[...]).astype(jnp.bfloat16)
    products(half, capacity, mine_ref, got_ref, hs_ref, *outs[2:])


def weight_parts(half, own_ref, got_refs):
    mine = lax.axis_index("dp")
    yield pl.ds(pl.multiple_of(mine * half, 16), half), own_ref
    low = (1 - mine) * half
    for ref in got_refs:
        yield pl.ds(pl.multiple_of(low, 16), ref.shape[0]), ref
        low = low + ref.shape[0]


def raw_parts(half, cols, rows_ref, own_ref, got_refs):
    for units, w_ref in weight_parts(half, own_ref, got_refs):
        yield units, lax.dot_general(
            w_ref[:, cols], rows_ref[...], NT, preferred_element_type=jnp.float32
        )


def raw_part_kernel(half, capacity, cols, rows_ref, own_ref, *refs):
    *got_refs, hidden_ref, raw_ref, back_ref = refs
    total = jnp.zeros((1, rows_ref.shape[0]), jnp.float32)
    for units, raw in raw_parts(half, cols, rows_ref, own_ref, got_refs):
        raw_ref[units, :] = raw
        total += jnp.sum(
            raw * hidden_ref[units, :].astype(jnp.float32), axis=0, keepdims=True
        )
    blocks = total.shape[1] // capacity
    for i in range(blocks):
        to = pl.ds(pl.program_id(0) * blocks + i, 1)
        back_ref[to, :] = total[:, i * capacity : (i + 1) * capacity]


def raw_kernel(half, cols, rows_ref, own_ref, *refs):
    *got_refs, sum_ref, gates_ref, grad_ref = refs
    for units, raw in raw_parts(half, cols, rows_ref, own_ref, got_refs):
        grad_ref[units, :] = ((raw + sum_ref[units, :]) * gates_ref[...]).astype(jnp.bfloat16)


def forward_kernel(half, cols, own_ref, *refs):
    *got_refs, hidden_ref, out_ref = refs
    out_ref[...] = sum(
        lax.dot_general(
            hidden_ref[units, :],
            w_ref[:, cols],
            (((0,), (0,)), ((), ())),
            preferred_element_type=jnp.float32,
        )
        for units, w_ref in weight_parts(half, own_ref, got_refs)
    ).astype(out_ref.dtype)


def slot_grads_kernel(rows_ref, forward_ref, part_ref, back_ref):
    capacity = back_ref.shape[1]
    pair = 2 * capacity
    for p in range(rows_ref.shape[0] // pair):
        at = slice(p * pair, (p + 1) * pair)
        some = jnp.zeros((pair, LANES), jnp.float32)
        for n in range(0, rows_ref.shape[1], LANES):
            cols = slice(n, n + LANES)
            some += rows_ref[at, cols].astype(jnp.float32) * forward_ref[at, cols].astype(
                jnp.float32
            )
        total = jnp.sum(some.T, axis=0, keepdims=True)
        for i in range(2):
            to = slice(2 * p + i, 2 * p + i + 1)
            back_ref[to, :] = part_ref[to, :] + total[:, i * capacity : (i + 1) * capacity]


def gates_kernel(routes_ref, slots_ref, back_ref, out_ref):
    back = back_ref[...]
    routes = routes_ref[...]
    experts, capacity = back.shape
    tokens = routes.shape[1]
    slots = slots_ref[experts : 2 * experts, :].astype(jnp.float32)
    expert = lax.broadcasted_iota(jnp.int32, (experts, tokens), 0)
    slot = lax.broadcasted_iota(jnp.int32, (capacity, tokens), 0).astype(jnp.float32)
    for k in range(out_ref.shape[0]):
        hit = expert == routes[k : k + 1, :]
        number = jnp.sum(jnp.where(hit, slots, 0.0), axis=0, keepdims=True)
        by_expert = jnp.dot(
            back,
            jnp.where(slot == number, 1.0, 0.0),
            preferred_element_type=jnp.float32,
            precision=lax.Precision.HIGHEST,
        )
        out_ref[k : k + 1, :] = jnp.sum(jnp.where(hit, by_expert, 0.0), axis=0, keepdims=True)


def finish_kernel(own_ref, got_ref, *refs):
    refs[-1][...] = (
        own_ref[...].astype(jnp.float32) + got_ref[...].astype(jnp.float32)
    ).astype(jnp.bfloat16)


def ring_shards(grad_out, gates, routes, hidden, down_weight):
    experts = lax.axis_size("expert")
    tokens, chosen = routes.shape
    model = grad_out.shape[1]
    slots, units = hidden.shape[2:]
    half = down_weight.shape[1]
    capacity = slots // experts
    widths = [model // 8 * n for n in CHUNKS]
    columns = [slice(0, widths[0]), slice(widths[0], model)]
    tile = 256
    bf16, f32 = jnp.bfloat16, jnp.float32
    shape = jax.ShapeDtypeStruct
    hidden_t = hidden[0, 0].T
    routes_t, gates_t = routes.T, gates.T
    weight = down_weight[0]
    split = half // 32 * 16
    weight_specs = [
        pl.BlockSpec((n, model), lambda i: (0, 0)) for n in (half, split, half - split)
    ]
    dma = pltpu.SemaphoreType.DMA

    def forward(x):
        return lax.ppermute(x, "expert", ring_pairs(1))

    def backward(x):
        return lax.ppermute(x, "expert", ring_pairs(-1))

    def across(x):
        return lax.ppermute(x, "expert", swap_pairs(2))

    def sibling(x):
        return lax.ppermute(x, "expert", swap_pairs(1))

    def swap(x):
        return lax.ppermute(x, "dp", [(0, 1), (1, 0)])

    def behind(x, *others):
        return lax.optimization_barrier((x, *others))[0]

    def pack():
        return pl.pallas_call(
            functools.partial(pack_kernel, experts, widths[0]),
            out_shape=[
                shape((tokens, widths[0] + tokens), bf16),
                shape((split, model), bf16),
                shape((half - split, model), bf16),
            ],
            in_specs=[ANY] * 4,
            out_specs=[VMEM] * 3,
            scratch_shapes=[
                pltpu.VMEM(routes_t.shape, routes_t.dtype),
                pltpu.VMEM(gates_t.shape, gates_t.dtype),
                dma((5,)),
            ],
            compiler_params=params(48),
            name="pack",
        )(routes_t, gates_t, grad_out, weight)

    def later_pack(after):
        return pl.pallas_call(
            functools.partial(later_pack_kernel, widths[0]),
            out_shape=shape((tokens, widths[1]), bf16),
            in_specs=[ANY] * 2,
            out_specs=VMEM,
            scratch_shapes=[dma],
            compiler_params=params(48),
            name="later_pack",
        )(grad_out, after)

    def first_pick(blocks):
        return pl.pallas_call(
            functools.partial(first_pick_kernel, experts, capacity),
            out_shape=[
                shape((slots // 2, widths[0]), bf16),
                shape((slots // 2 + 16, widths[0]), bf16),
                shape((slots, tokens), bf16),
                shape((experts // 2, 2 * capacity), f32),
            ],
            in_specs=[VMEM] * len(blocks),
            out_specs=[VMEM] * 4,
            scratch_shapes=[pltpu.VMEM((16, 2 * capacity), f32)],
            compiler_params=params(24),
            cost_estimate=cost(3),
            name="first_pick",
        )(*blocks)

    def later_pick(blocks, pmat):
        return pl.pallas_call(
            pick_kernel,
            out_shape=[shape((slots // 2, widths[1]), bf16)] * 2,
            in_specs=[VMEM] * (len(blocks) + 1),
            out_specs=[VMEM] * 2,
            compiler_params=params(24),
            name="pick",
        )(*blocks, pmat)

    def product_shapes(c):
        piece = shape((half, widths[c] // PIECES[c]), bf16)
        return [shape((slots, widths[c]), bf16)] + [piece] * (2 * PIECES[c])

    def first_products(mine, got, gslot):
        slot_gates, hs, rows, *halves = pl.pallas_call(
            functools.partial(first_products_kernel, half, capacity),
            out_shape=[shape((1, slots), f32), shape((units, slots), bf16)] + product_shapes(0),
            in_specs=[VMEM] * 4,
            out_specs=[VMEM] * (3 + 2 * PIECES[0]),
            compiler_params=params(24),
            cost_estimate=cost(3),
            name="first_products",
        )(mine, got, gslot, hidden_t)
        return rows, halves[: PIECES[0]], halves[PIECES[0] :], slot_gates, hs

    def later_products(mine, got, hs):
        rows, *halves = pl.pallas_call(
            functools.partial(products, half, capacity),
            out_shape=product_shapes(1),
            in_specs=[VMEM] * 3,
            out_specs=[VMEM] * (1 + 2 * PIECES[1]),
            compiler_params=params(24),
            name="products",
        )(mine, got, hs)
        return rows, halves[: PIECES[1]], halves[PIECES[1] :]

    by_slot = pl.BlockSpec((units, tile), lambda i: (0, i))
    by_row = [pl.BlockSpec((tile, n), lambda i: (i, 0)) for n in widths]
    back_shape = shape((experts, capacity), f32)

    def raw_part(rows, got_weight):
        return pl.pallas_call(
            functools.partial(raw_part_kernel, half, capacity, columns[0]),
            grid=(slots // tile,),
            out_shape=[shape((units, slots), f32), back_shape],
            in_specs=[by_row[0], *weight_specs, by_slot],
            out_specs=[by_slot, pl.BlockSpec((experts, capacity), lambda i: (0, 0))],
            compiler_params=params(24),
            cost_estimate=cost(3),
            name="raw_part",
        )(rows, weight, *got_weight, hidden_t)

    def raw_rest(rows, got_weight, raw, slot_gates):
        return pl.pallas_call(
            functools.partial(raw_kernel, half, columns[1]),
            grid=(slots // tile,),
            out_shape=shape((units, slots), bf16),
            in_specs=[
                by_row[1],
                *weight_specs,
                by_slot,
                pl.BlockSpec((1, tile), lambda i: (0, i)),
            ],
            out_specs=by_slot,
            compiler_params=params(20),
            name="raw",
        )(rows, weight, *got_weight, raw, slot_gates)

    def forward_columns(got_weight):
        return pl.pallas_call(
            functools.partial(forward_kernel, half, columns[1]),
            grid=(slots // tile,),
            out_shape=shape((slots, widths[1]), bf16),
            in_specs=[*weight_specs, by_slot],
            out_specs=by_row[1],
            compiler_params=params(24),
            cost_estimate=cost(3),
            name="hidden_weight",
        )(weight, *got_weight, hidden_t)

    def slot_grads(rows, forwarded, part):
        return pl.pallas_call(
            slot_grads_kernel,
            out_shape=back_shape,
            in_specs=[VMEM] * 3,
            out_specs=VMEM,
            compiler_params=params(24),
            name="slot_grads",
        )(rows, forwarded, part)

    def finish(low, own, got, *before):
        piece = own.shape[1]
        spec = pl.BlockSpec((half // 2, piece), lambda i: (i, 0))
        return pl.pallas_call(
            finish_kernel,
            grid=(2,),
            out_shape=shape((half, model), bf16),
            in_specs=[spec, spec] + [ANY] * len(before),
            out_specs=pl.BlockSpec((half // 2, piece), lambda i: (i, low // piece)),
            input_output_aliases={2: 0} if before else {},
            compiler_params=params(8),
            name="finish",
        )(own, got, *before)

    x0, *w = pack()
    w = [swap(part) for part in w]
    f0, r0, y0 = forward(x0), backward(x0), across(x0)
    ff0, yf0 = forward(f0), across(f0)
    x1 = later_pack(r0)
    f1, yr0 = forward(x1), across(behind(r0, y0))
    yff0 = across(behind(ff0, yf0, w[0]))
    mine0, theirs0, pmat, gslot = first_pick(
        [x0, y0, f0, yf0, ff0, yff0, r0, behind(yr0, f1, w[1])]
    )
    ff1, y1 = forward(f1), across(behind(x1, yr0))
    r1, yf1 = backward(behind(x1, ff0)), across(behind(f1, yr0))
    got = sibling(theirs0)
    rows0, send0, own0, slot_gates, hs = first_products(mine0, got, gslot)
    got0 = [swap(part) for part in send0]
    done = (yf1, r1, rows0)
    yff1, ry1 = across(behind(ff1, y1, *done)), backward(behind(y1, *done))
    raw, part = raw_part(rows0, w)
    mine1, theirs1 = later_pick(
        [x1, y1, f1, yf1, ff1, yff1, r1, ry1], behind(pmat, raw)
    )
    got = sibling(behind(theirs1, *got0))
    forwarded = forward_columns([behind(w[0], theirs1), w[1]])
    rows1, send1, own1 = later_products(mine1, got, behind(hs, forwarded))
    got1 = [swap(part) for part in send1]

    back = slot_grads(rows1, forwarded, part)
    returned = lax.all_to_all(back, "expert", split_axis=0, concat_axis=0, tiled=True)
    grad_gates = pl.pallas_call(
        gates_kernel,
        grid=(1,),
        out_shape=shape((chosen, tokens), f32),
        in_specs=[
            pl.BlockSpec((chosen, tokens), lambda i: (0, 0)),
            pl.BlockSpec((2 * experts, tokens), lambda i: (0, widths[0] // tokens)),
            pl.BlockSpec((experts, capacity), lambda i: (0, 0)),
        ],
        out_specs=pl.BlockSpec((chosen, tokens), lambda i: (0, 0)),
        name="grad_gates",
    )(routes_t, x0, returned)

    grad_hidden = raw_rest(rows1, w, raw, slot_gates)
    grad_weight = finish(0, behind(own0[0], back), got0[0])
    grad_weight = finish(widths[0] // 2, own0[1], got0[1], grad_weight)
    grad_weight = finish(widths[0], own1[0], got1[0], grad_weight)
    grad_weight = finish(widths[0] + widths[1] // 2, own1[1], got1[1], grad_weight)
    return grad_weight[None], grad_hidden.T[None, None], grad_gates.T


def shards(grad_out, gates, routes, hidden, down_weight):
    owners = lax.axis_size("expert")
    token_count, chosen = routes.shape
    width = grad_out.shape[1]
    slots = hidden.shape[2]
    capacity = slots // owners
    flat = routes.reshape(-1)
    onehot = (flat[:, None] == jnp.arange(owners, dtype=jnp.int32)[None, :]).astype(jnp.int32)
    before = jnp.cumsum(onehot, axis=0) - onehot
    slot = jnp.sum(before * onehot, axis=1)
    target = flat * capacity + slot
    send_rows = (
        jnp.zeros((owners * capacity, width), grad_out.dtype)
        .at[target]
        .set(jnp.repeat(grad_out, chosen, axis=0))
    )
    send_gate = jnp.zeros((owners * capacity,), gates.dtype).at[target].set(gates.reshape(-1))
    send_rows = send_rows.reshape(owners, capacity, width)
    send_gate = send_gate.reshape(owners, capacity)
    saved = hidden[0, 0]
    local_weight = down_weight[0]
    contract = (((1,), (1,)), ((), ()))
    rows, gate_slots = (
        lax.all_to_all(send_rows, "expert", split_axis=0, concat_axis=0, tiled=True),
        lax.all_to_all(send_gate, "expert", split_axis=0, concat_axis=0, tiled=True),
    )
    rows = rows.reshape(slots, width)
    whole_weight = lax.all_gather(local_weight, "dp", axis=0, tiled=True)
    raw = lax.dot_general(rows, whole_weight, contract, preferred_element_type=jnp.float32)
    factor = gate_slots.reshape(slots, 1).astype(jnp.float32)
    grad_hidden = (factor * raw).astype(jnp.bfloat16)
    slot_grads = jnp.sum(raw * saved.astype(jnp.float32), axis=1)
    returned = lax.all_to_all(
        slot_grads.reshape(owners, capacity), "expert", split_axis=0, concat_axis=0, tiled=True
    )
    grad_gates = returned.reshape(-1)[target].reshape(token_count, chosen)
    scaled = (factor * rows.astype(jnp.float32)).astype(jnp.bfloat16)
    summed = lax.psum_scatter(
        lax.dot_general(
            saved, scaled, (((0,), (0,)), ((), ())), preferred_element_type=jnp.float32
        ).astype(jnp.bfloat16),
        "dp",
        scatter_dimension=0,
        tiled=True,
    )
    return (summed[None], grad_hidden[None, None], grad_gates)


def solution(mesh):
    small = mesh.shape["dp"] == 2 and mesh.shape["expert"] == NZ * NY * NC
    return jax.shard_map(
        ring_shards if small else shards,
        mesh=mesh,
        in_specs=(
            P(("dp", "expert"), None),
            P(("dp", "expert"), None),
            P(("dp", "expert"), None),
            P("dp", "expert", None, None),
            P("expert", "dp", None),
        ),
        out_specs=(
            P("expert", "dp", None),
            P("dp", "expert", None, None),
            P(("dp", "expert"), None),
        ),
        check_vma=False,
    )
```

```python
import functools

import jax
import jax.numpy as jnp
from jax import lax
from jax.experimental import pallas as pl
from jax.experimental.pallas import tpu as pltpu
from jax.sharding import PartitionSpec as P

NZ, NY, NC = 4, 2, 2
CHUNKS = (4, 4)
PIECES = (2, 1)
LANES = 128
NT = (((1,), (1,)), ((), ()))
VMEM = pl.BlockSpec(memory_space=pltpu.VMEM)
ANY = pl.BlockSpec(memory_space=pl.ANY)


def params(mib):
    return pltpu.CompilerParams(vmem_limit_bytes=mib * 2**20)


def cost(micros):
    return pl.CostEstimate(
        flops=micros * 10**9, bytes_accessed=micros * 3 * 2**20, transcendentals=0
    )


def ring(z):
    return z ^ (z >> 1)


def ring_pairs(step):
    size = NY * NC
    return [
        (ring(p) * size + rest, ring((p + step) % NZ) * size + rest)
        for p in range(NZ)
        for rest in range(size)
    ]


def swap_pairs(bit):
    return [(i, i ^ bit) for i in range(NZ * NY * NC)]


def pack_kernel(experts, width, routes_hbm, gates_hbm, grad_hbm, out_ref, *scratch):
    routes_ref, gates_ref, sems = scratch
    copies = [
        pltpu.make_async_copy(src, dst, sems.at[i])
        for i, (src, dst) in enumerate(
            (
                (routes_hbm, routes_ref),
                (gates_hbm, gates_ref),
                (grad_hbm.at[:, :width], out_ref.at[:, :width]),
            )
        )
    ]
    for copy in copies:
        copy.start()
    copies[0].wait()
    copies[1].wait()
    chosen, tokens = routes_ref.shape
    routes = routes_ref[...]
    gates = gates_ref[...].astype(jnp.float32)
    expert = lax.broadcasted_iota(jnp.int32, (experts, tokens), 0)
    dense = jnp.zeros((experts, tokens), jnp.float32)
    named = jnp.zeros((experts, tokens), jnp.float32)
    for k in range(chosen):
        hit = routes[k : k + 1, :] == expert
        dense = jnp.where(hit, gates[k : k + 1, :], dense)
        named = jnp.where(hit, 1.0, named)
    earlier = (
        lax.broadcasted_iota(jnp.int32, (tokens, tokens), 0)
        < lax.broadcasted_iota(jnp.int32, (tokens, tokens), 1)
    )
    slots = jnp.dot(
        named.astype(jnp.bfloat16),
        jnp.where(earlier, 1.0, 0.0).astype(jnp.bfloat16),
        preferred_element_type=jnp.float32,
    )
    slots = jnp.where(named > 0, slots, -1.0)
    out_ref[:, width:] = jnp.zeros((tokens, tokens), jnp.bfloat16)
    out_ref[:experts, width:] = dense.astype(jnp.bfloat16)
    out_ref[experts : 2 * experts, width:] = slots.astype(jnp.bfloat16)
    copies[2].wait()


def later_pack_kernel(low, grad_hbm, after_ref, out_ref, sem):
    del after_ref
    copy = pltpu.make_async_copy(grad_hbm.at[:, pl.ds(low, out_ref.shape[1])], out_ref, sem)
    copy.start()
    copy.wait()


def pair_place(arrival):
    index = lax.axis_index("expert")
    z, y = index >> 2, (index >> 1) & 1
    z = ring((ring(z) - arrival // NY) & (NZ - 1))
    return z * NY + (y ^ (arrival % NY))


def pick(xs, pmat_ref, mine_ref, theirs_ref):
    capacity = mine_ref.shape[0] // len(xs)

    @pl.loop(0, mine_ref.shape[1] // 256)
    def _(n):
        cols = pl.ds(pl.multiple_of(n * 256, 256), 256)
        for a, x_ref in enumerate(xs):
            rows = jnp.dot(
                pmat_ref[a * 2 * capacity : (a + 1) * 2 * capacity, :],
                x_ref[:, cols],
                preferred_element_type=jnp.float32,
            ).astype(jnp.bfloat16)
            where = pl.ds(pl.multiple_of(pair_place(a) * capacity, capacity), capacity)
            mine_ref[where, cols] = rows[:capacity]
            theirs_ref[where, cols] = rows[capacity:]


def first_pick_kernel(experts, capacity, *refs):
    pairs = experts // 2
    xs = refs[:pairs]
    mine_ref, theirs_ref, pmat_ref, gslot_ref, other_ref = refs[pairs:]
    width = mine_ref.shape[1]
    me = lax.axis_index("expert")
    core = me & 1
    tokens = xs[0].shape[0]
    expert = lax.broadcasted_iota(jnp.int32, (experts, tokens), 0)
    slot = lax.broadcasted_iota(jnp.int32, (2 * capacity, tokens), 0).astype(jnp.float32)
    offset = (core * capacity).astype(jnp.float32)
    other_ref[...] = jnp.zeros(other_ref.shape, jnp.float32)
    for a, x_ref in enumerate(xs):
        place = pl.ds(pair_place(a), 1)
        ext = x_ref[: 2 * experts, width:].astype(jnp.float32)
        one_hot = jnp.zeros(slot.shape, jnp.float32)
        for s, (who, to_ref) in enumerate(((me, gslot_ref), (me ^ 1, other_ref))):
            gate = jnp.sum(jnp.where(expert == who, ext[:experts], 0.0), axis=0, keepdims=True)
            number = jnp.sum(jnp.where(expert == who, ext[experts:], 0.0), axis=0, keepdims=True)
            routed = number >= 0
            spot = jnp.where(routed, number + s * capacity, -1.0)
            one_hot = jnp.where(slot == spot, 1.0, one_hot)
            spot = jnp.where(routed, number + offset, -1.0)
            by_slot = lax.dot_general(
                jnp.broadcast_to(gate.astype(jnp.bfloat16), (16, tokens)),
                jnp.where(slot == spot, 1.0, 0.0).astype(jnp.bfloat16),
                NT,
                preferred_element_type=jnp.float32,
            )
            to_ref[place, :] = by_slot[:1]
        pmat_ref[a * 2 * capacity : (a + 1) * 2 * capacity, :] = one_hot.astype(jnp.bfloat16)
    theirs_ref[pairs * capacity :, :] = jnp.zeros((16, width), jnp.bfloat16)
    theirs_ref[pairs * capacity :, : 2 * capacity] = other_ref[...].astype(jnp.bfloat16)
    pick(xs, pmat_ref, mine_ref, theirs_ref)


def pick_kernel(*refs):
    pick(refs[:-3], *refs[-3:])


def products(half, capacity, mine_ref, got_ref, hs_ref, rows_ref, *outs):
    mine = lax.axis_index("dp")
    core = lax.axis_index("expert") & 1
    pairs = mine_ref.shape[0] // capacity
    pieces = len(outs) // 2
    piece = mine_ref.shape[1] // pieces
    for q in range(pieces):

        @pl.loop(0, piece // 256)
        def _(n, q=q):
            cols = pl.ds(pl.multiple_of(q * piece + n * 256, 256), 256)
            out = pl.ds(pl.multiple_of(n * 256, 256), 256)
            for p in range(pairs):
                for c, ref in ((core, mine_ref), (1 - core, got_ref)):
                    to = pl.ds(pl.multiple_of((2 * p + c) * capacity, capacity), capacity)
                    rows_ref[to, cols] = ref[p * capacity : (p + 1) * capacity, cols]
            block = rows_ref[:, cols]
            for d, ref in ((1 - mine, outs[q]), (mine, outs[pieces + q])):
                units = pl.ds(pl.multiple_of(d * half, 16), half)
                ref[:, out] = jnp.dot(
                    hs_ref[units, :], block, preferred_element_type=jnp.float32
                ).astype(jnp.bfloat16)


def first_products_kernel(half, capacity, mine_ref, got_ref, gslot_ref, hidden_ref, *outs):
    gates_ref, hs_ref = outs[:2]
    pairs = mine_ref.shape[0] // capacity
    got = got_ref[pairs * capacity :, : 2 * capacity].astype(jnp.float32)
    by_pair = gslot_ref[...] + got[:pairs]
    for p in range(pairs):
        gates_ref[:, p * 2 * capacity : (p + 1) * 2 * capacity] = by_pair[p : p + 1, :]
    hs_ref[...] = (hidden_ref[...].astype(jnp.float32) * gates_ref[...]).astype(jnp.bfloat16)
    products(half, capacity, mine_ref, got_ref, hs_ref, *outs[2:])


def weight_parts(half, own_ref, got_refs):
    mine = lax.axis_index("dp")
    yield pl.ds(pl.multiple_of(mine * half, 16), half), own_ref
    low = (1 - mine) * half
    for ref in got_refs:
        yield pl.ds(pl.multiple_of(low, 16), ref.shape[0]), ref
        low = low + ref.shape[0]


def raw_parts(half, cols, rows_ref, own_ref, got_refs):
    for units, w_ref in weight_parts(half, own_ref, got_refs):
        yield units, lax.dot_general(
            w_ref[:, cols], rows_ref[...], NT, preferred_element_type=jnp.float32
        )


def raw_part_kernel(half, capacity, cols, rows_ref, own_ref, *refs):
    *got_refs, hidden_ref, raw_ref, back_ref = refs
    total = jnp.zeros((1, rows_ref.shape[0]), jnp.float32)
    for units, raw in raw_parts(half, cols, rows_ref, own_ref, got_refs):
        raw_ref[units, :] = raw
        total += jnp.sum(
            raw * hidden_ref[units, :].astype(jnp.float32), axis=0, keepdims=True
        )
    blocks = total.shape[1] // capacity
    for i in range(blocks):
        to = pl.ds(pl.program_id(0) * blocks + i, 1)
        back_ref[to, :] = total[:, i * capacity : (i + 1) * capacity]


def raw_kernel(half, cols, rows_ref, own_ref, *refs):
    *got_refs, sum_ref, gates_ref, grad_ref = refs
    for units, raw in raw_parts(half, cols, rows_ref, own_ref, got_refs):
        grad_ref[units, :] = ((raw + sum_ref[units, :]) * gates_ref[...]).astype(jnp.bfloat16)


def forward_kernel(half, cols, own_ref, *refs):
    *got_refs, hidden_ref, out_ref = refs
    out_ref[...] = sum(
        lax.dot_general(
            hidden_ref[units, :],
            w_ref[:, cols],
            (((0,), (0,)), ((), ())),
            preferred_element_type=jnp.float32,
        )
        for units, w_ref in weight_parts(half, own_ref, got_refs)
    ).astype(out_ref.dtype)


def slot_grads_kernel(rows_ref, forward_ref, part_ref, back_ref):
    capacity = back_ref.shape[1]
    pair = 2 * capacity
    for p in range(rows_ref.shape[0] // pair):
        at = slice(p * pair, (p + 1) * pair)
        some = jnp.zeros((pair, LANES), jnp.float32)
        for n in range(0, rows_ref.shape[1], LANES):
            cols = slice(n, n + LANES)
            some += rows_ref[at, cols].astype(jnp.float32) * forward_ref[at, cols].astype(
                jnp.float32
            )
        total = jnp.sum(some.T, axis=0, keepdims=True)
        for i in range(2):
            to = slice(2 * p + i, 2 * p + i + 1)
            back_ref[to, :] = part_ref[to, :] + total[:, i * capacity : (i + 1) * capacity]


def gates_kernel(routes_ref, slots_ref, back_ref, out_ref):
    back = back_ref[...]
    routes = routes_ref[...]
    experts, capacity = back.shape
    tokens = routes.shape[1]
    slots = slots_ref[experts : 2 * experts, :].astype(jnp.float32)
    expert = lax.broadcasted_iota(jnp.int32, (experts, tokens), 0)
    slot = lax.broadcasted_iota(jnp.int32, (capacity, tokens), 0).astype(jnp.float32)
    for k in range(out_ref.shape[0]):
        hit = expert == routes[k : k + 1, :]
        number = jnp.sum(jnp.where(hit, slots, 0.0), axis=0, keepdims=True)
        by_expert = jnp.dot(
            back,
            jnp.where(slot == number, 1.0, 0.0),
            preferred_element_type=jnp.float32,
            precision=lax.Precision.HIGHEST,
        )
        out_ref[k : k + 1, :] = jnp.sum(jnp.where(hit, by_expert, 0.0), axis=0, keepdims=True)


def finish_kernel(own_ref, got_ref, *refs):
    refs[-1][...] = (
        own_ref[...].astype(jnp.float32) + got_ref[...].astype(jnp.float32)
    ).astype(jnp.bfloat16)


def ring_shards(grad_out, gates, routes, hidden, down_weight):
    experts = lax.axis_size("expert")
    tokens, chosen = routes.shape
    model = grad_out.shape[1]
    slots, units = hidden.shape[2:]
    half = down_weight.shape[1]
    capacity = slots // experts
    widths = [model // 8 * n for n in CHUNKS]
    columns = [slice(0, widths[0]), slice(widths[0], model)]
    tile = 256
    bf16, f32 = jnp.bfloat16, jnp.float32
    shape = jax.ShapeDtypeStruct
    hidden_t = hidden[0, 0].T
    routes_t, gates_t = routes.T, gates.T
    weight = down_weight[0]
    split = half // 32 * 16
    weight_specs = [
        pl.BlockSpec((n, model), lambda i: (0, 0)) for n in (half, split, half - split)
    ]
    dma = pltpu.SemaphoreType.DMA

    def forward(x):
        return lax.ppermute(x, "expert", ring_pairs(1))

    def backward(x):
        return lax.ppermute(x, "expert", ring_pairs(-1))

    def across(x):
        return lax.ppermute(x, "expert", swap_pairs(2))

    def sibling(x):
        return lax.ppermute(x, "expert", swap_pairs(1))

    def swap(x):
        return lax.ppermute(x, "dp", [(0, 1), (1, 0)])

    def behind(x, *others):
        return lax.optimization_barrier((x, *others))[0]

    def pack():
        return pl.pallas_call(
            functools.partial(pack_kernel, experts, widths[0]),
            out_shape=shape((tokens, widths[0] + tokens), bf16),
            in_specs=[ANY] * 3,
            out_specs=VMEM,
            scratch_shapes=[
                pltpu.VMEM(routes_t.shape, routes_t.dtype),
                pltpu.VMEM(gates_t.shape, gates_t.dtype),
                dma((3,)),
            ],
            compiler_params=params(48),
            name="pack",
        )(routes_t, gates_t, grad_out)

    def later_pack(after):
        return pl.pallas_call(
            functools.partial(later_pack_kernel, widths[0]),
            out_shape=shape((tokens, widths[1]), bf16),
            in_specs=[ANY] * 2,
            out_specs=VMEM,
            scratch_shapes=[dma],
            compiler_params=params(48),
            name="later_pack",
        )(grad_out, after)

    def first_pick(blocks):
        return pl.pallas_call(
            functools.partial(first_pick_kernel, experts, capacity),
            out_shape=[
                shape((slots // 2, widths[0]), bf16),
                shape((slots // 2 + 16, widths[0]), bf16),
                shape((slots, tokens), bf16),
                shape((experts // 2, 2 * capacity), f32),
            ],
            in_specs=[VMEM] * len(blocks),
            out_specs=[VMEM] * 4,
            scratch_shapes=[pltpu.VMEM((16, 2 * capacity), f32)],
            compiler_params=params(24),
            cost_estimate=cost(3),
            name="first_pick",
        )(*blocks)

    def later_pick(blocks, pmat):
        return pl.pallas_call(
            pick_kernel,
            out_shape=[shape((slots // 2, widths[1]), bf16)] * 2,
            in_specs=[VMEM] * (len(blocks) + 1),
            out_specs=[VMEM] * 2,
            compiler_params=params(24),
            name="pick",
        )(*blocks, pmat)

    def product_shapes(c):
        piece = shape((half, widths[c] // PIECES[c]), bf16)
        return [shape((slots, widths[c]), bf16)] + [piece] * (2 * PIECES[c])

    def first_products(mine, got, gslot):
        slot_gates, hs, rows, *halves = pl.pallas_call(
            functools.partial(first_products_kernel, half, capacity),
            out_shape=[shape((1, slots), f32), shape((units, slots), bf16)] + product_shapes(0),
            in_specs=[VMEM] * 4,
            out_specs=[VMEM] * (3 + 2 * PIECES[0]),
            compiler_params=params(24),
            cost_estimate=cost(3),
            name="first_products",
        )(mine, got, gslot, hidden_t)
        return rows, halves[: PIECES[0]], halves[PIECES[0] :], slot_gates, hs

    def later_products(mine, got, hs):
        rows, *halves = pl.pallas_call(
            functools.partial(products, half, capacity),
            out_shape=product_shapes(1),
            in_specs=[VMEM] * 3,
            out_specs=[VMEM] * (1 + 2 * PIECES[1]),
            compiler_params=params(24),
            name="products",
        )(mine, got, hs)
        return rows, halves[: PIECES[1]], halves[PIECES[1] :]

    by_slot = pl.BlockSpec((units, tile), lambda i: (0, i))
    by_row = [pl.BlockSpec((tile, n), lambda i: (i, 0)) for n in widths]
    back_shape = shape((experts, capacity), f32)

    def raw_part(rows, got_weight):
        return pl.pallas_call(
            functools.partial(raw_part_kernel, half, capacity, columns[0]),
            grid=(slots // tile,),
            out_shape=[shape((units, slots), f32), back_shape],
            in_specs=[by_row[0], *weight_specs, by_slot],
            out_specs=[by_slot, pl.BlockSpec((experts, capacity), lambda i: (0, 0))],
            compiler_params=params(24),
            cost_estimate=cost(3),
            name="raw_part",
        )(rows, weight, *got_weight, hidden_t)

    def raw_rest(rows, got_weight, raw, slot_gates):
        return pl.pallas_call(
            functools.partial(raw_kernel, half, columns[1]),
            grid=(slots // tile,),
            out_shape=shape((units, slots), bf16),
            in_specs=[
                by_row[1],
                *weight_specs,
                by_slot,
                pl.BlockSpec((1, tile), lambda i: (0, i)),
            ],
            out_specs=by_slot,
            compiler_params=params(60),
            name="raw",
        )(rows, weight, *got_weight, raw, slot_gates)

    def forward_columns(got_weight):
        return pl.pallas_call(
            functools.partial(forward_kernel, half, columns[1]),
            grid=(slots // tile,),
            out_shape=shape((slots, widths[1]), bf16),
            in_specs=[*weight_specs, by_slot],
            out_specs=by_row[1],
            compiler_params=params(24),
            cost_estimate=cost(3),
            name="hidden_weight",
        )(weight, *got_weight, hidden_t)

    def slot_grads(rows, forwarded, part):
        return pl.pallas_call(
            slot_grads_kernel,
            out_shape=back_shape,
            in_specs=[VMEM] * 3,
            out_specs=VMEM,
            compiler_params=params(24),
            name="slot_grads",
        )(rows, forwarded, part)

    def finish(low, own, got, *before):
        piece = own.shape[1]
        spec = pl.BlockSpec((half // 2, piece), lambda i: (i, 0))
        return pl.pallas_call(
            finish_kernel,
            grid=(2,),
            out_shape=shape((half, model), bf16),
            in_specs=[spec, spec] + [ANY] * len(before),
            out_specs=pl.BlockSpec((half // 2, piece), lambda i: (i, low // piece)),
            input_output_aliases={2: 0} if before else {},
            compiler_params=params(8),
            name="finish",
        )(own, got, *before)

    x0 = pack()
    w = [swap(weight[:split]), swap(weight[split:])]
    f0, r0, y0 = forward(x0), backward(x0), across(x0)
    ff0, yf0 = forward(f0), across(f0)
    x1 = later_pack(r0)
    f1, yr0 = forward(x1), across(behind(r0, y0))
    yff0 = across(behind(ff0, yf0, w[0]))
    mine0, theirs0, pmat, gslot = first_pick(
        [x0, y0, f0, yf0, ff0, yff0, r0, behind(yr0, f1, w[1])]
    )
    ff1, y1 = forward(f1), across(behind(x1, yr0))
    r1, yf1 = backward(behind(x1, ff0)), across(behind(f1, yr0))
    got = sibling(theirs0)
    rows0, send0, own0, slot_gates, hs = first_products(mine0, got, gslot)
    got0 = [swap(part) for part in send0]
    done = (yf1, r1, rows0)
    yff1, ry1 = across(behind(ff1, y1, *done)), backward(behind(y1, *done))
    forwarded = forward_columns(w)
    raw, part = raw_part(rows0, w)
    mine1, theirs1 = later_pick(
        [x1, y1, f1, yf1, ff1, yff1, r1, ry1], behind(pmat, raw, forwarded)
    )
    grad_weight = finish(0, own0[0], got0[0])
    grad_weight = finish(widths[0] // 2, own0[1], got0[1], grad_weight)
    got = sibling(behind(theirs1, *got0))
    rows1, send1, own1 = later_products(mine1, got, behind(hs, grad_weight))
    got1 = [swap(part) for part in send1]

    back = slot_grads(rows1, forwarded, part)
    returned = lax.all_to_all(back, "expert", split_axis=0, concat_axis=0, tiled=True)
    grad_gates = pl.pallas_call(
        gates_kernel,
        grid=(1,),
        out_shape=shape((chosen, tokens), f32),
        in_specs=[
            pl.BlockSpec((chosen, tokens), lambda i: (0, 0)),
            pl.BlockSpec((2 * experts, tokens), lambda i: (0, widths[0] // tokens)),
            pl.BlockSpec((experts, capacity), lambda i: (0, 0)),
        ],
        out_specs=pl.BlockSpec((chosen, tokens), lambda i: (0, 0)),
        name="grad_gates",
    )(routes_t, x0, returned)

    grad_hidden = raw_rest(rows1, w, raw, slot_gates)
    grad_weight = finish(widths[0], own1[0], got1[0], grad_weight)
    return grad_weight[None], grad_hidden.T[None, None], grad_gates.T


def shards(grad_out, gates, routes, hidden, down_weight):
    owners = lax.axis_size("expert")
    token_count, chosen = routes.shape
    width = grad_out.shape[1]
    slots = hidden.shape[2]
    capacity = slots // owners
    flat = routes.reshape(-1)
    onehot = (flat[:, None] == jnp.arange(owners, dtype=jnp.int32)[None, :]).astype(jnp.int32)
    before = jnp.cumsum(onehot, axis=0) - onehot
    slot = jnp.sum(before * onehot, axis=1)
    target = flat * capacity + slot
    send_rows = (
        jnp.zeros((owners * capacity, width), grad_out.dtype)
        .at[target]
        .set(jnp.repeat(grad_out, chosen, axis=0))
    )
    send_gate = jnp.zeros((owners * capacity,), gates.dtype).at[target].set(gates.reshape(-1))
    send_rows = send_rows.reshape(owners, capacity, width)
    send_gate = send_gate.reshape(owners, capacity)
    saved = hidden[0, 0]
    local_weight = down_weight[0]
    contract = (((1,), (1,)), ((), ()))
    rows, gate_slots = (
        lax.all_to_all(send_rows, "expert", split_axis=0, concat_axis=0, tiled=True),
        lax.all_to_all(send_gate, "expert", split_axis=0, concat_axis=0, tiled=True),
    )
    rows = rows.reshape(slots, width)
    whole_weight = lax.all_gather(local_weight, "dp", axis=0, tiled=True)
    raw = lax.dot_general(rows, whole_weight, contract, preferred_element_type=jnp.float32)
    factor = gate_slots.reshape(slots, 1).astype(jnp.float32)
    grad_hidden = (factor * raw).astype(jnp.bfloat16)
    slot_grads = jnp.sum(raw * saved.astype(jnp.float32), axis=1)
    returned = lax.all_to_all(
        slot_grads.reshape(owners, capacity), "expert", split_axis=0, concat_axis=0, tiled=True
    )
    grad_gates = returned.reshape(-1)[target].reshape(token_count, chosen)
    scaled = (factor * rows.astype(jnp.float32)).astype(jnp.bfloat16)
    summed = lax.psum_scatter(
        lax.dot_general(
            saved, scaled, (((0,), (0,)), ((), ())), preferred_element_type=jnp.float32
        ).astype(jnp.bfloat16),
        "dp",
        scatter_dimension=0,
        tiled=True,
    )
    return (summed[None], grad_hidden[None, None], grad_gates)


def solution(mesh):
    small = mesh.shape["dp"] == 2 and mesh.shape["expert"] == NZ * NY * NC
    return jax.shard_map(
        ring_shards if small else shards,
        mesh=mesh,
        in_specs=(
            P(("dp", "expert"), None),
            P(("dp", "expert"), None),
            P(("dp", "expert"), None),
            P("dp", "expert", None, None),
            P("expert", "dp", None),
        ),
        out_specs=(
            P("expert", "dp", None),
            P("dp", "expert", None, None),
            P(("dp", "expert"), None),
        ),
        check_vma=False,
    )
```

```python
import functools

import jax
import jax.numpy as jnp
from jax import lax
from jax.experimental import pallas as pl
from jax.experimental.pallas import tpu as pltpu
from jax.sharding import PartitionSpec as P

NZ, NY, NC = 4, 2, 2
CHUNKS = (4, 4)
PIECES = (2, 1)
LANES = 128
NT = (((1,), (1,)), ((), ()))
VMEM = pl.BlockSpec(memory_space=pltpu.VMEM)
ANY = pl.BlockSpec(memory_space=pl.ANY)


def params(mib):
    return pltpu.CompilerParams(vmem_limit_bytes=mib * 2**20)


def cost(micros):
    return pl.CostEstimate(
        flops=micros * 10**9, bytes_accessed=micros * 3 * 2**20, transcendentals=0
    )


def ring(z):
    return z ^ (z >> 1)


def ring_pairs(step):
    size = NY * NC
    return [
        (ring(p) * size + rest, ring((p + step) % NZ) * size + rest)
        for p in range(NZ)
        for rest in range(size)
    ]


def swap_pairs(bit):
    return [(i, i ^ bit) for i in range(NZ * NY * NC)]


def pack_kernel(experts, width, routes_hbm, gates_hbm, grad_hbm, out_ref, *scratch):
    routes_ref, gates_ref, sems = scratch
    copies = [
        pltpu.make_async_copy(src, dst, sems.at[i])
        for i, (src, dst) in enumerate(
            (
                (routes_hbm, routes_ref),
                (gates_hbm, gates_ref),
                (grad_hbm.at[:, :width], out_ref.at[:, :width]),
            )
        )
    ]
    for copy in copies:
        copy.start()
    copies[0].wait()
    copies[1].wait()
    chosen, tokens = routes_ref.shape
    routes = routes_ref[...]
    gates = gates_ref[...].astype(jnp.float32)
    expert = lax.broadcasted_iota(jnp.int32, (experts, tokens), 0)
    dense = jnp.zeros((experts, tokens), jnp.float32)
    named = jnp.zeros((experts, tokens), jnp.float32)
    for k in range(chosen):
        hit = routes[k : k + 1, :] == expert
        dense = jnp.where(hit, gates[k : k + 1, :], dense)
        named = jnp.where(hit, 1.0, named)
    earlier = (
        lax.broadcasted_iota(jnp.int32, (tokens, tokens), 0)
        < lax.broadcasted_iota(jnp.int32, (tokens, tokens), 1)
    )
    slots = jnp.dot(
        named.astype(jnp.bfloat16),
        jnp.where(earlier, 1.0, 0.0).astype(jnp.bfloat16),
        preferred_element_type=jnp.float32,
    )
    slots = jnp.where(named > 0, slots, -1.0)
    out_ref[:, width:] = jnp.zeros((tokens, tokens), jnp.bfloat16)
    out_ref[:experts, width:] = dense.astype(jnp.bfloat16)
    out_ref[experts : 2 * experts, width:] = slots.astype(jnp.bfloat16)
    copies[2].wait()


def later_pack_kernel(low, grad_hbm, after_ref, out_ref, sem):
    del after_ref
    copy = pltpu.make_async_copy(grad_hbm.at[:, pl.ds(low, out_ref.shape[1])], out_ref, sem)
    copy.start()
    copy.wait()


def pair_place(arrival):
    index = lax.axis_index("expert")
    z, y = index >> 2, (index >> 1) & 1
    z = ring((ring(z) - arrival // NY) & (NZ - 1))
    return z * NY + (y ^ (arrival % NY))


def pick(xs, pmat_ref, mine_ref, theirs_ref):
    capacity = mine_ref.shape[0] // len(xs)

    @pl.loop(0, mine_ref.shape[1] // 256)
    def _(n):
        cols = pl.ds(pl.multiple_of(n * 256, 256), 256)
        for a, x_ref in enumerate(xs):
            rows = jnp.dot(
                pmat_ref[a * 2 * capacity : (a + 1) * 2 * capacity, :],
                x_ref[:, cols],
                preferred_element_type=jnp.float32,
            ).astype(jnp.bfloat16)
            where = pl.ds(pl.multiple_of(pair_place(a) * capacity, capacity), capacity)
            mine_ref[where, cols] = rows[:capacity]
            theirs_ref[where, cols] = rows[capacity:]


def first_pick_kernel(experts, capacity, *refs):
    pairs = experts // 2
    xs = refs[:pairs]
    mine_ref, theirs_ref, pmat_ref, gslot_ref, other_ref = refs[pairs:]
    width = mine_ref.shape[1]
    me = lax.axis_index("expert")
    core = me & 1
    tokens = xs[0].shape[0]
    expert = lax.broadcasted_iota(jnp.int32, (experts, tokens), 0)
    slot = lax.broadcasted_iota(jnp.int32, (2 * capacity, tokens), 0).astype(jnp.float32)
    offset = (core * capacity).astype(jnp.float32)
    other_ref[...] = jnp.zeros(other_ref.shape, jnp.float32)
    for a, x_ref in enumerate(xs):
        place = pl.ds(pair_place(a), 1)
        ext = x_ref[: 2 * experts, width:].astype(jnp.float32)
        one_hot = jnp.zeros(slot.shape, jnp.float32)
        for s, (who, to_ref) in enumerate(((me, gslot_ref), (me ^ 1, other_ref))):
            gate = jnp.sum(jnp.where(expert == who, ext[:experts], 0.0), axis=0, keepdims=True)
            number = jnp.sum(jnp.where(expert == who, ext[experts:], 0.0), axis=0, keepdims=True)
            routed = number >= 0
            spot = jnp.where(routed, number + s * capacity, -1.0)
            one_hot = jnp.where(slot == spot, 1.0, one_hot)
            spot = jnp.where(routed, number + offset, -1.0)
            by_slot = lax.dot_general(
                jnp.broadcast_to(gate.astype(jnp.bfloat16), (16, tokens)),
                jnp.where(slot == spot, 1.0, 0.0).astype(jnp.bfloat16),
                NT,
                preferred_element_type=jnp.float32,
            )
            to_ref[place, :] = by_slot[:1]
        pmat_ref[a * 2 * capacity : (a + 1) * 2 * capacity, :] = one_hot.astype(jnp.bfloat16)
    theirs_ref[pairs * capacity :, :] = jnp.zeros((16, width), jnp.bfloat16)
    theirs_ref[pairs * capacity :, : 2 * capacity] = other_ref[...].astype(jnp.bfloat16)
    pick(xs, pmat_ref, mine_ref, theirs_ref)


def pick_kernel(*refs):
    pick(refs[:-3], *refs[-3:])


def products(half, capacity, mine_ref, got_ref, hs_ref, rows_ref, *outs):
    mine = lax.axis_index("dp")
    core = lax.axis_index("expert") & 1
    pairs = mine_ref.shape[0] // capacity
    pieces = len(outs) // 2
    piece = mine_ref.shape[1] // pieces
    for q in range(pieces):

        @pl.loop(0, piece // 256)
        def _(n, q=q):
            cols = pl.ds(pl.multiple_of(q * piece + n * 256, 256), 256)
            out = pl.ds(pl.multiple_of(n * 256, 256), 256)
            for p in range(pairs):
                for c, ref in ((core, mine_ref), (1 - core, got_ref)):
                    to = pl.ds(pl.multiple_of((2 * p + c) * capacity, capacity), capacity)
                    rows_ref[to, cols] = ref[p * capacity : (p + 1) * capacity, cols]
            block = rows_ref[:, cols]
            for d, ref in ((1 - mine, outs[q]), (mine, outs[pieces + q])):
                units = pl.ds(pl.multiple_of(d * half, 16), half)
                ref[:, out] = jnp.dot(
                    hs_ref[units, :], block, preferred_element_type=jnp.float32
                ).astype(jnp.bfloat16)


def first_products_kernel(half, capacity, mine_ref, got_ref, gslot_ref, hidden_ref, *outs):
    gates_ref, hs_ref = outs[:2]
    pairs = mine_ref.shape[0] // capacity
    got = got_ref[pairs * capacity :, : 2 * capacity].astype(jnp.float32)
    by_pair = gslot_ref[...] + got[:pairs]
    for p in range(pairs):
        gates_ref[:, p * 2 * capacity : (p + 1) * 2 * capacity] = by_pair[p : p + 1, :]
    hs_ref[...] = (hidden_ref[...].astype(jnp.float32) * gates_ref[...]).astype(jnp.bfloat16)
    products(half, capacity, mine_ref, got_ref, hs_ref, *outs[2:])


def weight_parts(half, own_ref, got_refs):
    mine = lax.axis_index("dp")
    yield pl.ds(pl.multiple_of(mine * half, 16), half), own_ref
    low = (1 - mine) * half
    for ref in got_refs:
        yield pl.ds(pl.multiple_of(low, 16), ref.shape[0]), ref
        low = low + ref.shape[0]


def raw_parts(half, cols, rows_ref, own_ref, got_refs):
    for units, w_ref in weight_parts(half, own_ref, got_refs):
        yield units, lax.dot_general(
            w_ref[:, cols], rows_ref[...], NT, preferred_element_type=jnp.float32
        )


def raw_part_kernel(half, capacity, cols, rows_ref, own_ref, *refs):
    *got_refs, hidden_ref, raw_ref, back_ref = refs
    total = jnp.zeros((1, rows_ref.shape[0]), jnp.float32)
    for units, raw in raw_parts(half, cols, rows_ref, own_ref, got_refs):
        raw_ref[units, :] = raw
        total += jnp.sum(
            raw * hidden_ref[units, :].astype(jnp.float32), axis=0, keepdims=True
        )
    blocks = total.shape[1] // capacity
    for i in range(blocks):
        to = pl.ds(pl.program_id(0) * blocks + i, 1)
        back_ref[to, :] = total[:, i * capacity : (i + 1) * capacity]


def raw_kernel(half, cols, rows_ref, own_ref, *refs):
    *got_refs, sum_ref, gates_ref, grad_ref = refs
    for units, raw in raw_parts(half, cols, rows_ref, own_ref, got_refs):
        grad_ref[units, :] = ((raw + sum_ref[units, :]) * gates_ref[...]).astype(jnp.bfloat16)


def forward_kernel(half, cols, own_ref, *refs):
    *got_refs, hidden_ref, out_ref = refs
    out_ref[...] = sum(
        lax.dot_general(
            hidden_ref[units, :],
            w_ref[:, cols],
            (((0,), (0,)), ((), ())),
            preferred_element_type=jnp.float32,
        )
        for units, w_ref in weight_parts(half, own_ref, got_refs)
    ).astype(out_ref.dtype)


def slot_grads_kernel(rows_ref, forward_ref, part_ref, back_ref):
    capacity = back_ref.shape[1]
    pair = 2 * capacity
    for p in range(rows_ref.shape[0] // pair):
        at = slice(p * pair, (p + 1) * pair)
        some = jnp.zeros((pair, LANES), jnp.float32)
        for n in range(0, rows_ref.shape[1], LANES):
            cols = slice(n, n + LANES)
            some += rows_ref[at, cols].astype(jnp.float32) * forward_ref[at, cols].astype(
                jnp.float32
            )
        total = jnp.sum(some.T, axis=0, keepdims=True)
        for i in range(2):
            to = slice(2 * p + i, 2 * p + i + 1)
            back_ref[to, :] = part_ref[to, :] + total[:, i * capacity : (i + 1) * capacity]


def gates_kernel(routes_ref, slots_ref, back_ref, out_ref):
    back = back_ref[...]
    routes = routes_ref[...]
    experts, capacity = back.shape
    tokens = routes.shape[1]
    slots = slots_ref[experts : 2 * experts, :].astype(jnp.float32)
    expert = lax.broadcasted_iota(jnp.int32, (experts, tokens), 0)
    slot = lax.broadcasted_iota(jnp.int32, (capacity, tokens), 0).astype(jnp.float32)
    for k in range(out_ref.shape[0]):
        hit = expert == routes[k : k + 1, :]
        number = jnp.sum(jnp.where(hit, slots, 0.0), axis=0, keepdims=True)
        by_expert = jnp.dot(
            back,
            jnp.where(slot == number, 1.0, 0.0),
            preferred_element_type=jnp.float32,
            precision=lax.Precision.HIGHEST,
        )
        out_ref[k : k + 1, :] = jnp.sum(jnp.where(hit, by_expert, 0.0), axis=0, keepdims=True)


def finish_kernel(own_ref, got_ref, *refs):
    refs[-1][...] = (
        own_ref[...].astype(jnp.float32) + got_ref[...].astype(jnp.float32)
    ).astype(jnp.bfloat16)


def ring_shards(grad_out, gates, routes, hidden, down_weight):
    experts = lax.axis_size("expert")
    tokens, chosen = routes.shape
    model = grad_out.shape[1]
    slots, units = hidden.shape[2:]
    half = down_weight.shape[1]
    capacity = slots // experts
    widths = [model // 8 * n for n in CHUNKS]
    columns = [slice(0, widths[0]), slice(widths[0], model)]
    tile = 256
    bf16, f32 = jnp.bfloat16, jnp.float32
    shape = jax.ShapeDtypeStruct
    hidden_t = hidden[0, 0].T
    routes_t, gates_t = routes.T, gates.T
    weight = down_weight[0]
    weight_specs = [pl.BlockSpec((half, model), lambda i: (0, 0))] * 2
    dma = pltpu.SemaphoreType.DMA

    def forward(x):
        return lax.ppermute(x, "expert", ring_pairs(1))

    def backward(x):
        return lax.ppermute(x, "expert", ring_pairs(-1))

    def across(x):
        return lax.ppermute(x, "expert", swap_pairs(2))

    def sibling(x):
        return lax.ppermute(x, "expert", swap_pairs(1))

    def swap(x):
        return lax.ppermute(x, "dp", [(0, 1), (1, 0)])

    def behind(x, *others):
        return lax.optimization_barrier((x, *others))[0]

    def pack():
        return pl.pallas_call(
            functools.partial(pack_kernel, experts, widths[0]),
            out_shape=shape((tokens, widths[0] + tokens), bf16),
            in_specs=[ANY] * 3,
            out_specs=VMEM,
            scratch_shapes=[
                pltpu.VMEM(routes_t.shape, routes_t.dtype),
                pltpu.VMEM(gates_t.shape, gates_t.dtype),
                dma((3,)),
            ],
            compiler_params=params(48),
            name="pack",
        )(routes_t, gates_t, grad_out)

    def later_pack(after):
        return pl.pallas_call(
            functools.partial(later_pack_kernel, widths[0]),
            out_shape=shape((tokens, widths[1]), bf16),
            in_specs=[ANY] * 2,
            out_specs=VMEM,
            scratch_shapes=[dma],
            compiler_params=params(48),
            name="later_pack",
        )(grad_out, after)

    def first_pick(blocks):
        return pl.pallas_call(
            functools.partial(first_pick_kernel, experts, capacity),
            out_shape=[
                shape((slots // 2, widths[0]), bf16),
                shape((slots // 2 + 16, widths[0]), bf16),
                shape((slots, tokens), bf16),
                shape((experts // 2, 2 * capacity), f32),
            ],
            in_specs=[VMEM] * len(blocks),
            out_specs=[VMEM] * 4,
            scratch_shapes=[pltpu.VMEM((16, 2 * capacity), f32)],
            compiler_params=params(24),
            cost_estimate=cost(3),
            name="first_pick",
        )(*blocks)

    def later_pick(blocks, pmat):
        return pl.pallas_call(
            pick_kernel,
            out_shape=[shape((slots // 2, widths[1]), bf16)] * 2,
            in_specs=[VMEM] * (len(blocks) + 1),
            out_specs=[VMEM] * 2,
            compiler_params=params(24),
            name="pick",
        )(*blocks, pmat)

    def product_shapes(c):
        piece = shape((half, widths[c] // PIECES[c]), bf16)
        return [shape((slots, widths[c]), bf16)] + [piece] * (2 * PIECES[c])

    def first_products(mine, got, gslot):
        slot_gates, hs, rows, *halves = pl.pallas_call(
            functools.partial(first_products_kernel, half, capacity),
            out_shape=[shape((1, slots), f32), shape((units, slots), bf16)] + product_shapes(0),
            in_specs=[VMEM] * 4,
            out_specs=[VMEM] * (3 + 2 * PIECES[0]),
            compiler_params=params(24),
            cost_estimate=cost(3),
            name="first_products",
        )(mine, got, gslot, hidden_t)
        return rows, halves[: PIECES[0]], halves[PIECES[0] :], slot_gates, hs

    def later_products(mine, got, hs):
        rows, *halves = pl.pallas_call(
            functools.partial(products, half, capacity),
            out_shape=product_shapes(1),
            in_specs=[VMEM] * 3,
            out_specs=[VMEM] * (1 + 2 * PIECES[1]),
            compiler_params=params(24),
            name="products",
        )(mine, got, hs)
        return rows, halves[: PIECES[1]], halves[PIECES[1] :]

    by_slot = pl.BlockSpec((units, tile), lambda i: (0, i))
    by_row = [pl.BlockSpec((tile, n), lambda i: (i, 0)) for n in widths]
    back_shape = shape((experts, capacity), f32)

    def raw_part(rows, got_weight):
        return pl.pallas_call(
            functools.partial(raw_part_kernel, half, capacity, columns[0]),
            grid=(slots // tile,),
            out_shape=[shape((units, slots), f32), back_shape],
            in_specs=[by_row[0], *weight_specs, by_slot],
            out_specs=[by_slot, pl.BlockSpec((experts, capacity), lambda i: (0, 0))],
            compiler_params=params(24),
            cost_estimate=cost(3),
            name="raw_part",
        )(rows, weight, *got_weight, hidden_t)

    def raw_rest(rows, got_weight, raw, slot_gates):
        return pl.pallas_call(
            functools.partial(raw_kernel, half, columns[1]),
            grid=(slots // tile,),
            out_shape=shape((units, slots), bf16),
            in_specs=[
                by_row[1],
                *weight_specs,
                by_slot,
                pl.BlockSpec((1, tile), lambda i: (0, i)),
            ],
            out_specs=by_slot,
            compiler_params=params(60),
            name="raw",
        )(rows, weight, *got_weight, raw, slot_gates)

    def forward_columns(got_weight):
        return pl.pallas_call(
            functools.partial(forward_kernel, half, columns[1]),
            grid=(slots // tile,),
            out_shape=shape((slots, widths[1]), bf16),
            in_specs=[*weight_specs, by_slot],
            out_specs=by_row[1],
            compiler_params=params(24),
            cost_estimate=cost(3),
            name="hidden_weight",
        )(weight, *got_weight, hidden_t)

    def slot_grads(rows, forwarded, part):
        return pl.pallas_call(
            slot_grads_kernel,
            out_shape=back_shape,
            in_specs=[VMEM] * 3,
            out_specs=VMEM,
            compiler_params=params(24),
            name="slot_grads",
        )(rows, forwarded, part)

    def finish(low, own, got, *before):
        piece = own.shape[1]
        spec = pl.BlockSpec((half // 2, piece), lambda i: (i, 0))
        return pl.pallas_call(
            finish_kernel,
            grid=(2,),
            out_shape=shape((half, model), bf16),
            in_specs=[spec, spec] + [ANY] * len(before),
            out_specs=pl.BlockSpec((half // 2, piece), lambda i: (i, low // piece)),
            input_output_aliases={2: 0} if before else {},
            compiler_params=params(8),
            name="finish",
        )(own, got, *before)

    x0 = pack()
    w = [swap(weight)]
    f0, r0, y0 = forward(x0), backward(x0), across(x0)
    x1 = later_pack(f0)
    ff0, yf0 = forward(f0), across(f0)
    y1 = across(behind(x1, y0))
    f1, r1, yr0 = forward(x1), backward(behind(x1, ff0)), across(behind(r0, y0))
    yff0 = across(behind(ff0, yf0, y1))
    mine0, theirs0, pmat, gslot = first_pick(
        [x0, y0, f0, yf0, ff0, yff0, r0, behind(yr0, f1, r1, w[0])]
    )
    ff1, yf1 = forward(f1), across(behind(f1, yr0))
    got = sibling(theirs0)
    rows0, send0, own0, slot_gates, hs = first_products(mine0, got, gslot)
    got0 = [swap(part) for part in send0]
    yff1, ry1 = across(behind(ff1, rows0)), backward(behind(y1, ff1, rows0))
    forwarded = forward_columns(w)
    raw, part = raw_part(rows0, w)
    mine1, theirs1 = later_pick(
        [x1, y1, f1, yf1, ff1, yff1, r1, ry1], behind(pmat, raw, forwarded)
    )
    grad_weight = finish(0, own0[0], got0[0])
    grad_weight = finish(widths[0] // 2, own0[1], got0[1], grad_weight)
    got = sibling(behind(theirs1, *got0))
    rows1, send1, own1 = later_products(mine1, got, behind(hs, grad_weight))
    got1 = [swap(part) for part in send1]

    back = slot_grads(rows1, forwarded, part)
    returned = lax.all_to_all(back, "expert", split_axis=0, concat_axis=0, tiled=True)
    grad_gates = pl.pallas_call(
        gates_kernel,
        grid=(1,),
        out_shape=shape((chosen, tokens), f32),
        in_specs=[
            pl.BlockSpec((chosen, tokens), lambda i: (0, 0)),
            pl.BlockSpec((2 * experts, tokens), lambda i: (0, widths[0] // tokens)),
            pl.BlockSpec((experts, capacity), lambda i: (0, 0)),
        ],
        out_specs=pl.BlockSpec((chosen, tokens), lambda i: (0, 0)),
        name="grad_gates",
    )(routes_t, x0, returned)

    grad_hidden = raw_rest(rows1, w, raw, slot_gates)
    grad_weight = finish(widths[0], own1[0], got1[0], grad_weight)
    return grad_weight[None], grad_hidden.T[None, None], grad_gates.T


def shards(grad_out, gates, routes, hidden, down_weight):
    owners = lax.axis_size("expert")
    token_count, chosen = routes.shape
    width = grad_out.shape[1]
    slots = hidden.shape[2]
    capacity = slots // owners
    flat = routes.reshape(-1)
    onehot = (flat[:, None] == jnp.arange(owners, dtype=jnp.int32)[None, :]).astype(jnp.int32)
    before = jnp.cumsum(onehot, axis=0) - onehot
    slot = jnp.sum(before * onehot, axis=1)
    target = flat * capacity + slot
    send_rows = (
        jnp.zeros((owners * capacity, width), grad_out.dtype)
        .at[target]
        .set(jnp.repeat(grad_out, chosen, axis=0))
    )
    send_gate = jnp.zeros((owners * capacity,), gates.dtype).at[target].set(gates.reshape(-1))
    send_rows = send_rows.reshape(owners, capacity, width)
    send_gate = send_gate.reshape(owners, capacity)
    saved = hidden[0, 0]
    local_weight = down_weight[0]
    contract = (((1,), (1,)), ((), ()))
    rows, gate_slots = (
        lax.all_to_all(send_rows, "expert", split_axis=0, concat_axis=0, tiled=True),
        lax.all_to_all(send_gate, "expert", split_axis=0, concat_axis=0, tiled=True),
    )
    rows = rows.reshape(slots, width)
    whole_weight = lax.all_gather(local_weight, "dp", axis=0, tiled=True)
    raw = lax.dot_general(rows, whole_weight, contract, preferred_element_type=jnp.float32)
    factor = gate_slots.reshape(slots, 1).astype(jnp.float32)
    grad_hidden = (factor * raw).astype(jnp.bfloat16)
    slot_grads = jnp.sum(raw * saved.astype(jnp.float32), axis=1)
    returned = lax.all_to_all(
        slot_grads.reshape(owners, capacity), "expert", split_axis=0, concat_axis=0, tiled=True
    )
    grad_gates = returned.reshape(-1)[target].reshape(token_count, chosen)
    scaled = (factor * rows.astype(jnp.float32)).astype(jnp.bfloat16)
    summed = lax.psum_scatter(
        lax.dot_general(
            saved, scaled, (((0,), (0,)), ((), ())), preferred_element_type=jnp.float32
        ).astype(jnp.bfloat16),
        "dp",
        scatter_dimension=0,
        tiled=True,
    )
    return (summed[None], grad_hidden[None, None], grad_gates)


def solution(mesh):
    small = mesh.shape["dp"] == 2 and mesh.shape["expert"] == NZ * NY * NC
    return jax.shard_map(
        ring_shards if small else shards,
        mesh=mesh,
        in_specs=(
            P(("dp", "expert"), None),
            P(("dp", "expert"), None),
            P(("dp", "expert"), None),
            P("dp", "expert", None, None),
            P("expert", "dp", None),
        ),
        out_specs=(
            P("expert", "dp", None),
            P("dp", "expert", None, None),
            P(("dp", "expert"), None),
        ),
        check_vma=False,
    )
```

```python
import functools

import jax
import jax.numpy as jnp
from jax import lax
from jax.experimental import pallas as pl
from jax.experimental.pallas import tpu as pltpu
from jax.sharding import PartitionSpec as P

NZ, NY, NC = 4, 2, 2
CHUNKS = (4, 4)
PIECES = (2, 1)
LANES = 128
NT = (((1,), (1,)), ((), ()))
VMEM = pl.BlockSpec(memory_space=pltpu.VMEM)
ANY = pl.BlockSpec(memory_space=pl.ANY)


def params(mib):
    return pltpu.CompilerParams(vmem_limit_bytes=mib * 2**20)


def cost(micros):
    return pl.CostEstimate(
        flops=micros * 10**9, bytes_accessed=micros * 3 * 2**20, transcendentals=0
    )


def ring(z):
    return z ^ (z >> 1)


def ring_pairs(step):
    size = NY * NC
    return [
        (ring(p) * size + rest, ring((p + step) % NZ) * size + rest)
        for p in range(NZ)
        for rest in range(size)
    ]


def swap_pairs(bit):
    return [(i, i ^ bit) for i in range(NZ * NY * NC)]


def pack_kernel(experts, width, routes_hbm, gates_hbm, grad_hbm, out_ref, *scratch):
    routes_ref, gates_ref, sems = scratch
    copies = [
        pltpu.make_async_copy(src, dst, sems.at[i])
        for i, (src, dst) in enumerate(
            (
                (routes_hbm, routes_ref),
                (gates_hbm, gates_ref),
                (grad_hbm.at[:, :width], out_ref.at[:, :width]),
            )
        )
    ]
    for copy in copies:
        copy.start()
    copies[0].wait()
    copies[1].wait()
    chosen, tokens = routes_ref.shape
    routes = routes_ref[...]
    gates = gates_ref[...].astype(jnp.float32)
    expert = lax.broadcasted_iota(jnp.int32, (experts, tokens), 0)
    dense = jnp.zeros((experts, tokens), jnp.float32)
    named = jnp.zeros((experts, tokens), jnp.float32)
    for k in range(chosen):
        hit = routes[k : k + 1, :] == expert
        dense = jnp.where(hit, gates[k : k + 1, :], dense)
        named = jnp.where(hit, 1.0, named)
    earlier = (
        lax.broadcasted_iota(jnp.int32, (tokens, tokens), 0)
        < lax.broadcasted_iota(jnp.int32, (tokens, tokens), 1)
    )
    slots = jnp.dot(
        named.astype(jnp.bfloat16),
        jnp.where(earlier, 1.0, 0.0).astype(jnp.bfloat16),
        preferred_element_type=jnp.float32,
    )
    slots = jnp.where(named > 0, slots, -1.0)
    out_ref[:, width:] = jnp.zeros((tokens, tokens), jnp.bfloat16)
    out_ref[:experts, width:] = dense.astype(jnp.bfloat16)
    out_ref[experts : 2 * experts, width:] = slots.astype(jnp.bfloat16)
    copies[2].wait()


def later_pack_kernel(low, grad_hbm, after_ref, out_ref, sem):
    del after_ref
    copy = pltpu.make_async_copy(grad_hbm.at[:, pl.ds(low, out_ref.shape[1])], out_ref, sem)
    copy.start()
    copy.wait()


def pair_place(arrival):
    index = lax.axis_index("expert")
    z, y = index >> 2, (index >> 1) & 1
    z = ring((ring(z) - arrival // NY) & (NZ - 1))
    return z * NY + (y ^ (arrival % NY))


def pick(xs, pmat_ref, mine_ref, theirs_ref):
    capacity = mine_ref.shape[0] // len(xs)

    @pl.loop(0, mine_ref.shape[1] // 256)
    def _(n):
        cols = pl.ds(pl.multiple_of(n * 256, 256), 256)
        for a, x_ref in enumerate(xs):
            rows = jnp.dot(
                pmat_ref[a * 2 * capacity : (a + 1) * 2 * capacity, :],
                x_ref[:, cols],
                preferred_element_type=jnp.float32,
            ).astype(jnp.bfloat16)
            where = pl.ds(pl.multiple_of(pair_place(a) * capacity, capacity), capacity)
            mine_ref[where, cols] = rows[:capacity]
            theirs_ref[where, cols] = rows[capacity:]


def first_pick_kernel(experts, capacity, *refs):
    pairs = experts // 2
    xs = refs[:pairs]
    mine_ref, theirs_ref, pmat_ref, gslot_ref, other_ref = refs[pairs:]
    width = mine_ref.shape[1]
    me = lax.axis_index("expert")
    core = me & 1
    tokens = xs[0].shape[0]
    expert = lax.broadcasted_iota(jnp.int32, (experts, tokens), 0)
    slot = lax.broadcasted_iota(jnp.int32, (2 * capacity, tokens), 0).astype(jnp.float32)
    offset = (core * capacity).astype(jnp.float32)
    other_ref[...] = jnp.zeros(other_ref.shape, jnp.float32)
    for a, x_ref in enumerate(xs):
        place = pl.ds(pair_place(a), 1)
        ext = x_ref[: 2 * experts, width:].astype(jnp.float32)
        one_hot = jnp.zeros(slot.shape, jnp.float32)
        for s, (who, to_ref) in enumerate(((me, gslot_ref), (me ^ 1, other_ref))):
            gate = jnp.sum(jnp.where(expert == who, ext[:experts], 0.0), axis=0, keepdims=True)
            number = jnp.sum(jnp.where(expert == who, ext[experts:], 0.0), axis=0, keepdims=True)
            routed = number >= 0
            spot = jnp.where(routed, number + s * capacity, -1.0)
            one_hot = jnp.where(slot == spot, 1.0, one_hot)
            spot = jnp.where(routed, number + offset, -1.0)
            by_slot = lax.dot_general(
                jnp.broadcast_to(gate.astype(jnp.bfloat16), (16, tokens)),
                jnp.where(slot == spot, 1.0, 0.0).astype(jnp.bfloat16),
                NT,
                preferred_element_type=jnp.float32,
            )
            to_ref[place, :] = by_slot[:1]
        pmat_ref[a * 2 * capacity : (a + 1) * 2 * capacity, :] = one_hot.astype(jnp.bfloat16)
    theirs_ref[pairs * capacity :, :] = jnp.zeros((16, width), jnp.bfloat16)
    theirs_ref[pairs * capacity :, : 2 * capacity] = other_ref[...].astype(jnp.bfloat16)
    pick(xs, pmat_ref, mine_ref, theirs_ref)


def pick_kernel(*refs):
    pick(refs[:-3], *refs[-3:])


def products(half, capacity, mine_ref, got_ref, hs_ref, rows_ref, *outs):
    mine = lax.axis_index("dp")
    core = lax.axis_index("expert") & 1
    pairs = mine_ref.shape[0] // capacity
    pieces = len(outs) // 2
    piece = mine_ref.shape[1] // pieces
    for q in range(pieces):

        @pl.loop(0, piece // 256)
        def _(n, q=q):
            cols = pl.ds(pl.multiple_of(q * piece + n * 256, 256), 256)
            out = pl.ds(pl.multiple_of(n * 256, 256), 256)
            for p in range(pairs):
                for c, ref in ((core, mine_ref), (1 - core, got_ref)):
                    to = pl.ds(pl.multiple_of((2 * p + c) * capacity, capacity), capacity)
                    rows_ref[to, cols] = ref[p * capacity : (p + 1) * capacity, cols]
            block = rows_ref[:, cols]
            for d, ref in ((1 - mine, outs[q]), (mine, outs[pieces + q])):
                units = pl.ds(pl.multiple_of(d * half, 16), half)
                ref[:, out] = jnp.dot(
                    hs_ref[units, :], block, preferred_element_type=jnp.float32
                ).astype(jnp.bfloat16)


def first_products_kernel(half, capacity, mine_ref, got_ref, gslot_ref, hidden_ref, *outs):
    gates_ref, hs_ref = outs[:2]
    pairs = mine_ref.shape[0] // capacity
    got = got_ref[pairs * capacity :, : 2 * capacity].astype(jnp.float32)
    by_pair = gslot_ref[...] + got[:pairs]
    for p in range(pairs):
        gates_ref[:, p * 2 * capacity : (p + 1) * 2 * capacity] = by_pair[p : p + 1, :]
    hs_ref[...] = (hidden_ref[...].astype(jnp.float32) * gates_ref[...]).astype(jnp.bfloat16)
    products(half, capacity, mine_ref, got_ref, hs_ref, *outs[2:])


def weight_parts(half, own_ref, got_refs):
    mine = lax.axis_index("dp")
    yield pl.ds(pl.multiple_of(mine * half, 16), half), own_ref
    low = (1 - mine) * half
    for ref in got_refs:
        yield pl.ds(pl.multiple_of(low, 16), ref.shape[0]), ref
        low = low + ref.shape[0]


def raw_parts(half, cols, rows_ref, own_ref, got_refs):
    for units, w_ref in weight_parts(half, own_ref, got_refs):
        yield units, lax.dot_general(
            w_ref[:, cols], rows_ref[...], NT, preferred_element_type=jnp.float32
        )


def raw_part_kernel(half, capacity, cols, rows_ref, own_ref, *refs):
    *got_refs, hidden_ref, raw_ref, back_ref = refs
    total = jnp.zeros((1, rows_ref.shape[0]), jnp.float32)
    for units, raw in raw_parts(half, cols, rows_ref, own_ref, got_refs):
        raw_ref[units, :] = raw
        total += jnp.sum(
            raw * hidden_ref[units, :].astype(jnp.float32), axis=0, keepdims=True
        )
    blocks = total.shape[1] // capacity
    for i in range(blocks):
        to = pl.ds(pl.program_id(0) * blocks + i, 1)
        back_ref[to, :] = total[:, i * capacity : (i + 1) * capacity]


def raw_kernel(half, cols, rows_ref, own_ref, *refs):
    *got_refs, sum_ref, gates_ref, grad_ref = refs
    for units, raw in raw_parts(half, cols, rows_ref, own_ref, got_refs):
        grad_ref[units, :] = ((raw + sum_ref[units, :]) * gates_ref[...]).astype(jnp.bfloat16)


def forward_kernel(half, cols, own_ref, *refs):
    *got_refs, hidden_ref, out_ref = refs
    out_ref[...] = sum(
        lax.dot_general(
            hidden_ref[units, :],
            w_ref[:, cols],
            (((0,), (0,)), ((), ())),
            preferred_element_type=jnp.float32,
        )
        for units, w_ref in weight_parts(half, own_ref, got_refs)
    ).astype(out_ref.dtype)


def slot_grads_kernel(rows_ref, forward_ref, part_ref, back_ref):
    capacity = back_ref.shape[1]
    pair = 2 * capacity
    for p in range(rows_ref.shape[0] // pair):
        at = slice(p * pair, (p + 1) * pair)
        some = jnp.zeros((pair, LANES), jnp.float32)
        for n in range(0, rows_ref.shape[1], LANES):
            cols = slice(n, n + LANES)
            some += rows_ref[at, cols].astype(jnp.float32) * forward_ref[at, cols].astype(
                jnp.float32
            )
        total = jnp.sum(some.T, axis=0, keepdims=True)
        for i in range(2):
            to = slice(2 * p + i, 2 * p + i + 1)
            back_ref[to, :] = part_ref[to, :] + total[:, i * capacity : (i + 1) * capacity]


def gates_kernel(routes_ref, slots_ref, back_ref, out_ref):
    back = back_ref[...]
    routes = routes_ref[...]
    experts, capacity = back.shape
    tokens = routes.shape[1]
    slots = slots_ref[experts : 2 * experts, :].astype(jnp.float32)
    expert = lax.broadcasted_iota(jnp.int32, (experts, tokens), 0)
    slot = lax.broadcasted_iota(jnp.int32, (capacity, tokens), 0).astype(jnp.float32)
    for k in range(out_ref.shape[0]):
        hit = expert == routes[k : k + 1, :]
        number = jnp.sum(jnp.where(hit, slots, 0.0), axis=0, keepdims=True)
        by_expert = jnp.dot(
            back,
            jnp.where(slot == number, 1.0, 0.0),
            preferred_element_type=jnp.float32,
            precision=lax.Precision.HIGHEST,
        )
        out_ref[k : k + 1, :] = jnp.sum(jnp.where(hit, by_expert, 0.0), axis=0, keepdims=True)


def finish_kernel(own_ref, got_ref, *refs):
    refs[-1][...] = (
        own_ref[...].astype(jnp.float32) + got_ref[...].astype(jnp.float32)
    ).astype(jnp.bfloat16)


def ring_shards(grad_out, gates, routes, hidden, down_weight):
    experts = lax.axis_size("expert")
    tokens, chosen = routes.shape
    model = grad_out.shape[1]
    slots, units = hidden.shape[2:]
    half = down_weight.shape[1]
    capacity = slots // experts
    widths = [model // 8 * n for n in CHUNKS]
    columns = [slice(0, widths[0]), slice(widths[0], model)]
    tile = 256
    bf16, f32 = jnp.bfloat16, jnp.float32
    shape = jax.ShapeDtypeStruct
    hidden_t = hidden[0, 0].T
    routes_t, gates_t = routes.T, gates.T
    weight = down_weight[0]
    weight_specs = [pl.BlockSpec((half, model), lambda i: (0, 0))] * 2
    dma = pltpu.SemaphoreType.DMA

    def forward(x):
        return lax.ppermute(x, "expert", ring_pairs(1))

    def backward(x):
        return lax.ppermute(x, "expert", ring_pairs(-1))

    def across(x):
        return lax.ppermute(x, "expert", swap_pairs(2))

    def sibling(x):
        return lax.ppermute(x, "expert", swap_pairs(1))

    def swap(x):
        return lax.ppermute(x, "dp", [(0, 1), (1, 0)])

    def behind(x, *others):
        return lax.optimization_barrier((x, *others))[0]

    def pack():
        return pl.pallas_call(
            functools.partial(pack_kernel, experts, widths[0]),
            out_shape=shape((tokens, widths[0] + tokens), bf16),
            in_specs=[ANY] * 3,
            out_specs=VMEM,
            scratch_shapes=[
                pltpu.VMEM(routes_t.shape, routes_t.dtype),
                pltpu.VMEM(gates_t.shape, gates_t.dtype),
                dma((3,)),
            ],
            compiler_params=params(48),
            name="pack",
        )(routes_t, gates_t, grad_out)

    def later_pack(after):
        return pl.pallas_call(
            functools.partial(later_pack_kernel, widths[0]),
            out_shape=shape((tokens, widths[1]), bf16),
            in_specs=[ANY] * 2,
            out_specs=VMEM,
            scratch_shapes=[dma],
            compiler_params=params(48),
            name="later_pack",
        )(grad_out, after)

    def first_pick(blocks):
        return pl.pallas_call(
            functools.partial(first_pick_kernel, experts, capacity),
            out_shape=[
                shape((slots // 2, widths[0]), bf16),
                shape((slots // 2 + 16, widths[0]), bf16),
                shape((slots, tokens), bf16),
                shape((experts // 2, 2 * capacity), f32),
            ],
            in_specs=[VMEM] * len(blocks),
            out_specs=[VMEM] * 4,
            scratch_shapes=[pltpu.VMEM((16, 2 * capacity), f32)],
            compiler_params=params(24),
            cost_estimate=cost(3),
            name="first_pick",
        )(*blocks)

    def later_pick(blocks, pmat):
        return pl.pallas_call(
            pick_kernel,
            out_shape=[shape((slots // 2, widths[1]), bf16)] * 2,
            in_specs=[VMEM] * (len(blocks) + 1),
            out_specs=[VMEM] * 2,
            compiler_params=params(24),
            name="pick",
        )(*blocks, pmat)

    def product_shapes(c):
        piece = shape((half, widths[c] // PIECES[c]), bf16)
        return [shape((slots, widths[c]), bf16)] + [piece] * (2 * PIECES[c])

    def first_products(mine, got, gslot):
        slot_gates, hs, rows, *halves = pl.pallas_call(
            functools.partial(first_products_kernel, half, capacity),
            out_shape=[shape((1, slots), f32), shape((units, slots), bf16)] + product_shapes(0),
            in_specs=[VMEM] * 4,
            out_specs=[VMEM] * (3 + 2 * PIECES[0]),
            compiler_params=params(24),
            cost_estimate=cost(3),
            name="first_products",
        )(mine, got, gslot, hidden_t)
        return rows, halves[: PIECES[0]], halves[PIECES[0] :], slot_gates, hs

    def later_products(mine, got, hs):
        rows, *halves = pl.pallas_call(
            functools.partial(products, half, capacity),
            out_shape=product_shapes(1),
            in_specs=[VMEM] * 3,
            out_specs=[VMEM] * (1 + 2 * PIECES[1]),
            compiler_params=params(24),
            name="products",
        )(mine, got, hs)
        return rows, halves[: PIECES[1]], halves[PIECES[1] :]

    by_slot = pl.BlockSpec((units, tile), lambda i: (0, i))
    by_row = [pl.BlockSpec((tile, n), lambda i: (i, 0)) for n in widths]
    back_shape = shape((experts, capacity), f32)

    def raw_part(rows, got_weight):
        return pl.pallas_call(
            functools.partial(raw_part_kernel, half, capacity, columns[0]),
            grid=(slots // tile,),
            out_shape=[shape((units, slots), f32), back_shape],
            in_specs=[by_row[0], *weight_specs, by_slot],
            out_specs=[by_slot, pl.BlockSpec((experts, capacity), lambda i: (0, 0))],
            compiler_params=params(24),
            cost_estimate=cost(3),
            name="raw_part",
        )(rows, weight, *got_weight, hidden_t)

    def raw_rest(rows, got_weight, raw, slot_gates):
        return pl.pallas_call(
            functools.partial(raw_kernel, half, columns[1]),
            grid=(slots // tile,),
            out_shape=shape((units, slots), bf16),
            in_specs=[
                by_row[1],
                *weight_specs,
                by_slot,
                pl.BlockSpec((1, tile), lambda i: (0, i)),
            ],
            out_specs=by_slot,
            compiler_params=params(60),
            name="raw",
        )(rows, weight, *got_weight, raw, slot_gates)

    def forward_columns(got_weight):
        return pl.pallas_call(
            functools.partial(forward_kernel, half, columns[1]),
            grid=(slots // tile,),
            out_shape=shape((slots, widths[1]), bf16),
            in_specs=[*weight_specs, by_slot],
            out_specs=by_row[1],
            compiler_params=params(24),
            cost_estimate=cost(3),
            name="hidden_weight",
        )(weight, *got_weight, hidden_t)

    def slot_grads(rows, forwarded, part):
        return pl.pallas_call(
            slot_grads_kernel,
            out_shape=back_shape,
            in_specs=[VMEM] * 3,
            out_specs=VMEM,
            compiler_params=params(24),
            name="slot_grads",
        )(rows, forwarded, part)

    def finish(low, own, got, *before):
        piece = own.shape[1]
        spec = pl.BlockSpec((half // 2, piece), lambda i: (i, 0))
        return pl.pallas_call(
            finish_kernel,
            grid=(2,),
            out_shape=shape((half, model), bf16),
            in_specs=[spec, spec] + [ANY] * len(before),
            out_specs=pl.BlockSpec((half // 2, piece), lambda i: (i, low // piece)),
            input_output_aliases={2: 0} if before else {},
            compiler_params=params(8),
            name="finish",
        )(own, got, *before)

    x0 = pack()
    w = [swap(weight)]
    f0, r0, y0 = forward(x0), backward(x0), across(x0)
    x1 = later_pack(f0)
    ff0, yf0 = forward(f0), across(f0)
    f1, r1, yr0 = forward(x1), backward(behind(x1, ff0)), across(behind(r0, y0))
    yff0 = across(behind(ff0, yf0))
    mine0, theirs0, pmat, gslot = first_pick(
        [x0, y0, f0, yf0, ff0, yff0, r0, behind(yr0, f1, r1, w[0])]
    )
    ff1, yf1, y1 = forward(f1), across(behind(f1, yr0)), across(behind(x1, yr0))
    got = sibling(theirs0)
    rows0, send0, own0, slot_gates, hs = first_products(mine0, got, gslot)
    got0 = [swap(part) for part in send0]
    yff1, ry1 = across(behind(ff1, rows0)), backward(behind(y1, ff1, rows0))
    forwarded = forward_columns(w)
    raw, part = raw_part(rows0, w)
    mine1, theirs1 = later_pick(
        [x1, y1, f1, yf1, ff1, yff1, r1, ry1], behind(pmat, raw, forwarded)
    )
    grad_weight = finish(0, own0[0], got0[0])
    grad_weight = finish(widths[0] // 2, own0[1], got0[1], grad_weight)
    got = sibling(behind(theirs1, *got0))
    rows1, send1, own1 = later_products(mine1, got, behind(hs, grad_weight))
    got1 = [swap(part) for part in send1]

    back = slot_grads(rows1, forwarded, part)
    returned = lax.all_to_all(back, "expert", split_axis=0, concat_axis=0, tiled=True)
    grad_gates = pl.pallas_call(
        gates_kernel,
        grid=(1,),
        out_shape=shape((chosen, tokens), f32),
        in_specs=[
            pl.BlockSpec((chosen, tokens), lambda i: (0, 0)),
            pl.BlockSpec((2 * experts, tokens), lambda i: (0, widths[0] // tokens)),
            pl.BlockSpec((experts, capacity), lambda i: (0, 0)),
        ],
        out_specs=pl.BlockSpec((chosen, tokens), lambda i: (0, 0)),
        name="grad_gates",
    )(routes_t, x0, returned)

    grad_hidden = raw_rest(rows1, w, raw, slot_gates)
    grad_weight = finish(widths[0], own1[0], got1[0], grad_weight)
    return grad_weight[None], grad_hidden.T[None, None], grad_gates.T


def shards(grad_out, gates, routes, hidden, down_weight):
    owners = lax.axis_size("expert")
    token_count, chosen = routes.shape
    width = grad_out.shape[1]
    slots = hidden.shape[2]
    capacity = slots // owners
    flat = routes.reshape(-1)
    onehot = (flat[:, None] == jnp.arange(owners, dtype=jnp.int32)[None, :]).astype(jnp.int32)
    before = jnp.cumsum(onehot, axis=0) - onehot
    slot = jnp.sum(before * onehot, axis=1)
    target = flat * capacity + slot
    send_rows = (
        jnp.zeros((owners * capacity, width), grad_out.dtype)
        .at[target]
        .set(jnp.repeat(grad_out, chosen, axis=0))
    )
    send_gate = jnp.zeros((owners * capacity,), gates.dtype).at[target].set(gates.reshape(-1))
    send_rows = send_rows.reshape(owners, capacity, width)
    send_gate = send_gate.reshape(owners, capacity)
    saved = hidden[0, 0]
    local_weight = down_weight[0]
    contract = (((1,), (1,)), ((), ()))
    rows, gate_slots = (
        lax.all_to_all(send_rows, "expert", split_axis=0, concat_axis=0, tiled=True),
        lax.all_to_all(send_gate, "expert", split_axis=0, concat_axis=0, tiled=True),
    )
    rows = rows.reshape(slots, width)
    whole_weight = lax.all_gather(local_weight, "dp", axis=0, tiled=True)
    raw = lax.dot_general(rows, whole_weight, contract, preferred_element_type=jnp.float32)
    factor = gate_slots.reshape(slots, 1).astype(jnp.float32)
    grad_hidden = (factor * raw).astype(jnp.bfloat16)
    slot_grads = jnp.sum(raw * saved.astype(jnp.float32), axis=1)
    returned = lax.all_to_all(
        slot_grads.reshape(owners, capacity), "expert", split_axis=0, concat_axis=0, tiled=True
    )
    grad_gates = returned.reshape(-1)[target].reshape(token_count, chosen)
    scaled = (factor * rows.astype(jnp.float32)).astype(jnp.bfloat16)
    summed = lax.psum_scatter(
        lax.dot_general(
            saved, scaled, (((0,), (0,)), ((), ())), preferred_element_type=jnp.float32
        ).astype(jnp.bfloat16),
        "dp",
        scatter_dimension=0,
        tiled=True,
    )
    return (summed[None], grad_hidden[None, None], grad_gates)


def solution(mesh):
    small = mesh.shape["dp"] == 2 and mesh.shape["expert"] == NZ * NY * NC
    return jax.shard_map(
        ring_shards if small else shards,
        mesh=mesh,
        in_specs=(
            P(("dp", "expert"), None),
            P(("dp", "expert"), None),
            P(("dp", "expert"), None),
            P("dp", "expert", None, None),
            P("expert", "dp", None),
        ),
        out_specs=(
            P("expert", "dp", None),
            P("dp", "expert", None, None),
            P(("dp", "expert"), None),
        ),
        check_vma=False,
    )
```

```python
import functools

import jax
import jax.numpy as jnp
from jax import lax
from jax.experimental import pallas as pl
from jax.experimental.pallas import tpu as pltpu
from jax.sharding import PartitionSpec as P

NZ, NY, NC = 4, 2, 2
CHUNKS = (4, 4)
PIECES = (2, 1)
LANES = 128
NT = (((1,), (1,)), ((), ()))
VMEM = pl.BlockSpec(memory_space=pltpu.VMEM)
ANY = pl.BlockSpec(memory_space=pl.ANY)


def params(mib):
    return pltpu.CompilerParams(vmem_limit_bytes=mib * 2**20)


def cost(micros):
    return pl.CostEstimate(
        flops=micros * 10**9, bytes_accessed=micros * 3 * 2**20, transcendentals=0
    )


def ring(z):
    return z ^ (z >> 1)


def ring_pairs(step):
    size = NY * NC
    return [
        (ring(p) * size + rest, ring((p + step) % NZ) * size + rest)
        for p in range(NZ)
        for rest in range(size)
    ]


def swap_pairs(bit):
    return [(i, i ^ bit) for i in range(NZ * NY * NC)]


def pack_kernel(experts, width, routes_hbm, gates_hbm, grad_hbm, out_ref, later_ref, *scratch):
    routes_ref, gates_ref, sems = scratch
    copies = [
        pltpu.make_async_copy(src, dst, sems.at[i])
        for i, (src, dst) in enumerate(
            (
                (routes_hbm, routes_ref),
                (gates_hbm, gates_ref),
                (grad_hbm.at[:, :width], out_ref.at[:, :width]),
                (grad_hbm.at[:, width:], later_ref),
            )
        )
    ]
    for copy in copies:
        copy.start()
    copies[0].wait()
    copies[1].wait()
    chosen, tokens = routes_ref.shape
    routes = routes_ref[...]
    gates = gates_ref[...].astype(jnp.float32)
    expert = lax.broadcasted_iota(jnp.int32, (experts, tokens), 0)
    dense = jnp.zeros((experts, tokens), jnp.float32)
    named = jnp.zeros((experts, tokens), jnp.float32)
    for k in range(chosen):
        hit = routes[k : k + 1, :] == expert
        dense = jnp.where(hit, gates[k : k + 1, :], dense)
        named = jnp.where(hit, 1.0, named)
    earlier = (
        lax.broadcasted_iota(jnp.int32, (tokens, tokens), 0)
        < lax.broadcasted_iota(jnp.int32, (tokens, tokens), 1)
    )
    slots = jnp.dot(
        named.astype(jnp.bfloat16),
        jnp.where(earlier, 1.0, 0.0).astype(jnp.bfloat16),
        preferred_element_type=jnp.float32,
    )
    slots = jnp.where(named > 0, slots, -1.0)
    out_ref[:, width:] = jnp.zeros((tokens, tokens), jnp.bfloat16)
    out_ref[:experts, width:] = dense.astype(jnp.bfloat16)
    out_ref[experts : 2 * experts, width:] = slots.astype(jnp.bfloat16)
    copies[2].wait()
    copies[3].wait()


def pair_place(arrival):
    index = lax.axis_index("expert")
    z, y = index >> 2, (index >> 1) & 1
    z = ring((ring(z) - arrival // NY) & (NZ - 1))
    return z * NY + (y ^ (arrival % NY))


def pick(xs, pmat_ref, mine_ref, theirs_ref):
    capacity = mine_ref.shape[0] // len(xs)

    @pl.loop(0, mine_ref.shape[1] // 256)
    def _(n):
        cols = pl.ds(pl.multiple_of(n * 256, 256), 256)
        for a, x_ref in enumerate(xs):
            rows = jnp.dot(
                pmat_ref[a * 2 * capacity : (a + 1) * 2 * capacity, :],
                x_ref[:, cols],
                preferred_element_type=jnp.float32,
            ).astype(jnp.bfloat16)
            where = pl.ds(pl.multiple_of(pair_place(a) * capacity, capacity), capacity)
            mine_ref[where, cols] = rows[:capacity]
            theirs_ref[where, cols] = rows[capacity:]


def first_pick_kernel(experts, capacity, *refs):
    pairs = experts // 2
    xs = refs[:pairs]
    mine_ref, theirs_ref, pmat_ref, gslot_ref, other_ref = refs[pairs:]
    width = mine_ref.shape[1]
    me = lax.axis_index("expert")
    core = me & 1
    tokens = xs[0].shape[0]
    expert = lax.broadcasted_iota(jnp.int32, (experts, tokens), 0)
    slot = lax.broadcasted_iota(jnp.int32, (2 * capacity, tokens), 0).astype(jnp.float32)
    offset = (core * capacity).astype(jnp.float32)
    other_ref[...] = jnp.zeros(other_ref.shape, jnp.float32)
    for a, x_ref in enumerate(xs):
        place = pl.ds(pair_place(a), 1)
        ext = x_ref[: 2 * experts, width:].astype(jnp.float32)
        one_hot = jnp.zeros(slot.shape, jnp.float32)
        for s, (who, to_ref) in enumerate(((me, gslot_ref), (me ^ 1, other_ref))):
            gate = jnp.sum(jnp.where(expert == who, ext[:experts], 0.0), axis=0, keepdims=True)
            number = jnp.sum(jnp.where(expert == who, ext[experts:], 0.0), axis=0, keepdims=True)
            routed = number >= 0
            spot = jnp.where(routed, number + s * capacity, -1.0)
            one_hot = jnp.where(slot == spot, 1.0, one_hot)
            spot = jnp.where(routed, number + offset, -1.0)
            by_slot = lax.dot_general(
                jnp.broadcast_to(gate.astype(jnp.bfloat16), (16, tokens)),
                jnp.where(slot == spot, 1.0, 0.0).astype(jnp.bfloat16),
                NT,
                preferred_element_type=jnp.float32,
            )
            to_ref[place, :] = by_slot[:1]
        pmat_ref[a * 2 * capacity : (a + 1) * 2 * capacity, :] = one_hot.astype(jnp.bfloat16)
    theirs_ref[pairs * capacity :, :] = jnp.zeros((16, width), jnp.bfloat16)
    theirs_ref[pairs * capacity :, : 2 * capacity] = other_ref[...].astype(jnp.bfloat16)
    pick(xs, pmat_ref, mine_ref, theirs_ref)


def pick_kernel(*refs):
    pick(refs[:-3], *refs[-3:])


def products(half, capacity, mine_ref, got_ref, hs_ref, rows_ref, *outs):
    mine = lax.axis_index("dp")
    core = lax.axis_index("expert") & 1
    pairs = mine_ref.shape[0] // capacity
    pieces = len(outs) // 2
    piece = mine_ref.shape[1] // pieces
    for q in range(pieces):

        @pl.loop(0, piece // 256)
        def _(n, q=q):
            cols = pl.ds(pl.multiple_of(q * piece + n * 256, 256), 256)
            out = pl.ds(pl.multiple_of(n * 256, 256), 256)
            for p in range(pairs):
                for c, ref in ((core, mine_ref), (1 - core, got_ref)):
                    to = pl.ds(pl.multiple_of((2 * p + c) * capacity, capacity), capacity)
                    rows_ref[to, cols] = ref[p * capacity : (p + 1) * capacity, cols]
            block = rows_ref[:, cols]
            for d, ref in ((1 - mine, outs[q]), (mine, outs[pieces + q])):
                units = pl.ds(pl.multiple_of(d * half, 16), half)
                ref[:, out] = jnp.dot(
                    hs_ref[units, :], block, preferred_element_type=jnp.float32
                ).astype(jnp.bfloat16)


def first_products_kernel(half, capacity, mine_ref, got_ref, gslot_ref, hidden_ref, *outs):
    gates_ref, hs_ref = outs[:2]
    pairs = mine_ref.shape[0] // capacity
    got = got_ref[pairs * capacity :, : 2 * capacity].astype(jnp.float32)
    by_pair = gslot_ref[...] + got[:pairs]
    for p in range(pairs):
        gates_ref[:, p * 2 * capacity : (p + 1) * 2 * capacity] = by_pair[p : p + 1, :]
    hs_ref[...] = (hidden_ref[...].astype(jnp.float32) * gates_ref[...]).astype(jnp.bfloat16)
    products(half, capacity, mine_ref, got_ref, hs_ref, *outs[2:])


def weight_parts(half, own_ref, got_refs):
    mine = lax.axis_index("dp")
    yield pl.ds(pl.multiple_of(mine * half, 16), half), own_ref
    low = (1 - mine) * half
    for ref in got_refs:
        yield pl.ds(pl.multiple_of(low, 16), ref.shape[0]), ref
        low = low + ref.shape[0]


def raw_parts(half, cols, rows_ref, own_ref, got_refs):
    for units, w_ref in weight_parts(half, own_ref, got_refs):
        yield units, lax.dot_general(
            w_ref[:, cols], rows_ref[...], NT, preferred_element_type=jnp.float32
        )


def raw_part_kernel(half, capacity, cols, rows_ref, own_ref, *refs):
    *got_refs, hidden_ref, raw_ref, back_ref = refs
    total = jnp.zeros((1, rows_ref.shape[0]), jnp.float32)
    for units, raw in raw_parts(half, cols, rows_ref, own_ref, got_refs):
        raw_ref[units, :] = raw
        total += jnp.sum(
            raw * hidden_ref[units, :].astype(jnp.float32), axis=0, keepdims=True
        )
    blocks = total.shape[1] // capacity
    for i in range(blocks):
        to = pl.ds(pl.program_id(0) * blocks + i, 1)
        back_ref[to, :] = total[:, i * capacity : (i + 1) * capacity]


def raw_kernel(half, cols, rows_ref, own_ref, *refs):
    *got_refs, sum_ref, gates_ref, grad_ref = refs
    for units, raw in raw_parts(half, cols, rows_ref, own_ref, got_refs):
        grad_ref[units, :] = ((raw + sum_ref[units, :]) * gates_ref[...]).astype(jnp.bfloat16)


def forward_kernel(half, cols, own_ref, *refs):
    *got_refs, hidden_ref, out_ref = refs
    out_ref[...] = sum(
        lax.dot_general(
            hidden_ref[units, :],
            w_ref[:, cols],
            (((0,), (0,)), ((), ())),
            preferred_element_type=jnp.float32,
        )
        for units, w_ref in weight_parts(half, own_ref, got_refs)
    ).astype(out_ref.dtype)


def slot_grads_kernel(rows_ref, forward_ref, part_ref, back_ref):
    capacity = back_ref.shape[1]
    pair = 2 * capacity
    for p in range(rows_ref.shape[0] // pair):
        at = slice(p * pair, (p + 1) * pair)
        some = jnp.zeros((pair, LANES), jnp.float32)
        for n in range(0, rows_ref.shape[1], LANES):
            cols = slice(n, n + LANES)
            some += rows_ref[at, cols].astype(jnp.float32) * forward_ref[at, cols].astype(
                jnp.float32
            )
        total = jnp.sum(some.T, axis=0, keepdims=True)
        for i in range(2):
            to = slice(2 * p + i, 2 * p + i + 1)
            back_ref[to, :] = part_ref[to, :] + total[:, i * capacity : (i + 1) * capacity]


def gates_kernel(routes_ref, slots_ref, back_ref, out_ref):
    back = back_ref[...]
    routes = routes_ref[...]
    experts, capacity = back.shape
    tokens = routes.shape[1]
    slots = slots_ref[experts : 2 * experts, :].astype(jnp.float32)
    expert = lax.broadcasted_iota(jnp.int32, (experts, tokens), 0)
    slot = lax.broadcasted_iota(jnp.int32, (capacity, tokens), 0).astype(jnp.float32)
    for k in range(out_ref.shape[0]):
        hit = expert == routes[k : k + 1, :]
        number = jnp.sum(jnp.where(hit, slots, 0.0), axis=0, keepdims=True)
        by_expert = jnp.dot(
            back,
            jnp.where(slot == number, 1.0, 0.0),
            preferred_element_type=jnp.float32,
            precision=lax.Precision.HIGHEST,
        )
        out_ref[k : k + 1, :] = jnp.sum(jnp.where(hit, by_expert, 0.0), axis=0, keepdims=True)


def finish_kernel(own_ref, got_ref, *refs):
    refs[-1][...] = (
        own_ref[...].astype(jnp.float32) + got_ref[...].astype(jnp.float32)
    ).astype(jnp.bfloat16)


def ring_shards(grad_out, gates, routes, hidden, down_weight):
    experts = lax.axis_size("expert")
    tokens, chosen = routes.shape
    model = grad_out.shape[1]
    slots, units = hidden.shape[2:]
    half = down_weight.shape[1]
    capacity = slots // experts
    widths = [model // 8 * n for n in CHUNKS]
    columns = [slice(0, widths[0]), slice(widths[0], model)]
    tile = 256
    bf16, f32 = jnp.bfloat16, jnp.float32
    shape = jax.ShapeDtypeStruct
    hidden_t = hidden[0, 0].T
    routes_t, gates_t = routes.T, gates.T
    weight = down_weight[0]
    weight_specs = [pl.BlockSpec((half, model), lambda i: (0, 0))] * 2
    dma = pltpu.SemaphoreType.DMA

    def forward(x):
        return lax.ppermute(x, "expert", ring_pairs(1))

    def backward(x):
        return lax.ppermute(x, "expert", ring_pairs(-1))

    def across(x):
        return lax.ppermute(x, "expert", swap_pairs(2))

    def sibling(x):
        return lax.ppermute(x, "expert", swap_pairs(1))

    def swap(x):
        return lax.ppermute(x, "dp", [(0, 1), (1, 0)])

    def behind(x, *others):
        return lax.optimization_barrier((x, *others))[0]

    def pack():
        return pl.pallas_call(
            functools.partial(pack_kernel, experts, widths[0]),
            out_shape=[
                shape((tokens, widths[0] + tokens), bf16),
                shape((tokens, widths[1]), bf16),
            ],
            in_specs=[ANY] * 3,
            out_specs=[VMEM] * 2,
            scratch_shapes=[
                pltpu.VMEM(routes_t.shape, routes_t.dtype),
                pltpu.VMEM(gates_t.shape, gates_t.dtype),
                dma((4,)),
            ],
            compiler_params=params(60),
            name="pack",
        )(routes_t, gates_t, grad_out)

    def first_pick(blocks):
        return pl.pallas_call(
            functools.partial(first_pick_kernel, experts, capacity),
            out_shape=[
                shape((slots // 2, widths[0]), bf16),
                shape((slots // 2 + 16, widths[0]), bf16),
                shape((slots, tokens), bf16),
                shape((experts // 2, 2 * capacity), f32),
            ],
            in_specs=[VMEM] * len(blocks),
            out_specs=[VMEM] * 4,
            scratch_shapes=[pltpu.VMEM((16, 2 * capacity), f32)],
            compiler_params=params(24),
            cost_estimate=cost(3),
            name="first_pick",
        )(*blocks)

    def later_pick(blocks, pmat):
        return pl.pallas_call(
            pick_kernel,
            out_shape=[shape((slots // 2, widths[1]), bf16)] * 2,
            in_specs=[VMEM] * (len(blocks) + 1),
            out_specs=[VMEM] * 2,
            compiler_params=params(24),
            name="pick",
        )(*blocks, pmat)

    def product_shapes(c):
        piece = shape((half, widths[c] // PIECES[c]), bf16)
        return [shape((slots, widths[c]), bf16)] + [piece] * (2 * PIECES[c])

    def first_products(mine, got, gslot):
        slot_gates, hs, rows, *halves = pl.pallas_call(
            functools.partial(first_products_kernel, half, capacity),
            out_shape=[shape((1, slots), f32), shape((units, slots), bf16)] + product_shapes(0),
            in_specs=[VMEM] * 4,
            out_specs=[VMEM] * (3 + 2 * PIECES[0]),
            compiler_params=params(24),
            cost_estimate=cost(3),
            name="first_products",
        )(mine, got, gslot, hidden_t)
        return rows, halves[: PIECES[0]], halves[PIECES[0] :], slot_gates, hs

    def later_products(mine, got, hs):
        rows, *halves = pl.pallas_call(
            functools.partial(products, half, capacity),
            out_shape=product_shapes(1),
            in_specs=[VMEM] * 3,
            out_specs=[VMEM] * (1 + 2 * PIECES[1]),
            compiler_params=params(24),
            name="products",
        )(mine, got, hs)
        return rows, halves[: PIECES[1]], halves[PIECES[1] :]

    by_slot = pl.BlockSpec((units, tile), lambda i: (0, i))
    by_row = [pl.BlockSpec((tile, n), lambda i: (i, 0)) for n in widths]
    back_shape = shape((experts, capacity), f32)

    def raw_part(rows, got_weight):
        return pl.pallas_call(
            functools.partial(raw_part_kernel, half, capacity, columns[0]),
            grid=(slots // tile,),
            out_shape=[shape((units, slots), f32), back_shape],
            in_specs=[by_row[0], *weight_specs, by_slot],
            out_specs=[by_slot, pl.BlockSpec((experts, capacity), lambda i: (0, 0))],
            compiler_params=params(24),
            cost_estimate=cost(3),
            name="raw_part",
        )(rows, weight, *got_weight, hidden_t)

    def raw_rest(rows, got_weight, raw, slot_gates):
        return pl.pallas_call(
            functools.partial(raw_kernel, half, columns[1]),
            grid=(slots // tile,),
            out_shape=shape((units, slots), bf16),
            in_specs=[
                by_row[1],
                *weight_specs,
                by_slot,
                pl.BlockSpec((1, tile), lambda i: (0, i)),
            ],
            out_specs=by_slot,
            compiler_params=params(60),
            name="raw",
        )(rows, weight, *got_weight, raw, slot_gates)

    def forward_columns(got_weight):
        return pl.pallas_call(
            functools.partial(forward_kernel, half, columns[1]),
            grid=(slots // tile,),
            out_shape=shape((slots, widths[1]), bf16),
            in_specs=[*weight_specs, by_slot],
            out_specs=by_row[1],
            compiler_params=params(24),
            cost_estimate=cost(3),
            name="hidden_weight",
        )(weight, *got_weight, hidden_t)

    def slot_grads(rows, forwarded, part):
        return pl.pallas_call(
            slot_grads_kernel,
            out_shape=back_shape,
            in_specs=[VMEM] * 3,
            out_specs=VMEM,
            compiler_params=params(24),
            name="slot_grads",
        )(rows, forwarded, part)

    def finish(low, own, got, *before):
        piece = own.shape[1]
        spec = pl.BlockSpec((half // 2, piece), lambda i: (i, 0))
        return pl.pallas_call(
            finish_kernel,
            grid=(2,),
            out_shape=shape((half, model), bf16),
            in_specs=[spec, spec] + [ANY] * len(before),
            out_specs=pl.BlockSpec((half // 2, piece), lambda i: (i, low // piece)),
            input_output_aliases={2: 0} if before else {},
            compiler_params=params(8),
            name="finish",
        )(own, got, *before)

    x0, x1 = pack()
    w = [swap(weight)]
    f0, y0 = forward(x0), across(x0)
    ff0, yf0 = forward(behind(f0, y0)), across(behind(f0, y0))
    r0 = backward(behind(x0, ff0, yf0))
    yff0 = across(behind(ff0, yf0))
    f1, yr0 = forward(behind(x1, r0)), across(behind(r0, yff0))
    r1 = backward(behind(x1, r0))
    mine0, theirs0, pmat, gslot = first_pick(
        [x0, y0, f0, yf0, ff0, yff0, r0, behind(yr0, w[0])]
    )
    ff1, yf1, y1 = forward(f1), across(behind(f1, yr0)), across(behind(x1, yr0))
    got = sibling(behind(theirs0, f1, r1))
    rows0, send0, own0, slot_gates, hs = first_products(mine0, got, gslot)
    got0 = [swap(part) for part in send0]
    yff1, ry1 = across(behind(ff1, rows0)), backward(behind(y1, ff1, rows0))
    forwarded = forward_columns(w)
    raw, part = raw_part(rows0, w)
    mine1, theirs1 = later_pick(
        [x1, y1, f1, yf1, ff1, yff1, r1, ry1], behind(pmat, raw, forwarded)
    )
    grad_weight = finish(0, own0[0], got0[0])
    grad_weight = finish(widths[0] // 2, own0[1], got0[1], grad_weight)
    got = sibling(behind(theirs1, *got0))
    rows1, send1, own1 = later_products(mine1, got, behind(hs, grad_weight))
    got1 = [swap(part) for part in send1]

    back = slot_grads(rows1, forwarded, part)
    returned = lax.all_to_all(back, "expert", split_axis=0, concat_axis=0, tiled=True)
    grad_gates = pl.pallas_call(
        gates_kernel,
        grid=(1,),
        out_shape=shape((chosen, tokens), f32),
        in_specs=[
            pl.BlockSpec((chosen, tokens), lambda i: (0, 0)),
            pl.BlockSpec((2 * experts, tokens), lambda i: (0, widths[0] // tokens)),
            pl.BlockSpec((experts, capacity), lambda i: (0, 0)),
        ],
        out_specs=pl.BlockSpec((chosen, tokens), lambda i: (0, 0)),
        name="grad_gates",
    )(routes_t, x0, returned)

    grad_hidden = raw_rest(rows1, w, raw, slot_gates)
    grad_weight = finish(widths[0], own1[0], got1[0], grad_weight)
    return grad_weight[None], grad_hidden.T[None, None], grad_gates.T


def shards(grad_out, gates, routes, hidden, down_weight):
    owners = lax.axis_size("expert")
    token_count, chosen = routes.shape
    width = grad_out.shape[1]
    slots = hidden.shape[2]
    capacity = slots // owners
    flat = routes.reshape(-1)
    onehot = (flat[:, None] == jnp.arange(owners, dtype=jnp.int32)[None, :]).astype(jnp.int32)
    before = jnp.cumsum(onehot, axis=0) - onehot
    slot = jnp.sum(before * onehot, axis=1)
    target = flat * capacity + slot
    send_rows = (
        jnp.zeros((owners * capacity, width), grad_out.dtype)
        .at[target]
        .set(jnp.repeat(grad_out, chosen, axis=0))
    )
    send_gate = jnp.zeros((owners * capacity,), gates.dtype).at[target].set(gates.reshape(-1))
    send_rows = send_rows.reshape(owners, capacity, width)
    send_gate = send_gate.reshape(owners, capacity)
    saved = hidden[0, 0]
    local_weight = down_weight[0]
    contract = (((1,), (1,)), ((), ()))
    rows, gate_slots = (
        lax.all_to_all(send_rows, "expert", split_axis=0, concat_axis=0, tiled=True),
        lax.all_to_all(send_gate, "expert", split_axis=0, concat_axis=0, tiled=True),
    )
    rows = rows.reshape(slots, width)
    whole_weight = lax.all_gather(local_weight, "dp", axis=0, tiled=True)
    raw = lax.dot_general(rows, whole_weight, contract, preferred_element_type=jnp.float32)
    factor = gate_slots.reshape(slots, 1).astype(jnp.float32)
    grad_hidden = (factor * raw).astype(jnp.bfloat16)
    slot_grads = jnp.sum(raw * saved.astype(jnp.float32), axis=1)
    returned = lax.all_to_all(
        slot_grads.reshape(owners, capacity), "expert", split_axis=0, concat_axis=0, tiled=True
    )
    grad_gates = returned.reshape(-1)[target].reshape(token_count, chosen)
    scaled = (factor * rows.astype(jnp.float32)).astype(jnp.bfloat16)
    summed = lax.psum_scatter(
        lax.dot_general(
            saved, scaled, (((0,), (0,)), ((), ())), preferred_element_type=jnp.float32
        ).astype(jnp.bfloat16),
        "dp",
        scatter_dimension=0,
        tiled=True,
    )
    return (summed[None], grad_hidden[None, None], grad_gates)


def solution(mesh):
    small = mesh.shape["dp"] == 2 and mesh.shape["expert"] == NZ * NY * NC
    return jax.shard_map(
        ring_shards if small else shards,
        mesh=mesh,
        in_specs=(
            P(("dp", "expert"), None),
            P(("dp", "expert"), None),
            P(("dp", "expert"), None),
            P("dp", "expert", None, None),
            P("expert", "dp", None),
        ),
        out_specs=(
            P("expert", "dp", None),
            P("dp", "expert", None, None),
            P(("dp", "expert"), None),
        ),
        check_vma=False,
    )
```

```python
import functools

import jax
import jax.numpy as jnp
from jax import lax
from jax.experimental import pallas as pl
from jax.experimental.pallas import tpu as pltpu
from jax.sharding import PartitionSpec as P

NZ, NY, NC = 4, 2, 2
CHUNKS = (4, 4)
PIECES = (2, 1)
LANES = 128
NT = (((1,), (1,)), ((), ()))
VMEM = pl.BlockSpec(memory_space=pltpu.VMEM)
ANY = pl.BlockSpec(memory_space=pl.ANY)


def params(mib):
    return pltpu.CompilerParams(vmem_limit_bytes=mib * 2**20)


def cost(micros):
    return pl.CostEstimate(
        flops=micros * 10**9, bytes_accessed=micros * 3 * 2**20, transcendentals=0
    )


def ring(z):
    return z ^ (z >> 1)


def ring_pairs(step):
    size = NY * NC
    return [
        (ring(p) * size + rest, ring((p + step) % NZ) * size + rest)
        for p in range(NZ)
        for rest in range(size)
    ]


def swap_pairs(bit):
    return [(i, i ^ bit) for i in range(NZ * NY * NC)]


def pack_kernel(experts, width, routes_hbm, gates_hbm, grad_hbm, out_ref, later_ref, *scratch):
    routes_ref, gates_ref, sems = scratch
    copies = [
        pltpu.make_async_copy(src, dst, sems.at[i])
        for i, (src, dst) in enumerate(
            (
                (routes_hbm, routes_ref),
                (gates_hbm, gates_ref),
                (grad_hbm.at[:, :width], out_ref.at[:, :width]),
                (grad_hbm.at[:, width:], later_ref),
            )
        )
    ]
    for copy in copies:
        copy.start()
    copies[0].wait()
    copies[1].wait()
    chosen, tokens = routes_ref.shape
    routes = routes_ref[...]
    gates = gates_ref[...].astype(jnp.float32)
    expert = lax.broadcasted_iota(jnp.int32, (experts, tokens), 0)
    dense = jnp.zeros((experts, tokens), jnp.float32)
    named = jnp.zeros((experts, tokens), jnp.float32)
    for k in range(chosen):
        hit = routes[k : k + 1, :] == expert
        dense = jnp.where(hit, gates[k : k + 1, :], dense)
        named = jnp.where(hit, 1.0, named)
    earlier = (
        lax.broadcasted_iota(jnp.int32, (tokens, tokens), 0)
        < lax.broadcasted_iota(jnp.int32, (tokens, tokens), 1)
    )
    slots = jnp.dot(
        named.astype(jnp.bfloat16),
        jnp.where(earlier, 1.0, 0.0).astype(jnp.bfloat16),
        preferred_element_type=jnp.float32,
    )
    slots = jnp.where(named > 0, slots, -1.0)
    out_ref[:, width:] = jnp.zeros((tokens, tokens), jnp.bfloat16)
    out_ref[:experts, width:] = dense.astype(jnp.bfloat16)
    out_ref[experts : 2 * experts, width:] = slots.astype(jnp.bfloat16)
    copies[2].wait()
    copies[3].wait()


def pair_place(arrival):
    index = lax.axis_index("expert")
    z, y = index >> 2, (index >> 1) & 1
    z = ring((ring(z) - arrival // NY) & (NZ - 1))
    return z * NY + (y ^ (arrival % NY))


def pick(xs, pmat_ref, mine_ref, theirs_ref):
    capacity = mine_ref.shape[0] // len(xs)

    @pl.loop(0, mine_ref.shape[1] // 256)
    def _(n):
        cols = pl.ds(pl.multiple_of(n * 256, 256), 256)
        for a, x_ref in enumerate(xs):
            rows = jnp.dot(
                pmat_ref[a * 2 * capacity : (a + 1) * 2 * capacity, :],
                x_ref[:, cols],
                preferred_element_type=jnp.float32,
            ).astype(jnp.bfloat16)
            where = pl.ds(pl.multiple_of(pair_place(a) * capacity, capacity), capacity)
            mine_ref[where, cols] = rows[:capacity]
            theirs_ref[where, cols] = rows[capacity:]


def first_pick_kernel(experts, capacity, *refs):
    pairs = experts // 2
    xs = refs[:pairs]
    mine_ref, theirs_ref, pmat_ref, gslot_ref, other_ref = refs[pairs:]
    width = mine_ref.shape[1]
    me = lax.axis_index("expert")
    core = me & 1
    tokens = xs[0].shape[0]
    expert = lax.broadcasted_iota(jnp.int32, (experts, tokens), 0)
    slot = lax.broadcasted_iota(jnp.int32, (2 * capacity, tokens), 0).astype(jnp.float32)
    offset = (core * capacity).astype(jnp.float32)
    other_ref[...] = jnp.zeros(other_ref.shape, jnp.float32)
    for a, x_ref in enumerate(xs):
        place = pl.ds(pair_place(a), 1)
        ext = x_ref[: 2 * experts, width:].astype(jnp.float32)
        one_hot = jnp.zeros(slot.shape, jnp.float32)
        for s, (who, to_ref) in enumerate(((me, gslot_ref), (me ^ 1, other_ref))):
            gate = jnp.sum(jnp.where(expert == who, ext[:experts], 0.0), axis=0, keepdims=True)
            number = jnp.sum(jnp.where(expert == who, ext[experts:], 0.0), axis=0, keepdims=True)
            routed = number >= 0
            spot = jnp.where(routed, number + s * capacity, -1.0)
            one_hot = jnp.where(slot == spot, 1.0, one_hot)
            spot = jnp.where(routed, number + offset, -1.0)
            by_slot = lax.dot_general(
                jnp.broadcast_to(gate.astype(jnp.bfloat16), (16, tokens)),
                jnp.where(slot == spot, 1.0, 0.0).astype(jnp.bfloat16),
                NT,
                preferred_element_type=jnp.float32,
            )
            to_ref[place, :] = by_slot[:1]
        pmat_ref[a * 2 * capacity : (a + 1) * 2 * capacity, :] = one_hot.astype(jnp.bfloat16)
    theirs_ref[pairs * capacity :, :] = jnp.zeros((16, width), jnp.bfloat16)
    theirs_ref[pairs * capacity :, : 2 * capacity] = other_ref[...].astype(jnp.bfloat16)
    pick(xs, pmat_ref, mine_ref, theirs_ref)


def pick_kernel(*refs):
    pick(refs[:-3], *refs[-3:])


def products(half, capacity, mine_ref, got_ref, hs_ref, rows_ref, *outs):
    mine = lax.axis_index("dp")
    core = lax.axis_index("expert") & 1
    pairs = mine_ref.shape[0] // capacity
    pieces = len(outs) // 2
    piece = mine_ref.shape[1] // pieces
    for q in range(pieces):

        @pl.loop(0, piece // 256)
        def _(n, q=q):
            cols = pl.ds(pl.multiple_of(q * piece + n * 256, 256), 256)
            out = pl.ds(pl.multiple_of(n * 256, 256), 256)
            for p in range(pairs):
                for c, ref in ((core, mine_ref), (1 - core, got_ref)):
                    to = pl.ds(pl.multiple_of((2 * p + c) * capacity, capacity), capacity)
                    rows_ref[to, cols] = ref[p * capacity : (p + 1) * capacity, cols]
            block = rows_ref[:, cols]
            for d, ref in ((1 - mine, outs[q]), (mine, outs[pieces + q])):
                units = pl.ds(pl.multiple_of(d * half, 16), half)
                ref[:, out] = jnp.dot(
                    hs_ref[units, :], block, preferred_element_type=jnp.float32
                ).astype(jnp.bfloat16)


def first_products_kernel(half, capacity, mine_ref, got_ref, gslot_ref, hidden_ref, *outs):
    gates_ref, hs_ref = outs[:2]
    pairs = mine_ref.shape[0] // capacity
    got = got_ref[pairs * capacity :, : 2 * capacity].astype(jnp.float32)
    by_pair = gslot_ref[...] + got[:pairs]
    for p in range(pairs):
        gates_ref[:, p * 2 * capacity : (p + 1) * 2 * capacity] = by_pair[p : p + 1, :]
    hs_ref[...] = (hidden_ref[...].astype(jnp.float32) * gates_ref[...]).astype(jnp.bfloat16)
    products(half, capacity, mine_ref, got_ref, hs_ref, *outs[2:])


def weight_parts(half, own_ref, got_refs):
    mine = lax.axis_index("dp")
    yield pl.ds(pl.multiple_of(mine * half, 16), half), own_ref
    low = (1 - mine) * half
    for ref in got_refs:
        yield pl.ds(pl.multiple_of(low, 16), ref.shape[0]), ref
        low = low + ref.shape[0]


def raw_parts(half, cols, rows_ref, own_ref, got_refs):
    for units, w_ref in weight_parts(half, own_ref, got_refs):
        yield units, lax.dot_general(
            w_ref[:, cols], rows_ref[...], NT, preferred_element_type=jnp.float32
        )


def raw_part_kernel(half, capacity, cols, rows_ref, own_ref, *refs):
    *got_refs, hidden_ref, raw_ref, back_ref = refs
    total = jnp.zeros((1, rows_ref.shape[0]), jnp.float32)
    for units, raw in raw_parts(half, cols, rows_ref, own_ref, got_refs):
        raw_ref[units, :] = raw
        total += jnp.sum(
            raw * hidden_ref[units, :].astype(jnp.float32), axis=0, keepdims=True
        )
    blocks = total.shape[1] // capacity
    for i in range(blocks):
        to = pl.ds(pl.program_id(0) * blocks + i, 1)
        back_ref[to, :] = total[:, i * capacity : (i + 1) * capacity]


def raw_kernel(half, cols, rows_ref, own_ref, *refs):
    *got_refs, sum_ref, gates_ref, grad_ref = refs
    for units, raw in raw_parts(half, cols, rows_ref, own_ref, got_refs):
        grad_ref[units, :] = ((raw + sum_ref[units, :]) * gates_ref[...]).astype(jnp.bfloat16)


def forward_kernel(half, cols, own_ref, *refs):
    *got_refs, hidden_ref, out_ref = refs
    out_ref[...] = sum(
        lax.dot_general(
            hidden_ref[units, :],
            w_ref[:, cols],
            (((0,), (0,)), ((), ())),
            preferred_element_type=jnp.float32,
        )
        for units, w_ref in weight_parts(half, own_ref, got_refs)
    ).astype(out_ref.dtype)


def slot_grads_kernel(rows_ref, forward_ref, part_ref, back_ref):
    capacity = back_ref.shape[1]
    pair = 2 * capacity
    for p in range(rows_ref.shape[0] // pair):
        at = slice(p * pair, (p + 1) * pair)
        some = jnp.zeros((pair, LANES), jnp.float32)
        for n in range(0, rows_ref.shape[1], LANES):
            cols = slice(n, n + LANES)
            some += rows_ref[at, cols].astype(jnp.float32) * forward_ref[at, cols].astype(
                jnp.float32
            )
        total = jnp.sum(some.T, axis=0, keepdims=True)
        for i in range(2):
            to = slice(2 * p + i, 2 * p + i + 1)
            back_ref[to, :] = part_ref[to, :] + total[:, i * capacity : (i + 1) * capacity]


def gates_kernel(routes_ref, slots_ref, back_ref, out_ref):
    back = back_ref[...]
    routes = routes_ref[...]
    experts, capacity = back.shape
    tokens = routes.shape[1]
    slots = slots_ref[experts : 2 * experts, :].astype(jnp.float32)
    expert = lax.broadcasted_iota(jnp.int32, (experts, tokens), 0)
    slot = lax.broadcasted_iota(jnp.int32, (capacity, tokens), 0).astype(jnp.float32)
    for k in range(out_ref.shape[0]):
        hit = expert == routes[k : k + 1, :]
        number = jnp.sum(jnp.where(hit, slots, 0.0), axis=0, keepdims=True)
        by_expert = jnp.dot(
            back,
            jnp.where(slot == number, 1.0, 0.0),
            preferred_element_type=jnp.float32,
            precision=lax.Precision.HIGHEST,
        )
        out_ref[k : k + 1, :] = jnp.sum(jnp.where(hit, by_expert, 0.0), axis=0, keepdims=True)


def finish_kernel(own_ref, got_ref, *refs):
    refs[-1][...] = (
        own_ref[...].astype(jnp.float32) + got_ref[...].astype(jnp.float32)
    ).astype(jnp.bfloat16)


def ring_shards(grad_out, gates, routes, hidden, down_weight):
    experts = lax.axis_size("expert")
    tokens, chosen = routes.shape
    model = grad_out.shape[1]
    slots, units = hidden.shape[2:]
    half = down_weight.shape[1]
    capacity = slots // experts
    widths = [model // 8 * n for n in CHUNKS]
    columns = [slice(0, widths[0]), slice(widths[0], model)]
    tile = 256
    bf16, f32 = jnp.bfloat16, jnp.float32
    shape = jax.ShapeDtypeStruct
    hidden_t = hidden[0, 0].T
    routes_t, gates_t = routes.T, gates.T
    weight = down_weight[0]
    weight_specs = [pl.BlockSpec((half, model), lambda i: (0, 0))] * 2
    dma = pltpu.SemaphoreType.DMA

    def forward(x):
        return lax.ppermute(x, "expert", ring_pairs(1))

    def backward(x):
        return lax.ppermute(x, "expert", ring_pairs(-1))

    def across(x):
        return lax.ppermute(x, "expert", swap_pairs(2))

    def sibling(x):
        return lax.ppermute(x, "expert", swap_pairs(1))

    def swap(x):
        return lax.ppermute(x, "dp", [(0, 1), (1, 0)])

    def behind(x, *others):
        return lax.optimization_barrier((x, *others))[0]

    def pack():
        return pl.pallas_call(
            functools.partial(pack_kernel, experts, widths[0]),
            out_shape=[
                shape((tokens, widths[0] + tokens), bf16),
                shape((tokens, widths[1]), bf16),
            ],
            in_specs=[ANY] * 3,
            out_specs=[VMEM] * 2,
            scratch_shapes=[
                pltpu.VMEM(routes_t.shape, routes_t.dtype),
                pltpu.VMEM(gates_t.shape, gates_t.dtype),
                dma((4,)),
            ],
            compiler_params=params(60),
            name="pack",
        )(routes_t, gates_t, grad_out)

    def first_pick(blocks):
        return pl.pallas_call(
            functools.partial(first_pick_kernel, experts, capacity),
            out_shape=[
                shape((slots // 2, widths[0]), bf16),
                shape((slots // 2 + 16, widths[0]), bf16),
                shape((slots, tokens), bf16),
                shape((experts // 2, 2 * capacity), f32),
            ],
            in_specs=[VMEM] * len(blocks),
            out_specs=[VMEM] * 4,
            scratch_shapes=[pltpu.VMEM((16, 2 * capacity), f32)],
            compiler_params=params(24),
            cost_estimate=cost(3),
            name="first_pick",
        )(*blocks)

    def later_pick(blocks, pmat):
        return pl.pallas_call(
            pick_kernel,
            out_shape=[shape((slots // 2, widths[1]), bf16)] * 2,
            in_specs=[VMEM] * (len(blocks) + 1),
            out_specs=[VMEM] * 2,
            compiler_params=params(24),
            name="pick",
        )(*blocks, pmat)

    def product_shapes(c):
        piece = shape((half, widths[c] // PIECES[c]), bf16)
        return [shape((slots, widths[c]), bf16)] + [piece] * (2 * PIECES[c])

    def first_products(mine, got, gslot):
        slot_gates, hs, rows, *halves = pl.pallas_call(
            functools.partial(first_products_kernel, half, capacity),
            out_shape=[shape((1, slots), f32), shape((units, slots), bf16)] + product_shapes(0),
            in_specs=[VMEM] * 4,
            out_specs=[VMEM] * (3 + 2 * PIECES[0]),
            compiler_params=params(24),
            cost_estimate=cost(3),
            name="first_products",
        )(mine, got, gslot, hidden_t)
        return rows, halves[: PIECES[0]], halves[PIECES[0] :], slot_gates, hs

    def later_products(mine, got, hs):
        rows, *halves = pl.pallas_call(
            functools.partial(products, half, capacity),
            out_shape=product_shapes(1),
            in_specs=[VMEM] * 3,
            out_specs=[VMEM] * (1 + 2 * PIECES[1]),
            compiler_params=params(24),
            name="products",
        )(mine, got, hs)
        return rows, halves[: PIECES[1]], halves[PIECES[1] :]

    by_slot = pl.BlockSpec((units, tile), lambda i: (0, i))
    by_row = [pl.BlockSpec((tile, n), lambda i: (i, 0)) for n in widths]
    back_shape = shape((experts, capacity), f32)

    def raw_part(rows, got_weight):
        return pl.pallas_call(
            functools.partial(raw_part_kernel, half, capacity, columns[0]),
            grid=(slots // tile,),
            out_shape=[shape((units, slots), f32), back_shape],
            in_specs=[by_row[0], *weight_specs, by_slot],
            out_specs=[by_slot, pl.BlockSpec((experts, capacity), lambda i: (0, 0))],
            compiler_params=params(24),
            cost_estimate=cost(3),
            name="raw_part",
        )(rows, weight, *got_weight, hidden_t)

    def raw_rest(rows, got_weight, raw, slot_gates):
        return pl.pallas_call(
            functools.partial(raw_kernel, half, columns[1]),
            grid=(slots // tile,),
            out_shape=shape((units, slots), bf16),
            in_specs=[
                by_row[1],
                *weight_specs,
                by_slot,
                pl.BlockSpec((1, tile), lambda i: (0, i)),
            ],
            out_specs=by_slot,
            compiler_params=params(60),
            name="raw",
        )(rows, weight, *got_weight, raw, slot_gates)

    def forward_columns(got_weight):
        return pl.pallas_call(
            functools.partial(forward_kernel, half, columns[1]),
            grid=(slots // tile,),
            out_shape=shape((slots, widths[1]), bf16),
            in_specs=[*weight_specs, by_slot],
            out_specs=by_row[1],
            compiler_params=params(24),
            cost_estimate=cost(3),
            name="hidden_weight",
        )(weight, *got_weight, hidden_t)

    def slot_grads(rows, forwarded, part):
        return pl.pallas_call(
            slot_grads_kernel,
            out_shape=back_shape,
            in_specs=[VMEM] * 3,
            out_specs=VMEM,
            compiler_params=params(24),
            name="slot_grads",
        )(rows, forwarded, part)

    def finish(low, own, got, *before):
        piece = own.shape[1]
        spec = pl.BlockSpec((half // 2, piece), lambda i: (i, 0))
        return pl.pallas_call(
            finish_kernel,
            grid=(2,),
            out_shape=shape((half, model), bf16),
            in_specs=[spec, spec] + [ANY] * len(before),
            out_specs=pl.BlockSpec((half // 2, piece), lambda i: (i, low // piece)),
            input_output_aliases={2: 0} if before else {},
            compiler_params=params(8),
            name="finish",
        )(own, got, *before)

    x0, x1 = pack()
    w = [swap(weight)]
    f0, y0 = forward(x0), across(x0)
    ff0, yf0 = forward(behind(f0, y0)), across(behind(f0, y0))
    r0 = backward(behind(x0, ff0, yf0))
    yff0 = across(behind(ff0, yf0))
    f1, yr0 = forward(behind(x1, r0)), across(behind(r0, yff0))
    mine0, theirs0, pmat, gslot = first_pick(
        [x0, y0, f0, yf0, ff0, yff0, r0, behind(yr0, w[0])]
    )
    ff1, yf1, y1 = forward(f1), across(behind(f1, yr0)), across(behind(x1, yr0))
    r1 = backward(behind(x1, yr0))
    got = sibling(behind(theirs0, f1))
    rows0, send0, own0, slot_gates, hs = first_products(mine0, got, gslot)
    got0 = [swap(part) for part in send0]
    done = (r1, yf1, rows0)
    yff1, ry1 = across(behind(ff1, *done)), backward(behind(y1, *done))
    raw, part = raw_part(rows0, w)
    mine1, theirs1 = later_pick(
        [x1, y1, f1, yf1, ff1, yff1, r1, ry1], behind(pmat, raw)
    )
    got = sibling(behind(theirs1, *got0))
    forwarded = forward_columns([behind(w[0], theirs1)])
    rows1, send1, own1 = later_products(mine1, got, behind(hs, forwarded))
    got1 = [swap(part) for part in send1]

    back = slot_grads(rows1, forwarded, part)
    returned = lax.all_to_all(back, "expert", split_axis=0, concat_axis=0, tiled=True)
    grad_gates = pl.pallas_call(
        gates_kernel,
        grid=(1,),
        out_shape=shape((chosen, tokens), f32),
        in_specs=[
            pl.BlockSpec((chosen, tokens), lambda i: (0, 0)),
            pl.BlockSpec((2 * experts, tokens), lambda i: (0, widths[0] // tokens)),
            pl.BlockSpec((experts, capacity), lambda i: (0, 0)),
        ],
        out_specs=pl.BlockSpec((chosen, tokens), lambda i: (0, 0)),
        name="grad_gates",
    )(routes_t, x0, returned)

    grad_hidden = raw_rest(rows1, w, raw, slot_gates)
    grad_weight = finish(0, behind(own0[0], back), got0[0])
    grad_weight = finish(widths[0] // 2, own0[1], got0[1], grad_weight)
    grad_weight = finish(widths[0], own1[0], got1[0], grad_weight)
    return grad_weight[None], grad_hidden.T[None, None], grad_gates.T


def shards(grad_out, gates, routes, hidden, down_weight):
    owners = lax.axis_size("expert")
    token_count, chosen = routes.shape
    width = grad_out.shape[1]
    slots = hidden.shape[2]
    capacity = slots // owners
    flat = routes.reshape(-1)
    onehot = (flat[:, None] == jnp.arange(owners, dtype=jnp.int32)[None, :]).astype(jnp.int32)
    before = jnp.cumsum(onehot, axis=0) - onehot
    slot = jnp.sum(before * onehot, axis=1)
    target = flat * capacity + slot
    send_rows = (
        jnp.zeros((owners * capacity, width), grad_out.dtype)
        .at[target]
        .set(jnp.repeat(grad_out, chosen, axis=0))
    )
    send_gate = jnp.zeros((owners * capacity,), gates.dtype).at[target].set(gates.reshape(-1))
    send_rows = send_rows.reshape(owners, capacity, width)
    send_gate = send_gate.reshape(owners, capacity)
    saved = hidden[0, 0]
    local_weight = down_weight[0]
    contract = (((1,), (1,)), ((), ()))
    rows, gate_slots = (
        lax.all_to_all(send_rows, "expert", split_axis=0, concat_axis=0, tiled=True),
        lax.all_to_all(send_gate, "expert", split_axis=0, concat_axis=0, tiled=True),
    )
    rows = rows.reshape(slots, width)
    whole_weight = lax.all_gather(local_weight, "dp", axis=0, tiled=True)
    raw = lax.dot_general(rows, whole_weight, contract, preferred_element_type=jnp.float32)
    factor = gate_slots.reshape(slots, 1).astype(jnp.float32)
    grad_hidden = (factor * raw).astype(jnp.bfloat16)
    slot_grads = jnp.sum(raw * saved.astype(jnp.float32), axis=1)
    returned = lax.all_to_all(
        slot_grads.reshape(owners, capacity), "expert", split_axis=0, concat_axis=0, tiled=True
    )
    grad_gates = returned.reshape(-1)[target].reshape(token_count, chosen)
    scaled = (factor * rows.astype(jnp.float32)).astype(jnp.bfloat16)
    summed = lax.psum_scatter(
        lax.dot_general(
            saved, scaled, (((0,), (0,)), ((), ())), preferred_element_type=jnp.float32
        ).astype(jnp.bfloat16),
        "dp",
        scatter_dimension=0,
        tiled=True,
    )
    return (summed[None], grad_hidden[None, None], grad_gates)


def solution(mesh):
    small = mesh.shape["dp"] == 2 and mesh.shape["expert"] == NZ * NY * NC
    return jax.shard_map(
        ring_shards if small else shards,
        mesh=mesh,
        in_specs=(
            P(("dp", "expert"), None),
            P(("dp", "expert"), None),
            P(("dp", "expert"), None),
            P("dp", "expert", None, None),
            P("expert", "dp", None),
        ),
        out_specs=(
            P("expert", "dp", None),
            P("dp", "expert", None, None),
            P(("dp", "expert"), None),
        ),
        check_vma=False,
    )
```

```python
import functools

import jax
import jax.numpy as jnp
from jax import lax
from jax.experimental import pallas as pl
from jax.experimental.pallas import tpu as pltpu
from jax.sharding import PartitionSpec as P

NZ, NY, NC = 4, 2, 2
CHUNKS = (4, 4)
PIECES = 2
LANES = 128
NT = (((1,), (1,)), ((), ()))
VMEM = pl.BlockSpec(memory_space=pltpu.VMEM)
ANY = pl.BlockSpec(memory_space=pl.ANY)


def params(mib):
    return pltpu.CompilerParams(vmem_limit_bytes=mib * 2**20)


def cost(micros):
    return pl.CostEstimate(
        flops=micros * 10**9, bytes_accessed=micros * 3 * 2**20, transcendentals=0
    )


def ring(z):
    return z ^ (z >> 1)


def ring_pairs(step):
    size = NY * NC
    return [
        (ring(p) * size + rest, ring((p + step) % NZ) * size + rest)
        for p in range(NZ)
        for rest in range(size)
    ]


def swap_pairs(bit):
    return [(i, i ^ bit) for i in range(NZ * NY * NC)]


def pack_kernel(experts, width, routes_hbm, gates_hbm, grad_hbm, out_ref, later_ref, *scratch):
    routes_ref, gates_ref, sems = scratch
    copies = [
        pltpu.make_async_copy(src, dst, sems.at[i])
        for i, (src, dst) in enumerate(
            (
                (routes_hbm, routes_ref),
                (gates_hbm, gates_ref),
                (grad_hbm.at[:, :width], out_ref.at[:, :width]),
                (grad_hbm.at[:, width:], later_ref),
            )
        )
    ]
    for copy in copies:
        copy.start()
    copies[0].wait()
    copies[1].wait()
    chosen, tokens = routes_ref.shape
    routes = routes_ref[...]
    gates = gates_ref[...].astype(jnp.float32)
    expert = lax.broadcasted_iota(jnp.int32, (experts, tokens), 0)
    dense = jnp.zeros((experts, tokens), jnp.float32)
    named = jnp.zeros((experts, tokens), jnp.float32)
    for k in range(chosen):
        hit = routes[k : k + 1, :] == expert
        dense = jnp.where(hit, gates[k : k + 1, :], dense)
        named = jnp.where(hit, 1.0, named)
    earlier = (
        lax.broadcasted_iota(jnp.int32, (tokens, tokens), 0)
        < lax.broadcasted_iota(jnp.int32, (tokens, tokens), 1)
    )
    slots = jnp.dot(
        named.astype(jnp.bfloat16),
        jnp.where(earlier, 1.0, 0.0).astype(jnp.bfloat16),
        preferred_element_type=jnp.float32,
    )
    slots = jnp.where(named > 0, slots, -1.0)
    out_ref[:, width:] = jnp.zeros((tokens, tokens), jnp.bfloat16)
    out_ref[:experts, width:] = dense.astype(jnp.bfloat16)
    out_ref[experts : 2 * experts, width:] = slots.astype(jnp.bfloat16)
    copies[2].wait()
    copies[3].wait()


def pair_place(arrival):
    index = lax.axis_index("expert")
    z, y = index >> 2, (index >> 1) & 1
    z = ring((ring(z) - arrival // NY) & (NZ - 1))
    return z * NY + (y ^ (arrival % NY))


def pick(low, xs, pmat_ref, mine_ref, theirs_ref):
    capacity = mine_ref.shape[0] // len(xs)

    @pl.loop(0, mine_ref.shape[1] // 256)
    def _(n):
        cols = pl.ds(pl.multiple_of(n * 256, 256), 256)
        x_cols = pl.ds(pl.multiple_of(low + n * 256, 256), 256)
        for a, x_ref in enumerate(xs):
            rows = jnp.dot(
                pmat_ref[a * 2 * capacity : (a + 1) * 2 * capacity, :],
                x_ref[:, x_cols],
                preferred_element_type=jnp.float32,
            ).astype(jnp.bfloat16)
            where = pl.ds(pl.multiple_of(pair_place(a) * capacity, capacity), capacity)
            mine_ref[where, cols] = rows[:capacity]
            theirs_ref[where, cols] = rows[capacity:]


def first_pick_kernel(experts, capacity, *refs):
    pairs = experts // 2
    xs = refs[:pairs]
    mine_ref, theirs_ref, pmat_ref, gslot_ref, other_ref = refs[pairs:]
    width = mine_ref.shape[1]
    me = lax.axis_index("expert")
    core = me & 1
    tokens = xs[0].shape[0]
    expert = lax.broadcasted_iota(jnp.int32, (experts, tokens), 0)
    slot = lax.broadcasted_iota(jnp.int32, (2 * capacity, tokens), 0).astype(jnp.float32)
    offset = (core * capacity).astype(jnp.float32)
    other_ref[...] = jnp.zeros(other_ref.shape, jnp.float32)
    for a, x_ref in enumerate(xs):
        place = pl.ds(pair_place(a), 1)
        ext = x_ref[: 2 * experts, width:].astype(jnp.float32)
        one_hot = jnp.zeros(slot.shape, jnp.float32)
        for s, (who, to_ref) in enumerate(((me, gslot_ref), (me ^ 1, other_ref))):
            gate = jnp.sum(jnp.where(expert == who, ext[:experts], 0.0), axis=0, keepdims=True)
            number = jnp.sum(jnp.where(expert == who, ext[experts:], 0.0), axis=0, keepdims=True)
            routed = number >= 0
            spot = jnp.where(routed, number + s * capacity, -1.0)
            one_hot = jnp.where(slot == spot, 1.0, one_hot)
            spot = jnp.where(routed, number + offset, -1.0)
            by_slot = lax.dot_general(
                jnp.broadcast_to(gate.astype(jnp.bfloat16), (16, tokens)),
                jnp.where(slot == spot, 1.0, 0.0).astype(jnp.bfloat16),
                NT,
                preferred_element_type=jnp.float32,
            )
            to_ref[place, :] = by_slot[:1]
        pmat_ref[a * 2 * capacity : (a + 1) * 2 * capacity, :] = one_hot.astype(jnp.bfloat16)
    theirs_ref[pairs * capacity :, :] = jnp.zeros((16, width), jnp.bfloat16)
    theirs_ref[pairs * capacity :, : 2 * capacity] = other_ref[...].astype(jnp.bfloat16)
    pick(0, xs, pmat_ref, mine_ref, theirs_ref)


def pick_kernel(low, *refs):
    pick(low, refs[:-3], *refs[-3:])


def products(half, capacity, mine_ref, got_ref, hs_ref, rows_ref, *outs):
    mine = lax.axis_index("dp")
    core = lax.axis_index("expert") & 1
    pairs = mine_ref.shape[0] // capacity
    pieces = len(outs) // 2
    piece = mine_ref.shape[1] // pieces
    for q in range(pieces):

        @pl.loop(0, piece // 256)
        def _(n, q=q):
            cols = pl.ds(pl.multiple_of(q * piece + n * 256, 256), 256)
            out = pl.ds(pl.multiple_of(n * 256, 256), 256)
            for p in range(pairs):
                for c, ref in ((core, mine_ref), (1 - core, got_ref)):
                    to = pl.ds(pl.multiple_of((2 * p + c) * capacity, capacity), capacity)
                    rows_ref[to, cols] = ref[p * capacity : (p + 1) * capacity, cols]
            block = rows_ref[:, cols]
            for d, ref in ((1 - mine, outs[q]), (mine, outs[pieces + q])):
                units = pl.ds(pl.multiple_of(d * half, 16), half)
                ref[:, out] = jnp.dot(
                    hs_ref[units, :], block, preferred_element_type=jnp.float32
                ).astype(jnp.bfloat16)


def first_products_kernel(half, capacity, mine_ref, got_ref, gslot_ref, hidden_ref, *outs):
    gates_ref, hs_ref = outs[:2]
    pairs = mine_ref.shape[0] // capacity
    got = got_ref[pairs * capacity :, : 2 * capacity].astype(jnp.float32)
    by_pair = gslot_ref[...] + got[:pairs]
    for p in range(pairs):
        gates_ref[:, p * 2 * capacity : (p + 1) * 2 * capacity] = by_pair[p : p + 1, :]
    hs_ref[...] = (hidden_ref[...].astype(jnp.float32) * gates_ref[...]).astype(jnp.bfloat16)
    products(half, capacity, mine_ref, got_ref, hs_ref, *outs[2:])


def weight_parts(half, own_ref, got_refs):
    mine = lax.axis_index("dp")
    yield pl.ds(pl.multiple_of(mine * half, 16), half), own_ref
    low = (1 - mine) * half
    for ref in got_refs:
        yield pl.ds(pl.multiple_of(low, 16), ref.shape[0]), ref
        low = low + ref.shape[0]


def raw_parts(half, cols, rows_ref, own_ref, got_refs):
    for units, w_ref in weight_parts(half, own_ref, got_refs):
        yield units, lax.dot_general(
            w_ref[:, cols], rows_ref[...], NT, preferred_element_type=jnp.float32
        )


def raw_part_kernel(half, capacity, cols, rows_ref, own_ref, *refs):
    *got_refs, hidden_ref, raw_ref, back_ref = refs
    total = jnp.zeros((1, rows_ref.shape[0]), jnp.float32)
    for units, raw in raw_parts(half, cols, rows_ref, own_ref, got_refs):
        raw_ref[units, :] = raw
        total += jnp.sum(
            raw * hidden_ref[units, :].astype(jnp.float32), axis=0, keepdims=True
        )
    blocks = total.shape[1] // capacity
    for i in range(blocks):
        to = pl.ds(pl.program_id(0) * blocks + i, 1)
        back_ref[to, :] = total[:, i * capacity : (i + 1) * capacity]


def raw_kernel(half, cols, first_ref, second_ref, own_ref, *refs):
    *got_refs, sum_ref, gates_ref, grad_ref = refs
    parts = zip(
        raw_parts(half, cols[0], first_ref, own_ref, got_refs),
        raw_parts(half, cols[1], second_ref, own_ref, got_refs),
    )
    for (units, first), (_, second) in parts:
        raw = first + second + sum_ref[units, :]
        grad_ref[units, :] = (raw * gates_ref[...]).astype(jnp.bfloat16)


def forward_kernel(half, cols, own_ref, *refs):
    *got_refs, hidden_ref, out_ref = refs
    out_ref[...] = sum(
        lax.dot_general(
            hidden_ref[units, :],
            w_ref[:, cols],
            (((0,), (0,)), ((), ())),
            preferred_element_type=jnp.float32,
        )
        for units, w_ref in weight_parts(half, own_ref, got_refs)
    ).astype(out_ref.dtype)


def slot_grads_kernel(first_ref, second_ref, forward_ref, part_ref, back_ref):
    capacity = back_ref.shape[1]
    pair = 2 * capacity
    width = first_ref.shape[1]
    for p in range(first_ref.shape[0] // pair):
        at = slice(p * pair, (p + 1) * pair)
        some = jnp.zeros((pair, LANES), jnp.float32)
        for n in range(0, 2 * width, LANES):
            rows_ref, low = (first_ref, n) if n < width else (second_ref, n - width)
            some += rows_ref[at, low : low + LANES].astype(jnp.float32) * forward_ref[
                at, n : n + LANES
            ].astype(jnp.float32)
        total = jnp.sum(some.T, axis=0, keepdims=True)
        for i in range(2):
            to = slice(2 * p + i, 2 * p + i + 1)
            back_ref[to, :] = part_ref[to, :] + total[:, i * capacity : (i + 1) * capacity]


def gates_kernel(routes_ref, slots_ref, back_ref, out_ref):
    back = back_ref[...]
    routes = routes_ref[...]
    experts, capacity = back.shape
    tokens = routes.shape[1]
    slots = slots_ref[experts : 2 * experts, :].astype(jnp.float32)
    expert = lax.broadcasted_iota(jnp.int32, (experts, tokens), 0)
    slot = lax.broadcasted_iota(jnp.int32, (capacity, tokens), 0).astype(jnp.float32)
    for k in range(out_ref.shape[0]):
        hit = expert == routes[k : k + 1, :]
        number = jnp.sum(jnp.where(hit, slots, 0.0), axis=0, keepdims=True)
        by_expert = jnp.dot(
            back,
            jnp.where(slot == number, 1.0, 0.0),
            preferred_element_type=jnp.float32,
            precision=lax.Precision.HIGHEST,
        )
        out_ref[k : k + 1, :] = jnp.sum(jnp.where(hit, by_expert, 0.0), axis=0, keepdims=True)


def finish_kernel(own_ref, got_ref, *refs):
    refs[-1][...] = (
        own_ref[...].astype(jnp.float32) + got_ref[...].astype(jnp.float32)
    ).astype(jnp.bfloat16)


def ring_shards(grad_out, gates, routes, hidden, down_weight):
    experts = lax.axis_size("expert")
    tokens, chosen = routes.shape
    model = grad_out.shape[1]
    slots, units = hidden.shape[2:]
    half = down_weight.shape[1]
    capacity = slots // experts
    widths = [model // 8 * n for n in CHUNKS]
    columns = [slice(0, widths[0]), slice(widths[0], model)]
    tile = 256
    bf16, f32 = jnp.bfloat16, jnp.float32
    shape = jax.ShapeDtypeStruct
    hidden_t = hidden[0, 0].T
    routes_t, gates_t = routes.T, gates.T
    weight = down_weight[0]
    weight_specs = [pl.BlockSpec((half, model), lambda i: (0, 0))] * 2
    dma = pltpu.SemaphoreType.DMA

    def forward(x):
        return lax.ppermute(x, "expert", ring_pairs(1))

    def backward(x):
        return lax.ppermute(x, "expert", ring_pairs(-1))

    def across(x):
        return lax.ppermute(x, "expert", swap_pairs(2))

    def sibling(x):
        return lax.ppermute(x, "expert", swap_pairs(1))

    def swap(x):
        return lax.ppermute(x, "dp", [(0, 1), (1, 0)])

    def behind(x, *others):
        return lax.optimization_barrier((x, *others))[0]

    def pack():
        return pl.pallas_call(
            functools.partial(pack_kernel, experts, widths[0]),
            out_shape=[
                shape((tokens, widths[0] + tokens), bf16),
                shape((tokens, widths[1]), bf16),
            ],
            in_specs=[ANY] * 3,
            out_specs=[VMEM] * 2,
            scratch_shapes=[
                pltpu.VMEM(routes_t.shape, routes_t.dtype),
                pltpu.VMEM(gates_t.shape, gates_t.dtype),
                dma((4,)),
            ],
            compiler_params=params(60),
            name="pack",
        )(routes_t, gates_t, grad_out)

    def first_pick(blocks):
        return pl.pallas_call(
            functools.partial(first_pick_kernel, experts, capacity),
            out_shape=[
                shape((slots // 2, widths[0]), bf16),
                shape((slots // 2 + 16, widths[0]), bf16),
                shape((slots, tokens), bf16),
                shape((experts // 2, 2 * capacity), f32),
            ],
            in_specs=[VMEM] * len(blocks),
            out_specs=[VMEM] * 4,
            scratch_shapes=[pltpu.VMEM((16, 2 * capacity), f32)],
            compiler_params=params(24),
            cost_estimate=cost(3),
            name="first_pick",
        )(*blocks)

    piece = widths[1] // 2
    halves = [slice(widths[0] + low, widths[0] + low + piece) for low in (0, piece)]

    def later_pick(low, blocks, pmat):
        return pl.pallas_call(
            functools.partial(pick_kernel, low),
            out_shape=[shape((slots // 2, piece), bf16)] * 2,
            in_specs=[VMEM] * (len(blocks) + 1),
            out_specs=[VMEM] * 2,
            compiler_params=params(24),
            name="pick",
        )(*blocks, pmat)

    product_shapes = [shape((slots, widths[0]), bf16)] + [
        shape((half, widths[0] // PIECES), bf16)
    ] * (2 * PIECES)

    def first_products(mine, got, gslot):
        slot_gates, hs, rows, *halves = pl.pallas_call(
            functools.partial(first_products_kernel, half, capacity),
            out_shape=[shape((1, slots), f32), shape((units, slots), bf16)] + product_shapes,
            in_specs=[VMEM] * 4,
            out_specs=[VMEM] * (3 + 2 * PIECES),
            compiler_params=params(24),
            cost_estimate=cost(3),
            name="first_products",
        )(mine, got, gslot, hidden_t)
        return rows, halves[: PIECES], halves[PIECES :], slot_gates, hs

    def later_products(mine, got, hs):
        return pl.pallas_call(
            functools.partial(products, half, capacity),
            out_shape=[shape((slots, piece), bf16)] + [shape((half, piece), bf16)] * 2,
            in_specs=[VMEM] * 3,
            out_specs=[VMEM] * 3,
            compiler_params=params(24),
            name="products",
        )(mine, got, hs)

    by_slot = pl.BlockSpec((units, tile), lambda i: (0, i))
    by_row = [pl.BlockSpec((tile, n), lambda i: (i, 0)) for n in widths]
    back_shape = shape((experts, capacity), f32)

    def raw_part(rows, got_weight):
        return pl.pallas_call(
            functools.partial(raw_part_kernel, half, capacity, columns[0]),
            grid=(slots // tile,),
            out_shape=[shape((units, slots), f32), back_shape],
            in_specs=[by_row[0], *weight_specs, by_slot],
            out_specs=[by_slot, pl.BlockSpec((experts, capacity), lambda i: (0, 0))],
            compiler_params=params(24),
            cost_estimate=cost(3),
            name="raw_part",
        )(rows, weight, *got_weight, hidden_t)

    def raw_rest(rows, got_weight, raw, slot_gates):
        return pl.pallas_call(
            functools.partial(raw_kernel, half, halves),
            grid=(slots // tile,),
            out_shape=shape((units, slots), bf16),
            in_specs=[
                *[pl.BlockSpec((tile, piece), lambda i: (i, 0))] * 2,
                *weight_specs,
                by_slot,
                pl.BlockSpec((1, tile), lambda i: (0, i)),
            ],
            out_specs=by_slot,
            compiler_params=params(60),
            name="raw",
        )(*rows, weight, *got_weight, raw, slot_gates)

    def forward_columns(got_weight):
        return pl.pallas_call(
            functools.partial(forward_kernel, half, columns[1]),
            grid=(slots // tile,),
            out_shape=shape((slots, widths[1]), bf16),
            in_specs=[*weight_specs, by_slot],
            out_specs=by_row[1],
            compiler_params=params(24),
            cost_estimate=cost(3),
            name="hidden_weight",
        )(weight, *got_weight, hidden_t)

    def slot_grads(rows, forwarded, part):
        return pl.pallas_call(
            slot_grads_kernel,
            out_shape=back_shape,
            in_specs=[VMEM] * 4,
            out_specs=VMEM,
            compiler_params=params(24),
            name="slot_grads",
        )(*rows, forwarded, part)

    def finish(low, own, got, *before):
        piece = own.shape[1]
        spec = pl.BlockSpec((half // 2, piece), lambda i: (i, 0))
        return pl.pallas_call(
            finish_kernel,
            grid=(2,),
            out_shape=shape((half, model), bf16),
            in_specs=[spec, spec] + [ANY] * len(before),
            out_specs=pl.BlockSpec((half // 2, piece), lambda i: (i, low // piece)),
            input_output_aliases={2: 0} if before else {},
            compiler_params=params(8),
            name="finish",
        )(own, got, *before)

    x0, x1 = pack()
    w = [swap(weight)]
    f0, y0 = forward(x0), across(x0)
    ff0, yf0 = forward(behind(f0, y0)), across(behind(f0, y0))
    r0 = backward(behind(x0, ff0, yf0))
    yff0 = across(behind(ff0, yf0))
    f1, yr0 = forward(behind(x1, r0)), across(behind(r0, yff0))
    r1 = backward(behind(x1, r0))
    mine0, theirs0, pmat, gslot = first_pick(
        [x0, y0, f0, yf0, ff0, yff0, r0, behind(yr0, w[0])]
    )
    ff1, yf1, y1 = forward(f1), across(behind(f1, yr0)), across(behind(x1, yr0))
    got = sibling(behind(theirs0, f1, r1))
    rows0, send0, own0, slot_gates, hs = first_products(mine0, got, gslot)
    got0 = [swap(part) for part in send0]
    yff1, ry1 = across(behind(ff1, rows0)), backward(behind(y1, ff1, rows0))
    forwarded = forward_columns(w)
    raw, part = raw_part(rows0, w)
    blocks = [x1, y1, f1, yf1, ff1, yff1, r1, ry1]
    rows1, own1, got1 = [], [], []
    for low in (0, piece):
        mine, theirs = later_pick(low, blocks, behind(pmat, raw, forwarded))
        if low > 0:
            theirs = behind(theirs, *got0)
        rows, send, own = later_products(mine, sibling(theirs), hs)
        rows1.append(rows)
        own1.append(own)
        got1.append(swap(send))

    back = slot_grads(rows1, forwarded, part)
    returned = lax.all_to_all(back, "expert", split_axis=0, concat_axis=0, tiled=True)
    grad_gates = pl.pallas_call(
        gates_kernel,
        grid=(1,),
        out_shape=shape((chosen, tokens), f32),
        in_specs=[
            pl.BlockSpec((chosen, tokens), lambda i: (0, 0)),
            pl.BlockSpec((2 * experts, tokens), lambda i: (0, widths[0] // tokens)),
            pl.BlockSpec((experts, capacity), lambda i: (0, 0)),
        ],
        out_specs=pl.BlockSpec((chosen, tokens), lambda i: (0, 0)),
        name="grad_gates",
    )(routes_t, x0, returned)

    grad_hidden = raw_rest(rows1, w, raw, slot_gates)
    grad_weight = finish(0, behind(own0[0], back), got0[0])
    grad_weight = finish(widths[0] // 2, own0[1], got0[1], grad_weight)
    grad_weight = finish(widths[0], own1[0], got1[0], grad_weight)
    grad_weight = finish(widths[0] + piece, own1[1], got1[1], grad_weight)
    return grad_weight[None], grad_hidden.T[None, None], grad_gates.T


def shards(grad_out, gates, routes, hidden, down_weight):
    owners = lax.axis_size("expert")
    token_count, chosen = routes.shape
    width = grad_out.shape[1]
    slots = hidden.shape[2]
    capacity = slots // owners
    flat = routes.reshape(-1)
    onehot = (flat[:, None] == jnp.arange(owners, dtype=jnp.int32)[None, :]).astype(jnp.int32)
    before = jnp.cumsum(onehot, axis=0) - onehot
    slot = jnp.sum(before * onehot, axis=1)
    target = flat * capacity + slot
    send_rows = (
        jnp.zeros((owners * capacity, width), grad_out.dtype)
        .at[target]
        .set(jnp.repeat(grad_out, chosen, axis=0))
    )
    send_gate = jnp.zeros((owners * capacity,), gates.dtype).at[target].set(gates.reshape(-1))
    send_rows = send_rows.reshape(owners, capacity, width)
    send_gate = send_gate.reshape(owners, capacity)
    saved = hidden[0, 0]
    local_weight = down_weight[0]
    contract = (((1,), (1,)), ((), ()))
    rows, gate_slots = (
        lax.all_to_all(send_rows, "expert", split_axis=0, concat_axis=0, tiled=True),
        lax.all_to_all(send_gate, "expert", split_axis=0, concat_axis=0, tiled=True),
    )
    rows = rows.reshape(slots, width)
    whole_weight = lax.all_gather(local_weight, "dp", axis=0, tiled=True)
    raw = lax.dot_general(rows, whole_weight, contract, preferred_element_type=jnp.float32)
    factor = gate_slots.reshape(slots, 1).astype(jnp.float32)
    grad_hidden = (factor * raw).astype(jnp.bfloat16)
    slot_grads = jnp.sum(raw * saved.astype(jnp.float32), axis=1)
    returned = lax.all_to_all(
        slot_grads.reshape(owners, capacity), "expert", split_axis=0, concat_axis=0, tiled=True
    )
    grad_gates = returned.reshape(-1)[target].reshape(token_count, chosen)
    scaled = (factor * rows.astype(jnp.float32)).astype(jnp.bfloat16)
    summed = lax.psum_scatter(
        lax.dot_general(
            saved, scaled, (((0,), (0,)), ((), ())), preferred_element_type=jnp.float32
        ).astype(jnp.bfloat16),
        "dp",
        scatter_dimension=0,
        tiled=True,
    )
    return (summed[None], grad_hidden[None, None], grad_gates)


def solution(mesh):
    small = mesh.shape["dp"] == 2 and mesh.shape["expert"] == NZ * NY * NC
    return jax.shard_map(
        ring_shards if small else shards,
        mesh=mesh,
        in_specs=(
            P(("dp", "expert"), None),
            P(("dp", "expert"), None),
            P(("dp", "expert"), None),
            P("dp", "expert", None, None),
            P("expert", "dp", None),
        ),
        out_specs=(
            P("expert", "dp", None),
            P("dp", "expert", None, None),
            P(("dp", "expert"), None),
        ),
        check_vma=False,
    )
```

```python
import functools

import jax
import jax.numpy as jnp
from jax import lax
from jax.experimental import pallas as pl
from jax.experimental.pallas import tpu as pltpu
from jax.sharding import PartitionSpec as P

NZ, NY, NC = 4, 2, 2
CHUNKS = (4, 4)
PIECES = 2
LANES = 128
NT = (((1,), (1,)), ((), ()))
VMEM = pl.BlockSpec(memory_space=pltpu.VMEM)
ANY = pl.BlockSpec(memory_space=pl.ANY)


def params(mib):
    return pltpu.CompilerParams(vmem_limit_bytes=mib * 2**20)


def cost(micros):
    return pl.CostEstimate(
        flops=micros * 10**9, bytes_accessed=micros * 3 * 2**20, transcendentals=0
    )


def ring(z):
    return z ^ (z >> 1)


def ring_pairs(step):
    size = NY * NC
    return [
        (ring(p) * size + rest, ring((p + step) % NZ) * size + rest)
        for p in range(NZ)
        for rest in range(size)
    ]


def swap_pairs(bit):
    return [(i, i ^ bit) for i in range(NZ * NY * NC)]


def pack_kernel(experts, width, routes_hbm, gates_hbm, grad_hbm, out_ref, later_ref, *scratch):
    routes_ref, gates_ref, sems = scratch
    copies = [
        pltpu.make_async_copy(src, dst, sems.at[i])
        for i, (src, dst) in enumerate(
            (
                (routes_hbm, routes_ref),
                (gates_hbm, gates_ref),
                (grad_hbm.at[:, :width], out_ref.at[:, :width]),
                (grad_hbm.at[:, width:], later_ref),
            )
        )
    ]
    for copy in copies:
        copy.start()
    copies[0].wait()
    copies[1].wait()
    chosen, tokens = routes_ref.shape
    routes = routes_ref[...]
    gates = gates_ref[...].astype(jnp.float32)
    expert = lax.broadcasted_iota(jnp.int32, (experts, tokens), 0)
    dense = jnp.zeros((experts, tokens), jnp.float32)
    named = jnp.zeros((experts, tokens), jnp.float32)
    for k in range(chosen):
        hit = routes[k : k + 1, :] == expert
        dense = jnp.where(hit, gates[k : k + 1, :], dense)
        named = jnp.where(hit, 1.0, named)
    earlier = (
        lax.broadcasted_iota(jnp.int32, (tokens, tokens), 0)
        < lax.broadcasted_iota(jnp.int32, (tokens, tokens), 1)
    )
    slots = jnp.dot(
        named.astype(jnp.bfloat16),
        jnp.where(earlier, 1.0, 0.0).astype(jnp.bfloat16),
        preferred_element_type=jnp.float32,
    )
    slots = jnp.where(named > 0, slots, -1.0)
    out_ref[:, width:] = jnp.zeros((tokens, tokens), jnp.bfloat16)
    out_ref[:experts, width:] = dense.astype(jnp.bfloat16)
    out_ref[experts : 2 * experts, width:] = slots.astype(jnp.bfloat16)
    copies[2].wait()
    copies[3].wait()


def pair_place(arrival):
    index = lax.axis_index("expert")
    z, y = index >> 2, (index >> 1) & 1
    z = ring((ring(z) - arrival // NY) & (NZ - 1))
    return z * NY + (y ^ (arrival % NY))


def pick(low, xs, pmat_ref, mine_ref, theirs_ref):
    capacity = mine_ref.shape[0] // len(xs)

    @pl.loop(0, mine_ref.shape[1] // 256)
    def _(n):
        cols = pl.ds(pl.multiple_of(n * 256, 256), 256)
        x_cols = pl.ds(pl.multiple_of(low + n * 256, 256), 256)
        for a, x_ref in enumerate(xs):
            rows = jnp.dot(
                pmat_ref[a * 2 * capacity : (a + 1) * 2 * capacity, :],
                x_ref[:, x_cols],
                preferred_element_type=jnp.float32,
            ).astype(jnp.bfloat16)
            where = pl.ds(pl.multiple_of(pair_place(a) * capacity, capacity), capacity)
            mine_ref[where, cols] = rows[:capacity]
            theirs_ref[where, cols] = rows[capacity:]


def first_pick_kernel(experts, capacity, *refs):
    pairs = experts // 2
    xs = refs[:pairs]
    mine_ref, theirs_ref, pmat_ref, gslot_ref, other_ref = refs[pairs:]
    width = mine_ref.shape[1]
    me = lax.axis_index("expert")
    core = me & 1
    tokens = xs[0].shape[0]
    expert = lax.broadcasted_iota(jnp.int32, (experts, tokens), 0)
    slot = lax.broadcasted_iota(jnp.int32, (2 * capacity, tokens), 0).astype(jnp.float32)
    offset = (core * capacity).astype(jnp.float32)
    other_ref[...] = jnp.zeros(other_ref.shape, jnp.float32)
    for a, x_ref in enumerate(xs):
        place = pl.ds(pair_place(a), 1)
        ext = x_ref[: 2 * experts, width:].astype(jnp.float32)
        one_hot = jnp.zeros(slot.shape, jnp.float32)
        for s, (who, to_ref) in enumerate(((me, gslot_ref), (me ^ 1, other_ref))):
            gate = jnp.sum(jnp.where(expert == who, ext[:experts], 0.0), axis=0, keepdims=True)
            number = jnp.sum(jnp.where(expert == who, ext[experts:], 0.0), axis=0, keepdims=True)
            routed = number >= 0
            spot = jnp.where(routed, number + s * capacity, -1.0)
            one_hot = jnp.where(slot == spot, 1.0, one_hot)
            spot = jnp.where(routed, number + offset, -1.0)
            by_slot = lax.dot_general(
                jnp.broadcast_to(gate.astype(jnp.bfloat16), (16, tokens)),
                jnp.where(slot == spot, 1.0, 0.0).astype(jnp.bfloat16),
                NT,
                preferred_element_type=jnp.float32,
            )
            to_ref[place, :] = by_slot[:1]
        pmat_ref[a * 2 * capacity : (a + 1) * 2 * capacity, :] = one_hot.astype(jnp.bfloat16)
    theirs_ref[pairs * capacity :, :] = jnp.zeros((16, width), jnp.bfloat16)
    theirs_ref[pairs * capacity :, : 2 * capacity] = other_ref[...].astype(jnp.bfloat16)
    pick(0, xs, pmat_ref, mine_ref, theirs_ref)


def pick_kernel(low, *refs):
    pick(low, refs[:-3], *refs[-3:])


def products(half, capacity, mine_ref, got_ref, hs_ref, rows_ref, *outs):
    mine = lax.axis_index("dp")
    core = lax.axis_index("expert") & 1
    pairs = mine_ref.shape[0] // capacity
    pieces = len(outs) // 2
    piece = mine_ref.shape[1] // pieces
    for q in range(pieces):

        @pl.loop(0, piece // 256)
        def _(n, q=q):
            cols = pl.ds(pl.multiple_of(q * piece + n * 256, 256), 256)
            out = pl.ds(pl.multiple_of(n * 256, 256), 256)
            for p in range(pairs):
                for c, ref in ((core, mine_ref), (1 - core, got_ref)):
                    to = pl.ds(pl.multiple_of((2 * p + c) * capacity, capacity), capacity)
                    rows_ref[to, cols] = ref[p * capacity : (p + 1) * capacity, cols]
            block = rows_ref[:, cols]
            for d, ref in ((1 - mine, outs[q]), (mine, outs[pieces + q])):
                units = pl.ds(pl.multiple_of(d * half, 16), half)
                ref[:, out] = jnp.dot(
                    hs_ref[units, :], block, preferred_element_type=jnp.float32
                ).astype(jnp.bfloat16)


def first_products_kernel(half, capacity, mine_ref, got_ref, gslot_ref, hidden_ref, *outs):
    gates_ref, hs_ref = outs[:2]
    pairs = mine_ref.shape[0] // capacity
    got = got_ref[pairs * capacity :, : 2 * capacity].astype(jnp.float32)
    by_pair = gslot_ref[...] + got[:pairs]
    for p in range(pairs):
        gates_ref[:, p * 2 * capacity : (p + 1) * 2 * capacity] = by_pair[p : p + 1, :]
    hs_ref[...] = (hidden_ref[...].astype(jnp.float32) * gates_ref[...]).astype(jnp.bfloat16)
    products(half, capacity, mine_ref, got_ref, hs_ref, *outs[2:])


def weight_parts(half, own_ref, got_refs):
    mine = lax.axis_index("dp")
    yield pl.ds(pl.multiple_of(mine * half, 16), half), own_ref
    low = (1 - mine) * half
    for ref in got_refs:
        yield pl.ds(pl.multiple_of(low, 16), ref.shape[0]), ref
        low = low + ref.shape[0]


def raw_parts(half, cols, rows_ref, own_ref, got_refs):
    for units, w_ref in weight_parts(half, own_ref, got_refs):
        yield units, lax.dot_general(
            w_ref[:, cols], rows_ref[...], NT, preferred_element_type=jnp.float32
        )


def raw_part_kernel(half, capacity, cols, rows_ref, own_ref, *refs):
    *got_refs, hidden_ref, raw_ref, back_ref = refs
    total = jnp.zeros((1, rows_ref.shape[0]), jnp.float32)
    for units, raw in raw_parts(half, cols, rows_ref, own_ref, got_refs):
        raw_ref[units, :] = raw
        total += jnp.sum(
            raw * hidden_ref[units, :].astype(jnp.float32), axis=0, keepdims=True
        )
    blocks = total.shape[1] // capacity
    for i in range(blocks):
        to = pl.ds(pl.program_id(0) * blocks + i, 1)
        back_ref[to, :] = total[:, i * capacity : (i + 1) * capacity]


def raw_kernel(half, cols, first_ref, second_ref, own_ref, *refs):
    *got_refs, sum_ref, gates_ref, grad_ref = refs
    parts = zip(
        raw_parts(half, cols[0], first_ref, own_ref, got_refs),
        raw_parts(half, cols[1], second_ref, own_ref, got_refs),
    )
    for (units, first), (_, second) in parts:
        raw = first + second + sum_ref[units, :]
        grad_ref[units, :] = (raw * gates_ref[...]).astype(jnp.bfloat16)


def forward_kernel(half, cols, own_ref, *refs):
    *got_refs, hidden_ref, out_ref = refs
    out_ref[...] = sum(
        lax.dot_general(
            hidden_ref[units, :],
            w_ref[:, cols],
            (((0,), (0,)), ((), ())),
            preferred_element_type=jnp.float32,
        )
        for units, w_ref in weight_parts(half, own_ref, got_refs)
    ).astype(out_ref.dtype)


def slot_grads_kernel(first_ref, second_ref, forward_ref, part_ref, back_ref):
    capacity = back_ref.shape[1]
    pair = 2 * capacity
    width = first_ref.shape[1]
    for p in range(first_ref.shape[0] // pair):
        at = slice(p * pair, (p + 1) * pair)
        some = jnp.zeros((pair, LANES), jnp.float32)
        for n in range(0, 2 * width, LANES):
            rows_ref, low = (first_ref, n) if n < width else (second_ref, n - width)
            some += rows_ref[at, low : low + LANES].astype(jnp.float32) * forward_ref[
                at, n : n + LANES
            ].astype(jnp.float32)
        total = jnp.sum(some.T, axis=0, keepdims=True)
        for i in range(2):
            to = slice(2 * p + i, 2 * p + i + 1)
            back_ref[to, :] = part_ref[to, :] + total[:, i * capacity : (i + 1) * capacity]


def gates_kernel(routes_ref, slots_ref, back_ref, out_ref):
    rest = back_ref[...]
    routes = routes_ref[...]
    experts, capacity = rest.shape
    chosen, tokens = routes.shape
    pieces = []
    for _ in range(3):
        pieces.append(rest.astype(jnp.bfloat16))
        rest = rest - pieces[-1].astype(jnp.float32)
    slots = slots_ref[experts : 2 * experts, :].astype(jnp.float32)
    expert = lax.broadcasted_iota(jnp.int32, (experts, tokens), 0)
    slot = lax.broadcasted_iota(jnp.int32, (capacity, tokens), 0).astype(jnp.float32)
    hits = [expert == routes[k : k + 1, :] for k in range(chosen)]
    one_hots = []
    for hit in hits:
        number = jnp.sum(jnp.where(hit, slots, 0.0), axis=0, keepdims=True)
        one_hots.append(jnp.where(slot == number, 1.0, 0.0).astype(jnp.bfloat16))
    by_expert = jnp.dot(
        jnp.concatenate(pieces, axis=0),
        jnp.concatenate(one_hots, axis=1),
        preferred_element_type=jnp.float32,
    )
    by_expert = by_expert[:experts] + (
        by_expert[experts : 2 * experts] + by_expert[2 * experts :]
    )
    for k, hit in enumerate(hits):
        mine = by_expert[:, k * tokens : (k + 1) * tokens]
        out_ref[k : k + 1, :] = jnp.sum(jnp.where(hit, mine, 0.0), axis=0, keepdims=True)


def finish_kernel(*refs):
    own_refs, got_refs, out_ref = refs[:2], refs[2:4], refs[-1]
    piece = own_refs[0].shape[1]
    for q in range(2):
        out_ref[:, q * piece : (q + 1) * piece] = (
            own_refs[q][...].astype(jnp.float32) + got_refs[q][...].astype(jnp.float32)
        ).astype(jnp.bfloat16)


def ring_shards(grad_out, gates, routes, hidden, down_weight):
    experts = lax.axis_size("expert")
    tokens, chosen = routes.shape
    model = grad_out.shape[1]
    slots, units = hidden.shape[2:]
    half = down_weight.shape[1]
    capacity = slots // experts
    widths = [model // 8 * n for n in CHUNKS]
    columns = [slice(0, widths[0]), slice(widths[0], model)]
    tile = 256
    bf16, f32 = jnp.bfloat16, jnp.float32
    shape = jax.ShapeDtypeStruct
    hidden_t = hidden[0, 0].T
    routes_t, gates_t = routes.T, gates.T
    weight = down_weight[0]
    weight_specs = [pl.BlockSpec((half, model), lambda i: (0, 0))] * 2
    dma = pltpu.SemaphoreType.DMA

    def forward(x):
        return lax.ppermute(x, "expert", ring_pairs(1))

    def backward(x):
        return lax.ppermute(x, "expert", ring_pairs(-1))

    def across(x):
        return lax.ppermute(x, "expert", swap_pairs(2))

    def sibling(x):
        return lax.ppermute(x, "expert", swap_pairs(1))

    def swap(x):
        return lax.ppermute(x, "dp", [(0, 1), (1, 0)])

    def behind(x, *others):
        return lax.optimization_barrier((x, *others))[0]

    def pack():
        return pl.pallas_call(
            functools.partial(pack_kernel, experts, widths[0]),
            out_shape=[
                shape((tokens, widths[0] + tokens), bf16),
                shape((tokens, widths[1]), bf16),
            ],
            in_specs=[ANY] * 3,
            out_specs=[VMEM] * 2,
            scratch_shapes=[
                pltpu.VMEM(routes_t.shape, routes_t.dtype),
                pltpu.VMEM(gates_t.shape, gates_t.dtype),
                dma((4,)),
            ],
            compiler_params=params(60),
            name="pack",
        )(routes_t, gates_t, grad_out)

    def first_pick(blocks):
        return pl.pallas_call(
            functools.partial(first_pick_kernel, experts, capacity),
            out_shape=[
                shape((slots // 2, widths[0]), bf16),
                shape((slots // 2 + 16, widths[0]), bf16),
                shape((slots, tokens), bf16),
                shape((experts // 2, 2 * capacity), f32),
            ],
            in_specs=[VMEM] * len(blocks),
            out_specs=[VMEM] * 4,
            scratch_shapes=[pltpu.VMEM((16, 2 * capacity), f32)],
            compiler_params=params(24),
            cost_estimate=cost(3),
            name="first_pick",
        )(*blocks)

    piece = widths[1] // 2
    halves = [slice(widths[0] + low, widths[0] + low + piece) for low in (0, piece)]

    def later_pick(low, blocks, pmat):
        return pl.pallas_call(
            functools.partial(pick_kernel, low),
            out_shape=[shape((slots // 2, piece), bf16)] * 2,
            in_specs=[VMEM] * (len(blocks) + 1),
            out_specs=[VMEM] * 2,
            compiler_params=params(24),
            name="pick",
        )(*blocks, pmat)

    product_shapes = [shape((slots, widths[0]), bf16)] + [
        shape((half, widths[0] // PIECES), bf16)
    ] * (2 * PIECES)

    def first_products(mine, got, gslot):
        slot_gates, hs, rows, *halves = pl.pallas_call(
            functools.partial(first_products_kernel, half, capacity),
            out_shape=[shape((1, slots), f32), shape((units, slots), bf16)] + product_shapes,
            in_specs=[VMEM] * 4,
            out_specs=[VMEM] * (3 + 2 * PIECES),
            compiler_params=params(24),
            cost_estimate=cost(3),
            name="first_products",
        )(mine, got, gslot, hidden_t)
        return rows, halves[: PIECES], halves[PIECES :], slot_gates, hs

    def later_products(mine, got, hs):
        return pl.pallas_call(
            functools.partial(products, half, capacity),
            out_shape=[shape((slots, piece), bf16)] + [shape((half, piece), bf16)] * 2,
            in_specs=[VMEM] * 3,
            out_specs=[VMEM] * 3,
            compiler_params=params(24),
            name="products",
        )(mine, got, hs)

    by_slot = pl.BlockSpec((units, tile), lambda i: (0, i))
    by_row = [pl.BlockSpec((tile, n), lambda i: (i, 0)) for n in widths]
    back_shape = shape((experts, capacity), f32)

    def raw_part(rows, got_weight):
        return pl.pallas_call(
            functools.partial(raw_part_kernel, half, capacity, columns[0]),
            grid=(slots // tile,),
            out_shape=[shape((units, slots), f32), back_shape],
            in_specs=[by_row[0], *weight_specs, by_slot],
            out_specs=[by_slot, pl.BlockSpec((experts, capacity), lambda i: (0, 0))],
            compiler_params=params(24),
            cost_estimate=cost(3),
            name="raw_part",
        )(rows, weight, *got_weight, hidden_t)

    def raw_rest(rows, got_weight, raw, slot_gates):
        return pl.pallas_call(
            functools.partial(raw_kernel, half, halves),
            grid=(slots // tile,),
            out_shape=shape((units, slots), bf16),
            in_specs=[
                *[pl.BlockSpec((tile, piece), lambda i: (i, 0))] * 2,
                *weight_specs,
                by_slot,
                pl.BlockSpec((1, tile), lambda i: (0, i)),
            ],
            out_specs=by_slot,
            compiler_params=params(60),
            name="raw",
        )(*rows, weight, *got_weight, raw, slot_gates)

    def forward_columns(got_weight):
        return pl.pallas_call(
            functools.partial(forward_kernel, half, columns[1]),
            grid=(slots // tile,),
            out_shape=shape((slots, widths[1]), bf16),
            in_specs=[*weight_specs, by_slot],
            out_specs=by_row[1],
            compiler_params=params(24),
            cost_estimate=cost(3),
            name="hidden_weight",
        )(weight, *got_weight, hidden_t)

    def slot_grads(rows, forwarded, part):
        return pl.pallas_call(
            slot_grads_kernel,
            out_shape=back_shape,
            in_specs=[VMEM] * 4,
            out_specs=VMEM,
            compiler_params=params(24),
            name="slot_grads",
        )(*rows, forwarded, part)

    def finish(c, own, got, *before):
        spec = pl.BlockSpec((half // 2, widths[c] // 2), lambda i: (i, 0))
        return pl.pallas_call(
            finish_kernel,
            grid=(2,),
            out_shape=shape((half, model), bf16),
            in_specs=[spec] * 4 + [ANY] * len(before),
            out_specs=pl.BlockSpec((half // 2, widths[c]), lambda i: (i, c)),
            input_output_aliases={4: 0} if before else {},
            compiler_params=params(8),
            name="finish",
        )(*own, *got, *before)

    x0, x1 = pack()
    w = [swap(weight)]
    f0, y0 = forward(x0), across(x0)
    ff0, yf0 = forward(behind(f0, y0)), across(behind(f0, y0))
    r0 = backward(behind(x0, ff0, yf0))
    yff0 = across(behind(ff0, yf0))
    f1, yr0 = forward(behind(x1, r0)), across(behind(r0, yff0))
    r1 = backward(behind(x1, r0))
    mine0, theirs0, pmat, gslot = first_pick(
        [x0, y0, f0, yf0, ff0, yff0, r0, behind(yr0, w[0])]
    )
    ff1, yf1, y1 = forward(f1), across(behind(f1, yr0)), across(behind(x1, yr0))
    got = sibling(behind(theirs0, f1, r1))
    rows0, send0, own0, slot_gates, hs = first_products(mine0, got, gslot)
    got0 = [swap(part) for part in send0]
    yff1, ry1 = across(behind(ff1, rows0)), backward(behind(y1, ff1, rows0))
    forwarded = forward_columns(w)
    raw, part = raw_part(rows0, w)
    blocks = [x1, y1, f1, yf1, ff1, yff1, r1, ry1]
    rows1, own1, got1 = [], [], []
    for low in (0, piece):
        mine, theirs = later_pick(low, blocks, behind(pmat, raw, forwarded))
        if low > 0:
            theirs = behind(theirs, *got0)
        rows, send, own = later_products(mine, sibling(theirs), hs)
        rows1.append(rows)
        own1.append(own)
        got1.append(swap(send))

    back = slot_grads(rows1, forwarded, part)
    returned = lax.all_to_all(back, "expert", split_axis=0, concat_axis=0, tiled=True)
    grad_gates = pl.pallas_call(
        gates_kernel,
        grid=(1,),
        out_shape=shape((chosen, tokens), f32),
        in_specs=[
            pl.BlockSpec((chosen, tokens), lambda i: (0, 0)),
            pl.BlockSpec((2 * experts, tokens), lambda i: (0, widths[0] // tokens)),
            pl.BlockSpec((experts, capacity), lambda i: (0, 0)),
        ],
        out_specs=pl.BlockSpec((chosen, tokens), lambda i: (0, 0)),
        name="grad_gates",
    )(routes_t, x0, returned)

    grad_hidden = raw_rest(rows1, w, raw, slot_gates)
    grad_weight = finish(0, [behind(own0[0], back), own0[1]], got0)
    grad_weight = finish(1, own1, got1, grad_weight)
    return grad_weight[None], grad_hidden.T[None, None], grad_gates.T


def shards(grad_out, gates, routes, hidden, down_weight):
    owners = lax.axis_size("expert")
    token_count, chosen = routes.shape
    width = grad_out.shape[1]
    slots = hidden.shape[2]
    capacity = slots // owners
    flat = routes.reshape(-1)
    onehot = (flat[:, None] == jnp.arange(owners, dtype=jnp.int32)[None, :]).astype(jnp.int32)
    before = jnp.cumsum(onehot, axis=0) - onehot
    slot = jnp.sum(before * onehot, axis=1)
    target = flat * capacity + slot
    send_rows = (
        jnp.zeros((owners * capacity, width), grad_out.dtype)
        .at[target]
        .set(jnp.repeat(grad_out, chosen, axis=0))
    )
    send_gate = jnp.zeros((owners * capacity,), gates.dtype).at[target].set(gates.reshape(-1))
    send_rows = send_rows.reshape(owners, capacity, width)
    send_gate = send_gate.reshape(owners, capacity)
    saved = hidden[0, 0]
    local_weight = down_weight[0]
    contract = (((1,), (1,)), ((), ()))
    rows, gate_slots = (
        lax.all_to_all(send_rows, "expert", split_axis=0, concat_axis=0, tiled=True),
        lax.all_to_all(send_gate, "expert", split_axis=0, concat_axis=0, tiled=True),
    )
    rows = rows.reshape(slots, width)
    whole_weight = lax.all_gather(local_weight, "dp", axis=0, tiled=True)
    raw = lax.dot_general(rows, whole_weight, contract, preferred_element_type=jnp.float32)
    factor = gate_slots.reshape(slots, 1).astype(jnp.float32)
    grad_hidden = (factor * raw).astype(jnp.bfloat16)
    slot_grads = jnp.sum(raw * saved.astype(jnp.float32), axis=1)
    returned = lax.all_to_all(
        slot_grads.reshape(owners, capacity), "expert", split_axis=0, concat_axis=0, tiled=True
    )
    grad_gates = returned.reshape(-1)[target].reshape(token_count, chosen)
    scaled = (factor * rows.astype(jnp.float32)).astype(jnp.bfloat16)
    summed = lax.psum_scatter(
        lax.dot_general(
            saved, scaled, (((0,), (0,)), ((), ())), preferred_element_type=jnp.float32
        ).astype(jnp.bfloat16),
        "dp",
        scatter_dimension=0,
        tiled=True,
    )
    return (summed[None], grad_hidden[None, None], grad_gates)


def solution(mesh):
    small = mesh.shape["dp"] == 2 and mesh.shape["expert"] == NZ * NY * NC
    return jax.shard_map(
        ring_shards if small else shards,
        mesh=mesh,
        in_specs=(
            P(("dp", "expert"), None),
            P(("dp", "expert"), None),
            P(("dp", "expert"), None),
            P("dp", "expert", None, None),
            P("expert", "dp", None),
        ),
        out_specs=(
            P("expert", "dp", None),
            P("dp", "expert", None, None),
            P(("dp", "expert"), None),
        ),
        check_vma=False,
    )
```

```python
import functools

import jax
import jax.numpy as jnp
from jax import lax
from jax.experimental import pallas as pl
from jax.experimental.pallas import tpu as pltpu
from jax.sharding import PartitionSpec as P

NZ, NY, NC = 4, 2, 2
CHUNKS = (4, 4)
LANES = 128
NT = (((1,), (1,)), ((), ()))
VMEM = pl.BlockSpec(memory_space=pltpu.VMEM)
ANY = pl.BlockSpec(memory_space=pl.ANY)


def params(mib):
    return pltpu.CompilerParams(vmem_limit_bytes=mib * 2**20)


def cost(micros):
    return pl.CostEstimate(
        flops=micros * 10**9, bytes_accessed=micros * 3 * 2**20, transcendentals=0
    )


def ring(z):
    return z ^ (z >> 1)


def ring_pairs(step):
    size = NY * NC
    return [
        (ring(p) * size + rest, ring((p + step) % NZ) * size + rest)
        for p in range(NZ)
        for rest in range(size)
    ]


def swap_pairs(bit):
    return [(i, i ^ bit) for i in range(NZ * NY * NC)]


def pack_kernel(experts, width, routes_hbm, gates_hbm, grad_hbm, out_ref, later_ref, *scratch):
    routes_ref, gates_ref, sems = scratch
    copies = [
        pltpu.make_async_copy(src, dst, sems.at[i])
        for i, (src, dst) in enumerate(
            (
                (routes_hbm, routes_ref),
                (gates_hbm, gates_ref),
                (grad_hbm.at[:, :width], out_ref.at[:, :width]),
                (grad_hbm.at[:, width:], later_ref),
            )
        )
    ]
    for copy in copies:
        copy.start()
    copies[0].wait()
    copies[1].wait()
    chosen, tokens = routes_ref.shape
    routes = routes_ref[...]
    gates = gates_ref[...].astype(jnp.float32)
    expert = lax.broadcasted_iota(jnp.int32, (experts, tokens), 0)
    dense = jnp.zeros((experts, tokens), jnp.float32)
    named = jnp.zeros((experts, tokens), jnp.float32)
    for k in range(chosen):
        hit = routes[k : k + 1, :] == expert
        dense = jnp.where(hit, gates[k : k + 1, :], dense)
        named = jnp.where(hit, 1.0, named)
    earlier = (
        lax.broadcasted_iota(jnp.int32, (tokens, tokens), 0)
        < lax.broadcasted_iota(jnp.int32, (tokens, tokens), 1)
    )
    slots = jnp.dot(
        named.astype(jnp.bfloat16),
        jnp.where(earlier, 1.0, 0.0).astype(jnp.bfloat16),
        preferred_element_type=jnp.float32,
    )
    slots = jnp.where(named > 0, slots, -1.0)
    out_ref[:, width:] = jnp.zeros((tokens, tokens), jnp.bfloat16)
    out_ref[:experts, width:] = dense.astype(jnp.bfloat16)
    out_ref[experts : 2 * experts, width:] = slots.astype(jnp.bfloat16)
    copies[2].wait()
    copies[3].wait()


def pair_place(arrival):
    index = lax.axis_index("expert")
    z, y = index >> 2, (index >> 1) & 1
    z = ring((ring(z) - arrival // NY) & (NZ - 1))
    return z * NY + (y ^ (arrival % NY))


def pick(low, xs, pmat_ref, mine_ref, theirs_ref):
    capacity = mine_ref.shape[0] // len(xs)

    @pl.loop(0, mine_ref.shape[1] // 256)
    def _(n):
        cols = pl.ds(pl.multiple_of(n * 256, 256), 256)
        x_cols = pl.ds(pl.multiple_of(low + n * 256, 256), 256)
        for a, x_ref in enumerate(xs):
            rows = jnp.dot(
                pmat_ref[a * 2 * capacity : (a + 1) * 2 * capacity, :],
                x_ref[:, x_cols],
                preferred_element_type=jnp.float32,
            ).astype(jnp.bfloat16)
            where = pl.ds(pl.multiple_of(pair_place(a) * capacity, capacity), capacity)
            mine_ref[where, cols] = rows[:capacity]
            theirs_ref[where, cols] = rows[capacity:]


def first_pick_kernel(experts, capacity, *refs):
    pairs = experts // 2
    xs = refs[:pairs]
    mine_ref, theirs_ref, pmat_ref, gslot_ref, other_ref = refs[pairs:]
    width = mine_ref.shape[1]
    me = lax.axis_index("expert")
    core = me & 1
    tokens = xs[0].shape[0]
    expert = lax.broadcasted_iota(jnp.int32, (experts, tokens), 0)
    slot = lax.broadcasted_iota(jnp.int32, (2 * capacity, tokens), 0).astype(jnp.float32)
    offset = (core * capacity).astype(jnp.float32)
    other_ref[...] = jnp.zeros(other_ref.shape, jnp.float32)
    for a, x_ref in enumerate(xs):
        place = pl.ds(pair_place(a), 1)
        ext = x_ref[: 2 * experts, width:].astype(jnp.float32)
        one_hot = jnp.zeros(slot.shape, jnp.float32)
        for s, (who, to_ref) in enumerate(((me, gslot_ref), (me ^ 1, other_ref))):
            gate = jnp.sum(jnp.where(expert == who, ext[:experts], 0.0), axis=0, keepdims=True)
            number = jnp.sum(jnp.where(expert == who, ext[experts:], 0.0), axis=0, keepdims=True)
            routed = number >= 0
            spot = jnp.where(routed, number + s * capacity, -1.0)
            one_hot = jnp.where(slot == spot, 1.0, one_hot)
            spot = jnp.where(routed, number + offset, -1.0)
            by_slot = lax.dot_general(
                jnp.broadcast_to(gate.astype(jnp.bfloat16), (16, tokens)),
                jnp.where(slot == spot, 1.0, 0.0).astype(jnp.bfloat16),
                NT,
                preferred_element_type=jnp.float32,
            )
            to_ref[place, :] = by_slot[:1]
        pmat_ref[a * 2 * capacity : (a + 1) * 2 * capacity, :] = one_hot.astype(jnp.bfloat16)
    theirs_ref[pairs * capacity :, :] = jnp.zeros((16, width), jnp.bfloat16)
    theirs_ref[pairs * capacity :, : 2 * capacity] = other_ref[...].astype(jnp.bfloat16)
    pick(0, xs, pmat_ref, mine_ref, theirs_ref)


def pick_kernel(low, *refs):
    pick(low, refs[:-3], *refs[-3:])


def products(low, half, capacity, mine_ref, got_ref, hs_ref, rows_ref, *outs):
    mine = lax.axis_index("dp")
    core = lax.axis_index("expert") & 1
    pairs = mine_ref.shape[0] // capacity
    send_ref, own_ref = outs

    @pl.loop(0, rows_ref.shape[1] // 256)
    def _(n):
        cols = pl.ds(pl.multiple_of(n * 256, 256), 256)
        from_cols = pl.ds(pl.multiple_of(low + n * 256, 256), 256)
        for p in range(pairs):
            for c, ref in ((core, mine_ref), (1 - core, got_ref)):
                to = pl.ds(pl.multiple_of((2 * p + c) * capacity, capacity), capacity)
                rows_ref[to, cols] = ref[p * capacity : (p + 1) * capacity, from_cols]
        block = rows_ref[:, cols]
        for d, ref in ((1 - mine, send_ref), (mine, own_ref)):
            units = pl.ds(pl.multiple_of(d * half, 16), half)
            ref[:, cols] = jnp.dot(
                hs_ref[units, :], block, preferred_element_type=jnp.float32
            ).astype(jnp.bfloat16)


def first_products_kernel(half, capacity, mine_ref, got_ref, gslot_ref, hidden_ref, *outs):
    gates_ref, hs_ref = outs[:2]
    pairs = mine_ref.shape[0] // capacity
    got = got_ref[pairs * capacity :, : 2 * capacity].astype(jnp.float32)
    by_pair = gslot_ref[...] + got[:pairs]
    for p in range(pairs):
        gates_ref[:, p * 2 * capacity : (p + 1) * 2 * capacity] = by_pair[p : p + 1, :]
    hs_ref[...] = (hidden_ref[...].astype(jnp.float32) * gates_ref[...]).astype(jnp.bfloat16)
    products(0, half, capacity, mine_ref, got_ref, hs_ref, *outs[2:])


def weight_parts(half, own_ref, got_refs):
    mine = lax.axis_index("dp")
    yield pl.ds(pl.multiple_of(mine * half, 16), half), own_ref
    low = (1 - mine) * half
    for ref in got_refs:
        yield pl.ds(pl.multiple_of(low, 16), ref.shape[0]), ref
        low = low + ref.shape[0]


def raw_parts(half, cols, rows_ref, own_ref, got_refs):
    for units, w_ref in weight_parts(half, own_ref, got_refs):
        yield units, lax.dot_general(
            w_ref[:, cols], rows_ref[...], NT, preferred_element_type=jnp.float32
        )


def raw_part_kernel(half, capacity, cols, first_ref, second_ref, own_ref, *refs):
    *got_refs, hidden_ref, raw_ref, back_ref = refs
    total = jnp.zeros((1, first_ref.shape[0]), jnp.float32)
    terms = zip(
        raw_parts(half, cols[0], first_ref, own_ref, got_refs),
        raw_parts(half, cols[1], second_ref, own_ref, got_refs),
    )
    for (units, first), (_, second) in terms:
        raw = first + second
        raw_ref[units, :] = raw
        total += jnp.sum(
            raw * hidden_ref[units, :].astype(jnp.float32), axis=0, keepdims=True
        )
    blocks = total.shape[1] // capacity
    for i in range(blocks):
        to = pl.ds(pl.program_id(0) * blocks + i, 1)
        back_ref[to, :] = total[:, i * capacity : (i + 1) * capacity]


def raw_kernel(half, cols, first_ref, second_ref, own_ref, *refs):
    *got_refs, sum_ref, gates_ref, grad_ref = refs
    parts = zip(
        raw_parts(half, cols[0], first_ref, own_ref, got_refs),
        raw_parts(half, cols[1], second_ref, own_ref, got_refs),
    )
    for (units, first), (_, second) in parts:
        raw = first + second + sum_ref[units, :]
        grad_ref[units, :] = (raw * gates_ref[...]).astype(jnp.bfloat16)


def forward_kernel(half, cols, own_ref, *refs):
    *got_refs, hidden_ref, out_ref = refs
    out_ref[...] = sum(
        lax.dot_general(
            hidden_ref[units, :],
            w_ref[:, cols],
            (((0,), (0,)), ((), ())),
            preferred_element_type=jnp.float32,
        )
        for units, w_ref in weight_parts(half, own_ref, got_refs)
    ).astype(out_ref.dtype)


def slot_grads_kernel(first_ref, second_ref, forward_ref, part_ref, back_ref):
    capacity = back_ref.shape[1]
    pair = 2 * capacity
    width = first_ref.shape[1]
    for p in range(first_ref.shape[0] // pair):
        at = slice(p * pair, (p + 1) * pair)
        some = jnp.zeros((pair, LANES), jnp.float32)
        for n in range(0, 2 * width, LANES):
            rows_ref, low = (first_ref, n) if n < width else (second_ref, n - width)
            some += rows_ref[at, low : low + LANES].astype(jnp.float32) * forward_ref[
                at, n : n + LANES
            ].astype(jnp.float32)
        total = jnp.sum(some.T, axis=0, keepdims=True)
        for i in range(2):
            to = slice(2 * p + i, 2 * p + i + 1)
            back_ref[to, :] = part_ref[to, :] + total[:, i * capacity : (i + 1) * capacity]


def gates_kernel(routes_ref, slots_ref, back_ref, out_ref):
    rest = back_ref[...]
    routes = routes_ref[...]
    experts, capacity = rest.shape
    chosen, tokens = routes.shape
    pieces = []
    for _ in range(3):
        pieces.append(rest.astype(jnp.bfloat16))
        rest = rest - pieces[-1].astype(jnp.float32)
    slots = slots_ref[experts : 2 * experts, :].astype(jnp.float32)
    expert = lax.broadcasted_iota(jnp.int32, (experts, tokens), 0)
    slot = lax.broadcasted_iota(jnp.int32, (capacity, tokens), 0).astype(jnp.float32)
    hits = [expert == routes[k : k + 1, :] for k in range(chosen)]
    one_hots = []
    for hit in hits:
        number = jnp.sum(jnp.where(hit, slots, 0.0), axis=0, keepdims=True)
        one_hots.append(jnp.where(slot == number, 1.0, 0.0).astype(jnp.bfloat16))
    by_expert = jnp.dot(
        jnp.concatenate(pieces, axis=0),
        jnp.concatenate(one_hots, axis=1),
        preferred_element_type=jnp.float32,
    )
    by_expert = by_expert[:experts] + (
        by_expert[experts : 2 * experts] + by_expert[2 * experts :]
    )
    for k, hit in enumerate(hits):
        mine = by_expert[:, k * tokens : (k + 1) * tokens]
        out_ref[k : k + 1, :] = jnp.sum(jnp.where(hit, mine, 0.0), axis=0, keepdims=True)


def finish_kernel(*refs):
    own_refs, got_refs, out_ref = refs[:2], refs[2:4], refs[-1]
    piece = own_refs[0].shape[1]
    for q in range(2):
        out_ref[:, q * piece : (q + 1) * piece] = (
            own_refs[q][...].astype(jnp.float32) + got_refs[q][...].astype(jnp.float32)
        ).astype(jnp.bfloat16)


def ring_shards(grad_out, gates, routes, hidden, down_weight):
    experts = lax.axis_size("expert")
    tokens, chosen = routes.shape
    model = grad_out.shape[1]
    slots, units = hidden.shape[2:]
    half = down_weight.shape[1]
    capacity = slots // experts
    widths = [model // 8 * n for n in CHUNKS]
    columns = [slice(0, widths[0]), slice(widths[0], model)]
    tile = 256
    bf16, f32 = jnp.bfloat16, jnp.float32
    shape = jax.ShapeDtypeStruct
    hidden_t = hidden[0, 0].T
    routes_t, gates_t = routes.T, gates.T
    weight = down_weight[0]
    weight_specs = [pl.BlockSpec((half, model), lambda i: (0, 0))] * 2
    dma = pltpu.SemaphoreType.DMA

    def forward(x):
        return lax.ppermute(x, "expert", ring_pairs(1))

    def backward(x):
        return lax.ppermute(x, "expert", ring_pairs(-1))

    def across(x):
        return lax.ppermute(x, "expert", swap_pairs(2))

    def sibling(x):
        return lax.ppermute(x, "expert", swap_pairs(1))

    def swap(x):
        return lax.ppermute(x, "dp", [(0, 1), (1, 0)])

    def behind(x, *others):
        return lax.optimization_barrier((x, *others))[0]

    def pack():
        return pl.pallas_call(
            functools.partial(pack_kernel, experts, widths[0]),
            out_shape=[
                shape((tokens, widths[0] + tokens), bf16),
                shape((tokens, widths[1]), bf16),
            ],
            in_specs=[ANY] * 3,
            out_specs=[VMEM] * 2,
            scratch_shapes=[
                pltpu.VMEM(routes_t.shape, routes_t.dtype),
                pltpu.VMEM(gates_t.shape, gates_t.dtype),
                dma((4,)),
            ],
            compiler_params=params(60),
            name="pack",
        )(routes_t, gates_t, grad_out)

    def first_pick(blocks):
        return pl.pallas_call(
            functools.partial(first_pick_kernel, experts, capacity),
            out_shape=[
                shape((slots // 2, widths[0]), bf16),
                shape((slots // 2 + 16, widths[0]), bf16),
                shape((slots, tokens), bf16),
                shape((experts // 2, 2 * capacity), f32),
            ],
            in_specs=[VMEM] * len(blocks),
            out_specs=[VMEM] * 4,
            scratch_shapes=[pltpu.VMEM((16, 2 * capacity), f32)],
            compiler_params=params(24),
            cost_estimate=cost(3),
            name="first_pick",
        )(*blocks)

    piece = widths[1] // 2
    halves = [slice(widths[0] + low, widths[0] + low + piece) for low in (0, piece)]

    def later_pick(low, blocks, pmat):
        return pl.pallas_call(
            functools.partial(pick_kernel, low),
            out_shape=[shape((slots // 2, piece), bf16)] * 2,
            in_specs=[VMEM] * (len(blocks) + 1),
            out_specs=[VMEM] * 2,
            compiler_params=params(24),
            name="pick",
        )(*blocks, pmat)

    product_shapes = [shape((slots, piece), bf16)] + [shape((half, piece), bf16)] * 2

    def first_products(mine, got, gslot):
        return pl.pallas_call(
            functools.partial(first_products_kernel, half, capacity),
            out_shape=[shape((1, slots), f32), shape((units, slots), bf16)] + product_shapes,
            in_specs=[VMEM] * 4,
            out_specs=[VMEM] * 5,
            compiler_params=params(24),
            cost_estimate=cost(2),
            name="first_products",
        )(mine, got, gslot, hidden_t)

    def later_products(low, mine, got, hs):
        return pl.pallas_call(
            functools.partial(products, low, half, capacity),
            out_shape=product_shapes,
            in_specs=[VMEM] * 3,
            out_specs=[VMEM] * 3,
            compiler_params=params(24),
            name="products",
        )(mine, got, hs)

    by_slot = pl.BlockSpec((units, tile), lambda i: (0, i))
    by_row = [pl.BlockSpec((tile, n), lambda i: (i, 0)) for n in widths]
    back_shape = shape((experts, capacity), f32)

    def raw_part(rows, got_weight):
        return pl.pallas_call(
            functools.partial(raw_part_kernel, half, capacity, [slice(0, piece), slice(piece, 2 * piece)]),
            grid=(slots // tile,),
            out_shape=[shape((units, slots), f32), back_shape],
            in_specs=[
                *[pl.BlockSpec((tile, piece), lambda i: (i, 0))] * 2,
                *weight_specs,
                by_slot,
            ],
            out_specs=[by_slot, pl.BlockSpec((experts, capacity), lambda i: (0, 0))],
            compiler_params=params(24),
            cost_estimate=cost(3),
            name="raw_part",
        )(*rows, weight, *got_weight, hidden_t)

    def raw_rest(rows, got_weight, raw, slot_gates):
        return pl.pallas_call(
            functools.partial(raw_kernel, half, halves),
            grid=(slots // tile,),
            out_shape=shape((units, slots), bf16),
            in_specs=[
                *[pl.BlockSpec((tile, piece), lambda i: (i, 0))] * 2,
                *weight_specs,
                by_slot,
                pl.BlockSpec((1, tile), lambda i: (0, i)),
            ],
            out_specs=by_slot,
            compiler_params=params(60),
            name="raw",
        )(*rows, weight, *got_weight, raw, slot_gates)

    def forward_columns(got_weight):
        return pl.pallas_call(
            functools.partial(forward_kernel, half, columns[1]),
            grid=(slots // tile,),
            out_shape=shape((slots, widths[1]), bf16),
            in_specs=[*weight_specs, by_slot],
            out_specs=by_row[1],
            compiler_params=params(24),
            cost_estimate=cost(3),
            name="hidden_weight",
        )(weight, *got_weight, hidden_t)

    def slot_grads(rows, forwarded, part):
        return pl.pallas_call(
            slot_grads_kernel,
            out_shape=back_shape,
            in_specs=[VMEM] * 4,
            out_specs=VMEM,
            compiler_params=params(24),
            name="slot_grads",
        )(*rows, forwarded, part)

    def finish(c, own, got, *before):
        spec = pl.BlockSpec((half // 2, widths[c] // 2), lambda i: (i, 0))
        return pl.pallas_call(
            finish_kernel,
            grid=(2,),
            out_shape=shape((half, model), bf16),
            in_specs=[spec] * 4 + [ANY] * len(before),
            out_specs=pl.BlockSpec((half // 2, widths[c]), lambda i: (i, c)),
            input_output_aliases={4: 0} if before else {},
            compiler_params=params(8),
            name="finish",
        )(*own, *got, *before)

    x0, x1 = pack()
    w = [swap(weight)]
    f0, y0 = forward(x0), across(x0)
    ff0, yf0 = forward(behind(f0, y0)), across(behind(f0, y0))
    r0 = backward(behind(x0, ff0, yf0))
    yff0 = across(behind(ff0, yf0))
    f1, yr0 = forward(behind(x1, r0)), across(behind(r0, yff0))
    r1 = backward(behind(x1, r0))
    mine0, theirs0, pmat, gslot = first_pick(
        [x0, y0, f0, yf0, ff0, yff0, r0, behind(yr0, w[0])]
    )
    ff1, yf1, y1 = forward(f1), across(behind(f1, yr0)), across(behind(x1, yr0))
    forwarded = forward_columns(w)
    got = sibling(behind(theirs0, f1, r1, forwarded))
    slot_gates, hs, rows_a, send_a, own_a = first_products(mine0, got, gslot)
    rows_b, send_b, own_b = later_products(piece, mine0, got, hs)
    rows0, send0, own0 = [rows_a, rows_b], [send_a, send_b], [own_a, own_b]
    got0 = [swap(part) for part in send0]
    yff1, ry1 = across(behind(ff1, *rows0)), backward(behind(y1, ff1, *rows0))
    raw, part = raw_part(rows0, w)
    blocks = [x1, y1, f1, yf1, ff1, yff1, r1, ry1]
    rows1, own1, got1 = [], [], []
    for low in (0, piece):
        mine, theirs = later_pick(low, blocks, behind(pmat, raw, forwarded))
        if low > 0:
            theirs = behind(theirs, *got0)
        rows, send, own = later_products(0, mine, sibling(theirs), hs)
        rows1.append(rows)
        own1.append(own)
        got1.append(swap(send))

    back = slot_grads(rows1, forwarded, part)
    returned = lax.all_to_all(back, "expert", split_axis=0, concat_axis=0, tiled=True)
    grad_gates = pl.pallas_call(
        gates_kernel,
        grid=(1,),
        out_shape=shape((chosen, tokens), f32),
        in_specs=[
            pl.BlockSpec((chosen, tokens), lambda i: (0, 0)),
            pl.BlockSpec((2 * experts, tokens), lambda i: (0, widths[0] // tokens)),
            pl.BlockSpec((experts, capacity), lambda i: (0, 0)),
        ],
        out_specs=pl.BlockSpec((chosen, tokens), lambda i: (0, 0)),
        name="grad_gates",
    )(routes_t, x0, returned)

    grad_hidden = raw_rest(rows1, w, raw, slot_gates)
    grad_weight = finish(0, [behind(own0[0], back), own0[1]], got0)
    grad_weight = finish(1, own1, got1, grad_weight)
    return grad_weight[None], grad_hidden.T[None, None], grad_gates.T


def shards(grad_out, gates, routes, hidden, down_weight):
    owners = lax.axis_size("expert")
    token_count, chosen = routes.shape
    width = grad_out.shape[1]
    slots = hidden.shape[2]
    capacity = slots // owners
    flat = routes.reshape(-1)
    onehot = (flat[:, None] == jnp.arange(owners, dtype=jnp.int32)[None, :]).astype(jnp.int32)
    before = jnp.cumsum(onehot, axis=0) - onehot
    slot = jnp.sum(before * onehot, axis=1)
    target = flat * capacity + slot
    send_rows = (
        jnp.zeros((owners * capacity, width), grad_out.dtype)
        .at[target]
        .set(jnp.repeat(grad_out, chosen, axis=0))
    )
    send_gate = jnp.zeros((owners * capacity,), gates.dtype).at[target].set(gates.reshape(-1))
    send_rows = send_rows.reshape(owners, capacity, width)
    send_gate = send_gate.reshape(owners, capacity)
    saved = hidden[0, 0]
    local_weight = down_weight[0]
    contract = (((1,), (1,)), ((), ()))
    rows, gate_slots = (
        lax.all_to_all(send_rows, "expert", split_axis=0, concat_axis=0, tiled=True),
        lax.all_to_all(send_gate, "expert", split_axis=0, concat_axis=0, tiled=True),
    )
    rows = rows.reshape(slots, width)
    whole_weight = lax.all_gather(local_weight, "dp", axis=0, tiled=True)
    raw = lax.dot_general(rows, whole_weight, contract, preferred_element_type=jnp.float32)
    factor = gate_slots.reshape(slots, 1).astype(jnp.float32)
    grad_hidden = (factor * raw).astype(jnp.bfloat16)
    slot_grads = jnp.sum(raw * saved.astype(jnp.float32), axis=1)
    returned = lax.all_to_all(
        slot_grads.reshape(owners, capacity), "expert", split_axis=0, concat_axis=0, tiled=True
    )
    grad_gates = returned.reshape(-1)[target].reshape(token_count, chosen)
    scaled = (factor * rows.astype(jnp.float32)).astype(jnp.bfloat16)
    summed = lax.psum_scatter(
        lax.dot_general(
            saved, scaled, (((0,), (0,)), ((), ())), preferred_element_type=jnp.float32
        ).astype(jnp.bfloat16),
        "dp",
        scatter_dimension=0,
        tiled=True,
    )
    return (summed[None], grad_hidden[None, None], grad_gates)


def solution(mesh):
    small = mesh.shape["dp"] == 2 and mesh.shape["expert"] == NZ * NY * NC
    return jax.shard_map(
        ring_shards if small else shards,
        mesh=mesh,
        in_specs=(
            P(("dp", "expert"), None),
            P(("dp", "expert"), None),
            P(("dp", "expert"), None),
            P("dp", "expert", None, None),
            P("expert", "dp", None),
        ),
        out_specs=(
            P("expert", "dp", None),
            P("dp", "expert", None, None),
            P(("dp", "expert"), None),
        ),
        check_vma=False,
    )
```

```python
import functools

import jax
import jax.numpy as jnp
from jax import lax
from jax.experimental import pallas as pl
from jax.experimental.pallas import tpu as pltpu
from jax.sharding import PartitionSpec as P

NZ, NY, NC = 4, 2, 2
CHUNKS = (4, 4)
LANES = 128
NT = (((1,), (1,)), ((), ()))
VMEM = pl.BlockSpec(memory_space=pltpu.VMEM)
ANY = pl.BlockSpec(memory_space=pl.ANY)


def params(mib):
    return pltpu.CompilerParams(vmem_limit_bytes=mib * 2**20)


def cost(micros):
    return pl.CostEstimate(
        flops=micros * 10**9, bytes_accessed=micros * 3 * 2**20, transcendentals=0
    )


def ring(z):
    return z ^ (z >> 1)


def ring_pairs(step):
    size = NY * NC
    return [
        (ring(p) * size + rest, ring((p + step) % NZ) * size + rest)
        for p in range(NZ)
        for rest in range(size)
    ]


def swap_pairs(bit):
    return [(i, i ^ bit) for i in range(NZ * NY * NC)]


def pack_kernel(experts, width, routes_hbm, gates_hbm, grad_hbm, out_ref, later_ref, *scratch):
    routes_ref, gates_ref, sems = scratch
    copies = [
        pltpu.make_async_copy(src, dst, sems.at[i])
        for i, (src, dst) in enumerate(
            (
                (routes_hbm, routes_ref),
                (gates_hbm, gates_ref),
                (grad_hbm.at[:, :width], out_ref.at[:, :width]),
                (grad_hbm.at[:, width:], later_ref),
            )
        )
    ]
    for copy in copies:
        copy.start()
    copies[0].wait()
    copies[1].wait()
    chosen, tokens = routes_ref.shape
    routes = routes_ref[...]
    gates = gates_ref[...].astype(jnp.float32)
    expert = lax.broadcasted_iota(jnp.int32, (experts, tokens), 0)
    dense = jnp.zeros((experts, tokens), jnp.float32)
    named = jnp.zeros((experts, tokens), jnp.float32)
    for k in range(chosen):
        hit = routes[k : k + 1, :] == expert
        dense = jnp.where(hit, gates[k : k + 1, :], dense)
        named = jnp.where(hit, 1.0, named)
    earlier = (
        lax.broadcasted_iota(jnp.int32, (tokens, tokens), 0)
        < lax.broadcasted_iota(jnp.int32, (tokens, tokens), 1)
    )
    slots = jnp.dot(
        named.astype(jnp.bfloat16),
        jnp.where(earlier, 1.0, 0.0).astype(jnp.bfloat16),
        preferred_element_type=jnp.float32,
    )
    slots = jnp.where(named > 0, slots, -1.0)
    out_ref[:, width:] = jnp.zeros((tokens, tokens), jnp.bfloat16)
    out_ref[:experts, width:] = dense.astype(jnp.bfloat16)
    out_ref[experts : 2 * experts, width:] = slots.astype(jnp.bfloat16)
    copies[2].wait()
    copies[3].wait()


def pair_place(arrival):
    index = lax.axis_index("expert")
    z, y = index >> 2, (index >> 1) & 1
    z = ring((ring(z) - arrival // NY) & (NZ - 1))
    return z * NY + (y ^ (arrival % NY))


def pick(low, xs, pmat_ref, mine_ref, theirs_ref):
    capacity = mine_ref.shape[0] // len(xs)

    @pl.loop(0, mine_ref.shape[1] // 256)
    def _(n):
        cols = pl.ds(pl.multiple_of(n * 256, 256), 256)
        x_cols = pl.ds(pl.multiple_of(low + n * 256, 256), 256)
        for a, x_ref in enumerate(xs):
            rows = jnp.dot(
                pmat_ref[a * 2 * capacity : (a + 1) * 2 * capacity, :],
                x_ref[:, x_cols],
                preferred_element_type=jnp.float32,
            ).astype(jnp.bfloat16)
            where = pl.ds(pl.multiple_of(pair_place(a) * capacity, capacity), capacity)
            mine_ref[where, cols] = rows[:capacity]
            theirs_ref[where, cols] = rows[capacity:]


def first_pick_kernel(experts, capacity, *refs):
    pairs = experts // 2
    xs = refs[:pairs]
    mine_ref, theirs_ref, pmat_ref, gslot_ref, other_ref = refs[pairs:]
    width = mine_ref.shape[1]
    me = lax.axis_index("expert")
    core = me & 1
    tokens = xs[0].shape[0]
    expert = lax.broadcasted_iota(jnp.int32, (experts, tokens), 0)
    slot = lax.broadcasted_iota(jnp.int32, (2 * capacity, tokens), 0).astype(jnp.float32)
    offset = (core * capacity).astype(jnp.float32)
    other_ref[...] = jnp.zeros(other_ref.shape, jnp.float32)
    for a, x_ref in enumerate(xs):
        place = pl.ds(pair_place(a), 1)
        ext = x_ref[: 2 * experts, width:].astype(jnp.float32)
        one_hot = jnp.zeros(slot.shape, jnp.float32)
        for s, (who, to_ref) in enumerate(((me, gslot_ref), (me ^ 1, other_ref))):
            gate = jnp.sum(jnp.where(expert == who, ext[:experts], 0.0), axis=0, keepdims=True)
            number = jnp.sum(jnp.where(expert == who, ext[experts:], 0.0), axis=0, keepdims=True)
            routed = number >= 0
            spot = jnp.where(routed, number + s * capacity, -1.0)
            one_hot = jnp.where(slot == spot, 1.0, one_hot)
            spot = jnp.where(routed, number + offset, -1.0)
            by_slot = lax.dot_general(
                jnp.broadcast_to(gate.astype(jnp.bfloat16), (16, tokens)),
                jnp.where(slot == spot, 1.0, 0.0).astype(jnp.bfloat16),
                NT,
                preferred_element_type=jnp.float32,
            )
            to_ref[place, :] = by_slot[:1]
        pmat_ref[a * 2 * capacity : (a + 1) * 2 * capacity, :] = one_hot.astype(jnp.bfloat16)
    theirs_ref[pairs * capacity :, :] = jnp.zeros((16, width), jnp.bfloat16)
    theirs_ref[pairs * capacity :, : 2 * capacity] = other_ref[...].astype(jnp.bfloat16)
    pick(0, xs, pmat_ref, mine_ref, theirs_ref)


def pick_kernel(low, *refs):
    pick(low, refs[:-3], *refs[-3:])


def products(low, half, capacity, mine_ref, got_ref, hs_ref, rows_ref, *outs):
    mine = lax.axis_index("dp")
    core = lax.axis_index("expert") & 1
    pairs = mine_ref.shape[0] // capacity
    send_ref, own_ref = outs

    @pl.loop(0, rows_ref.shape[1] // 256)
    def _(n):
        cols = pl.ds(pl.multiple_of(n * 256, 256), 256)
        from_cols = pl.ds(pl.multiple_of(low + n * 256, 256), 256)
        for p in range(pairs):
            for c, ref in ((core, mine_ref), (1 - core, got_ref)):
                to = pl.ds(pl.multiple_of((2 * p + c) * capacity, capacity), capacity)
                rows_ref[to, cols] = ref[p * capacity : (p + 1) * capacity, from_cols]
        block = rows_ref[:, cols]
        for d, ref in ((1 - mine, send_ref), (mine, own_ref)):
            units = pl.ds(pl.multiple_of(d * half, 16), half)
            ref[:, cols] = jnp.dot(
                hs_ref[units, :], block, preferred_element_type=jnp.float32
            ).astype(jnp.bfloat16)


def first_products_kernel(half, capacity, mine_ref, got_ref, gslot_ref, hidden_ref, *outs):
    gates_ref, hs_ref = outs[:2]
    pairs = mine_ref.shape[0] // capacity
    got = got_ref[pairs * capacity :, : 2 * capacity].astype(jnp.float32)
    by_pair = gslot_ref[...] + got[:pairs]
    for p in range(pairs):
        gates_ref[:, p * 2 * capacity : (p + 1) * 2 * capacity] = by_pair[p : p + 1, :]
    hs_ref[...] = (hidden_ref[...].astype(jnp.float32) * gates_ref[...]).astype(jnp.bfloat16)
    products(0, half, capacity, mine_ref, got_ref, hs_ref, *outs[2:])


def weight_parts(half, own_ref, got_refs):
    mine = lax.axis_index("dp")
    yield pl.ds(pl.multiple_of(mine * half, 16), half), own_ref
    low = (1 - mine) * half
    for ref in got_refs:
        yield pl.ds(pl.multiple_of(low, 16), ref.shape[0]), ref
        low = low + ref.shape[0]


def raw_parts(half, cols, rows_ref, own_ref, got_refs):
    for units, w_ref in weight_parts(half, own_ref, got_refs):
        yield units, lax.dot_general(
            w_ref[:, cols], rows_ref[...], NT, preferred_element_type=jnp.float32
        )


def raw_part_kernel(half, capacity, cols, first_ref, second_ref, own_ref, *refs):
    *got_refs, hidden_ref, raw_ref, back_ref = refs
    total = jnp.zeros((1, first_ref.shape[0]), jnp.float32)
    terms = zip(
        raw_parts(half, cols[0], first_ref, own_ref, got_refs),
        raw_parts(half, cols[1], second_ref, own_ref, got_refs),
    )
    for (units, first), (_, second) in terms:
        raw = first + second
        raw_ref[units, :] = raw
        total += jnp.sum(
            raw * hidden_ref[units, :].astype(jnp.float32), axis=0, keepdims=True
        )
    blocks = total.shape[1] // capacity
    for i in range(blocks):
        to = pl.ds(pl.program_id(0) * blocks + i, 1)
        back_ref[to, :] = total[:, i * capacity : (i + 1) * capacity]


def raw_kernel(half, cols, first_ref, second_ref, own_ref, *refs):
    *got_refs, sum_ref, gates_ref, grad_ref = refs
    parts = zip(
        raw_parts(half, cols[0], first_ref, own_ref, got_refs),
        raw_parts(half, cols[1], second_ref, own_ref, got_refs),
    )
    for (units, first), (_, second) in parts:
        raw = first + second + sum_ref[units, :]
        grad_ref[units, :] = (raw * gates_ref[...]).astype(jnp.bfloat16)


def forward_kernel(half, cols, own_ref, *refs):
    *got_refs, hidden_ref, out_ref = refs
    out_ref[...] = sum(
        lax.dot_general(
            hidden_ref[units, :],
            w_ref[:, cols],
            (((0,), (0,)), ((), ())),
            preferred_element_type=jnp.float32,
        )
        for units, w_ref in weight_parts(half, own_ref, got_refs)
    ).astype(out_ref.dtype)


def slot_grads_kernel(first_ref, second_ref, forward_ref, part_ref, back_ref):
    capacity = back_ref.shape[1]
    pair = 2 * capacity
    width = first_ref.shape[1]
    for p in range(first_ref.shape[0] // pair):
        at = slice(p * pair, (p + 1) * pair)
        some = jnp.zeros((pair, LANES), jnp.float32)
        for n in range(0, 2 * width, LANES):
            rows_ref, low = (first_ref, n) if n < width else (second_ref, n - width)
            some += rows_ref[at, low : low + LANES].astype(jnp.float32) * forward_ref[
                at, n : n + LANES
            ].astype(jnp.float32)
        total = jnp.sum(some.T, axis=0, keepdims=True)
        for i in range(2):
            to = slice(2 * p + i, 2 * p + i + 1)
            back_ref[to, :] = part_ref[to, :] + total[:, i * capacity : (i + 1) * capacity]


def gates_kernel(routes_ref, slots_ref, back_ref, out_ref):
    rest = back_ref[...]
    routes = routes_ref[...]
    experts, capacity = rest.shape
    chosen, tokens = routes.shape
    pieces = []
    for _ in range(3):
        pieces.append(rest.astype(jnp.bfloat16))
        rest = rest - pieces[-1].astype(jnp.float32)
    slots = slots_ref[experts : 2 * experts, :].astype(jnp.float32)
    expert = lax.broadcasted_iota(jnp.int32, (experts, tokens), 0)
    slot = lax.broadcasted_iota(jnp.int32, (capacity, tokens), 0).astype(jnp.float32)
    hits = [expert == routes[k : k + 1, :] for k in range(chosen)]
    one_hots = []
    for hit in hits:
        number = jnp.sum(jnp.where(hit, slots, 0.0), axis=0, keepdims=True)
        one_hots.append(jnp.where(slot == number, 1.0, 0.0).astype(jnp.bfloat16))
    by_expert = jnp.dot(
        jnp.concatenate(pieces, axis=0),
        jnp.concatenate(one_hots, axis=1),
        preferred_element_type=jnp.float32,
    )
    by_expert = by_expert[:experts] + (
        by_expert[experts : 2 * experts] + by_expert[2 * experts :]
    )
    for k, hit in enumerate(hits):
        mine = by_expert[:, k * tokens : (k + 1) * tokens]
        out_ref[k : k + 1, :] = jnp.sum(jnp.where(hit, mine, 0.0), axis=0, keepdims=True)


def finish_kernel(*refs):
    own_refs, got_refs, out_ref = refs[:2], refs[2:4], refs[-1]
    piece = own_refs[0].shape[1]
    for q in range(2):
        out_ref[:, q * piece : (q + 1) * piece] = (
            own_refs[q][...].astype(jnp.float32) + got_refs[q][...].astype(jnp.float32)
        ).astype(jnp.bfloat16)


def ring_shards(grad_out, gates, routes, hidden, down_weight):
    experts = lax.axis_size("expert")
    tokens, chosen = routes.shape
    model = grad_out.shape[1]
    slots, units = hidden.shape[2:]
    half = down_weight.shape[1]
    capacity = slots // experts
    widths = [model // 8 * n for n in CHUNKS]
    columns = [slice(0, widths[0]), slice(widths[0], model)]
    tile = 256
    bf16, f32 = jnp.bfloat16, jnp.float32
    shape = jax.ShapeDtypeStruct
    hidden_t = hidden[0, 0].T
    routes_t, gates_t = routes.T, gates.T
    weight = down_weight[0]
    weight_specs = [pl.BlockSpec((half, model), lambda i: (0, 0))] * 2
    dma = pltpu.SemaphoreType.DMA

    def forward(x):
        return lax.ppermute(x, "expert", ring_pairs(1))

    def backward(x):
        return lax.ppermute(x, "expert", ring_pairs(-1))

    def across(x):
        return lax.ppermute(x, "expert", swap_pairs(2))

    def sibling(x):
        return lax.ppermute(x, "expert", swap_pairs(1))

    def swap(x):
        return lax.ppermute(x, "dp", [(0, 1), (1, 0)])

    def behind(x, *others):
        return lax.optimization_barrier((x, *others))[0]

    def pack():
        return pl.pallas_call(
            functools.partial(pack_kernel, experts, widths[0]),
            out_shape=[
                shape((tokens, widths[0] + tokens), bf16),
                shape((tokens, widths[1]), bf16),
            ],
            in_specs=[ANY] * 3,
            out_specs=[VMEM] * 2,
            scratch_shapes=[
                pltpu.VMEM(routes_t.shape, routes_t.dtype),
                pltpu.VMEM(gates_t.shape, gates_t.dtype),
                dma((4,)),
            ],
            compiler_params=params(60),
            name="pack",
        )(routes_t, gates_t, grad_out)

    def first_pick(blocks):
        return pl.pallas_call(
            functools.partial(first_pick_kernel, experts, capacity),
            out_shape=[
                shape((slots // 2, widths[0]), bf16),
                shape((slots // 2 + 16, widths[0]), bf16),
                shape((slots, tokens), bf16),
                shape((experts // 2, 2 * capacity), f32),
            ],
            in_specs=[VMEM] * len(blocks),
            out_specs=[VMEM] * 4,
            scratch_shapes=[pltpu.VMEM((16, 2 * capacity), f32)],
            compiler_params=params(24),
            cost_estimate=cost(3),
            name="first_pick",
        )(*blocks)

    piece = widths[1] // 2
    halves = [slice(widths[0] + low, widths[0] + low + piece) for low in (0, piece)]

    def later_pick(low, blocks, pmat):
        return pl.pallas_call(
            functools.partial(pick_kernel, low),
            out_shape=[shape((slots // 2, piece), bf16)] * 2,
            in_specs=[VMEM] * (len(blocks) + 1),
            out_specs=[VMEM] * 2,
            compiler_params=params(24),
            name="pick",
        )(*blocks, pmat)

    product_shapes = [shape((slots, piece), bf16)] + [shape((half, piece), bf16)] * 2

    def first_products(mine, got, gslot):
        return pl.pallas_call(
            functools.partial(first_products_kernel, half, capacity),
            out_shape=[shape((1, slots), f32), shape((units, slots), bf16)] + product_shapes,
            in_specs=[VMEM] * 4,
            out_specs=[VMEM] * 5,
            compiler_params=params(24),
            cost_estimate=cost(2),
            name="first_products",
        )(mine, got, gslot, hidden_t)

    def later_products(low, mine, got, hs):
        return pl.pallas_call(
            functools.partial(products, low, half, capacity),
            out_shape=product_shapes,
            in_specs=[VMEM] * 3,
            out_specs=[VMEM] * 3,
            compiler_params=params(24),
            name="products",
        )(mine, got, hs)

    by_slot = pl.BlockSpec((units, tile), lambda i: (0, i))
    by_row = [pl.BlockSpec((tile, n), lambda i: (i, 0)) for n in widths]
    back_shape = shape((experts, capacity), f32)

    def raw_part(rows, got_weight):
        return pl.pallas_call(
            functools.partial(raw_part_kernel, half, capacity, [slice(0, piece), slice(piece, 2 * piece)]),
            grid=(slots // tile,),
            out_shape=[shape((units, slots), f32), back_shape],
            in_specs=[
                *[pl.BlockSpec((tile, piece), lambda i: (i, 0))] * 2,
                *weight_specs,
                by_slot,
            ],
            out_specs=[by_slot, pl.BlockSpec((experts, capacity), lambda i: (0, 0))],
            compiler_params=params(24),
            cost_estimate=cost(3),
            name="raw_part",
        )(*rows, weight, *got_weight, hidden_t)

    def raw_rest(rows, got_weight, raw, slot_gates):
        return pl.pallas_call(
            functools.partial(raw_kernel, half, halves),
            grid=(slots // tile,),
            out_shape=shape((units, slots), bf16),
            in_specs=[
                *[pl.BlockSpec((tile, piece), lambda i: (i, 0))] * 2,
                *weight_specs,
                by_slot,
                pl.BlockSpec((1, tile), lambda i: (0, i)),
            ],
            out_specs=by_slot,
            compiler_params=params(60),
            name="raw",
        )(*rows, weight, *got_weight, raw, slot_gates)

    def forward_columns(got_weight):
        return pl.pallas_call(
            functools.partial(forward_kernel, half, columns[1]),
            grid=(slots // tile,),
            out_shape=shape((slots, widths[1]), bf16),
            in_specs=[*weight_specs, by_slot],
            out_specs=by_row[1],
            compiler_params=params(24),
            cost_estimate=cost(3),
            name="hidden_weight",
        )(weight, *got_weight, hidden_t)

    def slot_grads(rows, forwarded, part):
        return pl.pallas_call(
            slot_grads_kernel,
            out_shape=back_shape,
            in_specs=[VMEM] * 4,
            out_specs=VMEM,
            compiler_params=params(24),
            name="slot_grads",
        )(*rows, forwarded, part)

    def finish(c, own, got, *before):
        spec = pl.BlockSpec((half // 2, widths[c] // 2), lambda i: (i, 0))
        return pl.pallas_call(
            finish_kernel,
            grid=(2,),
            out_shape=shape((half, model), bf16),
            in_specs=[spec] * 4 + [ANY] * len(before),
            out_specs=pl.BlockSpec((half // 2, widths[c]), lambda i: (i, c)),
            input_output_aliases={4: 0} if before else {},
            compiler_params=params(8),
            name="finish",
        )(*own, *got, *before)

    x0, x1 = pack()
    w = [swap(weight)]
    f0, y0 = forward(x0), across(x0)
    ff0, yf0 = forward(behind(f0, y0)), across(behind(f0, y0))
    r0 = backward(behind(x0, ff0, yf0))
    yff0 = across(behind(ff0, yf0))
    f1, yr0 = forward(behind(x1, r0)), across(behind(r0, yff0))
    r1 = backward(behind(x1, r0))
    mine0, theirs0, pmat, gslot = first_pick(
        [x0, y0, f0, yf0, ff0, yff0, r0, behind(yr0, w[0])]
    )
    ff1, yf1, y1 = forward(f1), across(behind(f1, yr0)), across(behind(x1, yr0))
    got = sibling(behind(theirs0, f1, r1))
    slot_gates, hs, rows_a, send_a, own_a = first_products(mine0, got, gslot)
    rows_b, send_b, own_b = later_products(piece, mine0, got, hs)
    rows0, send0, own0 = [rows_a, rows_b], [send_a, send_b], [own_a, own_b]
    got0 = [swap(part) for part in send0]
    yff1, ry1 = across(behind(ff1, *rows0)), backward(behind(y1, ff1, *rows0))
    forwarded = forward_columns(w)
    raw, part = raw_part(rows0, w)
    blocks = [x1, y1, f1, yf1, ff1, yff1, r1, ry1]
    rows1, own1, got1 = [], [], []
    for low in (0, piece):
        mine, theirs = later_pick(low, blocks, behind(pmat, raw, forwarded))
        if low > 0:
            theirs = behind(theirs, *got0)
        rows, send, own = later_products(0, mine, sibling(theirs), hs)
        rows1.append(rows)
        own1.append(own)
        got1.append(swap(send))

    back = slot_grads(rows1, forwarded, part)
    returned = lax.all_to_all(back, "expert", split_axis=0, concat_axis=0, tiled=True)
    grad_gates = pl.pallas_call(
        gates_kernel,
        grid=(1,),
        out_shape=shape((chosen, tokens), f32),
        in_specs=[
            pl.BlockSpec((chosen, tokens), lambda i: (0, 0)),
            pl.BlockSpec((2 * experts, tokens), lambda i: (0, widths[0] // tokens)),
            pl.BlockSpec((experts, capacity), lambda i: (0, 0)),
        ],
        out_specs=pl.BlockSpec((chosen, tokens), lambda i: (0, 0)),
        name="grad_gates",
    )(routes_t, x0, returned)

    grad_hidden = raw_rest(rows1, w, raw, slot_gates)
    grad_weight = finish(0, [behind(own0[0], back), own0[1]], got0)
    grad_weight = finish(1, own1, got1, grad_weight)
    return grad_weight[None], grad_hidden.T[None, None], grad_gates.T


def shards(grad_out, gates, routes, hidden, down_weight):
    owners = lax.axis_size("expert")
    token_count, chosen = routes.shape
    width = grad_out.shape[1]
    slots = hidden.shape[2]
    capacity = slots // owners
    flat = routes.reshape(-1)
    onehot = (flat[:, None] == jnp.arange(owners, dtype=jnp.int32)[None, :]).astype(jnp.int32)
    before = jnp.cumsum(onehot, axis=0) - onehot
    slot = jnp.sum(before * onehot, axis=1)
    target = flat * capacity + slot
    send_rows = (
        jnp.zeros((owners * capacity, width), grad_out.dtype)
        .at[target]
        .set(jnp.repeat(grad_out, chosen, axis=0))
    )
    send_gate = jnp.zeros((owners * capacity,), gates.dtype).at[target].set(gates.reshape(-1))
    send_rows = send_rows.reshape(owners, capacity, width)
    send_gate = send_gate.reshape(owners, capacity)
    saved = hidden[0, 0]
    local_weight = down_weight[0]
    contract = (((1,), (1,)), ((), ()))
    rows, gate_slots = (
        lax.all_to_all(send_rows, "expert", split_axis=0, concat_axis=0, tiled=True),
        lax.all_to_all(send_gate, "expert", split_axis=0, concat_axis=0, tiled=True),
    )
    rows = rows.reshape(slots, width)
    whole_weight = lax.all_gather(local_weight, "dp", axis=0, tiled=True)
    raw = lax.dot_general(rows, whole_weight, contract, preferred_element_type=jnp.float32)
    factor = gate_slots.reshape(slots, 1).astype(jnp.float32)
    grad_hidden = (factor * raw).astype(jnp.bfloat16)
    slot_grads = jnp.sum(raw * saved.astype(jnp.float32), axis=1)
    returned = lax.all_to_all(
        slot_grads.reshape(owners, capacity), "expert", split_axis=0, concat_axis=0, tiled=True
    )
    grad_gates = returned.reshape(-1)[target].reshape(token_count, chosen)
    scaled = (factor * rows.astype(jnp.float32)).astype(jnp.bfloat16)
    summed = lax.psum_scatter(
        lax.dot_general(
            saved, scaled, (((0,), (0,)), ((), ())), preferred_element_type=jnp.float32
        ).astype(jnp.bfloat16),
        "dp",
        scatter_dimension=0,
        tiled=True,
    )
    return (summed[None], grad_hidden[None, None], grad_gates)


def solution(mesh):
    small = mesh.shape["dp"] == 2 and mesh.shape["expert"] == NZ * NY * NC
    return jax.shard_map(
        ring_shards if small else shards,
        mesh=mesh,
        in_specs=(
            P(("dp", "expert"), None),
            P(("dp", "expert"), None),
            P(("dp", "expert"), None),
            P("dp", "expert", None, None),
            P("expert", "dp", None),
        ),
        out_specs=(
            P("expert", "dp", None),
            P("dp", "expert", None, None),
            P(("dp", "expert"), None),
        ),
        check_vma=False,
    )
```
